32 devices in a mesh: seq: 8 (over y, x, core), dp: 4 (over z).
Axes of the slice: x: 2, y: 2, z: 4, core: 2. Of those that a mesh axis runs over, the one named last changes fastest.
Arguments:
- inputs: bfloat16 [4, 8, 512, 512], P('dp', 'seq'), may hold values from -6 to 6
- norm_gain: float32 [512], replicated, may hold values from 0.25 to 1.75
- qkv_weight: bfloat16 [512, 1536], replicated, may hold values from -2 to 2
- out_weight: bfloat16 [512, 512], replicated, may hold values from -0.25 to 0.25
- out_cotan: bfloat16 [4, 8, 512, 512], P('dp', 'seq'), may hold values from -6 to 6
Outputs:
- input_grad: bfloat16 [4, 8, 512, 512], P('dp', 'seq')
- qkv_weight_grad: float32 [512, 1536], P('seq')
- out_weight_grad: float32 [512, 512], P('seq')
- gain_grad: float32 [512], P('seq')
The draws below stay inside these ranges and needn't reach their ends.
All inputs are finite; a program needn't handle non-finite values.
Results may differ from the reference program's by a relative error of at most 0.0091.
Values may be sent and summed in bfloat16 or wider, within the bound.
No kernel may reach another device: no remote copies, remote signals or barrier semaphores. Data moves between devices by JAX's collectives and lax.ppermute only.
A program may use at most 64 MiB of HBM per device.

```python
import math
import jax
import jax.numpy as jnp
from jax import lax

D = 512
H = 8
HD = 64
COLS = 512
NROWS = 8
BATCH = 4


def draw_qkv_weight(key, part):
    sampled = jax.random.normal(key, (D, 3 * D), jnp.float32) * D ** (-0.5)
    return jnp.clip(sampled, -2.0, 2.0).astype(jnp.bfloat16)


def strengthened(values, stream_key, source, target, shards_of, factor):
    def block_of(axis_at):
        return (jnp.arange(values.shape[axis_at]) // (values.shape[axis_at] // shards_of)).reshape((-1,) + (1,) * (values.ndim - 1 - axis_at))

    near = jax.random.permutation(stream_key, shards_of)[block_of(target)]
    other_side = (block_of(target) + shards_of // 2) % shards_of
    return jnp.where((block_of(source) == near) | (block_of(source) == other_side), factor * values, values)


def steps_of(own_key, dims, split, least, largest):
    def one(dim, blocks):
        heights = jax.random.uniform(jax.random.fold_in(jax.random.fold_in(own_key, 6), dim), (blocks,), jnp.float32, least / len(split), largest / len(split))
        return jnp.repeat(jnp.exp(heights), dims[dim] // blocks).reshape((-1,) + (1,) * (len(dims) - dim - 1))

    factor_of = one(*split[0])
    for cut in split[1:]:
        factor_of = factor_of * one(*cut)
    return factor_of


def gaussian(rng, shape, scale, limit, cuts=(), kind=jnp.bfloat16):
    entries = jax.random.normal(rng, shape, jnp.float32) * scale
    if len(cuts) > 0:
        entries = steps_of(rng, shape, cuts, -0.22, 0.18) * entries
    return jnp.clip(entries, min=-limit, max=limit).astype(kind)


def gaussian_with(key, dims, scale, reach, shards, heavy, kind=jnp.bfloat16):
    values = scale * jax.random.normal(key, dims, jnp.float32)
    if shards:
        values = values * steps_of(key, dims, shards, -0.22, 0.18)
    return jnp.clip(strengthened(values, jax.random.fold_in(key, 3), *heavy), -reach, reach).astype(kind)


def setup_inputs(seed: int = 0) -> dict:
    key_of = jax.random.split(jax.random.key(seed), 6)
    inputs = gaussian_with(key_of[0], (BATCH, NROWS, COLS, D), 1.0, 6.0, ((0, 4), (1, 8)), (1, 3, 8, 2.0))
    norm_gain = jnp.clip(1.0 + 0.15 * jax.random.normal(key_of[1], (D,), jnp.float32), 0.25, 1.75)
    qkv_weight = draw_qkv_weight(jax.random.fold_in(key_of[5], 71), 0)
    out_weight = gaussian(key_of[3], (D, D), D ** -0.5, 0.25)
    out_cotan = gaussian(key_of[4], (BATCH, NROWS, COLS, D), 1.0, 6.0, ((0, 4), (1, 8)))
    return {"inputs": inputs, "norm_gain": norm_gain, "qkv_weight": qkv_weight, "out_weight": out_weight, "out_cotan": out_cotan}


def blocked(kernel, arrays, group_size):
    block_count = arrays[0].shape[0] // group_size
    split_arrays = tuple((member.reshape((block_count, group_size) + member.shape[1:]) for member in arrays))
    result = lax.map(lambda pieces: kernel(*pieces), split_arrays)
    return jax.tree.map(lambda member: member.reshape((block_count * group_size,) + member.shape[2:]), result)

def attend_probs(queries, key_vals):
    score_scale = HD ** (-0.5)
    scores = jnp.einsum('glhd,gmhd->ghlm', queries.astype(jnp.float32), key_vals.astype(jnp.float32)) * score_scale
    length = queries.shape[1]
    causal = lax.broadcasted_iota(jnp.int32, (length, length), 0) >= lax.broadcasted_iota(jnp.int32, (length, length), 1)
    scores = jnp.where(causal, scores, -1e+30)
    row_max = lax.optimization_barrier(jnp.max(scores, -1, keepdims=True))
    exponent = jnp.exp(scores - row_max)
    return exponent / lax.optimization_barrier(jnp.sum(exponent, -1, keepdims=True))

def forward_block(queries, key_vals, values):
    weights = attend_probs(queries, key_vals).astype(jnp.bfloat16)
    return jnp.einsum('ghlm,gmhd->glhd', weights.astype(jnp.float32), values.astype(jnp.float32)).astype(jnp.bfloat16)

def backward_block(queries, key_vals, values, attended, cotangent):
    score_scale = HD ** (-0.5)
    softmax_probs = attend_probs(queries, key_vals)
    weights = softmax_probs.astype(jnp.bfloat16)
    cot_float = cotangent.astype(jnp.float32)
    prob_grad = jnp.einsum('glhd,gmhd->ghlm', cot_float, values.astype(jnp.float32))
    row_delta = lax.optimization_barrier(jnp.sum(cot_float * attended.astype(jnp.float32), -1))
    row_delta = jnp.transpose(row_delta, (0, 2, 1))[..., None]
    score_grad = (softmax_probs * (prob_grad - row_delta)).astype(jnp.bfloat16).astype(jnp.float32)
    grad_query = (jnp.einsum('ghlm,gmhd->glhd', score_grad, key_vals.astype(jnp.float32)) * score_scale).astype(jnp.bfloat16)
    grad_keys = (jnp.einsum('ghlm,glhd->gmhd', score_grad, queries.astype(jnp.float32)) * score_scale).astype(jnp.bfloat16)
    grad_values = jnp.einsum('ghlm,glhd->gmhd', weights.astype(jnp.float32), cot_float).astype(jnp.bfloat16)
    return (grad_query, grad_keys, grad_values)

def one_sequence(seq_input, norm_gain, qkv_weight, out_weight, seq_cotan):
    half_heads = H // 2
    tokens = NROWS * COLS
    flat_input = seq_input.reshape(tokens, D).astype(jnp.float32)
    inverse_rms = lax.rsqrt(lax.optimization_barrier(jnp.mean(flat_input * flat_input, -1, keepdims=True)) + 1e-05)
    normed = flat_input * inverse_rms
    hidden = (normed * norm_gain).astype(jnp.bfloat16)
    projected = jnp.dot(hidden, qkv_weight, preferred_element_type=jnp.float32).astype(jnp.bfloat16)
    flat_cotan = seq_cotan.reshape(tokens, D)
    grad_att = jnp.dot(flat_cotan, out_weight.T, preferred_element_type=jnp.float32).astype(jnp.bfloat16)
    qkv_grid = projected.reshape(NROWS, COLS, 3, H, HD)
    att_cot_grid = grad_att.reshape(NROWS, COLS, H, HD)
    row_group = math.gcd(NROWS, max(1, 512 // COLS))
    rows_in = (qkv_grid[:, :, 0, :half_heads], qkv_grid[:, :, 1, :half_heads], qkv_grid[:, :, 2, :half_heads])
    row_att = blocked(forward_block, rows_in, row_group)
    row_grads = blocked(backward_block, rows_in + (row_att, att_cot_grid[:, :, :half_heads]), row_group)
    col_grid = jnp.swapaxes(qkv_grid[:, :, :, half_heads:], 0, 1)
    col_cot = jnp.swapaxes(att_cot_grid[:, :, half_heads:], 0, 1)
    col_group = math.gcd(COLS, max(1, 512 // NROWS))
    cols_in = (col_grid[:, :, 0], col_grid[:, :, 1], col_grid[:, :, 2])
    col_att = blocked(forward_block, cols_in, col_group)
    col_grads = blocked(backward_block, cols_in + (col_att, col_cot), col_group)
    attended = jnp.concatenate([row_att, jnp.swapaxes(col_att, 0, 1)], 2).reshape(tokens, D)
    row_dqkv = jnp.stack(row_grads, 2)
    col_dqkv = jnp.swapaxes(jnp.stack(col_grads, 2), 0, 1)
    grad_qkv = jnp.concatenate([row_dqkv, col_dqkv], 3).reshape(tokens, 3 * D)
    term_out = jnp.dot(attended.T, flat_cotan, preferred_element_type=jnp.float32)
    term_qkv = jnp.dot(hidden.T, grad_qkv, preferred_element_type=jnp.float32)
    grad_hidden = jnp.dot(grad_qkv, qkv_weight.T, preferred_element_type=jnp.float32)
    term_gain = lax.optimization_barrier(jnp.sum(grad_hidden * normed, 0))
    grad_normed = grad_hidden * norm_gain
    grad_input = inverse_rms * (grad_normed - normed * lax.optimization_barrier(jnp.mean(grad_normed * normed, -1, keepdims=True)))
    seq_grad = (flat_cotan.astype(jnp.float32) + grad_input).astype(jnp.bfloat16).reshape(NROWS, COLS, D)
    return (seq_grad, term_qkv, term_out, term_gain)

def reference(inputs, norm_gain, qkv_weight, out_weight, out_cotan):
    outputs = []
    total_qkv = jnp.zeros((D, 3 * D), jnp.float32)
    total_out = jnp.zeros((D, D), jnp.float32)
    total_gain = jnp.zeros((D,), jnp.float32)
    for seq_index in range(BATCH):
        seq_grad, term_qkv, term_out, term_gain = one_sequence(inputs[seq_index], norm_gain, qkv_weight, out_weight, out_cotan[seq_index])
        outputs.append(seq_grad)
        total_qkv = total_qkv + term_qkv
        total_out = total_out + term_out
        total_gain = total_gain + term_gain
    return (jnp.stack(outputs, 0), total_qkv, total_out, total_gain)
```

```python
import functools
import math

import jax
import jax.numpy as jnp
from jax import lax
from jax.experimental import pallas as pl
from jax.experimental.pallas import tpu as pltpu
from jax.sharding import PartitionSpec as P

H = 8
HD = 64
HH = H // 2
HW = HH * HD
SCALE = HD ** (-0.5)
F32 = jnp.float32
BF16 = jnp.bfloat16
GAIN_LANES = 128
QUERY_BLOCK = 128
VMEM_BYTES = 40 * 1024 * 1024


def dot_nn(a, b):
    return lax.dot_general(a, b, (((1,), (0,)), ((), ())), preferred_element_type=F32)


def dot_nt(a, b):
    return lax.dot_general(a, b, (((1,), (1,)), ((), ())), preferred_element_type=F32)


def rms_parts(x):
    inverse_rms = lax.rsqrt(jnp.mean(x * x, -1, keepdims=True) + 1e-05)
    return inverse_rms, x * inverse_rms


def head_step(q, k, v, g, qt, kt, vt, gt, mask):
    scores = jnp.where(mask, dot_nn(q, kt), -1e30)
    exponent = jnp.exp(scores - jnp.max(scores, -1, keepdims=True))
    probs = exponent * (1.0 / jnp.sum(exponent, -1, keepdims=True))
    weights = probs.astype(BF16)
    attended = dot_nn(weights, v).astype(BF16)
    delta = jnp.sum(g.astype(F32) * attended.astype(F32), -1, keepdims=True)
    score_grad = (probs * (dot_nn(g, vt) - delta)).astype(BF16)
    grad_q = (dot_nn(score_grad, k) * SCALE).astype(BF16)
    return attended, grad_q, dot_nn(qt, score_grad), dot_nn(gt, weights)


def part_columns(width, second):
    return [slice(i * width + second * HW, i * width + (second + 1) * HW) for i in range(3)]


def project(hidden, cot, wqkv_ref, wout_ref, second):
    parts = part_columns(wqkv_ref.shape[0], second)
    q, k, v = [dot_nn(hidden, wqkv_ref[:, cols]).astype(BF16) for cols in parts]
    g = dot_nt(cot, wout_ref[second * HW : (second + 1) * HW, :]).astype(BF16)
    return q * jnp.asarray(SCALE, BF16), k, v, g


def weight_terms(hidden, normed, cot, attended, grads, wqkv_ref, second):
    hidden_t = hidden.T
    parts = part_columns(wqkv_ref.shape[0], second)
    term_qkv = [dot_nn(hidden_t, grad) for grad in grads]
    term_out = dot_nn(attended.T, cot)
    grad_hidden = dot_nt(grads[0], wqkv_ref[:, parts[0]])
    grad_hidden += dot_nt(grads[1], wqkv_ref[:, parts[1]])
    grad_hidden += dot_nt(grads[2], wqkv_ref[:, parts[2]])
    term_gain = jnp.sum(grad_hidden * normed, 0, keepdims=True)
    return term_qkv, term_out, grad_hidden, term_gain


def row_kernel(
    x_ref, cot_ref, gain_ref, wqkv_ref, wout_ref,
    qkv_ref, out_ref, hidden_ref, gain_term_ref,
    dkt_ref, dvt_ref,
):
    tokens = x_ref.shape[0]
    _, normed = rms_parts(x_ref[...].astype(F32))
    hidden = (normed * gain_ref[...]).astype(BF16)
    cot = cot_ref[...]
    q, k, v, g = project(hidden, cot, wqkv_ref, wout_ref, 0)
    qt, kt, vt, gt = q.T, k.T, v.T, g.T
    dkt_ref[...] = jnp.zeros_like(dkt_ref)
    dvt_ref[...] = jnp.zeros_like(dvt_ref)
    step = math.gcd(tokens, QUERY_BLOCK)
    att_blocks, dq_blocks = [], []
    for start in range(0, tokens, step):
        rows, keys = slice(start, start + step), slice(0, start + step)
        shape = (step, start + step)
        mask = (
            lax.broadcasted_iota(jnp.int32, shape, 0) + start
            >= lax.broadcasted_iota(jnp.int32, shape, 1)
        )
        atts, dqs = [], []
        for head in range(HH):
            lanes = slice(head * HD, (head + 1) * HD)
            attended, dq, dkt, dvt = head_step(
                q[rows, lanes], k[keys, lanes], v[keys, lanes], g[rows, lanes],
                qt[lanes, rows], kt[lanes, keys], vt[lanes, keys], gt[lanes, rows], mask,
            )
            dkt_ref[lanes, keys] += dkt
            dvt_ref[lanes, keys] += dvt
            atts.append(attended)
            dqs.append(dq)
        att_blocks.append(jnp.concatenate(atts, 1))
        dq_blocks.append(jnp.concatenate(dqs, 1))
    attended = jnp.concatenate(att_blocks, 0)
    grads = (
        jnp.concatenate(dq_blocks, 0),
        dkt_ref[...].astype(BF16).T,
        dvt_ref[...].astype(BF16).T,
    )
    term_qkv, term_out, grad_hidden, term_gain = weight_terms(
        hidden, normed, cot, attended, grads, wqkv_ref, 0
    )
    for i in range(3):
        qkv_ref[:, i * HW : (i + 1) * HW] = term_qkv[i].astype(BF16)
    out_ref[...] = term_out.astype(BF16)
    hidden_ref[...] = grad_hidden
    gain_term_ref[...] = term_gain


def column_kernel(
    moved_ref, gain_ref, wqkv_ref, wout_ref, row_out_ref, row_gain_ref,
    back_ref, terms_ref,
):
    all_rows, _, share, width = moved_ref.shape
    group = math.gcd(share, 16)
    block = all_rows * group
    starts = range(0, share, group)

    def gathered(which):
        pieces = []
        for start in starts:
            piece = moved_ref[:, which, start : start + group, :]
            pieces.append(piece.astype(F32).reshape(block, width))
        return jnp.concatenate(pieces, 0)

    _, normed = rms_parts(gathered(0))
    hidden = (normed * gain_ref[...]).astype(BF16)
    cot = gathered(1).astype(BF16)
    q, k, v, g = project(hidden, cot, wqkv_ref, wout_ref, 1)
    qt, kt, vt, gt = q.T, k.T, v.T, g.T
    query = lax.broadcasted_iota(jnp.int32, (block, block), 0)
    key = lax.broadcasted_iota(jnp.int32, (block, block), 1)
    mask = (query >= key) & (query % group == key % group)
    att_blocks, dq_blocks, dkt_blocks, dvt_blocks = [], [], [], []
    for start in range(0, all_rows * share, block):
        rows = slice(start, start + block)
        results = []
        for head in range(HH):
            lanes = slice(head * HD, (head + 1) * HD)
            results.append(
                head_step(
                    q[rows, lanes], k[rows, lanes], v[rows, lanes], g[rows, lanes],
                    qt[lanes, rows], kt[lanes, rows], vt[lanes, rows], gt[lanes, rows], mask,
                )
            )
        att_blocks.append(jnp.concatenate([r[0] for r in results], 1))
        dq_blocks.append(jnp.concatenate([r[1] for r in results], 1))
        dkt_blocks.append(jnp.concatenate([r[2] for r in results], 0))
        dvt_blocks.append(jnp.concatenate([r[3] for r in results], 0))
    attended = jnp.concatenate(att_blocks, 0)
    grads = (
        jnp.concatenate(dq_blocks, 0),
        jnp.concatenate(dkt_blocks, 1).astype(BF16).T,
        jnp.concatenate(dvt_blocks, 1).astype(BF16).T,
    )
    term_qkv, term_out, grad_hidden, term_gain = weight_terms(
        hidden, normed, cot, attended, grads, wqkv_ref, 1
    )
    for i, start in enumerate(starts):
        piece = grad_hidden[i * block : (i + 1) * block].reshape(all_rows, group, width)
        back_ref[:, start : start + group, :] = piece.astype(BF16)
    for i in range(3):
        terms_ref[:, i * HW : (i + 1) * HW] = term_qkv[i].astype(BF16)
    out_lanes = slice(3 * HW, 3 * HW + width)
    terms_ref[:HW, out_lanes] = row_out_ref[...]
    terms_ref[HW:, out_lanes] = term_out.astype(BF16)
    gain = jnp.broadcast_to(term_gain + row_gain_ref[...], (GAIN_LANES, width)).T
    terms_ref[:, 3 * HW + width :] = split_gain(gain)


def split_gain(gain):
    lane = lax.broadcasted_iota(jnp.int32, gain.shape, 1)
    rounded = gain.astype(BF16).astype(F32)
    return jnp.where(lane < GAIN_LANES // 2, rounded, gain - rounded).astype(BF16)


def joined_gain(pairs):
    return pairs[:, :1] + pairs[:, GAIN_LANES // 2 : GAIN_LANES // 2 + 1]


def input_kernel(x_ref, cot_ref, gain_ref, row_ref, col_ref, grad_ref):
    inverse_rms, normed = rms_parts(x_ref[...].astype(F32))
    grad_normed = (row_ref[...] + col_ref[...].astype(F32)) * gain_ref[...]
    projected = jnp.mean(grad_normed * normed, -1, keepdims=True)
    grad = inverse_rms * (grad_normed - normed * projected)
    grad_ref[...] = (cot_ref[...].astype(F32) + grad).astype(BF16)


def call(kernel, name, outs, scratch=(), flops=0, args=()):
    size = sum(math.prod(a.shape) * a.dtype.itemsize for a in (*args, *outs))
    return pl.pallas_call(
        kernel,
        out_shape=outs,
        in_specs=[pl.BlockSpec(memory_space=pltpu.VMEM)] * len(args),
        out_specs=[pl.BlockSpec(memory_space=pltpu.VMEM)] * len(outs),
        scratch_shapes=scratch,
        name=name,
        cost_estimate=pl.CostEstimate(flops=flops, bytes_accessed=size, transcendentals=0),
        compiler_params=pltpu.CompilerParams(vmem_limit_bytes=VMEM_BYTES),
    )(*args)


def body(inputs, norm_gain, qkv_weight, out_weight, out_cotan):
    columns, width = inputs.shape[2:]
    n = lax.axis_size("seq")
    m = lax.axis_size("dp")
    share = columns // n
    row_share = width // n
    x = inputs.reshape(columns, width)
    cot = out_cotan.reshape(columns, width)
    gain = norm_gain.reshape(1, width)

    outgoing = jnp.stack([x.reshape(n, share, width), cot.reshape(n, share, width)], 1)
    moved = lax.all_to_all(outgoing, "seq", split_axis=0, concat_axis=0, tiled=True)

    shaped = jax.ShapeDtypeStruct
    row_qkv, row_out, row_hidden, row_gain = call(
        row_kernel,
        "row_heads",
        [
            shaped((width, 3 * HW), BF16),
            shaped((HW, width), BF16),
            shaped((columns, width), F32),
            shaped((1, width), F32),
        ],
        [pltpu.VMEM((HW, columns), F32), pltpu.VMEM((HW, columns), F32)],
        6_000_000_000,
        (x, cot, gain, qkv_weight, out_weight),
    )
    row_terms = lax.all_to_all(
        row_qkv.reshape(n, row_share, 3 * HW), "seq", split_axis=0, concat_axis=0, tiled=True
    )
    term_width = 3 * HW + width + GAIN_LANES
    back, col_terms = call(
        column_kernel,
        "column_heads",
        [shaped((n, share, width), BF16), shaped((width, term_width), BF16)],
        (),
        4_000_000_000,
        (moved, gain, qkv_weight, out_weight, row_out, row_gain),
    )
    returned = lax.all_to_all(back, "seq", split_axis=0, concat_axis=0, tiled=True)
    col_terms = lax.all_to_all(
        col_terms.reshape(n, row_share, term_width), "seq", split_axis=0, concat_axis=0, tiled=True
    )
    (input_grad,) = call(
        input_kernel,
        "input_grad",
        [shaped((columns, width), BF16)],
        (),
        10_000_000,
        (x, cot, gain, row_hidden, returned.reshape(columns, width)),
    )

    row_sum = jnp.sum(row_terms.astype(F32), 0)
    col_sum = jnp.sum(col_terms.astype(F32), 0)

    def over_dp(total, has_gain):
        for distance in (1, 2):
            sent = total.astype(BF16)
            if has_gain:
                sent = jnp.concatenate(
                    [sent[:, :-GAIN_LANES], split_gain(jnp.broadcast_to(joined_gain(total[:, -GAIN_LANES:]), (row_share, GAIN_LANES)))], 1
                )
            got = lax.ppermute(sent, "dp", [(i, i ^ distance) for i in range(m)])
            total = sent.astype(F32) + got.astype(F32)
        return total

    row_sum = over_dp(row_sum, False)
    col_sum = over_dp(col_sum, True)
    sum_qkv = jnp.concatenate(
        [part for i in range(3) for part in (row_sum[:, i * HW : (i + 1) * HW], col_sum[:, i * HW : (i + 1) * HW])], 1
    )
    sum_out = col_sum[:, 3 * HW : 3 * HW + width]
    sum_gain = joined_gain(col_sum[:, -GAIN_LANES:]).reshape(row_share)
    return (input_grad.reshape(inputs.shape), sum_qkv, sum_out, sum_gain)


def solution(mesh):
    return jax.shard_map(
        body,
        mesh=mesh,
        in_specs=(P("dp", "seq", None, None), P(), P(), P(), P("dp", "seq", None, None)),
        out_specs=(P("dp", "seq", None, None), P("seq", None), P("seq", None), P("seq")),
        check_vma=False,
    )
```

```python
import functools
import math

import jax
import jax.numpy as jnp
from jax import lax
from jax.experimental import pallas as pl
from jax.experimental.pallas import tpu as pltpu
from jax.sharding import PartitionSpec as P

H = 8
HD = 64
HH = H // 2
HW = HH * HD
SCALE = HD ** (-0.5)
F32 = jnp.float32
BF16 = jnp.bfloat16
GAIN_LANES = 128
QUERY_BLOCK = 128
VMEM_BYTES = 40 * 1024 * 1024


def dot_nn(a, b):
    return lax.dot_general(a, b, (((1,), (0,)), ((), ())), preferred_element_type=F32)


def dot_nt(a, b):
    return lax.dot_general(a, b, (((1,), (1,)), ((), ())), preferred_element_type=F32)


def rms_parts(x):
    inverse_rms = lax.rsqrt(jnp.mean(x * x, -1, keepdims=True) + 1e-05)
    return inverse_rms, x * inverse_rms


def transposed(x):
    block = math.gcd(x.shape[1], 256)
    eye = (
        lax.broadcasted_iota(jnp.int32, (block, block), 0)
        == lax.broadcasted_iota(jnp.int32, (block, block), 1)
    ).astype(F32).astype(BF16)
    parts = [
        dot_nt(eye, x[:, at : at + block]).astype(BF16) for at in range(0, x.shape[1], block)
    ]
    return parts[0] if len(parts) == 1 else jnp.concatenate(parts, 0)


def head_pair(x):
    lane = lax.broadcasted_iota(jnp.int32, x.shape, 1)
    zero = jnp.zeros_like(x)
    return jnp.concatenate([jnp.where(lane < HD, x, zero), jnp.where(lane < HD, zero, x)], 0)


def pair_step(q2, g2, gt, k, v, kt, vt, mask_at, mask):
    count = gt.shape[1]
    scores = dot_nt(k, q2)
    tail = jnp.where(mask, scores[mask_at:], -1e30)
    scores = tail if mask_at == 0 else jnp.concatenate([scores[:mask_at], tail], 0)
    exponent = jnp.exp(scores - jnp.max(scores, 0, keepdims=True))
    probs = exponent * (1.0 / jnp.sum(exponent, 0, keepdims=True))
    weights = probs.astype(BF16)
    both = dot_nn(vt, weights)
    attended = jnp.concatenate([both[:HD, :count], both[HD:, count:]], 0).astype(BF16)
    product = gt.astype(F32) * attended.astype(F32)
    delta = jnp.concatenate(
        [jnp.sum(product[:HD], 0, keepdims=True), jnp.sum(product[HD:], 0, keepdims=True)], 1
    )
    score_grad = (probs * (dot_nt(v, g2) - delta)).astype(BF16)
    both = dot_nn(kt, score_grad)
    grad_q = (jnp.concatenate([both[:HD, :count], both[HD:, count:]], 0) * SCALE).astype(BF16)
    return attended, grad_q, dot_nn(score_grad, q2), dot_nn(weights, g2)


def part_columns(width, second):
    return [slice(i * width + second * HW, i * width + (second + 1) * HW) for i in range(3)]


def project(hidden, cot, wqkv_ref, wout_ref, second):
    parts = part_columns(wqkv_ref.shape[0], second)
    q, k, v = [dot_nn(hidden, wqkv_ref[:, cols]).astype(BF16) for cols in parts]
    g = dot_nt(cot, wout_ref[second * HW : (second + 1) * HW, :]).astype(BF16)
    return q * jnp.asarray(SCALE, BF16), k, v, g


def weight_terms(hidden, normed, cot, attended_t, grads, wqkv_ref, second):
    hidden_t = transposed(hidden)
    parts = part_columns(wqkv_ref.shape[0], second)
    term_qkv = [dot_nn(hidden_t, grad) for grad in grads]
    term_out = dot_nn(attended_t, cot)
    grad_hidden = dot_nt(grads[0], wqkv_ref[:, parts[0]])
    grad_hidden += dot_nt(grads[1], wqkv_ref[:, parts[1]])
    grad_hidden += dot_nt(grads[2], wqkv_ref[:, parts[2]])
    term_gain = jnp.sum(grad_hidden * normed, 0, keepdims=True)
    return term_qkv, term_out, grad_hidden, term_gain


def row_kernel(
    x_ref, cot_ref, gain_ref, wqkv_ref, wout_ref,
    qkv_ref, out_ref, hidden_ref, gain_term_ref,
    dk_ref, dv_ref,
):
    tokens = x_ref.shape[0]
    _, normed = rms_parts(x_ref[...].astype(F32))
    hidden = (normed * gain_ref[...]).astype(BF16)
    cot = cot_ref[...]
    q, k, v, g = project(hidden, cot, wqkv_ref, wout_ref, 0)
    kt, vt, gt = transposed(k), transposed(v), transposed(g)
    dk_ref[...] = jnp.zeros_like(dk_ref)
    dv_ref[...] = jnp.zeros_like(dv_ref)
    step = math.gcd(tokens, QUERY_BLOCK)
    query = lax.broadcasted_iota(jnp.int32, (step, 2 * step), 1) % step
    mask = query >= lax.broadcasted_iota(jnp.int32, (step, 2 * step), 0)
    att_pairs, dq_pairs = [], []
    for pair in range(HH // 2):
        lanes = slice(pair * 2 * HD, (pair + 1) * 2 * HD)
        atts, dqs = [], []
        for start in range(0, tokens, step):
            rows, keys = slice(start, start + step), slice(0, start + step)
            attended, dq, dk, dv = pair_step(
                head_pair(q[rows, lanes]), head_pair(g[rows, lanes]), gt[lanes, rows],
                k[keys, lanes], v[keys, lanes], kt[lanes, keys], vt[lanes, keys], start, mask,
            )
            dk_ref[keys, lanes] += dk
            dv_ref[keys, lanes] += dv
            atts.append(attended)
            dqs.append(dq)
        att_pairs.append(jnp.concatenate(atts, 1))
        dq_pairs.append(jnp.concatenate(dqs, 1))
    attended = jnp.concatenate(att_pairs, 0)
    grads = (
        transposed(jnp.concatenate(dq_pairs, 0)),
        dk_ref[...].astype(BF16),
        dv_ref[...].astype(BF16),
    )
    term_qkv, term_out, grad_hidden, term_gain = weight_terms(
        hidden, normed, cot, attended, grads, wqkv_ref, 0
    )
    for i in range(3):
        qkv_ref[:, i * HW : (i + 1) * HW] = term_qkv[i].astype(BF16)
    out_ref[...] = term_out.astype(BF16)
    hidden_ref[...] = grad_hidden
    gain_term_ref[...] = term_gain


def column_kernel(
    moved_ref, gain_ref, wqkv_ref, wout_ref, row_out_ref, row_gain_ref,
    back_ref, terms_ref,
):
    all_rows, _, share, width = moved_ref.shape
    group = math.gcd(share, 16)
    block = all_rows * group
    starts = range(0, share, group)

    def gathered(which):
        pieces = []
        for start in starts:
            piece = moved_ref[:, which, start : start + group, :]
            pieces.append(piece.astype(F32).reshape(block, width))
        return jnp.concatenate(pieces, 0)

    _, normed = rms_parts(gathered(0))
    hidden = (normed * gain_ref[...]).astype(BF16)
    cot = gathered(1).astype(BF16)
    q, k, v, g = project(hidden, cot, wqkv_ref, wout_ref, 1)
    kt, vt, gt = transposed(k), transposed(v), transposed(g)
    query = lax.broadcasted_iota(jnp.int32, (block, 2 * block), 1) % block
    key = lax.broadcasted_iota(jnp.int32, (block, 2 * block), 0)
    mask = (query >= key) & (query % group == key % group)
    att_pairs, dq_pairs, dk_pairs, dv_pairs = [], [], [], []
    for pair in range(HH // 2):
        lanes = slice(pair * 2 * HD, (pair + 1) * 2 * HD)
        results = []
        for start in range(0, all_rows * share, block):
            rows = slice(start, start + block)
            results.append(
                pair_step(
                    head_pair(q[rows, lanes]), head_pair(g[rows, lanes]), gt[lanes, rows],
                    k[rows, lanes], v[rows, lanes], kt[lanes, rows], vt[lanes, rows], 0, mask,
                )
            )
        att_pairs.append(jnp.concatenate([r[0] for r in results], 1))
        dq_pairs.append(jnp.concatenate([r[1] for r in results], 1))
        dk_pairs.append(jnp.concatenate([r[2] for r in results], 0))
        dv_pairs.append(jnp.concatenate([r[3] for r in results], 0))
    attended = jnp.concatenate(att_pairs, 0)
    grads = (
        transposed(jnp.concatenate(dq_pairs, 0)),
        jnp.concatenate(dk_pairs, 1).astype(BF16),
        jnp.concatenate(dv_pairs, 1).astype(BF16),
    )
    term_qkv, term_out, grad_hidden, term_gain = weight_terms(
        hidden, normed, cot, attended, grads, wqkv_ref, 1
    )
    for i, start in enumerate(starts):
        piece = grad_hidden[i * block : (i + 1) * block].reshape(all_rows, group, width)
        back_ref[:, start : start + group, :] = piece.astype(BF16)
    for i in range(3):
        terms_ref[:, i * HW : (i + 1) * HW] = term_qkv[i].astype(BF16)
    out_lanes = slice(3 * HW, 3 * HW + width)
    terms_ref[:HW, out_lanes] = row_out_ref[...]
    terms_ref[HW:, out_lanes] = term_out.astype(BF16)
    gain = jnp.broadcast_to(term_gain + row_gain_ref[...], (GAIN_LANES, width)).T
    terms_ref[:, 3 * HW + width :] = split_gain(gain)


def split_gain(gain):
    lane = lax.broadcasted_iota(jnp.int32, gain.shape, 1)
    rounded = gain.astype(BF16).astype(F32)
    return jnp.where(lane < GAIN_LANES // 2, rounded, gain - rounded).astype(BF16)


def joined_gain(pairs):
    return pairs[:, :1] + pairs[:, GAIN_LANES // 2 : GAIN_LANES // 2 + 1]


def input_kernel(x_ref, cot_ref, gain_ref, row_ref, col_ref, grad_ref):
    inverse_rms, normed = rms_parts(x_ref[...].astype(F32))
    grad_normed = (row_ref[...] + col_ref[...].astype(F32)) * gain_ref[...]
    projected = jnp.mean(grad_normed * normed, -1, keepdims=True)
    grad = inverse_rms * (grad_normed - normed * projected)
    grad_ref[...] = (cot_ref[...].astype(F32) + grad).astype(BF16)


def call(kernel, name, outs, scratch=(), flops=0, args=()):
    size = sum(math.prod(a.shape) * a.dtype.itemsize for a in (*args, *outs))
    return pl.pallas_call(
        kernel,
        out_shape=outs,
        in_specs=[pl.BlockSpec(memory_space=pltpu.VMEM)] * len(args),
        out_specs=[pl.BlockSpec(memory_space=pltpu.VMEM)] * len(outs),
        scratch_shapes=scratch,
        name=name,
        cost_estimate=pl.CostEstimate(flops=flops, bytes_accessed=size, transcendentals=0),
        compiler_params=pltpu.CompilerParams(vmem_limit_bytes=VMEM_BYTES),
    )(*args)


def body(inputs, norm_gain, qkv_weight, out_weight, out_cotan):
    columns, width = inputs.shape[2:]
    n = lax.axis_size("seq")
    m = lax.axis_size("dp")
    share = columns // n
    row_share = width // n
    x = inputs.reshape(columns, width)
    cot = out_cotan.reshape(columns, width)
    gain = norm_gain.reshape(1, width)

    outgoing = jnp.stack([x.reshape(n, share, width), cot.reshape(n, share, width)], 1)
    moved = lax.all_to_all(outgoing, "seq", split_axis=0, concat_axis=0, tiled=True)

    shaped = jax.ShapeDtypeStruct
    row_qkv, row_out, row_hidden, row_gain = call(
        row_kernel,
        "row_heads",
        [
            shaped((width, 3 * HW), BF16),
            shaped((HW, width), BF16),
            shaped((columns, width), F32),
            shaped((1, width), F32),
        ],
        [pltpu.VMEM((columns, HW), F32), pltpu.VMEM((columns, HW), F32)],
        6_000_000_000,
        (x, cot, gain, qkv_weight, out_weight),
    )
    row_terms = lax.all_to_all(
        row_qkv.reshape(n, row_share, 3 * HW), "seq", split_axis=0, concat_axis=0, tiled=True
    )
    term_width = 3 * HW + width + GAIN_LANES
    back, col_terms = call(
        column_kernel,
        "column_heads",
        [shaped((n, share, width), BF16), shaped((width, term_width), BF16)],
        (),
        4_000_000_000,
        (moved, gain, qkv_weight, out_weight, row_out, row_gain),
    )
    returned = lax.all_to_all(back, "seq", split_axis=0, concat_axis=0, tiled=True)
    col_terms = lax.all_to_all(
        col_terms.reshape(n, row_share, term_width), "seq", split_axis=0, concat_axis=0, tiled=True
    )
    (input_grad,) = call(
        input_kernel,
        "input_grad",
        [shaped((columns, width), BF16)],
        (),
        10_000_000,
        (x, cot, gain, row_hidden, returned.reshape(columns, width)),
    )

    row_sum = jnp.sum(row_terms.astype(F32), 0)
    col_sum = jnp.sum(col_terms.astype(F32), 0)

    def over_dp(total, has_gain):
        for distance in (1, 2):
            sent = total.astype(BF16)
            if has_gain:
                sent = jnp.concatenate(
                    [sent[:, :-GAIN_LANES], split_gain(jnp.broadcast_to(joined_gain(total[:, -GAIN_LANES:]), (row_share, GAIN_LANES)))], 1
                )
            got = lax.ppermute(sent, "dp", [(i, i ^ distance) for i in range(m)])
            total = sent.astype(F32) + got.astype(F32)
        return total

    row_sum = over_dp(row_sum, False)
    col_sum = over_dp(col_sum, True)
    sum_qkv = jnp.concatenate(
        [part for i in range(3) for part in (row_sum[:, i * HW : (i + 1) * HW], col_sum[:, i * HW : (i + 1) * HW])], 1
    )
    sum_out = col_sum[:, 3 * HW : 3 * HW + width]
    sum_gain = joined_gain(col_sum[:, -GAIN_LANES:]).reshape(row_share)
    return (input_grad.reshape(inputs.shape), sum_qkv, sum_out, sum_gain)


def solution(mesh):
    return jax.shard_map(
        body,
        mesh=mesh,
        in_specs=(P("dp", "seq", None, None), P(), P(), P(), P("dp", "seq", None, None)),
        out_specs=(P("dp", "seq", None, None), P("seq", None), P("seq", None), P("seq")),
        check_vma=False,
    )
```

```python
import math

import jax
import jax.numpy as jnp
from jax import lax
from jax.experimental import pallas as pl
from jax.experimental.pallas import tpu as pltpu
from jax.sharding import PartitionSpec as P

H = 8
HD = 64
HH = H // 2
HW = HH * HD
SCALE = HD ** (-0.5)
F32 = jnp.float32
BF16 = jnp.bfloat16
QUERY_BLOCK = 128
BIG_VMEM = 32 * 1024 * 1024
SMALL_VMEM = 12 * 1024 * 1024
ANY = pl.BlockSpec(memory_space=pl.ANY)
VMEM = pl.BlockSpec(memory_space=pltpu.VMEM)
SMEM = pl.BlockSpec(memory_space=pltpu.SMEM)
shaped = jax.ShapeDtypeStruct


def dot_nn(a, b):
    return lax.dot_general(a, b, (((1,), (0,)), ((), ())), preferred_element_type=F32)


def dot_nt(a, b):
    return lax.dot_general(a, b, (((1,), (1,)), ((), ())), preferred_element_type=F32)


def rms_parts(x):
    inverse_rms = lax.rsqrt(jnp.mean(x * x, -1, keepdims=True) + 1e-05)
    return inverse_rms, x * inverse_rms


def transposed(x):
    block = math.gcd(x.shape[1], 256)
    eye = (
        lax.broadcasted_iota(jnp.int32, (block, block), 0)
        == lax.broadcasted_iota(jnp.int32, (block, block), 1)
    ).astype(F32).astype(BF16)
    parts = [
        dot_nt(eye, x[:, at : at + block]).astype(BF16) for at in range(0, x.shape[1], block)
    ]
    return parts[0] if len(parts) == 1 else jnp.concatenate(parts, 0)


def head_pair(x):
    lane = lax.broadcasted_iota(jnp.int32, x.shape, 1)
    zero = jnp.zeros_like(x)
    return jnp.concatenate([jnp.where(lane < HD, x, zero), jnp.where(lane < HD, zero, x)], 0)


def pair_step(q2, g2, gt, k, v, kt, vt, mask_at, mask):
    count = gt.shape[1]
    scores = dot_nt(k, q2)
    tail = jnp.where(mask, scores[mask_at:], -1e30)
    scores = tail if mask_at == 0 else jnp.concatenate([scores[:mask_at], tail], 0)
    exponent = jnp.exp(scores - jnp.max(scores, 0, keepdims=True))
    probs = exponent * (1.0 / jnp.sum(exponent, 0, keepdims=True))
    weights = probs.astype(BF16)
    both = dot_nn(vt, weights)
    attended = jnp.concatenate([both[:HD, :count], both[HD:, count:]], 0).astype(BF16)
    product = gt.astype(F32) * attended.astype(F32)
    delta = jnp.concatenate(
        [jnp.sum(product[:HD], 0, keepdims=True), jnp.sum(product[HD:], 0, keepdims=True)], 1
    )
    score_grad = (probs * (dot_nt(v, g2) - delta)).astype(BF16)
    both = dot_nn(kt, score_grad)
    grad_q = (jnp.concatenate([both[:HD, :count], both[HD:, count:]], 0) * SCALE).astype(BF16)
    return attended, grad_q, dot_nn(score_grad, q2), dot_nn(weights, g2)


def qkv_copies(wqkv_ref, w_ref, sems, second):
    width = wqkv_ref.shape[0]
    return [
        pltpu.make_async_copy(
            wqkv_ref.at[:, pl.ds(i * width + second * HW, HW)],
            w_ref.at[:, pl.ds(i * HW, HW)],
            sems.at[i],
        )
        for i in range(3)
    ]


def weight_copies(wqkv_ref, wout_ref, w_ref, wo_ref, sems, second):
    out_rows = wout_ref.at[pl.ds(second * HW, HW), :]
    return [
        *qkv_copies(wqkv_ref, w_ref, sems, second),
        pltpu.make_async_copy(out_rows, wo_ref, sems.at[3]),
    ]


def project(hidden, cot, w_ref, wo_ref):
    projected = dot_nn(hidden, w_ref[...]).astype(BF16)
    q, k, v = [projected[:, i * HW : (i + 1) * HW] for i in range(3)]
    g = dot_nt(cot, wo_ref[...]).astype(BF16)
    return q * jnp.asarray(SCALE, BF16), k, v, g


def row_kernel(
    x_any, cot_any, gain_ref, wqkv_any, wout_any,
    qkv_ref, out_ref, grads_ref,
    x_ref, cot_ref, w_ref, wo_ref, dk_ref, dv_ref, sems,
):
    copies = [
        pltpu.make_async_copy(x_any, x_ref, sems.at[4]),
        *weight_copies(wqkv_any, wout_any, w_ref, wo_ref, sems, 0),
        pltpu.make_async_copy(cot_any, cot_ref, sems.at[5]),
    ]
    for copy in copies:
        copy.start()
    dk_ref[...] = jnp.zeros_like(dk_ref)
    dv_ref[...] = jnp.zeros_like(dv_ref)
    copies[0].wait()
    tokens = x_ref.shape[0]
    _, normed = rms_parts(x_ref[...].astype(F32))
    hidden = (normed * gain_ref[...]).astype(BF16)
    hidden_t = transposed(hidden)
    for copy in copies[1:]:
        copy.wait()
    cot = cot_ref[...]
    q, k, v, g = project(hidden, cot, w_ref, wo_ref)
    kt, vt, gt = transposed(k), transposed(v), transposed(g)
    step = math.gcd(tokens, QUERY_BLOCK)
    query = lax.broadcasted_iota(jnp.int32, (step, 2 * step), 1) % step
    mask = query >= lax.broadcasted_iota(jnp.int32, (step, 2 * step), 0)
    att_pairs, dq_pairs = [], []
    for pair in range(HH // 2):
        lanes = slice(pair * 2 * HD, (pair + 1) * 2 * HD)
        atts, dqs = [], []
        for start in range(0, tokens, step):
            rows, keys = slice(start, start + step), slice(0, start + step)
            attended, dq, dk, dv = pair_step(
                head_pair(q[rows, lanes]), head_pair(g[rows, lanes]), gt[lanes, rows],
                k[keys, lanes], v[keys, lanes], kt[lanes, keys], vt[lanes, keys], start, mask,
            )
            dk_ref[keys, lanes] += dk
            dv_ref[keys, lanes] += dv
            atts.append(attended)
            dqs.append(dq)
        att_pairs.append(jnp.concatenate(atts, 1))
        dq_pairs.append(jnp.concatenate(dqs, 1))
    grads_ref[:, :HW] = transposed(jnp.concatenate(dq_pairs, 0))
    grads_ref[:, HW : 2 * HW] = dk_ref[...].astype(BF16)
    grads_ref[:, 2 * HW :] = dv_ref[...].astype(BF16)
    qkv_ref[...] = dot_nn(hidden_t, grads_ref[...]).astype(BF16)
    out_ref[...] = dot_nn(jnp.concatenate(att_pairs, 0), cot).astype(BF16)


def column_part(moved_ref, gain_ref, w_ref, wo_ref, weight_waits, grads_ref):
    all_rows, _, share, width = moved_ref.shape
    group = math.gcd(share, 16)
    block = all_rows * group

    def gathered(which):
        pieces = []
        for start in range(0, share, group):
            piece = moved_ref[:, which, start : start + group, :]
            if group % 16 == 0:
                pieces.append(piece.reshape(block, width))
            else:
                pieces.append(piece.astype(F32).reshape(block, width).astype(BF16))
        return jnp.concatenate(pieces, 0)

    _, normed = rms_parts(gathered(0).astype(F32))
    hidden = (normed * gain_ref[...]).astype(BF16)
    hidden_t = transposed(hidden)
    cot = gathered(1)
    for copy in weight_waits:
        copy.wait()
    q, k, v, g = project(hidden, cot, w_ref, wo_ref)
    kt, vt, gt = transposed(k), transposed(v), transposed(g)
    query = lax.broadcasted_iota(jnp.int32, (block, 2 * block), 1) % block
    key = lax.broadcasted_iota(jnp.int32, (block, 2 * block), 0)
    mask = (query >= key) & (query % group == key % group)
    att_pairs, dq_pairs = [], []
    for pair in range(HH // 2):
        lanes = slice(pair * 2 * HD, (pair + 1) * 2 * HD)
        atts, dqs = [], []
        for start in range(0, all_rows * share, block):
            rows = slice(start, start + block)
            attended, dq, dk, dv = pair_step(
                head_pair(q[rows, lanes]), head_pair(g[rows, lanes]), gt[lanes, rows],
                k[rows, lanes], v[rows, lanes], kt[lanes, rows], vt[lanes, rows], 0, mask,
            )
            grads_ref[rows, HW + lanes.start : HW + lanes.stop] = dk.astype(BF16)
            grads_ref[rows, 2 * HW + lanes.start : 2 * HW + lanes.stop] = dv.astype(BF16)
            atts.append(attended)
            dqs.append(dq)
        att_pairs.append(jnp.concatenate(atts, 1))
        dq_pairs.append(jnp.concatenate(dqs, 1))
    grads_ref[:, :HW] = transposed(jnp.concatenate(dq_pairs, 0))
    term_qkv = dot_nn(hidden_t, grads_ref[...]).astype(BF16)
    term_out = dot_nn(jnp.concatenate(att_pairs, 0), cot).astype(BF16)
    return term_qkv, term_out


def column_kernel(
    moved_any, gain_ref, wqkv_any, wout_any, row_qkv_ref, row_out_ref,
    terms_ref, grads_ref,
    moved_ref, w_ref, wo_ref, sems,
):
    copy = pltpu.make_async_copy(moved_any, moved_ref, sems.at[4])
    weights = weight_copies(wqkv_any, wout_any, w_ref, wo_ref, sems, 1)
    for one in (copy, *weights):
        one.start()
    copy.wait()
    term_qkv, term_out = column_part(moved_ref, gain_ref, w_ref, wo_ref, weights, grads_ref)
    width = terms_ref.shape[0]
    for i in range(3):
        at = i * width
        terms_ref[:, at : at + HW] = row_qkv_ref[:, i * HW : (i + 1) * HW]
        terms_ref[:, at + HW : at + 2 * HW] = term_qkv[:, i * HW : (i + 1) * HW]
    terms_ref[:HW, 3 * width :] = row_out_ref[...]
    terms_ref[HW:, 3 * width :] = term_out


def column_chip_kernel(
    place_ref, x_any, cot_any, own_any,
    near_1, near_2, near_3, far_1, far_2, far_3,
    gain_ref, wqkv_any, wout_any, row_qkv_ref, row_out_ref,
    send_ref, keep_ref, grads_ref,
    moved_ref, w_ref, wo_ref, sems,
):
    chip, core = place_ref[0], place_ref[1]
    share = moved_ref.shape[2]
    at = pl.multiple_of((chip * 2 + core) * share, share)
    half = pl.multiple_of(core * share, share)
    me, other = chip * 2 + core, chip * 2 + 1 - core
    copies = [
        pltpu.make_async_copy(x_any.at[pl.ds(at, share), :], moved_ref.at[me, 0], sems.at[4]),
        pltpu.make_async_copy(cot_any.at[pl.ds(at, share), :], moved_ref.at[me, 1], sems.at[5]),
        pltpu.make_async_copy(own_any, moved_ref.at[other], sems.at[6]),
    ]
    for i, (near, far) in enumerate(((near_1, far_1), (near_2, far_2), (near_3, far_3))):
        there = 2 * (chip ^ (i + 1))
        for j, (piece, row) in enumerate(((near, there + core), (far, there + 1 - core))):
            copies.append(
                pltpu.make_async_copy(
                    piece.at[:, pl.ds(half, share), :], moved_ref.at[row], sems.at[7 + 2 * i + j]
                )
            )
    weights = weight_copies(wqkv_any, wout_any, w_ref, wo_ref, sems, 1)
    for copy in (*copies, *weights):
        copy.start()
    for copy in copies:
        copy.wait()
    term_qkv, term_out = column_part(moved_ref, gain_ref, w_ref, wo_ref, weights, grads_ref)
    width = moved_ref.shape[3]
    first = core == 0

    def split(piece, chips, lanes):
        parts = piece.reshape(chips.stop - chips.start, 2, share, piece.shape[1])
        even, odd = parts[:, 0], parts[:, 1]
        send_ref[chips, :, lanes] = jnp.where(first, odd, even)
        keep_ref[chips, :, lanes] = jnp.where(first, even, odd)

    chips = send_ref.shape[0]
    for i in range(3):
        lanes = slice(i * HW, (i + 1) * HW)
        at = i * width
        split(row_qkv_ref[:, lanes], slice(0, chips), slice(at, at + HW))
        split(term_qkv[:, lanes], slice(0, chips), slice(at + HW, at + 2 * HW))
    split(row_out_ref[...], slice(0, chips // 2), slice(3 * width, 4 * width))
    split(term_out, slice(chips // 2, chips), slice(3 * width, 4 * width))


def back_kernel(grads_ref, wqkv_any, back_ref, w_ref, sems):
    copies = qkv_copies(wqkv_any, w_ref, sems, 1)
    for copy in copies:
        copy.start()
    for copy in copies:
        copy.wait()
    grad_hidden = dot_nt(grads_ref[...], w_ref[...])
    all_rows, share, width = back_ref.shape
    group = math.gcd(share, 16)
    block = all_rows * group
    for i in range(share // group):
        piece = grad_hidden[i * block : (i + 1) * block].reshape(all_rows, group, width)
        back_ref[:, i * group : (i + 1) * group, :] = piece.astype(BF16)


def input_kernel(x_ref, cot_ref, gain_ref, grads_ref, wqkv_any, back_ref, grad_ref, w_ref, sems):
    copies = qkv_copies(wqkv_any, w_ref, sems, 0)
    for copy in copies:
        copy.start()
    inverse_rms, normed = rms_parts(x_ref[...].astype(F32))
    for copy in copies:
        copy.wait()
    grad_hidden = dot_nt(grads_ref[...], w_ref[...]) + back_ref[...].astype(F32)
    grad_normed = grad_hidden * gain_ref[...]
    projected = jnp.mean(grad_normed * normed, -1, keepdims=True)
    grad = inverse_rms * (grad_normed - normed * projected)
    grad_ref[...] = (cot_ref[...].astype(F32) + grad).astype(BF16)


def pack_kernel(place_ref, x_any, cot_any, own_ref, off_1, off_2, off_3, sems):
    chip, core = place_ref[0], place_ref[1]
    share = own_ref.shape[1]
    at = pl.multiple_of((chip * 2 + 1 - core) * share, share)
    copies = []
    for which, source in enumerate((x_any, cot_any)):
        copies.append(
            pltpu.make_async_copy(
                source.at[pl.ds(at, share), :], own_ref.at[which], sems.at[which]
            )
        )
        for i, target in enumerate((off_1, off_2, off_3)):
            there = pl.multiple_of((chip ^ (i + 1)) * 2 * share, 2 * share)
            copies.append(
                pltpu.make_async_copy(
                    source.at[pl.ds(there, 2 * share), :],
                    target.at[which],
                    sems.at[2 + 2 * i + which],
                )
            )
    for copy in copies:
        copy.start()
    for copy in copies:
        copy.wait()


def chip_sum_kernel(place_ref, keep_ref, got_ref, own_ref, off_1, off_2, off_3):
    chip = place_ref[0]
    for i, target in enumerate((own_ref, off_1, off_2, off_3)):
        there = chip ^ i
        total = keep_ref[there].astype(F32) + got_ref[there].astype(F32)
        target[...] = total.astype(target.dtype)


def layer_sum_kernel(place_ref, own_ref, got_1, got_2, got_3, send_ref, keep_ref):
    upper = place_ref[2] == 1
    total = own_ref[...] + (
        (got_1[...].astype(F32) + got_2[...].astype(F32)) + got_3[...].astype(F32)
    )
    half = total.shape[0] // 2
    low, high = total[:half], total[half:]
    send_ref[...] = jnp.where(upper, low, high).astype(BF16)
    keep_ref[...] = jnp.where(upper, high, low)


def add_kernel(kept_ref, got_ref, out_ref):
    out_ref[...] = (kept_ref[...].astype(F32) + got_ref[...].astype(F32)).astype(BF16)


def result_kernel(place_ref, held_ref, got_ref, wqkv_any, gain_ref, qkv_ref, out_ref, grad_ref, w_ref, sem):
    rows = qkv_ref.shape[0]
    at = pl.multiple_of((place_ref[0] * 2 + place_ref[1]) * rows, rows)
    copy = pltpu.make_async_copy(wqkv_any.at[pl.ds(at, rows), :], w_ref, sem)
    copy.start()
    upper = place_ref[2] == 1
    held, got = held_ref[...].astype(F32), got_ref[...].astype(F32)
    half = rows // 2
    low, high = jnp.where(upper, got, held), jnp.where(upper, held, got)
    cut = qkv_ref.shape[1]
    qkv_ref[:half], qkv_ref[half:] = low[:, :cut], high[:, :cut]
    out_ref[:half], out_ref[half:] = low[:, cut:], high[:, cut:]
    copy.wait()
    total = jnp.sum(qkv_ref[...] * w_ref[...].astype(F32), -1, keepdims=True)
    grad_ref[...] = total / gain_ref[...]


def call(kernel, name, ins, outs, scratch=(), flops=0, vmem=SMALL_VMEM, out_specs=None):
    outs = [shaped(*out) for out in outs]
    args = [array for _, array in ins]
    size = sum(math.prod(a.shape) * a.dtype.itemsize for a in (*args, *outs))
    return pl.pallas_call(
        kernel,
        out_shape=outs,
        in_specs=[spec for spec, _ in ins],
        out_specs=out_specs or [VMEM] * len(outs),
        scratch_shapes=scratch,
        name=name,
        cost_estimate=pl.CostEstimate(flops=flops, bytes_accessed=size, transcendentals=0),
        compiler_params=pltpu.CompilerParams(vmem_limit_bytes=vmem),
    )(*args)


def body(inputs, norm_gain, qkv_weight, out_weight, out_cotan):
    columns, width = inputs.shape[2:]
    n = lax.axis_size("seq")
    m = lax.axis_size("dp")
    share = columns // n
    row_share = width // n
    term_width = 4 * width
    x = inputs.reshape(columns, width)
    cot = out_cotan.reshape(columns, width)
    gain = norm_gain.reshape(1, width)
    chips = 4
    layered = n == 2 * chips and m == 4 and row_share == share
    here = lax.axis_index("seq")
    place = jnp.stack([here // 2, here % 2, lax.axis_index("dp") % 2]).astype(jnp.int32)
    weight_scratch = [
        pltpu.VMEM((width, 3 * HW), BF16),
        pltpu.VMEM((HW, width), BF16),
    ]
    small_scratch = [pltpu.VMEM((width, 3 * HW), BF16), pltpu.SemaphoreType.DMA((3,))]

    def swap(array, axis, bits):
        count = lax.axis_size(axis)
        return lax.ppermute(array, axis, [(i, i ^ bits) for i in range(count)])

    if layered:
        packed = call(
            pack_kernel,
            "pack_columns",
            [(SMEM, place), (ANY, x), (ANY, cot)],
            [((2, share, width), BF16)] + [((2, 2 * share, width), BF16)] * 3,
            [pltpu.SemaphoreType.DMA((8,))],
            out_specs=[ANY] * 4,
        )
        near_3 = swap(packed[3], "seq", 6)
        near_1 = swap(packed[1], "seq", 2)
        near_2 = swap(packed[2], "seq", 4)
        own = swap(packed[0], "seq", 1)
    else:
        outgoing = jnp.stack([x.reshape(n, share, width), cot.reshape(n, share, width)], 1)
        moved = lax.all_to_all(outgoing, "seq", split_axis=0, concat_axis=0, tiled=True)

    row_qkv, row_out, row_grads = call(
        row_kernel,
        "row_heads",
        [(ANY, x), (ANY, cot), (VMEM, gain), (ANY, qkv_weight), (ANY, out_weight)],
        [((width, 3 * HW), BF16), ((HW, width), BF16), ((columns, 3 * HW), BF16)],
        [
            pltpu.VMEM((columns, width), BF16),
            pltpu.VMEM((columns, width), BF16),
            *weight_scratch,
            pltpu.VMEM((columns, HW), F32),
            pltpu.VMEM((columns, HW), F32),
            pltpu.SemaphoreType.DMA((6,)),
        ],
        5_000_000_000,
        BIG_VMEM,
    )
    moved_scratch = pltpu.VMEM((n, 2, share, width), BF16)
    if layered:
        near_1, near_2, near_3, row_qkv = lax.optimization_barrier((near_1, near_2, near_3, row_qkv))
        far_3, far_1, far_2 = swap(near_3, "seq", 1), swap(near_1, "seq", 1), swap(near_2, "seq", 1)
    shared = [
        (VMEM, gain), (ANY, qkv_weight), (ANY, out_weight), (VMEM, row_qkv), (VMEM, row_out),
    ]
    if layered:
        send, keep, col_grads = call(
            column_chip_kernel,
            "column_heads",
            [
                (SMEM, place), (ANY, x), (ANY, cot), (ANY, own),
                (ANY, near_1), (ANY, near_2), (ANY, near_3),
                (ANY, far_1), (ANY, far_2), (ANY, far_3), *shared,
            ],
            [((chips, row_share, term_width), BF16)] * 2 + [((columns, 3 * HW), BF16)],
            [moved_scratch, *weight_scratch, pltpu.SemaphoreType.DMA((13,))],
            4_000_000_000,
            BIG_VMEM,
        )
        got = swap(send, "seq", 1)
    else:
        terms, col_grads = call(
            column_kernel,
            "column_heads",
            [(ANY, moved), *shared],
            [((width, term_width), BF16), ((columns, 3 * HW), BF16)],
            [moved_scratch, *weight_scratch, pltpu.SemaphoreType.DMA((5,))],
            4_000_000_000,
            BIG_VMEM,
        )
    if layered:
        owned, off_1, off_2, off_3 = call(
            chip_sum_kernel,
            "add_cores",
            [(SMEM, place), (VMEM, keep), (VMEM, got)],
            [((row_share, term_width), F32)] + [((row_share, term_width), BF16)] * 3,
        )
        got_3 = swap(off_3, "seq", 6)
        got_1 = swap(off_1, "seq", 2)
        got_2 = swap(off_2, "seq", 4)
        col_grads, owned = lax.optimization_barrier((col_grads, owned))
    (back,) = call(
        back_kernel,
        "column_grad_hidden",
        [(VMEM, col_grads), (ANY, qkv_weight)],
        [((n, share, width), BF16)],
        small_scratch,
        400_000_000,
    )
    if layered:
        back, owned = lax.optimization_barrier((back, owned))
    returned = lax.all_to_all(back, "seq", split_axis=0, concat_axis=0, tiled=True)
    half_rows = (row_share // 2, term_width)
    if layered:
        to_next, kept = call(
            layer_sum_kernel,
            "add_chips",
            [(SMEM, place), (VMEM, owned), (VMEM, got_1), (VMEM, got_2), (VMEM, got_3)],
            [(half_rows, BF16), (half_rows, F32)],
        )
        from_next = swap(to_next, "dp", 1)
        (pair_sum,) = call(
            add_kernel, "add_pair", [(VMEM, kept), (VMEM, from_next)], [(half_rows, BF16)]
        )
        from_far = swap(pair_sum, "dp", 2)
        (held,) = call(
            add_kernel, "add_pairs", [(VMEM, pair_sum), (VMEM, from_far)], [(half_rows, BF16)]
        )
        other = swap(held, "dp", 1)
    (input_grad,) = call(
        input_kernel,
        "input_grad",
        [
            (VMEM, x), (VMEM, cot), (VMEM, gain), (VMEM, row_grads), (ANY, qkv_weight),
            (VMEM, returned.reshape(columns, width)),
        ],
        [((columns, width), BF16)],
        small_scratch,
        400_000_000,
    )
    own_gain = lax.dynamic_slice_in_dim(norm_gain, here * row_share, row_share, 0)
    if layered:
        sum_qkv, sum_out, sum_gain = call(
            result_kernel,
            "result",
            [
                (SMEM, place), (VMEM, held), (VMEM, other), (ANY, qkv_weight),
                (VMEM, own_gain.reshape(row_share, 1)),
            ],
            [((row_share, 3 * width), F32), ((row_share, width), F32), ((row_share, 1), F32)],
            [pltpu.VMEM((row_share, 3 * width), BF16), pltpu.SemaphoreType.DMA],
        )
        sum_gain = sum_gain.reshape(row_share)
    else:
        terms = lax.all_to_all(
            terms.reshape(n, row_share, term_width), "seq", split_axis=0, concat_axis=0, tiled=True
        )
        total = jnp.sum(terms.astype(F32), 0)
        for step in range(m.bit_length() - 1):
            sent = total.astype(BF16)
            total = sent.astype(F32) + swap(sent, "dp", 1 << step).astype(F32)
        sum_qkv, sum_out = total[:, : 3 * width], total[:, 3 * width :]
        own_weight = lax.dynamic_slice_in_dim(qkv_weight, here * row_share, row_share, 0)
        sum_gain = jnp.sum(sum_qkv * own_weight.astype(F32), -1) / own_gain
    return (input_grad.reshape(inputs.shape), sum_qkv, sum_out, sum_gain)


def solution(mesh):
    return jax.shard_map(
        body,
        mesh=mesh,
        in_specs=(P("dp", "seq", None, None), P(), P(), P(), P("dp", "seq", None, None)),
        out_specs=(P("dp", "seq", None, None), P("seq", None), P("seq", None), P("seq")),
        check_vma=False,
    )
```

```python
import math

import jax
import jax.numpy as jnp
from jax import lax
from jax.experimental import pallas as pl
from jax.experimental.pallas import tpu as pltpu
from jax.sharding import PartitionSpec as P

H = 8
HD = 64
HH = H // 2
HW = HH * HD
SCALE = HD ** (-0.5)
F32 = jnp.float32
BF16 = jnp.bfloat16
QUERY_BLOCK = 128
BIG_VMEM = 20 * 1024 * 1024
SMALL_VMEM = 8 * 1024 * 1024
ANY = pl.BlockSpec(memory_space=pl.ANY)
VMEM = pl.BlockSpec(memory_space=pltpu.VMEM)
SMEM = pl.BlockSpec(memory_space=pltpu.SMEM)
HBM = pl.BlockSpec(memory_space=pltpu.HBM)
shaped = jax.ShapeDtypeStruct


def dot_nn(a, b):
    return lax.dot_general(a, b, (((1,), (0,)), ((), ())), preferred_element_type=F32)


def dot_nt(a, b):
    return lax.dot_general(a, b, (((1,), (1,)), ((), ())), preferred_element_type=F32)


def rms_parts(x):
    inverse_rms = lax.rsqrt(jnp.mean(x * x, -1, keepdims=True) + 1e-05)
    return inverse_rms, x * inverse_rms


def transposed(x):
    block = math.gcd(x.shape[1], 256)
    eye = (
        lax.broadcasted_iota(jnp.int32, (block, block), 0)
        == lax.broadcasted_iota(jnp.int32, (block, block), 1)
    ).astype(F32).astype(BF16)
    parts = [
        dot_nt(eye, x[:, at : at + block]).astype(BF16) for at in range(0, x.shape[1], block)
    ]
    return parts[0] if len(parts) == 1 else jnp.concatenate(parts, 0)


def head_pair(x):
    lane = lax.broadcasted_iota(jnp.int32, x.shape, 1)
    zero = jnp.zeros_like(x)
    return jnp.concatenate([jnp.where(lane < HD, x, zero), jnp.where(lane < HD, zero, x)], 0)


def pair_step(q2, g2, gt, k, v, kt, vt, mask_at, mask):
    count = gt.shape[1]
    scores = dot_nt(k, q2)
    tail = jnp.where(mask, scores[mask_at:], -1e30)
    scores = tail if mask_at == 0 else jnp.concatenate([scores[:mask_at], tail], 0)
    exponent = jnp.exp(scores - jnp.max(scores, 0, keepdims=True))
    probs = exponent * (1.0 / jnp.sum(exponent, 0, keepdims=True))
    weights = probs.astype(BF16)
    both = dot_nn(vt, weights)
    attended = jnp.concatenate([both[:HD, :count], both[HD:, count:]], 0).astype(BF16)
    product = gt.astype(F32) * attended.astype(F32)
    delta = jnp.concatenate(
        [jnp.sum(product[:HD], 0, keepdims=True), jnp.sum(product[HD:], 0, keepdims=True)], 1
    )
    score_grad = (probs * (dot_nt(v, g2) - delta)).astype(BF16)
    both = dot_nn(kt, score_grad)
    grad_q = (jnp.concatenate([both[:HD, :count], both[HD:, count:]], 0) * SCALE).astype(BF16)
    return attended, grad_q, dot_nn(score_grad, q2), dot_nn(weights, g2)


def qkv_copies(wqkv_ref, w_ref, sems, second):
    width = wqkv_ref.shape[0]
    return [
        pltpu.make_async_copy(
            wqkv_ref.at[:, pl.ds(i * width + second * HW, HW)],
            w_ref.at[:, pl.ds(i * HW, HW)],
            sems.at[i],
        )
        for i in range(3)
    ]


def weight_copies(wqkv_ref, wout_ref, w_ref, wo_ref, sems, second):
    out_rows = wout_ref.at[pl.ds(second * HW, HW), :]
    return [
        *qkv_copies(wqkv_ref, w_ref, sems, second),
        pltpu.make_async_copy(out_rows, wo_ref, sems.at[3]),
    ]


def started(*copies):
    for copy in copies:
        copy.start()
    return copies


def finished(*copies):
    for copy in copies:
        copy.wait()


def project(hidden, cot, w_ref, wo_ref):
    projected = dot_nn(hidden, w_ref[...]).astype(BF16)
    q, k, v = [projected[:, i * HW : (i + 1) * HW] for i in range(3)]
    g = dot_nt(cot, wo_ref[...]).astype(BF16)
    return q * jnp.asarray(SCALE, BF16), k, v, g


def row_kernel(
    x_any, cot_any, gain_any, wqkv_any, wout_any,
    qkv_ref, out_ref, grads_any,
    x_ref, cot_ref, gain_ref, w_ref, wo_ref, dk_ref, dv_ref, grads_ref, sems,
):
    first = started(
        pltpu.make_async_copy(x_any, x_ref, sems.at[4]),
        pltpu.make_async_copy(gain_any, gain_ref, sems.at[5]),
    )
    later = started(
        *weight_copies(wqkv_any, wout_any, w_ref, wo_ref, sems, 0),
        pltpu.make_async_copy(cot_any, cot_ref, sems.at[6]),
    )
    dk_ref[...] = jnp.zeros_like(dk_ref)
    dv_ref[...] = jnp.zeros_like(dv_ref)
    finished(*first)
    tokens = x_ref.shape[0]
    _, normed = rms_parts(x_ref[...].astype(F32))
    hidden = (normed * gain_ref[...]).astype(BF16)
    hidden_t = transposed(hidden)
    finished(*later)
    cot = cot_ref[...]
    q, k, v, g = project(hidden, cot, w_ref, wo_ref)
    kt, vt, gt = transposed(k), transposed(v), transposed(g)
    step = math.gcd(tokens, QUERY_BLOCK)
    query = lax.broadcasted_iota(jnp.int32, (step, 2 * step), 1) % step
    mask = query >= lax.broadcasted_iota(jnp.int32, (step, 2 * step), 0)
    att_pairs, dq_pairs = [], []
    for pair in range(HH // 2):
        lanes = slice(pair * 2 * HD, (pair + 1) * 2 * HD)
        atts, dqs = [], []
        for start in range(0, tokens, step):
            rows, keys = slice(start, start + step), slice(0, start + step)
            attended, dq, dk, dv = pair_step(
                head_pair(q[rows, lanes]), head_pair(g[rows, lanes]), gt[lanes, rows],
                k[keys, lanes], v[keys, lanes], kt[lanes, keys], vt[lanes, keys], start, mask,
            )
            dk_ref[keys, lanes] += dk
            dv_ref[keys, lanes] += dv
            atts.append(attended)
            dqs.append(dq)
        att_pairs.append(jnp.concatenate(atts, 1))
        dq_pairs.append(jnp.concatenate(dqs, 1))
    grads_ref[:, :HW] = transposed(jnp.concatenate(dq_pairs, 0))
    grads_ref[:, HW : 2 * HW] = dk_ref[...].astype(BF16)
    grads_ref[:, 2 * HW :] = dv_ref[...].astype(BF16)
    handed = started(pltpu.make_async_copy(grads_ref, grads_any, sems.at[4]))
    qkv_ref[...] = dot_nn(hidden_t, grads_ref[...]).astype(BF16)
    out_ref[...] = dot_nn(jnp.concatenate(att_pairs, 0), cot).astype(BF16)
    finished(*handed)


def column_part(moved_ref, gain_ref, w_ref, wo_ref, weight_waits, grads_ref):
    all_rows, _, share, width = moved_ref.shape
    group = math.gcd(share, 16)
    block = all_rows * group

    def gathered(which):
        pieces = []
        for start in range(0, share, group):
            piece = moved_ref[:, which, start : start + group, :]
            if group % 16 == 0:
                pieces.append(piece.reshape(block, width))
            else:
                pieces.append(piece.astype(F32).reshape(block, width).astype(BF16))
        return jnp.concatenate(pieces, 0)

    _, normed = rms_parts(gathered(0).astype(F32))
    hidden = (normed * gain_ref[...]).astype(BF16)
    hidden_t = transposed(hidden)
    cot = gathered(1)
    finished(*weight_waits)
    q, k, v, g = project(hidden, cot, w_ref, wo_ref)
    kt, vt, gt = transposed(k), transposed(v), transposed(g)
    query = lax.broadcasted_iota(jnp.int32, (block, 2 * block), 1) % block
    key = lax.broadcasted_iota(jnp.int32, (block, 2 * block), 0)
    mask = (query >= key) & (query % group == key % group)
    att_pairs, dq_pairs = [], []
    for pair in range(HH // 2):
        lanes = slice(pair * 2 * HD, (pair + 1) * 2 * HD)
        atts, dqs = [], []
        for start in range(0, all_rows * share, block):
            rows = slice(start, start + block)
            attended, dq, dk, dv = pair_step(
                head_pair(q[rows, lanes]), head_pair(g[rows, lanes]), gt[lanes, rows],
                k[rows, lanes], v[rows, lanes], kt[lanes, rows], vt[lanes, rows], 0, mask,
            )
            grads_ref[rows, HW + lanes.start : HW + lanes.stop] = dk.astype(BF16)
            grads_ref[rows, 2 * HW + lanes.start : 2 * HW + lanes.stop] = dv.astype(BF16)
            atts.append(attended)
            dqs.append(dq)
        att_pairs.append(jnp.concatenate(atts, 1))
        dq_pairs.append(jnp.concatenate(dqs, 1))
    grads_ref[:, :HW] = transposed(jnp.concatenate(dq_pairs, 0))
    term_qkv = dot_nn(hidden_t, grads_ref[...]).astype(BF16)
    term_out = dot_nn(jnp.concatenate(att_pairs, 0), cot).astype(BF16)
    return term_qkv, term_out


def column_kernel(
    moved_any, gain_any, wqkv_any, wout_any, row_qkv_ref, row_out_ref,
    terms_ref, grads_ref,
    moved_ref, gain_ref, w_ref, wo_ref, sems,
):
    copies = started(
        pltpu.make_async_copy(moved_any, moved_ref, sems.at[4]),
        pltpu.make_async_copy(gain_any, gain_ref, sems.at[5]),
    )
    weights = started(*weight_copies(wqkv_any, wout_any, w_ref, wo_ref, sems, 1))
    finished(*copies)
    term_qkv, term_out = column_part(moved_ref, gain_ref, w_ref, wo_ref, weights, grads_ref)
    width = terms_ref.shape[0]
    for i in range(3):
        at = i * width
        terms_ref[:, at : at + HW] = row_qkv_ref[:, i * HW : (i + 1) * HW]
        terms_ref[:, at + HW : at + 2 * HW] = term_qkv[:, i * HW : (i + 1) * HW]
    terms_ref[:HW, 3 * width :] = row_out_ref[...]
    terms_ref[HW:, 3 * width :] = term_out


def column_chip_kernel(
    place_ref, x_any, cot_any, own_any,
    near_1, near_2, near_3, far_1, far_2, far_3,
    gain_any, wqkv_any, wout_any, row_qkv_ref, row_out_ref,
    send_ref, keep_ref, grads_ref,
    moved_ref, gain_ref, w_ref, wo_ref, sems,
):
    chip, core = place_ref[0], place_ref[1]
    share = moved_ref.shape[2]
    at = pl.multiple_of((chip * 2 + core) * share, share)
    half = pl.multiple_of(core * share, share)
    me, other = chip * 2 + core, chip * 2 + 1 - core
    copies = [
        pltpu.make_async_copy(x_any.at[pl.ds(at, share), :], moved_ref.at[me, 0], sems.at[4]),
        pltpu.make_async_copy(cot_any.at[pl.ds(at, share), :], moved_ref.at[me, 1], sems.at[5]),
        pltpu.make_async_copy(own_any, moved_ref.at[other], sems.at[6]),
        pltpu.make_async_copy(gain_any, gain_ref, sems.at[13]),
    ]
    for i, (near, far) in enumerate(((near_1, far_1), (near_2, far_2), (near_3, far_3))):
        there = 2 * (chip ^ (i + 1))
        for j, (piece, row) in enumerate(((near, there + core), (far, there + 1 - core))):
            copies.append(
                pltpu.make_async_copy(
                    piece.at[:, pl.ds(half, share), :], moved_ref.at[row], sems.at[7 + 2 * i + j]
                )
            )
    started(*copies)
    weights = started(*weight_copies(wqkv_any, wout_any, w_ref, wo_ref, sems, 1))
    finished(*copies)
    term_qkv, term_out = column_part(moved_ref, gain_ref, w_ref, wo_ref, weights, grads_ref)
    width = moved_ref.shape[3]
    first = core == 0

    def split(piece, chips, lanes):
        parts = piece.reshape(chips.stop - chips.start, 2, share, piece.shape[1])
        even, odd = parts[:, 0], parts[:, 1]
        send_ref[chips, :, lanes] = jnp.where(first, odd, even)
        keep_ref[chips, :, lanes] = jnp.where(first, even, odd)

    chips = send_ref.shape[0]
    for i in range(3):
        lanes = slice(i * HW, (i + 1) * HW)
        at = i * width
        split(row_qkv_ref[:, lanes], slice(0, chips), slice(at, at + HW))
        split(term_qkv[:, lanes], slice(0, chips), slice(at + HW, at + 2 * HW))
    split(row_out_ref[...], slice(0, chips // 2), slice(3 * width, 4 * width))
    split(term_out, slice(chips // 2, chips), slice(3 * width, 4 * width))


def back_kernel(grads_ref, wqkv_any, back_ref, w_ref, sems):
    finished(*started(*qkv_copies(wqkv_any, w_ref, sems, 1)))
    grad_hidden = dot_nt(grads_ref[...], w_ref[...])
    all_rows, share, width = back_ref.shape
    group = math.gcd(share, 16)
    block = all_rows * group
    for i in range(share // group):
        piece = grad_hidden[i * block : (i + 1) * block].reshape(all_rows, group, width)
        back_ref[:, i * group : (i + 1) * group, :] = piece.astype(BF16)


def input_kernel(
    x_any, cot_any, gain_any, grads_any, wqkv_any, back_ref, grad_ref,
    x_ref, cot_ref, gain_ref, grads_ref, w_ref, sems,
):
    products = started(
        pltpu.make_async_copy(grads_any, grads_ref, sems.at[3]),
        *qkv_copies(wqkv_any, w_ref, sems, 0),
    )
    others = started(
        pltpu.make_async_copy(x_any, x_ref, sems.at[4]),
        pltpu.make_async_copy(gain_any, gain_ref, sems.at[5]),
        pltpu.make_async_copy(cot_any, cot_ref, sems.at[6]),
    )
    finished(*products)
    grad_hidden = dot_nt(grads_ref[...], w_ref[...]) + back_ref[...].astype(F32)
    finished(*others)
    inverse_rms, normed = rms_parts(x_ref[...].astype(F32))
    grad_normed = grad_hidden * gain_ref[...]
    projected = jnp.mean(grad_normed * normed, -1, keepdims=True)
    grad = inverse_rms * (grad_normed - normed * projected)
    grad_ref[...] = (cot_ref[...].astype(F32) + grad).astype(BF16)


def pack_kernel(place_ref, x_any, cot_any, own_ref, off_1, off_2, off_3, sems):
    chip, core = place_ref[0], place_ref[1]
    share = own_ref.shape[1]
    at = pl.multiple_of((chip * 2 + 1 - core) * share, share)
    copies = []
    for which, source in enumerate((x_any, cot_any)):
        copies.append(
            pltpu.make_async_copy(
                source.at[pl.ds(at, share), :], own_ref.at[which], sems.at[which]
            )
        )
        for i, target in enumerate((off_1, off_2, off_3)):
            there = pl.multiple_of((chip ^ (i + 1)) * 2 * share, 2 * share)
            copies.append(
                pltpu.make_async_copy(
                    source.at[pl.ds(there, 2 * share), :],
                    target.at[which],
                    sems.at[2 + 2 * i + which],
                )
            )
    finished(*started(*copies))


def chip_sum_kernel(place_ref, keep_ref, got_ref, own_any, off_1, off_2, off_3, own_ref, sem):
    chip = place_ref[0]
    handed = None
    for i, target in enumerate((own_ref, off_1, off_2, off_3)):
        there = chip ^ i
        total = keep_ref[there].astype(F32) + got_ref[there].astype(F32)
        target[...] = total.astype(target.dtype)
        if handed is None:
            handed = started(pltpu.make_async_copy(own_ref, own_any, sem))
    finished(*handed)


def layer_sum_kernel(place_ref, own_any, got_1, got_2, got_3, send_ref, keep_ref, own_ref, sem):
    own = started(pltpu.make_async_copy(own_any, own_ref, sem))
    upper = place_ref[2] == 1
    total = (got_1[...].astype(F32) + got_2[...].astype(F32)) + got_3[...].astype(F32)
    finished(*own)
    total += own_ref[...]
    half = total.shape[0] // 2
    low, high = total[:half], total[half:]
    send_ref[...] = jnp.where(upper, low, high).astype(BF16)
    keep_ref[...] = jnp.where(upper, high, low)


def add_kernel(kept_ref, got_ref, out_ref):
    out_ref[...] = (kept_ref[...].astype(F32) + got_ref[...].astype(F32)).astype(BF16)


def result_kernel(
    place_ref, held_ref, got_ref, wqkv_any, gain_any, qkv_ref, out_ref, grad_ref,
    w_ref, gain_ref, sems,
):
    rows = qkv_ref.shape[0]
    at = pl.multiple_of((place_ref[0] * 2 + place_ref[1]) * rows, rows)
    copies = started(
        pltpu.make_async_copy(wqkv_any.at[pl.ds(at, rows), :], w_ref, sems.at[0]),
        pltpu.make_async_copy(gain_any, gain_ref, sems.at[1]),
    )
    upper = place_ref[2] == 1
    held, got = held_ref[...].astype(F32), got_ref[...].astype(F32)
    half = rows // 2
    low, high = jnp.where(upper, got, held), jnp.where(upper, held, got)
    cut = qkv_ref.shape[1]
    qkv_ref[:half], qkv_ref[half:] = low[:, :cut], high[:, :cut]
    out_ref[:half], out_ref[half:] = low[:, cut:], high[:, cut:]
    finished(*copies)
    total = jnp.sum(qkv_ref[...] * w_ref[...].astype(F32), -1, keepdims=True)
    shape = (rows, gain_ref.shape[1])
    row = lax.broadcasted_iota(jnp.int32, shape, 0)
    feature = lax.broadcasted_iota(jnp.int32, shape, 1)
    gain = jnp.sum(jnp.where(feature == row + at, gain_ref[...], 0.0), -1, keepdims=True)
    shape = (rows, grad_ref.shape[1])
    same = lax.broadcasted_iota(jnp.int32, shape, 0) == lax.broadcasted_iota(jnp.int32, shape, 1)
    grad_ref[...] = jnp.sum(jnp.where(same, total / gain, 0.0), 0, keepdims=True)


def call(kernel, name, ins, outs, scratch=(), flops=0, vmem=SMALL_VMEM, out_specs=None):
    out_specs = out_specs or [VMEM] * len(outs)
    places = [pltpu.HBM if spec is HBM else None for spec in out_specs]
    outs = [place(*out) if place else shaped(*out) for place, out in zip(places, outs)]
    args = [
        pltpu.with_memory_space_constraint(array, pltpu.HBM) if spec is HBM else array
        for spec, array in ins
    ]
    size = sum(math.prod(a.shape) * a.dtype.itemsize for a in (*args, *outs))
    return pl.pallas_call(
        kernel,
        out_shape=outs,
        in_specs=[spec for spec, _ in ins],
        out_specs=out_specs,
        scratch_shapes=scratch,
        name=name,
        cost_estimate=pl.CostEstimate(flops=flops, bytes_accessed=size, transcendentals=0),
        compiler_params=pltpu.CompilerParams(vmem_limit_bytes=vmem),
    )(*args)


def body(inputs, norm_gain, qkv_weight, out_weight, out_cotan):
    columns, width = inputs.shape[2:]
    n = lax.axis_size("seq")
    m = lax.axis_size("dp")
    share = columns // n
    row_share = width // n
    term_width = 4 * width
    x = inputs.reshape(columns, width)
    cot = out_cotan.reshape(columns, width)
    gain = norm_gain.reshape(1, width)
    chips = 4
    layered = n == 2 * chips and m == 4 and row_share == share
    here = lax.axis_index("seq")
    place = jnp.stack([here // 2, here % 2, lax.axis_index("dp") % 2]).astype(jnp.int32)
    weight_scratch = [
        pltpu.VMEM((1, width), F32),
        pltpu.VMEM((width, 3 * HW), BF16),
        pltpu.VMEM((HW, width), BF16),
    ]
    small_scratch = [pltpu.VMEM((width, 3 * HW), BF16), pltpu.SemaphoreType.DMA((3,))]

    def swap(array, axis, bits):
        count = lax.axis_size(axis)
        return lax.ppermute(array, axis, [(i, i ^ bits) for i in range(count)])

    if layered:
        packed = call(
            pack_kernel,
            "pack_columns",
            [(SMEM, place), (HBM, x), (HBM, cot)],
            [((2, share, width), BF16)] + [((2, 2 * share, width), BF16)] * 3,
            [pltpu.SemaphoreType.DMA((8,))],
            out_specs=[ANY] * 4,
        )
        near_3 = swap(packed[3], "seq", 6)
        near_1 = swap(packed[1], "seq", 2)
        near_2 = swap(packed[2], "seq", 4)
        own = swap(packed[0], "seq", 1)
    else:
        outgoing = jnp.stack([x.reshape(n, share, width), cot.reshape(n, share, width)], 1)
        moved = lax.all_to_all(outgoing, "seq", split_axis=0, concat_axis=0, tiled=True)

    row_qkv, row_out, row_grads = call(
        row_kernel,
        "row_heads",
        [(HBM, x), (HBM, cot), (HBM, gain), (HBM, qkv_weight), (HBM, out_weight)],
        [((width, 3 * HW), BF16), ((HW, width), BF16), ((columns, 3 * HW), BF16)],
        [
            pltpu.VMEM((columns, width), BF16),
            pltpu.VMEM((columns, width), BF16),
            *weight_scratch,
            pltpu.VMEM((columns, HW), F32),
            pltpu.VMEM((columns, HW), F32),
            pltpu.VMEM((columns, 3 * HW), BF16),
            pltpu.SemaphoreType.DMA((7,)),
        ],
        5_000_000_000,
        BIG_VMEM,
        [VMEM, VMEM, HBM],
    )
    moved_scratch = pltpu.VMEM((n, 2, share, width), BF16)
    if layered:
        near_1, near_2, near_3, row_qkv = lax.optimization_barrier((near_1, near_2, near_3, row_qkv))
        far_3, far_1, far_2 = swap(near_3, "seq", 1), swap(near_1, "seq", 1), swap(near_2, "seq", 1)
    shared = [
        (HBM, gain), (HBM, qkv_weight), (HBM, out_weight), (VMEM, row_qkv), (VMEM, row_out),
    ]
    if layered:
        send, keep, col_grads = call(
            column_chip_kernel,
            "column_heads",
            [
                (SMEM, place), (HBM, x), (HBM, cot), (ANY, own),
                (ANY, near_1), (ANY, near_2), (ANY, near_3),
                (ANY, far_1), (ANY, far_2), (ANY, far_3), *shared,
            ],
            [((chips, row_share, term_width), BF16)] * 2 + [((columns, 3 * HW), BF16)],
            [moved_scratch, *weight_scratch, pltpu.SemaphoreType.DMA((14,))],
            4_000_000_000,
            BIG_VMEM,
        )
        got = swap(send, "seq", 1)
    else:
        terms, col_grads = call(
            column_kernel,
            "column_heads",
            [(ANY, moved), *shared],
            [((width, term_width), BF16), ((columns, 3 * HW), BF16)],
            [moved_scratch, *weight_scratch, pltpu.SemaphoreType.DMA((6,))],
            4_000_000_000,
            BIG_VMEM,
        )
    if layered:
        owned, off_1, off_2, off_3 = call(
            chip_sum_kernel,
            "add_cores",
            [(SMEM, place), (VMEM, keep), (VMEM, got)],
            [((row_share, term_width), F32)] + [((row_share, term_width), BF16)] * 3,
            [pltpu.VMEM((row_share, term_width), F32), pltpu.SemaphoreType.DMA],
            out_specs=[HBM, VMEM, VMEM, VMEM],
        )
        got_3 = swap(off_3, "seq", 6)
        got_1 = swap(off_1, "seq", 2)
        got_2 = swap(off_2, "seq", 4)
        col_grads, owned = lax.optimization_barrier((col_grads, owned))
    (back,) = call(
        back_kernel,
        "column_grad_hidden",
        [(VMEM, col_grads), (HBM, qkv_weight)],
        [((n, share, width), BF16)],
        small_scratch,
        400_000_000,
    )
    half_rows = (row_share // 2, term_width)
    if layered:
        back, owned = lax.optimization_barrier((back, owned))
        to_next, kept = call(
            layer_sum_kernel,
            "add_chips",
            [(SMEM, place), (HBM, owned), (VMEM, got_1), (VMEM, got_2), (VMEM, got_3)],
            [(half_rows, BF16), (half_rows, F32)],
            [pltpu.VMEM((row_share, term_width), F32), pltpu.SemaphoreType.DMA],
        )
        from_next = swap(to_next, "dp", 1)
        back, to_next = lax.optimization_barrier((back, to_next))
    returned = lax.all_to_all(back, "seq", split_axis=0, concat_axis=0, tiled=True)
    if layered:
        (pair_sum,) = call(
            add_kernel, "add_pair", [(VMEM, kept), (VMEM, from_next)], [(half_rows, BF16)]
        )
        from_far = swap(pair_sum, "dp", 2)
        (held,) = call(
            add_kernel, "add_pairs", [(VMEM, pair_sum), (VMEM, from_far)], [(half_rows, BF16)]
        )
        other = swap(held, "dp", 1)
    (input_grad,) = call(
        input_kernel,
        "input_grad",
        [
            (HBM, x), (HBM, cot), (HBM, gain), (HBM, row_grads), (HBM, qkv_weight),
            (VMEM, returned.reshape(columns, width)),
        ],
        [((columns, width), BF16)],
        [
            pltpu.VMEM((columns, width), BF16),
            pltpu.VMEM((columns, width), BF16),
            pltpu.VMEM((1, width), F32),
            pltpu.VMEM((columns, 3 * HW), BF16),
            pltpu.VMEM((width, 3 * HW), BF16),
            pltpu.SemaphoreType.DMA((7,)),
        ],
        400_000_000,
    )
    if layered:
        sum_qkv, sum_out, sum_gain = call(
            result_kernel,
            "result",
            [
                (SMEM, place), (VMEM, held), (VMEM, other), (HBM, qkv_weight), (HBM, gain),
            ],
            [((row_share, 3 * width), F32), ((row_share, width), F32), ((1, row_share), F32)],
            [
                pltpu.VMEM((row_share, 3 * width), BF16),
                pltpu.VMEM((1, width), F32),
                pltpu.SemaphoreType.DMA((2,)),
            ],
        )
        sum_gain = sum_gain.reshape(row_share)
    else:
        terms = lax.all_to_all(
            terms.reshape(n, row_share, term_width), "seq", split_axis=0, concat_axis=0, tiled=True
        )
        total = jnp.sum(terms.astype(F32), 0)
        for step in range(m.bit_length() - 1):
            sent = total.astype(BF16)
            total = sent.astype(F32) + swap(sent, "dp", 1 << step).astype(F32)
        sum_qkv, sum_out = total[:, : 3 * width], total[:, 3 * width :]
        own_gain = lax.dynamic_slice_in_dim(norm_gain, here * row_share, row_share, 0)
        own_weight = lax.dynamic_slice_in_dim(qkv_weight, here * row_share, row_share, 0)
        sum_gain = jnp.sum(sum_qkv * own_weight.astype(F32), -1) / own_gain
    return (input_grad.reshape(inputs.shape), sum_qkv, sum_out, sum_gain)


def solution(mesh):
    return jax.shard_map(
        body,
        mesh=mesh,
        in_specs=(P("dp", "seq", None, None), P(), P(), P(), P("dp", "seq", None, None)),
        out_specs=(P("dp", "seq", None, None), P("seq", None), P("seq", None), P("seq")),
        check_vma=False,
    )
```

```python
import math

import jax
import jax.numpy as jnp
from jax import lax
from jax.experimental import pallas as pl
from jax.experimental.pallas import tpu as pltpu
from jax.sharding import PartitionSpec as P

H = 8
HD = 64
HH = H // 2
HW = HH * HD
SCALE = HD ** (-0.5)
F32 = jnp.float32
BF16 = jnp.bfloat16
QUERY_BLOCK = 128
BIG_VMEM = 20 * 1024 * 1024
SMALL_VMEM = 8 * 1024 * 1024
ANY = pl.BlockSpec(memory_space=pl.ANY)
VMEM = pl.BlockSpec(memory_space=pltpu.VMEM)
SMEM = pl.BlockSpec(memory_space=pltpu.SMEM)
HBM = pl.BlockSpec(memory_space=pltpu.HBM)
shaped = jax.ShapeDtypeStruct


def dot_nn(a, b):
    return lax.dot_general(a, b, (((1,), (0,)), ((), ())), preferred_element_type=F32)


def dot_nt(a, b):
    return lax.dot_general(a, b, (((1,), (1,)), ((), ())), preferred_element_type=F32)


def rms_parts(x):
    inverse_rms = lax.rsqrt(jnp.mean(x * x, -1, keepdims=True) + 1e-05)
    return inverse_rms, x * inverse_rms


def transposed(x):
    block = math.gcd(x.shape[1], 256)
    eye = (
        lax.broadcasted_iota(jnp.int32, (block, block), 0)
        == lax.broadcasted_iota(jnp.int32, (block, block), 1)
    ).astype(F32).astype(BF16)
    parts = [
        dot_nt(eye, x[:, at : at + block]).astype(BF16) for at in range(0, x.shape[1], block)
    ]
    return parts[0] if len(parts) == 1 else jnp.concatenate(parts, 0)


def head_pair(x):
    lane = lax.broadcasted_iota(jnp.int32, x.shape, 1)
    zero = jnp.zeros_like(x)
    return jnp.concatenate([jnp.where(lane < HD, x, zero), jnp.where(lane < HD, zero, x)], 0)


def both_heads(both, count):
    return jnp.concatenate([both[:HD, :count], both[HD:, count:]], 0)


def pair_steps(items, mask_rows, mask):
    count = items[0][2].shape[1]
    scores = [dot_nt(k, q2) for q2, _, _, k, _, _, _ in items]
    prob_grads = [dot_nt(v, g2) for _, g2, _, _, v, _, _ in items]
    probs = []
    for score in scores:
        first = score.shape[0] - mask_rows
        tail = jnp.where(mask, score[first:], -1e30)
        score = tail if first == 0 else jnp.concatenate([score[:first], tail], 0)
        exponent = jnp.exp(score - jnp.max(score, 0, keepdims=True))
        probs.append(exponent * (1.0 / jnp.sum(exponent, 0, keepdims=True)))
    weights = [prob.astype(BF16) for prob in probs]
    attended = [
        both_heads(dot_nn(item[6], weight), count).astype(BF16)
        for item, weight in zip(items, weights)
    ]
    score_grads = []
    for item, att, prob, prob_grad in zip(items, attended, probs, prob_grads):
        product = item[2].astype(F32) * att.astype(F32)
        delta = [jnp.sum(part, 0, keepdims=True) for part in (product[:HD], product[HD:])]
        score_grads.append((prob * (prob_grad - jnp.concatenate(delta, 1))).astype(BF16))
    grad_q = [
        (both_heads(dot_nn(item[5], score_grad), count) * SCALE).astype(BF16)
        for item, score_grad in zip(items, score_grads)
    ]
    grad_k = [dot_nn(score_grad, item[0]) for item, score_grad in zip(items, score_grads)]
    grad_v = [dot_nn(weight, item[1]) for item, weight in zip(items, weights)]
    return list(zip(attended, grad_q, grad_k, grad_v))


def split_cores(piece, core, send_ref, keep_ref, chips, lanes):
    rows = send_ref.shape[1]
    parts = piece.reshape(chips.stop - chips.start, 2, rows, piece.shape[1])
    even, odd = parts[:, 0], parts[:, 1]
    first = core == 0
    send_ref[chips, :, lanes] = jnp.where(first, odd, even)
    keep_ref[chips, :, lanes] = jnp.where(first, even, odd)


def qkv_copies(wqkv_ref, w_ref, sems, second):
    width = wqkv_ref.shape[0]
    return [
        pltpu.make_async_copy(
            wqkv_ref.at[:, pl.ds(i * width + second * HW, HW)],
            w_ref.at[:, pl.ds(i * HW, HW)],
            sems.at[i],
        )
        for i in range(3)
    ]


def weight_copies(wqkv_ref, wout_ref, w_ref, wo_ref, sems, second):
    out_rows = wout_ref.at[pl.ds(second * HW, HW), :]
    return [
        *qkv_copies(wqkv_ref, w_ref, sems, second),
        pltpu.make_async_copy(out_rows, wo_ref, sems.at[3]),
    ]


def started(*copies):
    for copy in copies:
        copy.start()
    return copies


def finished(*copies):
    for copy in copies:
        copy.wait()


def project(hidden, cot, w_ref, wo_ref):
    projected = dot_nn(hidden, w_ref[...]).astype(BF16)
    q, k, v = [projected[:, i * HW : (i + 1) * HW] for i in range(3)]
    g = dot_nt(cot, wo_ref[...]).astype(BF16)
    return q * jnp.asarray(SCALE, BF16), k, v, g


def row_part(
    x_any, cot_any, gain_any, wqkv_any, wout_any, out_ref, grads_any,
    x_ref, cot_ref, gain_ref, w_ref, wo_ref, dk_ref, dv_ref, grads_ref, sems,
):
    first = started(
        pltpu.make_async_copy(x_any, x_ref, sems.at[4]),
        pltpu.make_async_copy(gain_any, gain_ref, sems.at[5]),
    )
    later = started(
        *weight_copies(wqkv_any, wout_any, w_ref, wo_ref, sems, 0),
        pltpu.make_async_copy(cot_any, cot_ref, sems.at[6]),
    )
    dk_ref[...] = jnp.zeros_like(dk_ref)
    dv_ref[...] = jnp.zeros_like(dv_ref)
    finished(*first)
    tokens = x_ref.shape[0]
    _, normed = rms_parts(x_ref[...].astype(F32))
    hidden = (normed * gain_ref[...]).astype(BF16)
    hidden_t = transposed(hidden)
    finished(*later)
    cot = cot_ref[...]
    q, k, v, g = project(hidden, cot, w_ref, wo_ref)
    kt, vt, gt = transposed(k), transposed(v), transposed(g)
    step = math.gcd(tokens, QUERY_BLOCK)
    query = lax.broadcasted_iota(jnp.int32, (step, 2 * step), 1) % step
    mask = query >= lax.broadcasted_iota(jnp.int32, (step, 2 * step), 0)
    pairs = [slice(i * 2 * HD, (i + 1) * 2 * HD) for i in range(HH // 2)]
    att_blocks, dq_blocks = [], []
    for start in range(0, tokens, step):
        rows, keys = slice(start, start + step), slice(0, start + step)
        items = [
            (
                head_pair(q[rows, lanes]), head_pair(g[rows, lanes]), gt[lanes, rows],
                k[keys, lanes], v[keys, lanes], kt[lanes, keys], vt[lanes, keys],
            )
            for lanes in pairs
        ]
        results = pair_steps(items, step, mask)
        for lanes, (_, _, dk, dv) in zip(pairs, results):
            dk_ref[keys, lanes] += dk
            dv_ref[keys, lanes] += dv
        att_blocks.append(jnp.concatenate([result[0] for result in results], 0))
        dq_blocks.append(jnp.concatenate([result[1] for result in results], 0))
    grads_ref[:, :HW] = transposed(jnp.concatenate(dq_blocks, 1))
    grads_ref[:, HW : 2 * HW] = dk_ref[...].astype(BF16)
    grads_ref[:, 2 * HW :] = dv_ref[...].astype(BF16)
    handed = started(pltpu.make_async_copy(grads_ref, grads_any, sems.at[4]))
    term_qkv = dot_nn(hidden_t, grads_ref[...]).astype(BF16)
    out_ref[...] = dot_nn(jnp.concatenate(att_blocks, 1), cot).astype(BF16)
    finished(*handed)
    return term_qkv


def row_kernel(x_any, cot_any, gain_any, wqkv_any, wout_any, qkv_ref, *refs):
    qkv_ref[...] = row_part(x_any, cot_any, gain_any, wqkv_any, wout_any, *refs)


def row_chip_kernel(
    place_ref, x_any, cot_any, gain_any, wqkv_any, wout_any, send_ref, keep_ref, *refs
):
    term_qkv = row_part(x_any, cot_any, gain_any, wqkv_any, wout_any, *refs)
    whole = slice(0, send_ref.shape[0]), slice(0, send_ref.shape[2])
    split_cores(term_qkv, place_ref[1], send_ref, keep_ref, *whole)


def column_part(moved_ref, gain_ref, w_ref, wo_ref, weight_waits, grads_ref):
    all_rows, _, share, width = moved_ref.shape
    group = math.gcd(share, 16)
    block = all_rows * group

    def gathered(which):
        pieces = []
        for start in range(0, share, group):
            piece = moved_ref[:, which, start : start + group, :]
            if group % 16 == 0:
                pieces.append(piece.reshape(block, width))
            else:
                pieces.append(piece.astype(F32).reshape(block, width).astype(BF16))
        return jnp.concatenate(pieces, 0)

    _, normed = rms_parts(gathered(0).astype(F32))
    hidden = (normed * gain_ref[...]).astype(BF16)
    hidden_t = transposed(hidden)
    finished(*weight_waits)
    cot = gathered(1)
    q, k, v, g = project(hidden, cot, w_ref, wo_ref)
    kt, vt, gt = transposed(k), transposed(v), transposed(g)
    query = lax.broadcasted_iota(jnp.int32, (block, 2 * block), 1) % block
    key = lax.broadcasted_iota(jnp.int32, (block, 2 * block), 0)
    mask = (query >= key) & (query % group == key % group)
    pairs = [slice(i * 2 * HD, (i + 1) * 2 * HD) for i in range(HH // 2)]
    blocks = [slice(at, at + block) for at in range(0, all_rows * share, block)]
    items = [
        (
            head_pair(q[rows, lanes]), head_pair(g[rows, lanes]), gt[lanes, rows],
            k[rows, lanes], v[rows, lanes], kt[lanes, rows], vt[lanes, rows],
        )
        for lanes in pairs
        for rows in blocks
    ]
    results = pair_steps(items, block, mask)
    places = [(lanes, rows) for lanes in pairs for rows in blocks]
    for (lanes, rows), (_, _, dk, dv) in zip(places, results):
        grads_ref[rows, HW + lanes.start : HW + lanes.stop] = dk.astype(BF16)
        grads_ref[rows, 2 * HW + lanes.start : 2 * HW + lanes.stop] = dv.astype(BF16)
    by_pair = [results[i * len(blocks) : (i + 1) * len(blocks)] for i in range(len(pairs))]
    attended, grad_q = [
        jnp.concatenate([jnp.concatenate([r[i] for r in some], 1) for some in by_pair], 0)
        for i in range(2)
    ]
    grads_ref[:, :HW] = transposed(grad_q)
    term_qkv = dot_nn(hidden_t, grads_ref[...]).astype(BF16)
    term_out = dot_nn(attended, cot).astype(BF16)
    return term_qkv, term_out


def column_kernel(
    moved_any, gain_any, wqkv_any, wout_any, row_qkv_ref, row_out_ref,
    terms_ref, grads_ref,
    moved_ref, gain_ref, w_ref, wo_ref, sems,
):
    copies = started(
        pltpu.make_async_copy(moved_any, moved_ref, sems.at[4]),
        pltpu.make_async_copy(gain_any, gain_ref, sems.at[5]),
    )
    weights = started(*weight_copies(wqkv_any, wout_any, w_ref, wo_ref, sems, 1))
    finished(*copies)
    term_qkv, term_out = column_part(moved_ref, gain_ref, w_ref, wo_ref, weights, grads_ref)
    width = terms_ref.shape[0]
    for i in range(3):
        at = i * width
        terms_ref[:, at : at + HW] = row_qkv_ref[:, i * HW : (i + 1) * HW]
        terms_ref[:, at + HW : at + 2 * HW] = term_qkv[:, i * HW : (i + 1) * HW]
    terms_ref[:HW, 3 * width :] = row_out_ref[...]
    terms_ref[HW:, 3 * width :] = term_out


def column_chip_kernel(
    place_ref, x_any, cot_any, own_any,
    near_1, near_2, near_3, far_1, far_2, far_3,
    gain_any, wqkv_any, wout_any, row_out_ref,
    send_ref, keep_ref, grads_ref,
    moved_ref, gain_ref, w_ref, wo_ref, sems,
):
    chip, core = place_ref[0], place_ref[1]
    share = moved_ref.shape[2]
    at = pl.multiple_of((chip * 2 + core) * share, share)
    half = pl.multiple_of(core * share, share)
    me, other = chip * 2 + core, chip * 2 + 1 - core
    groups = []
    for which, source in enumerate((x_any, cot_any)):
        group = [
            (source.at[pl.ds(at, share), :], me),
            (own_any.at[which], other),
        ]
        for i, (near, far) in enumerate(((near_1, far_1), (near_2, far_2), (near_3, far_3))):
            there = 2 * (chip ^ (i + 1))
            group.append((near.at[which, pl.ds(half, share), :], there + core))
            group.append((far.at[which, pl.ds(half, share), :], there + 1 - core))
        base = 5 + which * len(group)
        groups.append([
            pltpu.make_async_copy(piece, moved_ref.at[row, which], sems.at[base + i])
            for i, (piece, row) in enumerate(group)
        ])
    first = started(*groups[0], pltpu.make_async_copy(gain_any, gain_ref, sems.at[4]))
    later = started(*weight_copies(wqkv_any, wout_any, w_ref, wo_ref, sems, 1), *groups[1])
    finished(*first)
    term_qkv, term_out = column_part(moved_ref, gain_ref, w_ref, wo_ref, later, grads_ref)
    chips = send_ref.shape[0]
    refs = core, send_ref, keep_ref
    out_lanes = slice(3 * HW, send_ref.shape[2])
    split_cores(term_qkv, *refs, slice(0, chips), slice(0, 3 * HW))
    split_cores(row_out_ref[...], *refs, slice(0, chips // 2), out_lanes)
    split_cores(term_out, *refs, slice(chips // 2, chips), out_lanes)


def back_kernel(grads_ref, wqkv_any, back_ref, w_ref, sems):
    finished(*started(*qkv_copies(wqkv_any, w_ref, sems, 1)))
    grad_hidden = dot_nt(grads_ref[...], w_ref[...])
    all_rows, share, width = back_ref.shape
    group = math.gcd(share, 16)
    block = all_rows * group
    for i in range(share // group):
        piece = grad_hidden[i * block : (i + 1) * block].reshape(all_rows, group, width)
        back_ref[:, i * group : (i + 1) * group, :] = piece.astype(BF16)


def input_kernel(
    x_any, cot_any, gain_any, grads_any, wqkv_any, back_ref, grad_ref,
    x_ref, cot_ref, gain_ref, grads_ref, w_ref, sems,
):
    products = started(
        pltpu.make_async_copy(grads_any, grads_ref, sems.at[3]),
        *qkv_copies(wqkv_any, w_ref, sems, 0),
    )
    others = started(
        pltpu.make_async_copy(x_any, x_ref, sems.at[4]),
        pltpu.make_async_copy(gain_any, gain_ref, sems.at[5]),
        pltpu.make_async_copy(cot_any, cot_ref, sems.at[6]),
    )
    finished(*products)
    grad_hidden = dot_nt(grads_ref[...], w_ref[...]) + back_ref[...].astype(F32)
    finished(*others)
    inverse_rms, normed = rms_parts(x_ref[...].astype(F32))
    grad_normed = grad_hidden * gain_ref[...]
    projected = jnp.mean(grad_normed * normed, -1, keepdims=True)
    grad = inverse_rms * (grad_normed - normed * projected)
    grad_ref[...] = (cot_ref[...].astype(F32) + grad).astype(BF16)


def pack_kernel(place_ref, x_any, cot_any, own_ref, off_1, off_2, off_3, sems):
    chip, core = place_ref[0], place_ref[1]
    share = own_ref.shape[1]
    at = pl.multiple_of((chip * 2 + 1 - core) * share, share)
    copies = []
    for which, source in enumerate((x_any, cot_any)):
        copies.append(
            pltpu.make_async_copy(
                source.at[pl.ds(at, share), :], own_ref.at[which], sems.at[which]
            )
        )
        for i, target in enumerate((off_1, off_2, off_3)):
            there = pl.multiple_of((chip ^ (i + 1)) * 2 * share, 2 * share)
            copies.append(
                pltpu.make_async_copy(
                    source.at[pl.ds(there, 2 * share), :],
                    target.at[which],
                    sems.at[2 + 2 * i + which],
                )
            )
    finished(*started(*copies))


def chip_sum_kernel(place_ref, keep_ref, got_ref, own_any, off_1, off_2, off_3, own_ref, sem):
    chip = place_ref[0]
    handed = None
    for i, target in enumerate((own_ref, off_1, off_2, off_3)):
        there = chip ^ i
        total = keep_ref[there].astype(F32) + got_ref[there].astype(F32)
        target[...] = total.astype(target.dtype)
        if handed is None:
            handed = started(pltpu.make_async_copy(own_ref, own_any, sem))
    finished(*handed)


def layer_sum_kernel(place_ref, own_any, got_1, got_2, got_3, send_ref, keep_ref, own_ref, sem):
    own = started(pltpu.make_async_copy(own_any, own_ref, sem))
    upper = place_ref[2] == 1
    total = (got_1[...].astype(F32) + got_2[...].astype(F32)) + got_3[...].astype(F32)
    finished(*own)
    total += own_ref[...]
    half = total.shape[0] // 2
    low, high = total[:half], total[half:]
    send_ref[...] = jnp.where(upper, low, high).astype(BF16)
    keep_ref[...] = jnp.where(upper, high, low)


def pass_kernel(any_ref, same_ref):
    pass


def add_kernel(kept_ref, got_ref, out_ref):
    out_ref[...] = (kept_ref[...].astype(F32) + got_ref[...].astype(F32)).astype(BF16)


def result_kernel(
    place_ref, row_held, row_got, held_ref, got_ref, wqkv_any, gain_any,
    qkv_ref, out_ref, grad_ref,
    w_ref, gain_ref, sems,
):
    rows = qkv_ref.shape[0]
    at = pl.multiple_of((place_ref[0] * 2 + place_ref[1]) * rows, rows)
    copies = started(
        pltpu.make_async_copy(wqkv_any.at[pl.ds(at, rows), :], w_ref, sems.at[0]),
        pltpu.make_async_copy(gain_any, gain_ref, sems.at[1]),
    )
    upper = place_ref[2] == 1
    half = rows // 2
    width = out_ref.shape[1]

    def ordered(held_ref, got_ref, lanes):
        held, got = held_ref[:, lanes].astype(F32), got_ref[:, lanes].astype(F32)
        return (jnp.where(upper, got, held), jnp.where(upper, held, got))

    for i in range(3):
        lanes = slice(i * HW, (i + 1) * HW)
        at_row, at_col = i * width, i * width + HW
        low, high = ordered(row_held, row_got, lanes)
        qkv_ref[:half, at_row : at_row + HW], qkv_ref[half:, at_row : at_row + HW] = low, high
        low, high = ordered(held_ref, got_ref, lanes)
        qkv_ref[:half, at_col : at_col + HW], qkv_ref[half:, at_col : at_col + HW] = low, high
    out_ref[:half], out_ref[half:] = ordered(held_ref, got_ref, slice(3 * HW, 3 * HW + width))
    finished(*copies)
    total = jnp.sum(qkv_ref[...] * w_ref[...].astype(F32), -1, keepdims=True)
    shape = (rows, gain_ref.shape[1])
    row = lax.broadcasted_iota(jnp.int32, shape, 0)
    feature = lax.broadcasted_iota(jnp.int32, shape, 1)
    gain = jnp.sum(jnp.where(feature == row + at, gain_ref[...], 0.0), -1, keepdims=True)
    shape = (rows, grad_ref.shape[1])
    same = lax.broadcasted_iota(jnp.int32, shape, 0) == lax.broadcasted_iota(jnp.int32, shape, 1)
    grad_ref[...] = jnp.sum(jnp.where(same, total / gain, 0.0), 0, keepdims=True)


def call(kernel, name, ins, outs, scratch=(), flops=0, vmem=SMALL_VMEM, out_specs=None, aliases=None):
    out_specs = out_specs or [VMEM] * len(outs)
    places = [pltpu.HBM if spec is HBM else None for spec in out_specs]
    outs = [place(*out) if place else shaped(*out) for place, out in zip(places, outs)]
    args = [
        pltpu.with_memory_space_constraint(array, pltpu.HBM) if spec is HBM else array
        for spec, array in ins
    ]
    size = sum(math.prod(a.shape) * a.dtype.itemsize for a in (*args, *outs))
    return pl.pallas_call(
        kernel,
        out_shape=outs,
        in_specs=[spec for spec, _ in ins],
        out_specs=out_specs,
        scratch_shapes=scratch,
        input_output_aliases=aliases or {},
        name=name,
        cost_estimate=pl.CostEstimate(flops=flops, bytes_accessed=size, transcendentals=0),
        compiler_params=pltpu.CompilerParams(vmem_limit_bytes=vmem),
    )(*args)


def swap(array, axis, bits):
    count = lax.axis_size(axis)
    return lax.ppermute(array, axis, [(i, i ^ bits) for i in range(count)])


def add_cores(place, keep, got, name):
    _, rows, wide = keep.shape
    return call(
        chip_sum_kernel,
        name + "_add_cores",
        [(SMEM, place), (VMEM, keep), (VMEM, got)],
        [((rows, wide), F32)] + [((rows, wide), BF16)] * 3,
        [pltpu.VMEM((rows, wide), F32), pltpu.SemaphoreType.DMA],
        out_specs=[HBM, VMEM, VMEM, VMEM],
    )


def cross_chips(off_1, off_2, off_3):
    got_3 = swap(off_3, "seq", 6)
    got_1 = swap(off_1, "seq", 2)
    got_2 = swap(off_2, "seq", 4)
    return got_1, got_2, got_3


def add_chips(place, owned, got, name):
    rows, wide = owned.shape
    return call(
        layer_sum_kernel,
        name + "_add_chips",
        [(SMEM, place), (HBM, owned), *[(VMEM, one) for one in got]],
        [((rows // 2, wide), BF16), ((rows // 2, wide), F32)],
        [pltpu.VMEM((rows, wide), F32), pltpu.SemaphoreType.DMA],
    )


def add_two(kept, got, name):
    (total,) = call(add_kernel, name, [(VMEM, kept), (VMEM, got)], [(kept.shape, BF16)])
    return total


def body(inputs, norm_gain, qkv_weight, out_weight, out_cotan):
    columns, width = inputs.shape[2:]
    n = lax.axis_size("seq")
    m = lax.axis_size("dp")
    share = columns // n
    row_share = width // n
    row_width, col_width = 3 * HW, 3 * HW + width
    x = inputs.reshape(columns, width)
    cot = out_cotan.reshape(columns, width)
    gain = norm_gain.reshape(1, width)
    chips = 4
    layered = n == 2 * chips and m == 4 and row_share == share
    here = lax.axis_index("seq")
    place = jnp.stack([here // 2, here % 2, lax.axis_index("dp") % 2]).astype(jnp.int32)
    weight_scratch = [
        pltpu.VMEM((1, width), F32),
        pltpu.VMEM((width, 3 * HW), BF16),
        pltpu.VMEM((HW, width), BF16),
    ]
    weights = [(HBM, gain), (HBM, qkv_weight), (HBM, out_weight)]
    grads_out = ((columns, 3 * HW), BF16)

    if layered:
        packed = call(
            pack_kernel,
            "pack_columns",
            [(SMEM, place), (HBM, x), (HBM, cot)],
            [((2, share, width), BF16)] + [((2, 2 * share, width), BF16)] * 3,
            [pltpu.SemaphoreType.DMA((8,))],
            out_specs=[ANY] * 4,
        )
        near_1, near_2, near_3 = cross_chips(*packed[1:])
        own = swap(packed[0], "seq", 1)
    else:
        outgoing = jnp.stack([x.reshape(n, share, width), cot.reshape(n, share, width)], 1)
        moved = lax.all_to_all(outgoing, "seq", split_axis=0, concat_axis=0, tiled=True)

    split_out = ((chips, row_share, row_width), BF16)
    term_outs = [split_out] * 2 if layered else [((width, row_width), BF16)]
    *row_terms, row_out, row_grads = call(
        row_chip_kernel if layered else row_kernel,
        "row_heads",
        [(SMEM, place)] * layered + [(HBM, x), (HBM, cot), *weights],
        [*term_outs, ((HW, width), BF16), grads_out],
        [
            pltpu.VMEM((columns, width), BF16),
            pltpu.VMEM((columns, width), BF16),
            *weight_scratch,
            pltpu.VMEM((columns, HW), F32),
            pltpu.VMEM((columns, HW), F32),
            pltpu.VMEM((columns, 3 * HW), BF16),
            pltpu.SemaphoreType.DMA((7,)),
        ],
        5_000_000_000,
        BIG_VMEM,
        [VMEM] * len(term_outs) + [VMEM, HBM],
    )
    moved_scratch = pltpu.VMEM((n, 2, share, width), BF16)
    if layered:
        row_send, row_keep = row_terms
        near_1, near_2, near_3, row_send = lax.optimization_barrier(
            (near_1, near_2, near_3, row_send)
        )
        far_3, far_1, far_2 = swap(near_3, "seq", 1), swap(near_1, "seq", 1), swap(near_2, "seq", 1)
        row_owned, *row_off = add_cores(place, row_keep, swap(row_send, "seq", 1), "row")
        row_got = cross_chips(*row_off)
        own, row_owned = lax.optimization_barrier((own, row_owned))
        send, keep, col_grads = call(
            column_chip_kernel,
            "column_heads",
            [
                (SMEM, place), (HBM, x), (HBM, cot), (ANY, own),
                (ANY, near_1), (ANY, near_2), (ANY, near_3),
                (ANY, far_1), (ANY, far_2), (ANY, far_3), *weights, (VMEM, row_out),
            ],
            [((chips, row_share, col_width), BF16)] * 2 + [grads_out],
            [moved_scratch, *weight_scratch, pltpu.SemaphoreType.DMA((21,))],
            4_000_000_000,
            BIG_VMEM,
        )
        send, row_got = lax.optimization_barrier((send, row_got))
        row_next, row_kept = add_chips(place, row_owned, row_got, "row")
        row_pair = add_two(row_kept, swap(row_next, "dp", 1), "row_add_pair")
        keep, row_kept = lax.optimization_barrier((keep, row_kept))
        owned, *off = add_cores(place, keep, swap(send, "seq", 1), "column")
        got = cross_chips(*off)
        col_grads, owned, row_pair = lax.optimization_barrier((col_grads, owned, row_pair))
        row_held = add_two(row_pair, swap(row_pair, "dp", 2), "row_add_pairs")
    else:
        terms, col_grads = call(
            column_kernel,
            "column_heads",
            [(ANY, moved), *weights, (VMEM, row_terms[0]), (VMEM, row_out)],
            [((width, 4 * width), BF16), grads_out],
            [moved_scratch, *weight_scratch, pltpu.SemaphoreType.DMA((6,))],
            4_000_000_000,
            BIG_VMEM,
        )
    (back,) = call(
        back_kernel,
        "column_grad_hidden",
        [(VMEM, col_grads), (HBM, qkv_weight)],
        [((n, share, width), BF16)],
        [pltpu.VMEM((width, 3 * HW), BF16), pltpu.SemaphoreType.DMA((3,))],
        400_000_000,
    )
    if layered:
        back, owned = lax.optimization_barrier((back, owned))
        to_next, kept = add_chips(place, owned, got, "column")
        back, kept = lax.optimization_barrier((back, kept))
        (back,) = call(
            pass_kernel, "pass_on", [(ANY, back)], [(back.shape, BF16)],
            out_specs=[ANY], aliases={0: 0},
        )
        kept, row_held = lax.optimization_barrier((kept, row_held))
        pair_sum = add_two(kept, swap(to_next, "dp", 1), "column_add_pair")
        row_other = swap(row_held, "dp", 1)
        held = add_two(pair_sum, swap(pair_sum, "dp", 2), "column_add_pairs")
    returned = lax.all_to_all(back, "seq", split_axis=0, concat_axis=0, tiled=True)
    (input_grad,) = call(
        input_kernel,
        "input_grad",
        [
            (HBM, x), (HBM, cot), (HBM, gain), (HBM, row_grads), (HBM, qkv_weight),
            (VMEM, returned.reshape(columns, width)),
        ],
        [((columns, width), BF16)],
        [
            pltpu.VMEM((columns, width), BF16),
            pltpu.VMEM((columns, width), BF16),
            pltpu.VMEM((1, width), F32),
            pltpu.VMEM((columns, 3 * HW), BF16),
            pltpu.VMEM((width, 3 * HW), BF16),
            pltpu.SemaphoreType.DMA((7,)),
        ],
        400_000_000,
    )
    if layered:
        other = swap(held, "dp", 1)
        held, input_grad = lax.optimization_barrier((held, input_grad))
        sum_qkv, sum_out, sum_gain = call(
            result_kernel,
            "result",
            [
                (SMEM, place), (VMEM, row_held), (VMEM, row_other), (VMEM, held), (VMEM, other),
                (HBM, qkv_weight), (HBM, gain),
            ],
            [((row_share, 3 * width), F32), ((row_share, width), F32), ((1, row_share), F32)],
            [
                pltpu.VMEM((row_share, 3 * width), BF16),
                pltpu.VMEM((1, width), F32),
                pltpu.SemaphoreType.DMA((2,)),
            ],
        )
        sum_gain = sum_gain.reshape(row_share)
    else:
        terms = lax.all_to_all(
            terms.reshape(n, row_share, 4 * width), "seq", split_axis=0, concat_axis=0, tiled=True
        )
        total = jnp.sum(terms.astype(F32), 0)
        for step in range(m.bit_length() - 1):
            sent = total.astype(BF16)
            total = sent.astype(F32) + swap(sent, "dp", 1 << step).astype(F32)
        sum_qkv, sum_out = total[:, : 3 * width], total[:, 3 * width :]
        own_gain = lax.dynamic_slice_in_dim(norm_gain, here * row_share, row_share, 0)
        own_weight = lax.dynamic_slice_in_dim(qkv_weight, here * row_share, row_share, 0)
        sum_gain = jnp.sum(sum_qkv * own_weight.astype(F32), -1) / own_gain
    return (input_grad.reshape(inputs.shape), sum_qkv, sum_out, sum_gain)


def solution(mesh):
    return jax.shard_map(
        body,
        mesh=mesh,
        in_specs=(P("dp", "seq", None, None), P(), P(), P(), P("dp", "seq", None, None)),
        out_specs=(P("dp", "seq", None, None), P("seq", None), P("seq", None), P("seq")),
        check_vma=False,
    )
```

```python
import math

import jax
import jax.numpy as jnp
from jax import lax
from jax.experimental import pallas as pl
from jax.experimental.pallas import tpu as pltpu
from jax.sharding import PartitionSpec as P

H = 8
HD = 64
HH = H // 2
HW = HH * HD
SCALE = HD ** (-0.5)
F32 = jnp.float32
BF16 = jnp.bfloat16
QUERY_BLOCK = 128
BIG_VMEM = 20 * 1024 * 1024
SMALL_VMEM = 8 * 1024 * 1024
ANY = pl.BlockSpec(memory_space=pl.ANY)
VMEM = pl.BlockSpec(memory_space=pltpu.VMEM)
SMEM = pl.BlockSpec(memory_space=pltpu.SMEM)
HBM = pl.BlockSpec(memory_space=pltpu.HBM)
PINNED = pl.BlockSpec(memory_space=pltpu.VMEM)
shaped = jax.ShapeDtypeStruct


def dot_nn(a, b):
    return lax.dot_general(a, b, (((1,), (0,)), ((), ())), preferred_element_type=F32)


def dot_nt(a, b):
    return lax.dot_general(a, b, (((1,), (1,)), ((), ())), preferred_element_type=F32)


def rms_parts(x):
    inverse_rms = lax.rsqrt(jnp.mean(x * x, -1, keepdims=True) + 1e-05)
    return inverse_rms, x * inverse_rms


def transposed(x):
    block = math.gcd(x.shape[1], 256)
    eye = (
        lax.broadcasted_iota(jnp.int32, (block, block), 0)
        == lax.broadcasted_iota(jnp.int32, (block, block), 1)
    ).astype(F32).astype(BF16)
    parts = [
        dot_nt(eye, x[:, at : at + block]).astype(BF16) for at in range(0, x.shape[1], block)
    ]
    return parts[0] if len(parts) == 1 else jnp.concatenate(parts, 0)


def head_pair(x):
    lane = lax.broadcasted_iota(jnp.int32, x.shape, 1)
    zero = jnp.zeros_like(x)
    return jnp.concatenate([jnp.where(lane < HD, x, zero), jnp.where(lane < HD, zero, x)], 0)


def both_heads(both, count):
    return jnp.concatenate([both[:HD, :count], both[HD:, count:]], 0)


def pair_steps(items, mask_rows, mask):
    count = items[0][2].shape[1]
    scores = [dot_nt(k, q2) for q2, _, _, k, _, _, _ in items]
    prob_grads = [dot_nt(v, g2) for _, g2, _, _, v, _, _ in items]
    probs = []
    for score in scores:
        first = score.shape[0] - mask_rows
        tail = jnp.where(mask, score[first:], -1e30)
        score = tail if first == 0 else jnp.concatenate([score[:first], tail], 0)
        exponent = jnp.exp(score - jnp.max(score, 0, keepdims=True))
        probs.append(exponent * (1.0 / jnp.sum(exponent, 0, keepdims=True)))
    weights = [prob.astype(BF16) for prob in probs]
    attended = [
        both_heads(dot_nn(item[6], weight), count).astype(BF16)
        for item, weight in zip(items, weights)
    ]
    score_grads = []
    for item, att, prob, prob_grad in zip(items, attended, probs, prob_grads):
        product = item[2].astype(F32) * att.astype(F32)
        delta = [jnp.sum(part, 0, keepdims=True) for part in (product[:HD], product[HD:])]
        score_grads.append((prob * (prob_grad - jnp.concatenate(delta, 1))).astype(BF16))
    grad_q = [
        (both_heads(dot_nn(item[5], score_grad), count) * SCALE).astype(BF16)
        for item, score_grad in zip(items, score_grads)
    ]
    grad_k = [dot_nn(score_grad, item[0]) for item, score_grad in zip(items, score_grads)]
    grad_v = [dot_nn(weight, item[1]) for item, weight in zip(items, weights)]
    return list(zip(attended, grad_q, grad_k, grad_v))


def split_cores(piece, core, send_ref, keep_ref, chips, lanes):
    rows = send_ref.shape[1]
    parts = piece.reshape(chips.stop - chips.start, 2, rows, piece.shape[1])
    even, odd = parts[:, 0], parts[:, 1]
    first = core == 0
    send_ref[chips, :, lanes] = jnp.where(first, odd, even)
    keep_ref[chips, :, lanes] = jnp.where(first, even, odd)


def qkv_copies(wqkv_ref, w_ref, sems, second):
    width = wqkv_ref.shape[0]
    return [
        pltpu.make_async_copy(
            wqkv_ref.at[:, pl.ds(i * width + second * HW, HW)],
            w_ref.at[:, pl.ds(i * HW, HW)],
            sems.at[i],
        )
        for i in range(3)
    ]


def weight_copies(wqkv_ref, wout_ref, w_ref, wo_ref, sems, second):
    out_rows = wout_ref.at[pl.ds(second * HW, HW), :]
    return [
        *qkv_copies(wqkv_ref, w_ref, sems, second),
        pltpu.make_async_copy(out_rows, wo_ref, sems.at[3]),
    ]


def started(*copies):
    for copy in copies:
        copy.start()
    return copies


def finished(*copies):
    for copy in copies:
        copy.wait()


def project(hidden, cot, w_ref, wo_ref):
    projected = dot_nn(hidden, w_ref[...]).astype(BF16)
    q, k, v = [projected[:, i * HW : (i + 1) * HW] for i in range(3)]
    g = dot_nt(cot, wo_ref[...]).astype(BF16)
    return q * jnp.asarray(SCALE, BF16), k, v, g


def row_part(
    x_any, cot_any, gain_any, wqkv_any, wout_any, out_ref, grads_any,
    x_ref, cot_ref, gain_ref, w_ref, wo_ref, dk_ref, dv_ref, grads_ref, sems,
):
    first = started(
        pltpu.make_async_copy(x_any, x_ref, sems.at[4]),
        pltpu.make_async_copy(gain_any, gain_ref, sems.at[5]),
    )
    later = started(
        *weight_copies(wqkv_any, wout_any, w_ref, wo_ref, sems, 0),
        pltpu.make_async_copy(cot_any, cot_ref, sems.at[6]),
    )
    dk_ref[...] = jnp.zeros_like(dk_ref)
    dv_ref[...] = jnp.zeros_like(dv_ref)
    finished(*first)
    tokens = x_ref.shape[0]
    _, normed = rms_parts(x_ref[...].astype(F32))
    hidden = (normed * gain_ref[...]).astype(BF16)
    hidden_t = transposed(hidden)
    finished(*later)
    cot = cot_ref[...]
    q, k, v, g = project(hidden, cot, w_ref, wo_ref)
    kt, vt, gt = transposed(k), transposed(v), transposed(g)
    step = math.gcd(tokens, QUERY_BLOCK)
    query = lax.broadcasted_iota(jnp.int32, (step, 2 * step), 1) % step
    mask = query >= lax.broadcasted_iota(jnp.int32, (step, 2 * step), 0)
    pairs = [slice(i * 2 * HD, (i + 1) * 2 * HD) for i in range(HH // 2)]
    att_blocks, dq_blocks = [], []
    for start in range(0, tokens, step):
        rows, keys = slice(start, start + step), slice(0, start + step)
        items = [
            (
                head_pair(q[rows, lanes]), head_pair(g[rows, lanes]), gt[lanes, rows],
                k[keys, lanes], v[keys, lanes], kt[lanes, keys], vt[lanes, keys],
            )
            for lanes in pairs
        ]
        results = pair_steps(items, step, mask)
        for lanes, (_, _, dk, dv) in zip(pairs, results):
            dk_ref[keys, lanes] += dk
            dv_ref[keys, lanes] += dv
        att_blocks.append(jnp.concatenate([result[0] for result in results], 0))
        dq_blocks.append(jnp.concatenate([result[1] for result in results], 0))
    grads_ref[:, :HW] = transposed(jnp.concatenate(dq_blocks, 1))
    grads_ref[:, HW : 2 * HW] = dk_ref[...].astype(BF16)
    grads_ref[:, 2 * HW :] = dv_ref[...].astype(BF16)
    handed = started(pltpu.make_async_copy(grads_ref, grads_any, sems.at[4]))
    term_qkv = dot_nn(hidden_t, grads_ref[...]).astype(BF16)
    out_ref[...] = dot_nn(jnp.concatenate(att_blocks, 1), cot).astype(BF16)
    finished(*handed)
    return term_qkv


def row_kernel(x_any, cot_any, gain_any, wqkv_any, wout_any, qkv_ref, *refs):
    qkv_ref[...] = row_part(x_any, cot_any, gain_any, wqkv_any, wout_any, *refs)


def row_chip_kernel(
    place_ref, x_any, cot_any, gain_any, wqkv_any, wout_any,
    send_1, send_2, keep_1, keep_2, *refs,
):
    term_qkv = row_part(x_any, cot_any, gain_any, wqkv_any, wout_any, *refs)
    chips, lanes = slice(0, send_1.shape[0]), slice(0, send_1.shape[2])
    split_cores(term_qkv[:, : lanes.stop], place_ref[1], send_1, keep_1, chips, lanes)
    split_cores(term_qkv[:, lanes.stop :], place_ref[1], send_2, keep_2, chips, lanes)


def column_part(moved_ref, gain_ref, w_ref, wo_ref, weight_waits, grads_ref):
    all_rows, _, share, width = moved_ref.shape
    group = math.gcd(share, 16)
    block = all_rows * group

    def gathered(which):
        pieces = []
        for start in range(0, share, group):
            piece = moved_ref[:, which, start : start + group, :]
            if group % 16 == 0:
                pieces.append(piece.reshape(block, width))
            else:
                pieces.append(piece.astype(F32).reshape(block, width).astype(BF16))
        return jnp.concatenate(pieces, 0)

    _, normed = rms_parts(gathered(0).astype(F32))
    hidden = (normed * gain_ref[...]).astype(BF16)
    hidden_t = transposed(hidden)
    finished(*weight_waits)
    cot = gathered(1)
    q, k, v, g = project(hidden, cot, w_ref, wo_ref)
    kt, vt, gt = transposed(k), transposed(v), transposed(g)
    query = lax.broadcasted_iota(jnp.int32, (block, 2 * block), 1) % block
    key = lax.broadcasted_iota(jnp.int32, (block, 2 * block), 0)
    mask = (query >= key) & (query % group == key % group)
    pairs = [slice(i * 2 * HD, (i + 1) * 2 * HD) for i in range(HH // 2)]
    blocks = [slice(at, at + block) for at in range(0, all_rows * share, block)]
    items = [
        (
            head_pair(q[rows, lanes]), head_pair(g[rows, lanes]), gt[lanes, rows],
            k[rows, lanes], v[rows, lanes], kt[lanes, rows], vt[lanes, rows],
        )
        for lanes in pairs
        for rows in blocks
    ]
    results = pair_steps(items, block, mask)
    places = [(lanes, rows) for lanes in pairs for rows in blocks]
    for (lanes, rows), (_, _, dk, dv) in zip(places, results):
        grads_ref[rows, HW + lanes.start : HW + lanes.stop] = dk.astype(BF16)
        grads_ref[rows, 2 * HW + lanes.start : 2 * HW + lanes.stop] = dv.astype(BF16)
    by_pair = [results[i * len(blocks) : (i + 1) * len(blocks)] for i in range(len(pairs))]
    attended, grad_q = [
        jnp.concatenate([jnp.concatenate([r[i] for r in some], 1) for some in by_pair], 0)
        for i in range(2)
    ]
    grads_ref[:, :HW] = transposed(grad_q)
    term_qkv = dot_nn(hidden_t, grads_ref[...]).astype(BF16)
    term_out = dot_nn(attended, cot).astype(BF16)
    return term_qkv, term_out


def column_kernel(
    moved_any, gain_any, wqkv_any, wout_any, row_qkv_ref, row_out_ref,
    terms_ref, grads_ref,
    moved_ref, gain_ref, w_ref, wo_ref, sems,
):
    copies = started(
        pltpu.make_async_copy(moved_any, moved_ref, sems.at[4]),
        pltpu.make_async_copy(gain_any, gain_ref, sems.at[5]),
    )
    weights = started(*weight_copies(wqkv_any, wout_any, w_ref, wo_ref, sems, 1))
    finished(*copies)
    term_qkv, term_out = column_part(moved_ref, gain_ref, w_ref, wo_ref, weights, grads_ref)
    width = terms_ref.shape[0]
    for i in range(3):
        at = i * width
        terms_ref[:, at : at + HW] = row_qkv_ref[:, i * HW : (i + 1) * HW]
        terms_ref[:, at + HW : at + 2 * HW] = term_qkv[:, i * HW : (i + 1) * HW]
    terms_ref[:HW, 3 * width :] = row_out_ref[...]
    terms_ref[HW:, 3 * width :] = term_out


def column_chip_kernel(
    place_ref, x_any, cot_any, own_any,
    near_1, near_2, near_3, far_1, far_2, far_3,
    gain_any, wqkv_any, wout_any, row_out_ref,
    send_ref, keep_ref, grads_ref,
    moved_ref, gain_ref, w_ref, wo_ref, sems,
):
    chip, core = place_ref[0], place_ref[1]
    share = moved_ref.shape[2]
    at = pl.multiple_of((chip * 2 + core) * share, share)
    half = pl.multiple_of(core * share, share)
    me, other = chip * 2 + core, chip * 2 + 1 - core
    groups = []
    for which, source in enumerate((x_any, cot_any)):
        group = [
            (source.at[pl.ds(at, share), :], me),
            (own_any.at[which], other),
        ]
        for i, (near, far) in enumerate(((near_1, far_1), (near_2, far_2), (near_3, far_3))):
            there = 2 * (chip ^ (i + 1))
            group.append((near.at[which, pl.ds(half, share), :], there + core))
            group.append((far.at[which, pl.ds(half, share), :], there + 1 - core))
        base = 5 + which * len(group)
        groups.append([
            pltpu.make_async_copy(piece, moved_ref.at[row, which], sems.at[base + i])
            for i, (piece, row) in enumerate(group)
        ])
    first = started(*groups[0], pltpu.make_async_copy(gain_any, gain_ref, sems.at[4]))
    later = started(*weight_copies(wqkv_any, wout_any, w_ref, wo_ref, sems, 1), *groups[1])
    finished(*first)
    term_qkv, term_out = column_part(moved_ref, gain_ref, w_ref, wo_ref, later, grads_ref)
    chips = send_ref.shape[0]
    refs = core, send_ref, keep_ref
    out_lanes = slice(3 * HW, send_ref.shape[2])
    split_cores(term_qkv, *refs, slice(0, chips), slice(0, 3 * HW))
    split_cores(row_out_ref[...], *refs, slice(0, chips // 2), out_lanes)
    split_cores(term_out, *refs, slice(chips // 2, chips), out_lanes)


def back_kernel(grads_ref, wqkv_any, back_ref, w_ref, sems):
    finished(*started(*qkv_copies(wqkv_any, w_ref, sems, 1)))
    grad_hidden = dot_nt(grads_ref[...], w_ref[...])
    all_rows, share, width = back_ref.shape
    group = math.gcd(share, 16)
    block = all_rows * group
    for i in range(share // group):
        piece = grad_hidden[i * block : (i + 1) * block].reshape(all_rows, group, width)
        back_ref[:, i * group : (i + 1) * group, :] = piece.astype(BF16)


def back_chip_kernel(place_ref, grads_ref, wqkv_any, send_1, send_2, keep_ref, w_ref, sems):
    finished(*started(*qkv_copies(wqkv_any, w_ref, sems, 1)))
    grad_hidden = dot_nt(grads_ref[...], w_ref[...])
    chips, share, width = keep_ref.shape
    half = width // 2
    group = math.gcd(share, 16)
    block = 2 * chips * group
    first = place_ref[1] == 0
    for i in range(share // group):
        piece = grad_hidden[i * block : (i + 1) * block].reshape(chips, 2, group, width)
        even, odd = piece[:, 0], piece[:, 1]
        at = slice(i * group, (i + 1) * group)
        sent = jnp.where(first, odd, even).astype(BF16)
        send_1[:, at, :], send_2[:, at, :] = sent[:, :, :half], sent[:, :, half:]
        keep_ref[:, at, :] = jnp.where(first, even, odd).astype(BF16)


def back_pack_kernel(place_ref, keep_ref, got_1, got_2, own_ref, off_1, off_2, off_3):
    chip, core = place_ref[0], place_ref[1]
    share, half = keep_ref.shape[1], got_1.shape[2]
    kept_at = pl.multiple_of(core * share, share)
    got_at = pl.multiple_of((1 - core) * share, share)
    for i, target in enumerate((own_ref, off_1, off_2, off_3)):
        target[pl.ds(kept_at, share), :] = keep_ref[chip ^ i]
        target[pl.ds(got_at, share), :half] = got_1[chip ^ i]
        target[pl.ds(got_at, share), half:] = got_2[chip ^ i]


def input_kernel(
    x_any, cot_any, gain_any, grads_any, wqkv_any, back_ref, grad_ref,
    x_ref, cot_ref, gain_ref, grads_ref, w_ref, sems,
):
    products = started(
        pltpu.make_async_copy(grads_any, grads_ref, sems.at[3]),
        *qkv_copies(wqkv_any, w_ref, sems, 0),
    )
    others = started(
        pltpu.make_async_copy(x_any, x_ref, sems.at[4]),
        pltpu.make_async_copy(gain_any, gain_ref, sems.at[5]),
        pltpu.make_async_copy(cot_any, cot_ref, sems.at[6]),
    )
    finished(*products)
    grad_hidden = dot_nt(grads_ref[...], w_ref[...]) + back_ref[...].astype(F32)
    finished(*others)
    inverse_rms, normed = rms_parts(x_ref[...].astype(F32))
    grad_ref[...] = input_grad(normed, inverse_rms, grad_hidden, gain_ref[...], cot_ref[...])


def input_grad(normed, inverse_rms, grad_hidden, gain, cot):
    grad_normed = grad_hidden * gain
    projected = jnp.mean(grad_normed * normed, -1, keepdims=True)
    grad = inverse_rms * (grad_normed - normed * projected)
    return (cot.astype(F32) + grad).astype(BF16)


def ready_kernel(
    place_ref, grads_any, wqkv_any, x_any, cot_any,
    hidden_ref, rows_ref, x_ref, cot_ref,
    grads_ref, w_ref, sems,
):
    rows = rows_ref.shape[0]
    at = pl.multiple_of((place_ref[0] * 2 + place_ref[1]) * rows, rows)
    products = started(
        pltpu.make_async_copy(grads_any, grads_ref, sems.at[3]),
        *qkv_copies(wqkv_any, w_ref, sems, 0),
    )
    others = started(
        pltpu.make_async_copy(wqkv_any.at[pl.ds(at, rows), :], rows_ref, sems.at[4]),
        pltpu.make_async_copy(x_any, x_ref, sems.at[5]),
        pltpu.make_async_copy(cot_any, cot_ref, sems.at[6]),
    )
    finished(*products)
    hidden_ref[...] = dot_nt(grads_ref[...], w_ref[...])
    finished(*others)


def input_chip_kernel(
    place_ref, x_ref, cot_ref, gain_ref, hidden_ref, own_ref, got_1, got_2, got_3, grad_ref
):
    chip = place_ref[0]
    count = own_ref.shape[0]
    for i, back_ref in enumerate((own_ref, got_1, got_2, got_3)):
        at = pl.ds(pl.multiple_of((chip ^ i) * count, count), count)
        inverse_rms, normed = rms_parts(x_ref[at, :].astype(F32))
        grad_hidden = hidden_ref[at, :] + back_ref[...].astype(F32)
        grad_ref[at, :] = input_grad(
            normed, inverse_rms, grad_hidden, gain_ref[...], cot_ref[at, :]
        )


def pack_kernel(place_ref, x_any, cot_any, own_ref, off_1, off_2, off_3, sems):
    chip, core = place_ref[0], place_ref[1]
    share = own_ref.shape[1]
    at = pl.multiple_of((chip * 2 + 1 - core) * share, share)
    copies = []
    for which, source in enumerate((x_any, cot_any)):
        copies.append(
            pltpu.make_async_copy(
                source.at[pl.ds(at, share), :], own_ref.at[which], sems.at[which]
            )
        )
        for i, target in enumerate((off_1, off_2, off_3)):
            there = pl.multiple_of((chip ^ (i + 1)) * 2 * share, 2 * share)
            copies.append(
                pltpu.make_async_copy(
                    source.at[pl.ds(there, 2 * share), :],
                    target.at[which],
                    sems.at[2 + 2 * i + which],
                )
            )
    finished(*started(*copies))


def chip_sum_kernel(place_ref, *refs):
    chip = place_ref[0]
    pieces, targets = refs[:-4], refs[-4:]
    count = len(pieces) // 2
    for i, target in enumerate(targets):
        at = 0
        for kept_ref, got_ref in zip(pieces[:count], pieces[count:]):
            total = kept_ref[chip ^ i].astype(F32) + got_ref[chip ^ i].astype(F32)
            target[:, at : at + total.shape[1]] = total.astype(target.dtype)
            at += total.shape[1]


def layer_sum_kernel(place_ref, own_ref, got_1, got_2, got_3, send_ref, keep_ref):
    upper = place_ref[2] == 1
    total = own_ref[...] + (
        (got_1[...].astype(F32) + got_2[...].astype(F32)) + got_3[...].astype(F32)
    )
    half = total.shape[0] // 2
    low, high = total[:half], total[half:]
    send_ref[...] = jnp.where(upper, low, high).astype(BF16)
    keep_ref[...] = jnp.where(upper, high, low)


def add_kernel(kept_ref, got_ref, out_ref):
    out_ref[...] = (kept_ref[...].astype(F32) + got_ref[...].astype(F32)).astype(BF16)


def join_kernel(row_ref, kept_ref, got_ref, out_ref):
    cut = row_ref.shape[1]
    out_ref[:, :cut] = row_ref[...]
    out_ref[:, cut:] = (kept_ref[...] + got_ref[...].astype(F32)).astype(BF16)


def result_kernel(place_ref, held_ref, got_ref, w_ref, gain_ref, qkv_ref, out_ref, grad_ref):
    rows = qkv_ref.shape[0]
    at = pl.multiple_of((place_ref[0] * 2 + place_ref[1]) * rows, rows)
    upper = place_ref[2] == 1
    half = rows // 2
    width = out_ref.shape[1]

    def ordered(lanes):
        held, got = held_ref[:, lanes].astype(F32), got_ref[:, lanes].astype(F32)
        return (jnp.where(upper, got, held), jnp.where(upper, held, got))

    for i in range(3):
        for at_from, at_to in ((i * HW, i * width), ((3 + i) * HW, i * width + HW)):
            to = slice(at_to, at_to + HW)
            qkv_ref[:half, to], qkv_ref[half:, to] = ordered(slice(at_from, at_from + HW))
    out_ref[:half], out_ref[half:] = ordered(slice(6 * HW, 6 * HW + width))
    total = jnp.sum(qkv_ref[...] * w_ref[...].astype(F32), -1, keepdims=True)
    shape = (rows, gain_ref.shape[1])
    row = lax.broadcasted_iota(jnp.int32, shape, 0)
    feature = lax.broadcasted_iota(jnp.int32, shape, 1)
    gain = jnp.sum(jnp.where(feature == row + at, gain_ref[...], 0.0), -1, keepdims=True)
    shape = (rows, grad_ref.shape[1])
    same = lax.broadcasted_iota(jnp.int32, shape, 0) == lax.broadcasted_iota(jnp.int32, shape, 1)
    grad_ref[...] = jnp.sum(jnp.where(same, total / gain, 0.0), 0, keepdims=True)


def call(kernel, name, ins, outs, scratch=(), vmem=SMALL_VMEM, out_specs=None):
    out_specs = out_specs or [VMEM] * len(outs)
    places = [{id(HBM): pltpu.HBM, id(PINNED): pltpu.VMEM}.get(id(spec)) for spec in out_specs]
    outs = [place(*out) if place else shaped(*out) for place, out in zip(places, outs)]
    args = [
        pltpu.with_memory_space_constraint(array, pltpu.HBM) if spec is HBM else array
        for spec, array in ins
    ]
    return pl.pallas_call(
        kernel,
        out_shape=outs,
        in_specs=[spec for spec, _ in ins],
        out_specs=out_specs,
        scratch_shapes=scratch,
        name=name,
        cost_estimate=pl.CostEstimate(flops=0, bytes_accessed=0, transcendentals=0),
        compiler_params=pltpu.CompilerParams(vmem_limit_bytes=vmem),
    )(*args)


def swap(array, axis, bits):
    count = lax.axis_size(axis)
    return lax.ppermute(array, axis, [(i, i ^ bits) for i in range(count)])


def add_cores(place, keep, got, name):
    rows, wide = keep[0].shape[1], sum(one.shape[2] for one in keep)
    return call(
        chip_sum_kernel,
        name + "_add_cores",
        [(SMEM, place), *[(VMEM, one) for one in (*keep, *got)]],
        [((rows, wide), F32)] + [((rows, wide), BF16)] * 3,
        out_specs=[PINNED, VMEM, VMEM, VMEM],
    )


def cross_chips(off_1, off_2, off_3):
    got_3 = swap(off_3, "seq", 6)
    got_1 = swap(off_1, "seq", 2)
    got_2 = swap(off_2, "seq", 4)
    return got_1, got_2, got_3


def add_chips(place, owned, got, name):
    rows, wide = owned.shape
    return call(
        layer_sum_kernel,
        name + "_add_chips",
        [(SMEM, place), (VMEM, owned), *[(VMEM, one) for one in got]],
        [((rows // 2, wide), BF16), ((rows // 2, wide), F32)],
        out_specs=[VMEM, PINNED],
    )


def add_two(kept, got, name):
    (total,) = call(add_kernel, name, [(VMEM, kept), (VMEM, got)], [(kept.shape, BF16)])
    return total


def body(inputs, norm_gain, qkv_weight, out_weight, out_cotan):
    columns, width = inputs.shape[2:]
    n = lax.axis_size("seq")
    m = lax.axis_size("dp")
    share = columns // n
    row_share = width // n
    row_width, col_width = 3 * HW, 3 * HW + width
    x = inputs.reshape(columns, width)
    cot = out_cotan.reshape(columns, width)
    gain = norm_gain.reshape(1, width)
    chips = 4
    layered = n == 2 * chips and m == 4 and row_share == share
    here = lax.axis_index("seq")
    place = jnp.stack([here // 2, here % 2, lax.axis_index("dp") % 2]).astype(jnp.int32)
    weight_scratch = [
        pltpu.VMEM((1, width), F32),
        pltpu.VMEM((width, 3 * HW), BF16),
        pltpu.VMEM((HW, width), BF16),
    ]
    weights = [(HBM, gain), (HBM, qkv_weight), (HBM, out_weight)]
    grads_out = ((columns, 3 * HW), BF16)

    if layered:
        packed = call(
            pack_kernel,
            "pack_columns",
            [(SMEM, place), (HBM, x), (HBM, cot)],
            [((2, share, width), BF16)] + [((2, 2 * share, width), BF16)] * 3,
            [pltpu.SemaphoreType.DMA((8,))],
            out_specs=[ANY] * 4,
        )
        near_1, near_2, near_3 = cross_chips(*packed[1:])
        own = swap(packed[0], "seq", 1)
        placed, _ = lax.optimization_barrier((place, packed[0]))
    else:
        outgoing = jnp.stack([x.reshape(n, share, width), cot.reshape(n, share, width)], 1)
        moved = lax.all_to_all(outgoing, "seq", split_axis=0, concat_axis=0, tiled=True)
        placed = place

    split_out = ((chips, row_share, row_width // 2), BF16)
    term_outs = [split_out] * 4 if layered else [((width, row_width), BF16)]
    *row_terms, row_out, row_grads = call(
        row_chip_kernel if layered else row_kernel,
        "row_heads",
        [(SMEM, placed)] * layered + [(HBM, x), (HBM, cot), *weights],
        [*term_outs, ((HW, width), BF16), grads_out],
        [
            pltpu.VMEM((columns, width), BF16),
            pltpu.VMEM((columns, width), BF16),
            *weight_scratch,
            pltpu.VMEM((columns, HW), F32),
            pltpu.VMEM((columns, HW), F32),
            pltpu.VMEM((columns, 3 * HW), BF16),
            pltpu.SemaphoreType.DMA((7,)),
        ],
        BIG_VMEM,
        [VMEM] * len(term_outs) + [VMEM, HBM],
    )
    moved_scratch = pltpu.VMEM((n, 2, share, width), BF16)
    if layered:
        near_1, *row_terms = lax.optimization_barrier((near_1, *row_terms))
        row_sent = [swap(one, "seq", 1) for one in row_terms[:2]]
        row_owned, *row_off = add_cores(place, row_terms[2:], row_sent, "row")
        near_1, near_2, near_3, row_owned = lax.optimization_barrier(
            (near_1, near_2, near_3, row_owned)
        )
        far_3, far_1, far_2 = swap(near_3, "seq", 1), swap(near_1, "seq", 1), swap(near_2, "seq", 1)
        row_got = cross_chips(*row_off)
        send, keep, col_grads = call(
            column_chip_kernel,
            "column_heads",
            [
                (SMEM, place), (HBM, x), (HBM, cot), (ANY, own),
                (ANY, near_1), (ANY, near_2), (ANY, near_3),
                (ANY, far_1), (ANY, far_2), (ANY, far_3), *weights, (VMEM, row_out),
            ],
            [((chips, row_share, col_width), BF16)] * 2 + [grads_out],
            [moved_scratch, *weight_scratch, pltpu.SemaphoreType.DMA((21,))],
            BIG_VMEM,
        )
        send, row_got = lax.optimization_barrier((send, row_got))
        row_next, row_kept = add_chips(place, row_owned, row_got, "row")
        row_pair = add_two(row_kept, swap(row_next, "dp", 1), "row_add_pair")
        keep, row_kept = lax.optimization_barrier((keep, row_kept))
        owned, *off = add_cores(place, [keep], [swap(send, "seq", 1)], "column")
        got = cross_chips(*off)
        col_grads, owned = lax.optimization_barrier((col_grads, owned))
        *back_parts, back_keep = call(
            back_chip_kernel,
            "column_grad_hidden",
            [(SMEM, place), (VMEM, col_grads), (HBM, qkv_weight)],
            [((chips, share, width // 2), BF16)] * 2 + [((chips, share, width), BF16)],
            [pltpu.VMEM((width, 3 * HW), BF16), pltpu.SemaphoreType.DMA((3,))],
        )
        back = call(
            back_pack_kernel,
            "pack_grad_hidden",
            [
                (SMEM, place), (VMEM, back_keep),
                *[(VMEM, swap(part, "seq", 1)) for part in back_parts],
            ],
            [((2 * share, width), BF16)] * 4,
        )
        *back, owned, row_pair = lax.optimization_barrier((*back, owned, row_pair))
        to_next, kept = add_chips(place, owned, got, "column")
        row_grads, kept = lax.optimization_barrier((row_grads, kept))
        row_hidden, weight_rows, x_near, cot_near = call(
            ready_kernel,
            "row_grad_hidden",
            [(SMEM, place), (HBM, row_grads), (HBM, qkv_weight), (HBM, x), (HBM, cot)],
            [
                ((columns, width), F32), ((row_share, 3 * width), BF16),
                ((columns, width), BF16), ((columns, width), BF16),
            ],
            [
                pltpu.VMEM((columns, 3 * HW), BF16),
                pltpu.VMEM((width, 3 * HW), BF16),
                pltpu.SemaphoreType.DMA((7,)),
            ],
            out_specs=[PINNED] * 4,
        )
        kept, row_hidden = lax.optimization_barrier((kept, row_hidden))
        (joined,) = call(
            join_kernel,
            "join_terms",
            [(VMEM, row_pair), (VMEM, kept), (VMEM, swap(to_next, "dp", 1))],
            [((row_share // 2, row_width + col_width), BF16)],
        )
        *back, joined = lax.optimization_barrier((*back, joined))
        held = add_two(joined, swap(joined, "dp", 2), "add_pairs")
        other = swap(held, "dp", 1)
        (grad,) = call(
            input_chip_kernel,
            "input_grad",
            [
                (SMEM, place), (VMEM, x_near), (VMEM, cot_near), (VMEM, gain), (VMEM, row_hidden),
                (VMEM, back[0]), *[(VMEM, one) for one in cross_chips(*back[1:])],
            ],
            [((columns, width), BF16)],
        )
        sum_qkv, sum_out, sum_gain = call(
            result_kernel,
            "result",
            [
                (SMEM, place), (VMEM, held), (VMEM, other), (VMEM, weight_rows), (VMEM, gain),
            ],
            [((row_share, 3 * width), F32), ((row_share, width), F32), ((1, row_share), F32)],
        )
        sum_gain = sum_gain.reshape(row_share)
    else:
        terms, col_grads = call(
            column_kernel,
            "column_heads",
            [(ANY, moved), *weights, (VMEM, row_terms[0]), (VMEM, row_out)],
            [((width, 4 * width), BF16), grads_out],
            [moved_scratch, *weight_scratch, pltpu.SemaphoreType.DMA((6,))],
            BIG_VMEM,
        )
        (back,) = call(
            back_kernel,
            "column_grad_hidden",
            [(VMEM, col_grads), (HBM, qkv_weight)],
            [((n, share, width), BF16)],
            [pltpu.VMEM((width, 3 * HW), BF16), pltpu.SemaphoreType.DMA((3,))],
        )
        returned = lax.all_to_all(back, "seq", split_axis=0, concat_axis=0, tiled=True)
        (grad,) = call(
            input_kernel,
            "input_grad",
            [
                (HBM, x), (HBM, cot), (HBM, gain), (HBM, row_grads), (HBM, qkv_weight),
                (VMEM, returned.reshape(columns, width)),
            ],
            [((columns, width), BF16)],
            [
                pltpu.VMEM((columns, width), BF16),
                pltpu.VMEM((columns, width), BF16),
                pltpu.VMEM((1, width), F32),
                pltpu.VMEM((columns, 3 * HW), BF16),
                pltpu.VMEM((width, 3 * HW), BF16),
                pltpu.SemaphoreType.DMA((7,)),
            ],
        )
        terms = lax.all_to_all(
            terms.reshape(n, row_share, 4 * width), "seq", split_axis=0, concat_axis=0, tiled=True
        )
        total = jnp.sum(terms.astype(F32), 0)
        for step in range(m.bit_length() - 1):
            sent = total.astype(BF16)
            total = sent.astype(F32) + swap(sent, "dp", 1 << step).astype(F32)
        sum_qkv, sum_out = total[:, : 3 * width], total[:, 3 * width :]
        own_gain = lax.dynamic_slice_in_dim(norm_gain, here * row_share, row_share, 0)
        own_weight = lax.dynamic_slice_in_dim(qkv_weight, here * row_share, row_share, 0)
        sum_gain = jnp.sum(sum_qkv * own_weight.astype(F32), -1) / own_gain
    return (grad.reshape(inputs.shape), sum_qkv, sum_out, sum_gain)


def solution(mesh):
    return jax.shard_map(
        body,
        mesh=mesh,
        in_specs=(P("dp", "seq", None, None), P(), P(), P(), P("dp", "seq", None, None)),
        out_specs=(P("dp", "seq", None, None), P("seq", None), P("seq", None), P("seq")),
        check_vma=False,
    )
```

```python
import math

import jax
import jax.numpy as jnp
from jax import lax
from jax.experimental import pallas as pl
from jax.experimental.pallas import tpu as pltpu
from jax.sharding import PartitionSpec as P

H = 8
HD = 64
HH = H // 2
HW = HH * HD
SCALE = HD ** (-0.5)
F32 = jnp.float32
BF16 = jnp.bfloat16
QUERY_BLOCK = 128
BIG_VMEM = 20 * 1024 * 1024
SMALL_VMEM = 8 * 1024 * 1024
ANY = pl.BlockSpec(memory_space=pl.ANY)
VMEM = pl.BlockSpec(memory_space=pltpu.VMEM)
SMEM = pl.BlockSpec(memory_space=pltpu.SMEM)
HBM = pl.BlockSpec(memory_space=pltpu.HBM)
PINNED = pl.BlockSpec(memory_space=pltpu.VMEM)
shaped = jax.ShapeDtypeStruct


def dot_nn(a, b):
    return lax.dot_general(a, b, (((1,), (0,)), ((), ())), preferred_element_type=F32)


def dot_nt(a, b):
    return lax.dot_general(a, b, (((1,), (1,)), ((), ())), preferred_element_type=F32)


def rms_parts(x):
    inverse_rms = lax.rsqrt(jnp.mean(x * x, -1, keepdims=True) + 1e-05)
    return inverse_rms, x * inverse_rms


def transposed(x):
    block = math.gcd(x.shape[1], 256)
    eye = (
        lax.broadcasted_iota(jnp.int32, (block, block), 0)
        == lax.broadcasted_iota(jnp.int32, (block, block), 1)
    ).astype(F32).astype(BF16)
    parts = [
        dot_nt(eye, x[:, at : at + block]).astype(BF16) for at in range(0, x.shape[1], block)
    ]
    return parts[0] if len(parts) == 1 else jnp.concatenate(parts, 0)


def head_pair(x):
    lane = lax.broadcasted_iota(jnp.int32, x.shape, 1)
    zero = jnp.zeros_like(x)
    return jnp.concatenate([jnp.where(lane < HD, x, zero), jnp.where(lane < HD, zero, x)], 0)


def both_heads(both, count):
    return jnp.concatenate([both[:HD, :count], both[HD:, count:]], 0)


def pair_steps(items, mask_rows, mask):
    count = items[0][2].shape[1]
    scores = [dot_nt(k, q2) for q2, _, _, k, _, _, _ in items]
    prob_grads = [dot_nt(v, g2) for _, g2, _, _, v, _, _ in items]
    probs = []
    for score in scores:
        first = score.shape[0] - mask_rows
        tail = jnp.where(mask, score[first:], -1e30)
        score = tail if first == 0 else jnp.concatenate([score[:first], tail], 0)
        exponent = jnp.exp(score - jnp.max(score, 0, keepdims=True))
        probs.append(exponent * (1.0 / jnp.sum(exponent, 0, keepdims=True)))
    weights = [prob.astype(BF16) for prob in probs]
    attended = [
        both_heads(dot_nn(item[6], weight), count).astype(BF16)
        for item, weight in zip(items, weights)
    ]
    score_grads = []
    for item, att, prob, prob_grad in zip(items, attended, probs, prob_grads):
        product = item[2].astype(F32) * att.astype(F32)
        delta = [jnp.sum(part, 0, keepdims=True) for part in (product[:HD], product[HD:])]
        score_grads.append((prob * (prob_grad - jnp.concatenate(delta, 1))).astype(BF16))
    grad_q = [
        (both_heads(dot_nn(item[5], score_grad), count) * SCALE).astype(BF16)
        for item, score_grad in zip(items, score_grads)
    ]
    grad_k = [dot_nn(score_grad, item[0]) for item, score_grad in zip(items, score_grads)]
    grad_v = [dot_nn(weight, item[1]) for item, weight in zip(items, weights)]
    return list(zip(attended, grad_q, grad_k, grad_v))


def split_cores(piece, core, send_ref, keep_ref, chips, lanes):
    rows = send_ref.shape[1]
    parts = piece.reshape(chips.stop - chips.start, 2, rows, piece.shape[1])
    even, odd = parts[:, 0], parts[:, 1]
    first = core == 0
    send_ref[chips, :, lanes] = jnp.where(first, odd, even)
    keep_ref[chips, :, lanes] = jnp.where(first, even, odd)


def qkv_copies(wqkv_ref, w_ref, sems, second):
    width = wqkv_ref.shape[0]
    return [
        pltpu.make_async_copy(
            wqkv_ref.at[:, pl.ds(i * width + second * HW, HW)],
            w_ref.at[:, pl.ds(i * HW, HW)],
            sems.at[i],
        )
        for i in range(3)
    ]


def weight_copies(wqkv_ref, wout_ref, w_ref, wo_ref, sems, second):
    out_rows = wout_ref.at[pl.ds(second * HW, HW), :]
    return [
        *qkv_copies(wqkv_ref, w_ref, sems, second),
        pltpu.make_async_copy(out_rows, wo_ref, sems.at[3]),
    ]


def started(*copies):
    for copy in copies:
        copy.start()
    return copies


def finished(*copies):
    for copy in copies:
        copy.wait()


def project(hidden, cot, w_ref, wo_ref):
    projected = dot_nn(hidden, w_ref[...]).astype(BF16)
    q, k, v = [projected[:, i * HW : (i + 1) * HW] for i in range(3)]
    g = dot_nt(cot, wo_ref[...]).astype(BF16)
    return q * jnp.asarray(SCALE, BF16), k, v, g


def row_part(
    x_any, cot_any, gain_any, wqkv_any, wout_any,
    out_ref, hidden_ref, x_ref, cot_ref,
    gain_ref, w_ref, wo_ref, dk_ref, dv_ref, grads_ref, sems,
):
    first = started(
        pltpu.make_async_copy(x_any, x_ref, sems.at[4]),
        pltpu.make_async_copy(gain_any, gain_ref, sems.at[5]),
    )
    later = started(
        *weight_copies(wqkv_any, wout_any, w_ref, wo_ref, sems, 0),
        pltpu.make_async_copy(cot_any, cot_ref, sems.at[6]),
    )
    dk_ref[...] = jnp.zeros_like(dk_ref)
    dv_ref[...] = jnp.zeros_like(dv_ref)
    finished(*first)
    tokens = x_ref.shape[0]
    _, normed = rms_parts(x_ref[...].astype(F32))
    hidden = (normed * gain_ref[...]).astype(BF16)
    hidden_t = transposed(hidden)
    finished(*later)
    cot = cot_ref[...]
    q, k, v, g = project(hidden, cot, w_ref, wo_ref)
    kt, vt, gt = transposed(k), transposed(v), transposed(g)
    step = math.gcd(tokens, QUERY_BLOCK)
    query = lax.broadcasted_iota(jnp.int32, (step, 2 * step), 1) % step
    mask = query >= lax.broadcasted_iota(jnp.int32, (step, 2 * step), 0)
    pairs = [slice(i * 2 * HD, (i + 1) * 2 * HD) for i in range(HH // 2)]
    att_blocks, dq_blocks = [], []
    for start in range(0, tokens, step):
        rows, keys = slice(start, start + step), slice(0, start + step)
        items = [
            (
                head_pair(q[rows, lanes]), head_pair(g[rows, lanes]), gt[lanes, rows],
                k[keys, lanes], v[keys, lanes], kt[lanes, keys], vt[lanes, keys],
            )
            for lanes in pairs
        ]
        results = pair_steps(items, step, mask)
        for lanes, (_, _, dk, dv) in zip(pairs, results):
            dk_ref[keys, lanes] += dk
            dv_ref[keys, lanes] += dv
        att_blocks.append(jnp.concatenate([result[0] for result in results], 0))
        dq_blocks.append(jnp.concatenate([result[1] for result in results], 0))
    grads_ref[:, :HW] = transposed(jnp.concatenate(dq_blocks, 1))
    grads_ref[:, HW : 2 * HW] = dk_ref[...].astype(BF16)
    grads_ref[:, 2 * HW :] = dv_ref[...].astype(BF16)
    term_qkv = dot_nn(hidden_t, grads_ref[...]).astype(BF16)
    out_ref[...] = dot_nn(jnp.concatenate(att_blocks, 1), cot).astype(BF16)
    hidden_ref[...] = dot_nt(grads_ref[...], w_ref[...])
    return term_qkv


def row_kernel(x_any, cot_any, gain_any, wqkv_any, wout_any, qkv_ref, *refs):
    qkv_ref[...] = row_part(x_any, cot_any, gain_any, wqkv_any, wout_any, *refs)


def row_chip_kernel(
    place_ref, x_any, cot_any, gain_any, wqkv_any, wout_any,
    send_1, send_2, keep_1, keep_2, rows_ref, *refs,
):
    rows = rows_ref.shape[0]
    at = pl.multiple_of((place_ref[0] * 2 + place_ref[1]) * rows, rows)
    own = started(pltpu.make_async_copy(wqkv_any.at[pl.ds(at, rows), :], rows_ref, refs[-1].at[7]))
    term_qkv = row_part(x_any, cot_any, gain_any, wqkv_any, wout_any, *refs)
    chips, lanes = slice(0, send_1.shape[0]), slice(0, send_1.shape[2])
    split_cores(term_qkv[:, : lanes.stop], place_ref[1], send_1, keep_1, chips, lanes)
    split_cores(term_qkv[:, lanes.stop :], place_ref[1], send_2, keep_2, chips, lanes)
    finished(*own)


def column_part(moved_ref, gain_ref, w_ref, wo_ref, weight_waits, grads_ref):
    all_rows, _, share, width = moved_ref.shape
    group = math.gcd(share, 16)
    block = all_rows * group

    def gathered(which):
        pieces = []
        for start in range(0, share, group):
            piece = moved_ref[:, which, start : start + group, :]
            if group % 16 == 0:
                pieces.append(piece.reshape(block, width))
            else:
                pieces.append(piece.astype(F32).reshape(block, width).astype(BF16))
        return jnp.concatenate(pieces, 0)

    _, normed = rms_parts(gathered(0).astype(F32))
    hidden = (normed * gain_ref[...]).astype(BF16)
    hidden_t = transposed(hidden)
    finished(*weight_waits)
    cot = gathered(1)
    q, k, v, g = project(hidden, cot, w_ref, wo_ref)
    kt, vt, gt = transposed(k), transposed(v), transposed(g)
    query = lax.broadcasted_iota(jnp.int32, (block, 2 * block), 1) % block
    key = lax.broadcasted_iota(jnp.int32, (block, 2 * block), 0)
    mask = (query >= key) & (query % group == key % group)
    pairs = [slice(i * 2 * HD, (i + 1) * 2 * HD) for i in range(HH // 2)]
    blocks = [slice(at, at + block) for at in range(0, all_rows * share, block)]
    items = [
        (
            head_pair(q[rows, lanes]), head_pair(g[rows, lanes]), gt[lanes, rows],
            k[rows, lanes], v[rows, lanes], kt[lanes, rows], vt[lanes, rows],
        )
        for lanes in pairs
        for rows in blocks
    ]
    results = pair_steps(items, block, mask)
    places = [(lanes, rows) for lanes in pairs for rows in blocks]
    for (lanes, rows), (_, _, dk, dv) in zip(places, results):
        grads_ref[rows, HW + lanes.start : HW + lanes.stop] = dk.astype(BF16)
        grads_ref[rows, 2 * HW + lanes.start : 2 * HW + lanes.stop] = dv.astype(BF16)
    by_pair = [results[i * len(blocks) : (i + 1) * len(blocks)] for i in range(len(pairs))]
    attended, grad_q = [
        jnp.concatenate([jnp.concatenate([r[i] for r in some], 1) for some in by_pair], 0)
        for i in range(2)
    ]
    grads_ref[:, :HW] = transposed(grad_q)
    term_qkv = dot_nn(hidden_t, grads_ref[...]).astype(BF16)
    term_out = dot_nn(attended, cot).astype(BF16)
    return term_qkv, term_out


def column_kernel(
    moved_any, gain_any, wqkv_any, wout_any, row_qkv_ref, row_out_ref,
    terms_ref, grads_ref, w_ref,
    moved_ref, gain_ref, wo_ref, sems,
):
    copies = started(
        pltpu.make_async_copy(moved_any, moved_ref, sems.at[4]),
        pltpu.make_async_copy(gain_any, gain_ref, sems.at[5]),
    )
    weights = started(*weight_copies(wqkv_any, wout_any, w_ref, wo_ref, sems, 1))
    finished(*copies)
    term_qkv, term_out = column_part(moved_ref, gain_ref, w_ref, wo_ref, weights, grads_ref)
    width = terms_ref.shape[0]
    for i in range(3):
        at = i * width
        terms_ref[:, at : at + HW] = row_qkv_ref[:, i * HW : (i + 1) * HW]
        terms_ref[:, at + HW : at + 2 * HW] = term_qkv[:, i * HW : (i + 1) * HW]
    terms_ref[:HW, 3 * width :] = row_out_ref[...]
    terms_ref[HW:, 3 * width :] = term_out


def column_chip_kernel(
    place_ref, x_any, cot_any, own_any,
    near_1, near_2, near_3, far_1, far_2, far_3,
    gain_any, wqkv_any, wout_any, row_out_ref,
    send_ref, keep_ref, grads_ref, w_ref,
    moved_ref, gain_ref, wo_ref, sems,
):
    chip, core = place_ref[0], place_ref[1]
    share = moved_ref.shape[2]
    at = pl.multiple_of((chip * 2 + core) * share, share)
    half = pl.multiple_of(core * share, share)
    me, other = chip * 2 + core, chip * 2 + 1 - core
    groups = []
    for which, source in enumerate((x_any, cot_any)):
        group = [
            (source.at[pl.ds(at, share), :], me),
            (own_any.at[which], other),
        ]
        for i, (near, far) in enumerate(((near_1, far_1), (near_2, far_2), (near_3, far_3))):
            there = 2 * (chip ^ (i + 1))
            group.append((near.at[which, pl.ds(half, share), :], there + core))
            group.append((far.at[which, pl.ds(half, share), :], there + 1 - core))
        base = 5 + which * len(group)
        groups.append([
            pltpu.make_async_copy(piece, moved_ref.at[row, which], sems.at[base + i])
            for i, (piece, row) in enumerate(group)
        ])
    first = started(*groups[0], pltpu.make_async_copy(gain_any, gain_ref, sems.at[4]))
    later = started(*weight_copies(wqkv_any, wout_any, w_ref, wo_ref, sems, 1), *groups[1])
    finished(*first)
    term_qkv, term_out = column_part(moved_ref, gain_ref, w_ref, wo_ref, later, grads_ref)
    chips = send_ref.shape[0]
    refs = core, send_ref, keep_ref
    out_lanes = slice(3 * HW, send_ref.shape[2])
    split_cores(term_qkv, *refs, slice(0, chips), slice(0, 3 * HW))
    split_cores(row_out_ref[...], *refs, slice(0, chips // 2), out_lanes)
    split_cores(term_out, *refs, slice(chips // 2, chips), out_lanes)


def back_kernel(grads_ref, w_ref, back_ref):
    grad_hidden = dot_nt(grads_ref[...], w_ref[...])
    all_rows, share, width = back_ref.shape
    group = math.gcd(share, 16)
    block = all_rows * group
    for i in range(share // group):
        piece = grad_hidden[i * block : (i + 1) * block].reshape(all_rows, group, width)
        back_ref[:, i * group : (i + 1) * group, :] = piece.astype(BF16)


def back_chip_kernel(place_ref, grads_ref, w_ref, send_ref, keep_ref):
    grad_hidden = dot_nt(grads_ref[...], w_ref[...])
    chips, share, width = keep_ref.shape
    group = math.gcd(share, 16)
    block = 2 * chips * group
    first = place_ref[1] == 0
    for i in range(share // group):
        piece = grad_hidden[i * block : (i + 1) * block].reshape(chips, 2, group, width)
        even, odd = piece[:, 0], piece[:, 1]
        at = slice(i * group, (i + 1) * group)
        send_ref[:, at, :] = jnp.where(first, odd, even).astype(BF16)
        keep_ref[:, at, :] = jnp.where(first, even, odd).astype(BF16)


def back_pack_kernel(place_ref, keep_ref, got_ref, own_ref, off_1, off_2, off_3):
    chip, core = place_ref[0], place_ref[1]
    share = keep_ref.shape[1]
    kept_at = pl.multiple_of(core * share, share)
    got_at = pl.multiple_of((1 - core) * share, share)
    for i, target in enumerate((own_ref, off_1, off_2, off_3)):
        target[pl.ds(kept_at, share), :] = keep_ref[chip ^ i]
        target[pl.ds(got_at, share), :] = got_ref[chip ^ i]


def input_kernel(x_ref, cot_ref, gain_ref, hidden_ref, back_ref, grad_ref):
    inverse_rms, normed = rms_parts(x_ref[...].astype(F32))
    grad_hidden = hidden_ref[...] + back_ref[...].astype(F32)
    grad_ref[...] = input_grad(normed, inverse_rms, grad_hidden, gain_ref[...], cot_ref[...])


def input_grad(normed, inverse_rms, grad_hidden, gain, cot):
    grad_normed = grad_hidden * gain
    projected = jnp.mean(grad_normed * normed, -1, keepdims=True)
    grad = inverse_rms * (grad_normed - normed * projected)
    return (cot.astype(F32) + grad).astype(BF16)


def input_chip_kernel(
    place_ref, x_ref, cot_ref, gain_ref, hidden_ref, own_ref, got_1, got_2, got_3, grad_ref
):
    chip = place_ref[0]
    count = own_ref.shape[0]
    for i, back_ref in enumerate((own_ref, got_1, got_2, got_3)):
        at = pl.ds(pl.multiple_of((chip ^ i) * count, count), count)
        inverse_rms, normed = rms_parts(x_ref[at, :].astype(F32))
        grad_hidden = hidden_ref[at, :] + back_ref[...].astype(F32)
        grad_ref[at, :] = input_grad(
            normed, inverse_rms, grad_hidden, gain_ref[...], cot_ref[at, :]
        )


def pack_kernel(place_ref, x_any, cot_any, own_ref, off_1, off_2, off_3, sems):
    chip, core = place_ref[0], place_ref[1]
    share = own_ref.shape[1]
    at = pl.multiple_of((chip * 2 + 1 - core) * share, share)
    copies = []
    for which, source in enumerate((x_any, cot_any)):
        copies.append(
            pltpu.make_async_copy(
                source.at[pl.ds(at, share), :], own_ref.at[which], sems.at[which]
            )
        )
        for i, target in enumerate((off_1, off_2, off_3)):
            there = pl.multiple_of((chip ^ (i + 1)) * 2 * share, 2 * share)
            copies.append(
                pltpu.make_async_copy(
                    source.at[pl.ds(there, 2 * share), :],
                    target.at[which],
                    sems.at[2 + 2 * i + which],
                )
            )
    finished(*started(*copies))


def chip_sum_kernel(place_ref, *refs):
    chip = place_ref[0]
    pieces, targets = refs[:-4], refs[-4:]
    count = len(pieces) // 2
    for i, target in enumerate(targets):
        at = 0
        for kept_ref, got_ref in zip(pieces[:count], pieces[count:]):
            total = kept_ref[chip ^ i].astype(F32) + got_ref[chip ^ i].astype(F32)
            target[:, at : at + total.shape[1]] = total.astype(target.dtype)
            at += total.shape[1]


def layer_sum_kernel(place_ref, own_ref, got_1, got_2, got_3, send_ref, keep_ref):
    upper = place_ref[2] == 1
    total = own_ref[...] + (
        (got_1[...].astype(F32) + got_2[...].astype(F32)) + got_3[...].astype(F32)
    )
    half = total.shape[0] // 2
    low, high = total[:half], total[half:]
    send_ref[...] = jnp.where(upper, low, high).astype(BF16)
    keep_ref[...] = jnp.where(upper, high, low)


def add_kernel(kept_ref, got_ref, out_ref):
    out_ref[...] = (kept_ref[...].astype(F32) + got_ref[...].astype(F32)).astype(BF16)


def result_kernel(
    place_ref, row_held, row_got, held_ref, got_ref, w_ref, gain_ref, qkv_ref, out_ref, grad_ref
):
    rows = qkv_ref.shape[0]
    at = pl.multiple_of((place_ref[0] * 2 + place_ref[1]) * rows, rows)
    upper = place_ref[2] == 1
    half = rows // 2
    width = out_ref.shape[1]

    def ordered(held_ref, got_ref, lanes):
        held, got = held_ref[:, lanes].astype(F32), got_ref[:, lanes].astype(F32)
        return (jnp.where(upper, got, held), jnp.where(upper, held, got))

    for i in range(3):
        lanes = slice(i * HW, (i + 1) * HW)
        for at_to, pair in ((i * width, (row_held, row_got)), (i * width + HW, (held_ref, got_ref))):
            to = slice(at_to, at_to + HW)
            qkv_ref[:half, to], qkv_ref[half:, to] = ordered(*pair, lanes)
    out_ref[:half], out_ref[half:] = ordered(held_ref, got_ref, slice(3 * HW, 3 * HW + width))
    total = jnp.sum(qkv_ref[...] * w_ref[...].astype(F32), -1, keepdims=True)
    shape = (rows, gain_ref.shape[1])
    row = lax.broadcasted_iota(jnp.int32, shape, 0)
    feature = lax.broadcasted_iota(jnp.int32, shape, 1)
    gain = jnp.sum(jnp.where(feature == row + at, gain_ref[...], 0.0), -1, keepdims=True)
    shape = (rows, grad_ref.shape[1])
    same = lax.broadcasted_iota(jnp.int32, shape, 0) == lax.broadcasted_iota(jnp.int32, shape, 1)
    grad_ref[...] = jnp.sum(jnp.where(same, total / gain, 0.0), 0, keepdims=True)


def call(kernel, name, ins, outs, scratch=(), vmem=SMALL_VMEM, out_specs=None):
    out_specs = out_specs or [VMEM] * len(outs)
    places = [{id(HBM): pltpu.HBM, id(PINNED): pltpu.VMEM}.get(id(spec)) for spec in out_specs]
    outs = [place(*out) if place else shaped(*out) for place, out in zip(places, outs)]
    args = [
        pltpu.with_memory_space_constraint(array, pltpu.HBM) if spec is HBM else array
        for spec, array in ins
    ]
    return pl.pallas_call(
        kernel,
        out_shape=outs,
        in_specs=[spec for spec, _ in ins],
        out_specs=out_specs,
        scratch_shapes=scratch,
        name=name,
        cost_estimate=pl.CostEstimate(flops=0, bytes_accessed=0, transcendentals=0),
        compiler_params=pltpu.CompilerParams(vmem_limit_bytes=vmem),
    )(*args)


def swap(array, axis, bits):
    count = lax.axis_size(axis)
    return lax.ppermute(array, axis, [(i, i ^ bits) for i in range(count)])


def add_cores(place, keep, got, name):
    rows, wide = keep[0].shape[1], sum(one.shape[2] for one in keep)
    return call(
        chip_sum_kernel,
        name + "_add_cores",
        [(SMEM, place), *[(VMEM, one) for one in (*keep, *got)]],
        [((rows, wide), F32)] + [((rows, wide), BF16)] * 3,
        out_specs=[PINNED, VMEM, VMEM, VMEM],
    )


def cross_chips(off_1, off_2, off_3):
    got_3 = swap(off_3, "seq", 6)
    got_1 = swap(off_1, "seq", 2)
    got_2 = swap(off_2, "seq", 4)
    return got_1, got_2, got_3


def add_chips(place, owned, got, name):
    rows, wide = owned.shape
    return call(
        layer_sum_kernel,
        name + "_add_chips",
        [(SMEM, place), (VMEM, owned), *[(VMEM, one) for one in got]],
        [((rows // 2, wide), BF16), ((rows // 2, wide), F32)],
        out_specs=[VMEM, PINNED],
    )


def add_two(kept, got, name):
    (total,) = call(add_kernel, name, [(VMEM, kept), (VMEM, got)], [(kept.shape, BF16)])
    return total


def body(inputs, norm_gain, qkv_weight, out_weight, out_cotan):
    columns, width = inputs.shape[2:]
    n = lax.axis_size("seq")
    m = lax.axis_size("dp")
    share = columns // n
    row_share = width // n
    row_width, col_width = 3 * HW, 3 * HW + width
    x = inputs.reshape(columns, width)
    cot = out_cotan.reshape(columns, width)
    gain = norm_gain.reshape(1, width)
    chips = 4
    layered = n == 2 * chips and m == 4 and row_share == share
    here = lax.axis_index("seq")
    place = jnp.stack([here // 2, here % 2, lax.axis_index("dp") % 2]).astype(jnp.int32)
    weight_scratch = [
        pltpu.VMEM((1, width), F32),
        pltpu.VMEM((width, 3 * HW), BF16),
        pltpu.VMEM((HW, width), BF16),
    ]
    weights = [(HBM, gain), (HBM, qkv_weight), (HBM, out_weight)]
    col_outs = [((columns, 3 * HW), BF16), ((width, 3 * HW), BF16)]

    if layered:
        packed = call(
            pack_kernel,
            "pack_columns",
            [(SMEM, place), (HBM, x), (HBM, cot)],
            [((2, share, width), BF16)] + [((2, 2 * share, width), BF16)] * 3,
            [pltpu.SemaphoreType.DMA((8,))],
            out_specs=[ANY] * 4,
        )
        near_1, near_2, near_3 = cross_chips(*packed[1:])
        own = swap(packed[0], "seq", 1)
        placed, _ = lax.optimization_barrier((place, packed[0]))
    else:
        outgoing = jnp.stack([x.reshape(n, share, width), cot.reshape(n, share, width)], 1)
        moved = lax.all_to_all(outgoing, "seq", split_axis=0, concat_axis=0, tiled=True)
        placed = place

    split_out = ((chips, row_share, row_width // 2), BF16)
    term_outs = [split_out] * 4 if layered else [((width, row_width), BF16)]
    if layered:
        term_outs.append(((row_share, 3 * width), BF16))
    *row_terms, row_out, row_hidden, x_near, cot_near = call(
        row_chip_kernel if layered else row_kernel,
        "row_heads",
        [(SMEM, placed)] * layered + [(HBM, x), (HBM, cot), *weights],
        [
            *term_outs, ((HW, width), BF16), ((columns, width), F32),
            ((columns, width), BF16), ((columns, width), BF16),
        ],
        [
            *weight_scratch,
            pltpu.VMEM((columns, HW), F32),
            pltpu.VMEM((columns, HW), F32),
            pltpu.VMEM((columns, 3 * HW), BF16),
            pltpu.SemaphoreType.DMA((8,)),
        ],
        BIG_VMEM,
        [VMEM] * 4 * layered + [PINNED] * 5 if layered else [VMEM] * 5,
    )
    moved_scratch = pltpu.VMEM((n, 2, share, width), BF16)
    if layered:
        *row_terms, weight_rows = row_terms
        near_1, *row_terms = lax.optimization_barrier((near_1, *row_terms))
        row_sent = [swap(one, "seq", 1) for one in row_terms[:2]]
        row_owned, *row_off = add_cores(place, row_terms[2:], row_sent, "row")
        near_1, near_2, near_3, row_owned = lax.optimization_barrier(
            (near_1, near_2, near_3, row_owned)
        )
        far_3, far_1, far_2 = swap(near_3, "seq", 1), swap(near_1, "seq", 1), swap(near_2, "seq", 1)
        row_got = cross_chips(*row_off)
        send, keep, *col_grads = call(
            column_chip_kernel,
            "column_heads",
            [
                (SMEM, place), (HBM, x), (HBM, cot), (ANY, own),
                (ANY, near_1), (ANY, near_2), (ANY, near_3),
                (ANY, far_1), (ANY, far_2), (ANY, far_3), *weights, (VMEM, row_out),
            ],
            [((chips, row_share, col_width), BF16)] * 2 + col_outs,
            [moved_scratch, weight_scratch[0], weight_scratch[2], pltpu.SemaphoreType.DMA((21,))],
            BIG_VMEM,
            [VMEM, VMEM, PINNED, PINNED],
        )
        send, row_got = lax.optimization_barrier((send, row_got))
        row_next, row_kept = add_chips(place, row_owned, row_got, "row")
        back_send, back_keep = call(
            back_chip_kernel,
            "column_grad_hidden",
            [(SMEM, place), *[(VMEM, one) for one in col_grads]],
            [((chips, share, width), BF16)] * 2,
        )
        keep, row_kept, back_keep = lax.optimization_barrier((keep, row_kept, back_keep))
        owned, *off = add_cores(place, [keep], [swap(send, "seq", 1)], "column")
        got = cross_chips(*off)
        row_pair = add_two(row_kept, swap(row_next, "dp", 1), "row_add_pair")
        row_pair, _ = lax.optimization_barrier((row_pair, owned))
        row_held = add_two(row_pair, swap(row_pair, "dp", 2), "row_add_pairs")
        back = call(
            back_pack_kernel,
            "pack_grad_hidden",
            [(SMEM, place), (VMEM, back_keep), (VMEM, swap(back_send, "seq", 1))],
            [((2 * share, width), BF16)] * 4,
        )
        *back, owned, row_held = lax.optimization_barrier((*back, owned, row_held))
        to_next, kept = add_chips(place, owned, got, "column")
        *back, kept = lax.optimization_barrier((*back, kept))
        row_other = swap(row_held, "dp", 1)
        pair_sum = add_two(kept, swap(to_next, "dp", 1), "column_add_pair")
        held = add_two(pair_sum, swap(pair_sum, "dp", 2), "column_add_pairs")
        (grad,) = call(
            input_chip_kernel,
            "input_grad",
            [
                (SMEM, place), (VMEM, x_near), (VMEM, cot_near), (VMEM, gain), (VMEM, row_hidden),
                (VMEM, back[0]), *[(VMEM, one) for one in cross_chips(*back[1:])],
            ],
            [((columns, width), BF16)],
        )
        held, row_other, grad = lax.optimization_barrier((held, row_other, grad))
        other = swap(held, "dp", 1)
        sum_qkv, sum_out, sum_gain = call(
            result_kernel,
            "result",
            [
                (SMEM, place), (VMEM, row_held), (VMEM, row_other), (VMEM, held), (VMEM, other),
                (VMEM, weight_rows), (VMEM, gain),
            ],
            [((row_share, 3 * width), F32), ((row_share, width), F32), ((1, row_share), F32)],
        )
        sum_gain = sum_gain.reshape(row_share)
    else:
        terms, *col_grads = call(
            column_kernel,
            "column_heads",
            [(ANY, moved), *weights, (VMEM, row_terms[0]), (VMEM, row_out)],
            [((width, 4 * width), BF16), *col_outs],
            [moved_scratch, weight_scratch[0], weight_scratch[2], pltpu.SemaphoreType.DMA((6,))],
            BIG_VMEM,
        )
        (back,) = call(
            back_kernel,
            "column_grad_hidden",
            [(VMEM, one) for one in col_grads],
            [((n, share, width), BF16)],
        )
        returned = lax.all_to_all(back, "seq", split_axis=0, concat_axis=0, tiled=True)
        (grad,) = call(
            input_kernel,
            "input_grad",
            [
                (VMEM, x_near), (VMEM, cot_near), (VMEM, gain), (VMEM, row_hidden),
                (VMEM, returned.reshape(columns, width)),
            ],
            [((columns, width), BF16)],
        )
        terms = lax.all_to_all(
            terms.reshape(n, row_share, 4 * width), "seq", split_axis=0, concat_axis=0, tiled=True
        )
        total = jnp.sum(terms.astype(F32), 0)
        for step in range(m.bit_length() - 1):
            sent = total.astype(BF16)
            total = sent.astype(F32) + swap(sent, "dp", 1 << step).astype(F32)
        sum_qkv, sum_out = total[:, : 3 * width], total[:, 3 * width :]
        own_gain = lax.dynamic_slice_in_dim(norm_gain, here * row_share, row_share, 0)
        own_weight = lax.dynamic_slice_in_dim(qkv_weight, here * row_share, row_share, 0)
        sum_gain = jnp.sum(sum_qkv * own_weight.astype(F32), -1) / own_gain
    return (grad.reshape(inputs.shape), sum_qkv, sum_out, sum_gain)


def solution(mesh):
    return jax.shard_map(
        body,
        mesh=mesh,
        in_specs=(P("dp", "seq", None, None), P(), P(), P(), P("dp", "seq", None, None)),
        out_specs=(P("dp", "seq", None, None), P("seq", None), P("seq", None), P("seq")),
        check_vma=False,
    )
```

```python
import math

import jax
import jax.numpy as jnp
from jax import lax
from jax.experimental import pallas as pl
from jax.experimental.pallas import tpu as pltpu
from jax.sharding import PartitionSpec as P

H = 8
HD = 64
HH = H // 2
HW = HH * HD
SCALE = HD ** (-0.5)
F32 = jnp.float32
BF16 = jnp.bfloat16
QUERY_BLOCK = 128
BIG_VMEM = 20 * 1024 * 1024
SMALL_VMEM = 8 * 1024 * 1024
ANY = pl.BlockSpec(memory_space=pl.ANY)
VMEM = pl.BlockSpec(memory_space=pltpu.VMEM)
SMEM = pl.BlockSpec(memory_space=pltpu.SMEM)
HBM = pl.BlockSpec(memory_space=pltpu.HBM)
CHIP_STEPS = (3, 2, 1)
PINNED = pl.BlockSpec(memory_space=pltpu.VMEM)
shaped = jax.ShapeDtypeStruct


def dot_nn(a, b):
    return lax.dot_general(a, b, (((1,), (0,)), ((), ())), preferred_element_type=F32)


def dot_nt(a, b):
    return lax.dot_general(a, b, (((1,), (1,)), ((), ())), preferred_element_type=F32)


def rms_parts(x):
    inverse_rms = lax.rsqrt(jnp.mean(x * x, -1, keepdims=True) + 1e-05)
    return inverse_rms, x * inverse_rms


def transposed(x):
    block = math.gcd(x.shape[1], 256)
    eye = (
        lax.broadcasted_iota(jnp.int32, (block, block), 0)
        == lax.broadcasted_iota(jnp.int32, (block, block), 1)
    ).astype(F32).astype(BF16)
    parts = [
        dot_nt(eye, x[:, at : at + block]).astype(BF16) for at in range(0, x.shape[1], block)
    ]
    return parts[0] if len(parts) == 1 else jnp.concatenate(parts, 0)


def head_pair(x):
    lane = lax.broadcasted_iota(jnp.int32, x.shape, 1)
    zero = jnp.zeros_like(x)
    return jnp.concatenate([jnp.where(lane < HD, x, zero), jnp.where(lane < HD, zero, x)], 0)


def both_heads(both, count):
    return jnp.concatenate([both[:HD, :count], both[HD:, count:]], 0)


def pair_steps(items, mask_rows, mask):
    count = items[0][2].shape[1]
    scores = [dot_nt(k, q2) for q2, _, _, k, _, _, _ in items]
    prob_grads = [dot_nt(v, g2) for _, g2, _, _, v, _, _ in items]
    probs = []
    for score in scores:
        first = score.shape[0] - mask_rows
        tail = jnp.where(mask, score[first:], -1e30)
        score = tail if first == 0 else jnp.concatenate([score[:first], tail], 0)
        exponent = jnp.exp(score - jnp.max(score, 0, keepdims=True))
        probs.append(exponent * (1.0 / jnp.sum(exponent, 0, keepdims=True)))
    weights = [prob.astype(BF16) for prob in probs]
    attended = [
        both_heads(dot_nn(item[6], weight), count).astype(BF16)
        for item, weight in zip(items, weights)
    ]
    score_grads = []
    for item, att, prob, prob_grad in zip(items, attended, probs, prob_grads):
        product = item[2].astype(F32) * att.astype(F32)
        delta = [jnp.sum(part, 0, keepdims=True) for part in (product[:HD], product[HD:])]
        score_grads.append((prob * (prob_grad - jnp.concatenate(delta, 1))).astype(BF16))
    grad_q = [
        (both_heads(dot_nn(item[5], score_grad), count) * SCALE).astype(BF16)
        for item, score_grad in zip(items, score_grads)
    ]
    grad_k = [dot_nn(score_grad, item[0]) for item, score_grad in zip(items, score_grads)]
    grad_v = [dot_nn(weight, item[1]) for item, weight in zip(items, weights)]
    return list(zip(attended, grad_q, grad_k, grad_v))


def split_cores(piece, core, send_ref, keep_ref, chips, lanes):
    rows = send_ref.shape[1]
    parts = piece.reshape(chips.stop - chips.start, 2, rows, piece.shape[1])
    even, odd = parts[:, 0], parts[:, 1]
    first = core == 0
    send_ref[chips, :, lanes] = jnp.where(first, odd, even)
    keep_ref[chips, :, lanes] = jnp.where(first, even, odd)


def qkv_copies(wqkv_ref, w_ref, sems, second):
    width = wqkv_ref.shape[0]
    return [
        pltpu.make_async_copy(
            wqkv_ref.at[:, pl.ds(i * width + second * HW, HW)],
            w_ref.at[:, pl.ds(i * HW, HW)],
            sems.at[i],
        )
        for i in range(3)
    ]


def weight_copies(wqkv_ref, wout_ref, w_ref, wo_ref, sems, second):
    out_rows = wout_ref.at[pl.ds(second * HW, HW), :]
    return [
        *qkv_copies(wqkv_ref, w_ref, sems, second),
        pltpu.make_async_copy(out_rows, wo_ref, sems.at[3]),
    ]


def started(*copies):
    for copy in copies:
        copy.start()
    return copies


def finished(*copies):
    for copy in copies:
        copy.wait()


def project(hidden, cot, w_ref, wo_ref):
    projected = dot_nn(hidden, w_ref[...]).astype(BF16)
    q, k, v = [projected[:, i * HW : (i + 1) * HW] for i in range(3)]
    g = dot_nt(cot, wo_ref[...]).astype(BF16)
    return q * jnp.asarray(SCALE, BF16), k, v, g


def row_part(
    x_any, cot_any, gain_any, wqkv_any, wout_any,
    out_ref, base_ref, normed_ref, inverse_ref,
    x_ref, cot_ref, gain_ref, w_ref, wo_ref, dk_ref, dv_ref, grads_ref, sems,
):
    first = started(
        pltpu.make_async_copy(x_any, x_ref, sems.at[4]),
        pltpu.make_async_copy(gain_any, gain_ref, sems.at[5]),
    )
    later = started(
        *weight_copies(wqkv_any, wout_any, w_ref, wo_ref, sems, 0),
        pltpu.make_async_copy(cot_any, cot_ref, sems.at[6]),
    )
    dk_ref[...] = jnp.zeros_like(dk_ref)
    dv_ref[...] = jnp.zeros_like(dv_ref)
    finished(*first)
    tokens = x_ref.shape[0]
    inverse_ref[...], normed_ref[...] = rms_parts(x_ref[...].astype(F32))
    hidden = (normed_ref[...] * gain_ref[...]).astype(BF16)
    hidden_t = transposed(hidden)
    finished(*later)
    cot = cot_ref[...]
    q, k, v, g = project(hidden, cot, w_ref, wo_ref)
    kt, vt, gt = transposed(k), transposed(v), transposed(g)
    step = math.gcd(tokens, QUERY_BLOCK)
    query = lax.broadcasted_iota(jnp.int32, (step, 2 * step), 1) % step
    mask = query >= lax.broadcasted_iota(jnp.int32, (step, 2 * step), 0)
    pairs = [slice(i * 2 * HD, (i + 1) * 2 * HD) for i in range(HH // 2)]
    att_blocks, dq_blocks = [], []
    for start in range(0, tokens, step):
        rows, keys = slice(start, start + step), slice(0, start + step)
        items = [
            (
                head_pair(q[rows, lanes]), head_pair(g[rows, lanes]), gt[lanes, rows],
                k[keys, lanes], v[keys, lanes], kt[lanes, keys], vt[lanes, keys],
            )
            for lanes in pairs
        ]
        results = pair_steps(items, step, mask)
        for lanes, (_, _, dk, dv) in zip(pairs, results):
            dk_ref[keys, lanes] += dk
            dv_ref[keys, lanes] += dv
        att_blocks.append(jnp.concatenate([result[0] for result in results], 0))
        dq_blocks.append(jnp.concatenate([result[1] for result in results], 0))
    grads_ref[:, :HW] = transposed(jnp.concatenate(dq_blocks, 1))
    grads_ref[:, HW : 2 * HW] = dk_ref[...].astype(BF16)
    grads_ref[:, 2 * HW :] = dv_ref[...].astype(BF16)
    term_qkv = dot_nn(hidden_t, grads_ref[...]).astype(BF16)
    out_ref[...] = dot_nn(jnp.concatenate(att_blocks, 1), cot).astype(BF16)
    grad_normed = dot_nt(grads_ref[...], w_ref[...]) * gain_ref[...]
    base_ref[...] = input_grad(
        cot_ref[...].astype(F32), normed_ref[...], inverse_ref[...], grad_normed
    )
    return term_qkv


def row_kernel(x_any, cot_any, gain_any, wqkv_any, wout_any, qkv_ref, *refs):
    qkv_ref[...] = row_part(x_any, cot_any, gain_any, wqkv_any, wout_any, *refs)


def row_chip_kernel(
    place_ref, x_any, cot_any, gain_any, wqkv_any, wout_any,
    send_1, send_2, keep_1, keep_2, rows_ref, *refs,
):
    rows = rows_ref.shape[0]
    at = pl.multiple_of((place_ref[0] * 2 + place_ref[1]) * rows, rows)
    own = started(pltpu.make_async_copy(wqkv_any.at[pl.ds(at, rows), :], rows_ref, refs[-1].at[7]))
    term_qkv = row_part(x_any, cot_any, gain_any, wqkv_any, wout_any, *refs)
    chips, lanes = slice(0, send_1.shape[0]), slice(0, send_1.shape[2])
    split_cores(term_qkv[:, : lanes.stop], place_ref[1], send_1, keep_1, chips, lanes)
    split_cores(term_qkv[:, lanes.stop :], place_ref[1], send_2, keep_2, chips, lanes)
    finished(*own)


def column_part(moved_ref, gain_ref, w_ref, wo_ref, weight_waits, grads_ref):
    all_rows, _, share, width = moved_ref.shape
    group = math.gcd(share, 16)
    block = all_rows * group

    def gathered(which):
        pieces = []
        for start in range(0, share, group):
            piece = moved_ref[:, which, start : start + group, :]
            if group % 16 == 0:
                pieces.append(piece.reshape(block, width))
            else:
                pieces.append(piece.astype(F32).reshape(block, width).astype(BF16))
        return jnp.concatenate(pieces, 0)

    _, normed = rms_parts(gathered(0).astype(F32))
    hidden = (normed * gain_ref[...]).astype(BF16)
    hidden_t = transposed(hidden)
    finished(*weight_waits)
    cot = gathered(1)
    q, k, v, g = project(hidden, cot, w_ref, wo_ref)
    kt, vt, gt = transposed(k), transposed(v), transposed(g)
    query = lax.broadcasted_iota(jnp.int32, (block, 2 * block), 1) % block
    key = lax.broadcasted_iota(jnp.int32, (block, 2 * block), 0)
    mask = (query >= key) & (query % group == key % group)
    pairs = [slice(i * 2 * HD, (i + 1) * 2 * HD) for i in range(HH // 2)]
    blocks = [slice(at, at + block) for at in range(0, all_rows * share, block)]
    items = [
        (
            head_pair(q[rows, lanes]), head_pair(g[rows, lanes]), gt[lanes, rows],
            k[rows, lanes], v[rows, lanes], kt[lanes, rows], vt[lanes, rows],
        )
        for lanes in pairs
        for rows in blocks
    ]
    results = pair_steps(items, block, mask)
    places = [(lanes, rows) for lanes in pairs for rows in blocks]
    for (lanes, rows), (_, _, dk, dv) in zip(places, results):
        grads_ref[rows, HW + lanes.start : HW + lanes.stop] = dk.astype(BF16)
        grads_ref[rows, 2 * HW + lanes.start : 2 * HW + lanes.stop] = dv.astype(BF16)
    by_pair = [results[i * len(blocks) : (i + 1) * len(blocks)] for i in range(len(pairs))]
    attended, grad_q = [
        jnp.concatenate([jnp.concatenate([r[i] for r in some], 1) for some in by_pair], 0)
        for i in range(2)
    ]
    grads_ref[:, :HW] = transposed(grad_q)
    term_qkv = dot_nn(hidden_t, grads_ref[...]).astype(BF16)
    term_out = dot_nn(attended, cot).astype(BF16)
    return term_qkv, term_out


def column_kernel(
    moved_any, gain_any, wqkv_any, wout_any, row_qkv_ref, row_out_ref,
    terms_ref, grads_ref, w_ref,
    moved_ref, gain_ref, wo_ref, sems,
):
    copies = started(
        pltpu.make_async_copy(moved_any, moved_ref, sems.at[4]),
        pltpu.make_async_copy(gain_any, gain_ref, sems.at[5]),
    )
    weights = started(*weight_copies(wqkv_any, wout_any, w_ref, wo_ref, sems, 1))
    finished(*copies)
    term_qkv, term_out = column_part(moved_ref, gain_ref, w_ref, wo_ref, weights, grads_ref)
    width = terms_ref.shape[0]
    for i in range(3):
        at = i * width
        terms_ref[:, at : at + HW] = row_qkv_ref[:, i * HW : (i + 1) * HW]
        terms_ref[:, at + HW : at + 2 * HW] = term_qkv[:, i * HW : (i + 1) * HW]
    terms_ref[:HW, 3 * width :] = row_out_ref[...]
    terms_ref[HW:, 3 * width :] = term_out


def column_chip_kernel(
    place_ref, x_any, cot_any, own_any,
    near_1, near_2, near_3, far_1, far_2, far_3,
    gain_any, wqkv_any, wout_any, row_out_ref,
    send_ref, keep_ref, grads_ref, w_ref,
    moved_ref, gain_ref, wo_ref, sems,
):
    chip, core = place_ref[0], place_ref[1]
    share = moved_ref.shape[2]
    at = pl.multiple_of((chip * 2 + core) * share, share)
    half = pl.multiple_of(core * share, share)
    me, other = chip * 2 + core, chip * 2 + 1 - core
    groups = []
    for which, source in enumerate((x_any, cot_any)):
        group = [
            (source.at[pl.ds(at, share), :], me),
            (own_any.at[which], other),
        ]
        for step, near, far in zip(CHIP_STEPS, (near_1, near_2, near_3), (far_1, far_2, far_3)):
            there = 2 * (chip ^ step)
            group.append((near.at[which, pl.ds(half, share), :], there + core))
            group.append((far.at[which, pl.ds(half, share), :], there + 1 - core))
        base = 5 + which * len(group)
        groups.append([
            pltpu.make_async_copy(piece, moved_ref.at[row, which], sems.at[base + i])
            for i, (piece, row) in enumerate(group)
        ])
    first = started(*groups[0], pltpu.make_async_copy(gain_any, gain_ref, sems.at[4]))
    later = started(*weight_copies(wqkv_any, wout_any, w_ref, wo_ref, sems, 1), *groups[1])
    finished(*first)
    term_qkv, term_out = column_part(moved_ref, gain_ref, w_ref, wo_ref, later, grads_ref)
    chips = send_ref.shape[0]
    refs = core, send_ref, keep_ref
    out_lanes = slice(3 * HW, send_ref.shape[2])
    split_cores(term_qkv, *refs, slice(0, chips), slice(0, 3 * HW))
    split_cores(row_out_ref[...], *refs, slice(0, chips // 2), out_lanes)
    split_cores(term_out, *refs, slice(chips // 2, chips), out_lanes)


def back_kernel(grads_ref, w_ref, back_ref):
    grad_hidden = dot_nt(grads_ref[...], w_ref[...])
    all_rows, share, width = back_ref.shape
    group = math.gcd(share, 16)
    block = all_rows * group
    for i in range(share // group):
        piece = grad_hidden[i * block : (i + 1) * block].reshape(all_rows, group, width)
        back_ref[:, i * group : (i + 1) * group, :] = piece.astype(BF16)


def back_chip_kernel(place_ref, grads_ref, w_ref, send_ref, keep_ref):
    grad_hidden = dot_nt(grads_ref[...], w_ref[...])
    chips, share, width = keep_ref.shape
    group = math.gcd(share, 16)
    block = 2 * chips * group
    first = place_ref[1] == 0
    for i in range(share // group):
        piece = grad_hidden[i * block : (i + 1) * block].reshape(chips, 2, group, width)
        even, odd = piece[:, 0], piece[:, 1]
        at = slice(i * group, (i + 1) * group)
        send_ref[:, at, :] = jnp.where(first, odd, even).astype(BF16)
        keep_ref[:, at, :] = jnp.where(first, even, odd).astype(BF16)


def back_pack_kernel(place_ref, keep_ref, got_ref, own_ref, off_1, off_2, off_3):
    chip, core = place_ref[0], place_ref[1]
    share = keep_ref.shape[1]
    kept_at = pl.multiple_of(core * share, share)
    got_at = pl.multiple_of((1 - core) * share, share)
    for step, target in zip((0, *CHIP_STEPS), (own_ref, off_1, off_2, off_3)):
        target[pl.ds(kept_at, share), :] = keep_ref[chip ^ step]
        target[pl.ds(got_at, share), :] = got_ref[chip ^ step]


def input_kernel(base_ref, normed_ref, inverse_ref, gain_ref, back_ref, grad_ref):
    grad_ref[...] = input_grad(
        base_ref[...], normed_ref[...], inverse_ref[...], back_ref[...].astype(F32) * gain_ref[...]
    ).astype(BF16)


def input_grad(base, normed, inverse_rms, grad_normed):
    projected = jnp.mean(grad_normed * normed, -1, keepdims=True)
    return base + inverse_rms * (grad_normed - normed * projected)


def input_chip_kernel(
    place_ref, base_ref, normed_ref, inverse_ref, gain_ref, own_ref, got_1, got_2, got_3,
    grad_any, grad_ref, sems,
):
    chip = place_ref[0]
    count = own_ref.shape[0]
    copies = []
    for i, (step, back_ref) in enumerate(zip((0, *CHIP_STEPS), (own_ref, got_1, got_2, got_3))):
        at = pl.ds(pl.multiple_of((chip ^ step) * count, count), count)
        grad_normed = back_ref[...].astype(F32) * gain_ref[...]
        grad = input_grad(base_ref[at, :], normed_ref[at, :], inverse_ref[at, :], grad_normed)
        grad_ref[i] = grad.astype(BF16)
        copies += started(pltpu.make_async_copy(grad_ref.at[i], grad_any.at[at, :], sems.at[i]))
    finished(*copies)


def pack_kernel(place_ref, x_any, cot_any, own_ref, off_1, off_2, off_3, sems):
    chip, core = place_ref[0], place_ref[1]
    share = own_ref.shape[1]
    at = pl.multiple_of((chip * 2 + 1 - core) * share, share)
    copies = []
    for which, source in enumerate((x_any, cot_any)):
        copies.append(
            pltpu.make_async_copy(
                source.at[pl.ds(at, share), :], own_ref.at[which], sems.at[which]
            )
        )
        for i, (step, target) in enumerate(zip(CHIP_STEPS, (off_1, off_2, off_3))):
            there = pl.multiple_of((chip ^ step) * 2 * share, 2 * share)
            copies.append(
                pltpu.make_async_copy(
                    source.at[pl.ds(there, 2 * share), :],
                    target.at[which],
                    sems.at[2 + 2 * i + which],
                )
            )
    finished(*started(*copies))


def chip_sum_kernel(
    place_ref, keep_ref, got_ref, row_kept, row_got, own_ref, off_1, off_2, off_3
):
    chip = place_ref[0]
    cut, rows, fold = keep_ref.shape[2], row_kept.shape[1], row_kept.shape[2] // 2
    for step, target in zip((0, *CHIP_STEPS), (own_ref, off_1, off_2, off_3)):
        there = chip ^ step
        total = keep_ref[there].astype(F32) + got_ref[there].astype(F32)
        target[:, :cut] = total.astype(target.dtype)
        total = (row_kept[there] + row_got[there].astype(F32)).astype(target.dtype)
        target[:rows, cut:] = total[:, :fold]
        target[rows:, cut:] = total[:, fold:]


def row_cores_kernel(place_ref, keep_1, keep_2, got_1, got_2, send_ref, kept_ref):
    upper = place_ref[2] == 1
    half, cut = kept_ref.shape[1], keep_1.shape[2]
    for i, (keep_ref, got_ref) in enumerate(((keep_1, got_1), (keep_2, got_2))):
        lanes = slice(i * cut, (i + 1) * cut)
        total = keep_ref[...].astype(F32) + got_ref[...].astype(F32)
        low, high = total[:, :half], total[:, half:]
        send_ref[:, :, lanes] = jnp.where(upper, low, high).astype(BF16)
        kept_ref[:, :, lanes] = jnp.where(upper, high, low)


def layer_sum_kernel(place_ref, own_ref, got_1, got_2, got_3, send_ref, keep_ref, row_ref):
    upper = place_ref[2] == 1
    total = own_ref[...] + (
        (got_1[...].astype(F32) + got_2[...].astype(F32)) + got_3[...].astype(F32)
    )
    half, cut, fold = keep_ref.shape[0], keep_ref.shape[1], row_ref.shape[1] // 2
    low, high = total[:half], total[half:]
    send_ref[...] = jnp.where(upper, low[:, :cut], high[:, :cut]).astype(BF16)
    keep_ref[...] = jnp.where(upper, high[:, :cut], low[:, :cut])
    row_ref[:, :fold] = low[:, cut:].astype(BF16)
    row_ref[:, fold:] = high[:, cut:].astype(BF16)


def join_kernel(kept_ref, got_ref, row_ref, out_ref):
    cut = kept_ref.shape[1]
    out_ref[:, :cut] = (kept_ref[...] + got_ref[...].astype(F32)).astype(BF16)
    out_ref[:, cut:] = row_ref[...]


def add_kernel(kept_ref, got_ref, out_ref):
    out_ref[...] = (kept_ref[...].astype(F32) + got_ref[...].astype(F32)).astype(BF16)


def result_kernel(place_ref, held_ref, got_ref, w_ref, gain_ref, qkv_ref, out_ref, grad_ref):
    rows = qkv_ref.shape[0]
    at = pl.multiple_of((place_ref[0] * 2 + place_ref[1]) * rows, rows)
    upper = place_ref[2] == 1
    half = rows // 2
    width = out_ref.shape[1]

    def ordered(lanes):
        held, got = held_ref[:, lanes].astype(F32), got_ref[:, lanes].astype(F32)
        return (jnp.where(upper, got, held), jnp.where(upper, held, got))

    row_at = 3 * HW + width
    for i in range(3):
        for at_from, at_to in ((row_at + i * HW, i * width), (i * HW, i * width + HW)):
            to = slice(at_to, at_to + HW)
            qkv_ref[:half, to], qkv_ref[half:, to] = ordered(slice(at_from, at_from + HW))
    out_ref[:half], out_ref[half:] = ordered(slice(3 * HW, row_at))
    total = jnp.sum(qkv_ref[...] * w_ref[...].astype(F32), -1, keepdims=True)
    shape = (rows, gain_ref.shape[1])
    row = lax.broadcasted_iota(jnp.int32, shape, 0)
    feature = lax.broadcasted_iota(jnp.int32, shape, 1)
    gain = jnp.sum(jnp.where(feature == row + at, gain_ref[...], 0.0), -1, keepdims=True)
    shape = (rows, grad_ref.shape[1])
    same = lax.broadcasted_iota(jnp.int32, shape, 0) == lax.broadcasted_iota(jnp.int32, shape, 1)
    grad_ref[...] = jnp.sum(jnp.where(same, total / gain, 0.0), 0, keepdims=True)


def call(kernel, name, ins, outs, scratch=(), vmem=SMALL_VMEM, out_specs=None):
    out_specs = out_specs or [VMEM] * len(outs)
    places = [{id(HBM): pltpu.HBM, id(PINNED): pltpu.VMEM}.get(id(spec)) for spec in out_specs]
    outs = [place(*out) if place else shaped(*out) for place, out in zip(places, outs)]
    args = [
        pltpu.with_memory_space_constraint(array, pltpu.HBM) if spec is HBM else array
        for spec, array in ins
    ]
    return pl.pallas_call(
        kernel,
        out_shape=outs,
        in_specs=[spec for spec, _ in ins],
        out_specs=out_specs,
        scratch_shapes=scratch,
        name=name,
        cost_estimate=pl.CostEstimate(flops=0, bytes_accessed=0, transcendentals=0),
        compiler_params=pltpu.CompilerParams(vmem_limit_bytes=vmem),
    )(*args)


def swap(array, axis, bits):
    count = lax.axis_size(axis)
    return lax.ppermute(array, axis, [(i, i ^ bits) for i in range(count)])


def cross_chips(*offs):
    return [swap(off, "seq", 2 * step) for off, step in zip(offs, CHIP_STEPS)]


def add_two(kept, got, name):
    (total,) = call(add_kernel, name, [(VMEM, kept), (VMEM, got)], [(kept.shape, BF16)])
    return total


def body(inputs, norm_gain, qkv_weight, out_weight, out_cotan):
    columns, width = inputs.shape[2:]
    n = lax.axis_size("seq")
    m = lax.axis_size("dp")
    share = columns // n
    row_share = width // n
    row_width, col_width = 3 * HW, 3 * HW + width
    x = inputs.reshape(columns, width)
    cot = out_cotan.reshape(columns, width)
    gain = norm_gain.reshape(1, width)
    chips = 4
    layered = n == 2 * chips and m == 4 and row_share == share
    here = lax.axis_index("seq")
    layer = lax.axis_index("dp")
    place = jnp.stack([here // 2, here % 2, layer % 2, layer // 2]).astype(jnp.int32)
    weight_scratch = [
        pltpu.VMEM((1, width), F32),
        pltpu.VMEM((width, 3 * HW), BF16),
        pltpu.VMEM((HW, width), BF16),
    ]
    weights = [(HBM, gain), (HBM, qkv_weight), (HBM, out_weight)]
    col_outs = [((columns, 3 * HW), BF16), ((width, 3 * HW), BF16)]

    if layered:
        packed = call(
            pack_kernel,
            "pack_columns",
            [(SMEM, place), (HBM, x), (HBM, cot)],
            [((2, share, width), BF16)] + [((2, 2 * share, width), BF16)] * 3,
            [pltpu.SemaphoreType.DMA((8,))],
            out_specs=[ANY] * 4,
        )
        near_1, near_2, near_3 = cross_chips(*packed[1:])
        own = swap(packed[0], "seq", 1)
        placed, _ = lax.optimization_barrier((place, own))
    else:
        outgoing = jnp.stack([x.reshape(n, share, width), cot.reshape(n, share, width)], 1)
        moved = lax.all_to_all(outgoing, "seq", split_axis=0, concat_axis=0, tiled=True)
        placed = place

    split_out = ((chips, row_share, row_width // 2), BF16)
    term_outs = [split_out] * 4 if layered else [((width, row_width), BF16)]
    if layered:
        term_outs.append(((row_share, 3 * width), BF16))
    *row_terms, row_out, base, normed, inverse_rms = call(
        row_chip_kernel if layered else row_kernel,
        "row_heads",
        [(SMEM, placed)] * layered + [(HBM, x), (HBM, cot), *weights],
        [
            *term_outs, ((HW, width), BF16), ((columns, width), F32),
            ((columns, width), F32), ((columns, 1), F32),
        ],
        [
            pltpu.VMEM((columns, width), BF16),
            pltpu.VMEM((columns, width), BF16),
            *weight_scratch,
            pltpu.VMEM((columns, HW), F32),
            pltpu.VMEM((columns, HW), F32),
            pltpu.VMEM((columns, 3 * HW), BF16),
            pltpu.SemaphoreType.DMA((8,)),
        ],
        BIG_VMEM,
        [VMEM] * 4 * layered + [PINNED] * 5 if layered else [VMEM] * 5,
    )
    moved_scratch = pltpu.VMEM((n, 2, share, width), BF16)
    if layered:
        *row_terms, weight_rows = row_terms
        row_sent = [swap(one, "seq", 1) for one in row_terms[:2]]
        half_block = (chips, row_share // 2, row_width)
        row_next, row_kept = call(
            row_cores_kernel,
            "row_add_cores",
            [(SMEM, place), *[(VMEM, one) for one in (*row_terms[2:], *row_sent)]],
            [(half_block, BF16), (half_block, F32)],
            out_specs=[VMEM, PINNED],
        )
        near_1, near_2, near_3, row_kept = lax.optimization_barrier(
            (near_1, near_2, near_3, row_kept)
        )
        far_3, far_1, far_2 = swap(near_3, "seq", 1), swap(near_1, "seq", 1), swap(near_2, "seq", 1)
        row_got = swap(row_next, "dp", 1)
        send, keep, *col_grads = call(
            column_chip_kernel,
            "column_heads",
            [
                (SMEM, place), (HBM, x), (HBM, cot), (ANY, own),
                (ANY, near_1), (ANY, near_2), (ANY, near_3),
                (ANY, far_1), (ANY, far_2), (ANY, far_3), *weights, (VMEM, row_out),
            ],
            [((chips, row_share, col_width), BF16)] * 2 + col_outs,
            [moved_scratch, weight_scratch[0], weight_scratch[2], pltpu.SemaphoreType.DMA((21,))],
            BIG_VMEM,
            [VMEM, VMEM, PINNED, PINNED],
        )
        send, row_got = lax.optimization_barrier((send, row_got))
        back_send, back_keep = call(
            back_chip_kernel,
            "column_grad_hidden",
            [(SMEM, place), *[(VMEM, one) for one in col_grads]],
            [((chips, share, width), BF16)] * 2,
        )
        keep, back_keep = lax.optimization_barrier((keep, back_keep))
        joint_width = col_width + row_width // 2
        owned, *off = call(
            chip_sum_kernel,
            "add_cores",
            [
                (SMEM, place), (VMEM, keep), (VMEM, swap(send, "seq", 1)),
                (VMEM, row_kept), (VMEM, row_got),
            ],
            [((row_share, joint_width), F32)] + [((row_share, joint_width), BF16)] * 3,
            out_specs=[PINNED, VMEM, VMEM, VMEM],
        )
        got = cross_chips(*off)
        back = call(
            back_pack_kernel,
            "pack_grad_hidden",
            [(SMEM, place), (VMEM, back_keep), (VMEM, swap(back_send, "seq", 1))],
            [((2 * share, width), BF16)] * 4,
        )
        *back, owned = lax.optimization_barrier((*back, owned))
        half_rows = row_share // 2
        to_next, kept, row_sum = call(
            layer_sum_kernel,
            "add_chips",
            [(SMEM, place), (VMEM, owned), *[(VMEM, one) for one in got]],
            [((half_rows, col_width), BF16), ((half_rows, col_width), F32), ((half_rows, row_width), BF16)],
            out_specs=[VMEM, PINNED, VMEM],
        )
        (pair_sum,) = call(
            join_kernel,
            "add_pair",
            [(VMEM, kept), (VMEM, swap(to_next, "dp", 1)), (VMEM, row_sum)],
            [((half_rows, col_width + row_width), BF16)],
        )
        *back, pair_sum = lax.optimization_barrier((*back, pair_sum))
        held = add_two(pair_sum, swap(pair_sum, "dp", 2), "add_pairs")
        other = swap(held, "dp", 1)
        (grad,) = call(
            input_chip_kernel,
            "input_grad",
            [
                (SMEM, place), (VMEM, base), (VMEM, normed), (VMEM, inverse_rms), (VMEM, gain),
                (VMEM, back[0]), *[(VMEM, one) for one in cross_chips(*back[1:])],
            ],
            [((columns, width), BF16)],
            [pltpu.VMEM((chips, 2 * share, width), BF16), pltpu.SemaphoreType.DMA((chips,))],
            out_specs=[HBM],
        )
        sum_qkv, sum_out, sum_gain = call(
            result_kernel,
            "result",
            [
                (SMEM, place), (VMEM, held), (VMEM, other), (VMEM, weight_rows), (VMEM, gain),
            ],
            [((row_share, 3 * width), F32), ((row_share, width), F32), ((1, row_share), F32)],
        )
        sum_gain = sum_gain.reshape(row_share)
    else:
        terms, *col_grads = call(
            column_kernel,
            "column_heads",
            [(ANY, moved), *weights, (VMEM, row_terms[0]), (VMEM, row_out)],
            [((width, 4 * width), BF16), *col_outs],
            [moved_scratch, weight_scratch[0], weight_scratch[2], pltpu.SemaphoreType.DMA((6,))],
            BIG_VMEM,
        )
        (back,) = call(
            back_kernel,
            "column_grad_hidden",
            [(VMEM, one) for one in col_grads],
            [((n, share, width), BF16)],
        )
        returned = lax.all_to_all(back, "seq", split_axis=0, concat_axis=0, tiled=True)
        (grad,) = call(
            input_kernel,
            "input_grad",
            [
                (VMEM, base), (VMEM, normed), (VMEM, inverse_rms), (VMEM, gain),
                (VMEM, returned.reshape(columns, width)),
            ],
            [((columns, width), BF16)],
        )
        terms = lax.all_to_all(
            terms.reshape(n, row_share, 4 * width), "seq", split_axis=0, concat_axis=0, tiled=True
        )
        total = jnp.sum(terms.astype(F32), 0)
        for step in range(m.bit_length() - 1):
            sent = total.astype(BF16)
            total = sent.astype(F32) + swap(sent, "dp", 1 << step).astype(F32)
        sum_qkv, sum_out = total[:, : 3 * width], total[:, 3 * width :]
        own_gain = lax.dynamic_slice_in_dim(norm_gain, here * row_share, row_share, 0)
        own_weight = lax.dynamic_slice_in_dim(qkv_weight, here * row_share, row_share, 0)
        sum_gain = jnp.sum(sum_qkv * own_weight.astype(F32), -1) / own_gain
    return (grad.reshape(inputs.shape), sum_qkv, sum_out, sum_gain)


def solution(mesh):
    return jax.shard_map(
        body,
        mesh=mesh,
        in_specs=(P("dp", "seq", None, None), P(), P(), P(), P("dp", "seq", None, None)),
        out_specs=(P("dp", "seq", None, None), P("seq", None), P("seq", None), P("seq")),
        check_vma=False,
    )
```

```python
import math

import jax
import jax.numpy as jnp
from jax import lax
from jax.experimental import pallas as pl
from jax.experimental.pallas import tpu as pltpu
from jax.sharding import PartitionSpec as P

H = 8
HD = 64
HH = H // 2
HW = HH * HD
SCALE = HD ** (-0.5)
F32 = jnp.float32
BF16 = jnp.bfloat16
QUERY_BLOCK = 128
BIG_VMEM = 20 * 1024 * 1024
SMALL_VMEM = 8 * 1024 * 1024
ANY = pl.BlockSpec(memory_space=pl.ANY)
VMEM = pl.BlockSpec(memory_space=pltpu.VMEM)
HBM = pl.BlockSpec(memory_space=pltpu.HBM)
CHIP_STEPS = (3, 2, 1)
PINNED = pl.BlockSpec(memory_space=pltpu.VMEM)
shaped = jax.ShapeDtypeStruct


def here():
    device = lax.axis_index("seq")
    return device >> 1, device & 1, lax.axis_index("dp")


def dot_nn(a, b):
    return lax.dot_general(a, b, (((1,), (0,)), ((), ())), preferred_element_type=F32)


def dot_nt(a, b):
    return lax.dot_general(a, b, (((1,), (1,)), ((), ())), preferred_element_type=F32)


def rms_parts(x):
    inverse_rms = lax.rsqrt(jnp.mean(x * x, -1, keepdims=True) + 1e-05)
    return inverse_rms, x * inverse_rms


def transposed(x):
    block = math.gcd(x.shape[1], 256)
    eye = (
        lax.broadcasted_iota(jnp.int32, (block, block), 0)
        == lax.broadcasted_iota(jnp.int32, (block, block), 1)
    ).astype(F32).astype(BF16)
    parts = [
        dot_nt(eye, x[:, at : at + block]).astype(BF16) for at in range(0, x.shape[1], block)
    ]
    return parts[0] if len(parts) == 1 else jnp.concatenate(parts, 0)


def head_pair(x):
    lane = lax.broadcasted_iota(jnp.int32, x.shape, 1)
    zero = jnp.zeros_like(x)
    return jnp.concatenate([jnp.where(lane < HD, x, zero), jnp.where(lane < HD, zero, x)], 0)


def both_heads(both, count):
    return jnp.concatenate([both[:HD, :count], both[HD:, count:]], 0)


def pair_steps(items, mask_rows, mask):
    count = items[0][2].shape[1]
    scores = [dot_nt(k, q2) for q2, _, _, k, _, _, _ in items]
    prob_grads = [dot_nt(v, g2) for _, g2, _, _, v, _, _ in items]
    probs = []
    for score in scores:
        first = score.shape[0] - mask_rows
        tail = jnp.where(mask, score[first:], -1e30)
        score = tail if first == 0 else jnp.concatenate([score[:first], tail], 0)
        exponent = jnp.exp(score - jnp.max(score, 0, keepdims=True))
        probs.append(exponent * (1.0 / jnp.sum(exponent, 0, keepdims=True)))
    weights = [prob.astype(BF16) for prob in probs]
    attended = [
        both_heads(dot_nn(item[6], weight), count).astype(BF16)
        for item, weight in zip(items, weights)
    ]
    score_grads = []
    for item, att, prob, prob_grad in zip(items, attended, probs, prob_grads):
        product = item[2].astype(F32) * att.astype(F32)
        delta = [jnp.sum(part, 0, keepdims=True) for part in (product[:HD], product[HD:])]
        score_grads.append((prob * (prob_grad - jnp.concatenate(delta, 1))).astype(BF16))
    grad_q = [
        (both_heads(dot_nn(item[5], score_grad), count) * SCALE).astype(BF16)
        for item, score_grad in zip(items, score_grads)
    ]
    grad_k = [dot_nn(score_grad, item[0]) for item, score_grad in zip(items, score_grads)]
    grad_v = [dot_nn(weight, item[1]) for item, weight in zip(items, weights)]
    return list(zip(attended, grad_q, grad_k, grad_v))


def split_cores(piece, send_ref, keep_ref, chips, lanes):
    rows = send_ref.shape[1]
    parts = piece.reshape(chips.stop - chips.start, 2, rows, piece.shape[1])
    even, odd = parts[:, 0], parts[:, 1]
    first = here()[1] == 0
    send_ref[chips, :, lanes] = jnp.where(first, odd, even)
    keep_ref[chips, :, lanes] = jnp.where(first, even, odd)


def qkv_copies(wqkv_ref, w_ref, sems, second):
    width = wqkv_ref.shape[0]
    return [
        pltpu.make_async_copy(
            wqkv_ref.at[:, pl.ds(i * width + second * HW, HW)],
            w_ref.at[:, pl.ds(i * HW, HW)],
            sems.at[i],
        )
        for i in range(3)
    ]


def weight_copies(wqkv_ref, wout_ref, w_ref, wo_ref, sems, second):
    out_rows = wout_ref.at[pl.ds(second * HW, HW), :]
    return [
        *qkv_copies(wqkv_ref, w_ref, sems, second),
        pltpu.make_async_copy(out_rows, wo_ref, sems.at[3]),
    ]


def started(*copies):
    for copy in copies:
        copy.start()
    return copies


def finished(*copies):
    for copy in copies:
        copy.wait()


def project(hidden, cot, w_ref, wo_ref):
    projected = dot_nn(hidden, w_ref[...]).astype(BF16)
    q, k, v = [projected[:, i * HW : (i + 1) * HW] for i in range(3)]
    g = dot_nt(cot, wo_ref[...]).astype(BF16)
    return q * jnp.asarray(SCALE, BF16), k, v, g


def row_part(
    x_any, cot_any, gain_any, wqkv_any, wout_any,
    out_ref, base_ref, normed_ref, inverse_ref, x_ref, cot_ref,
    gain_ref, w_ref, wo_ref, dk_ref, dv_ref, grads_ref, sems,
):
    first = started(
        pltpu.make_async_copy(x_any, x_ref, sems.at[4]),
        pltpu.make_async_copy(gain_any, gain_ref, sems.at[5]),
    )
    later = started(
        *weight_copies(wqkv_any, wout_any, w_ref, wo_ref, sems, 0),
        pltpu.make_async_copy(cot_any, cot_ref, sems.at[6]),
    )
    dk_ref[...] = jnp.zeros_like(dk_ref)
    dv_ref[...] = jnp.zeros_like(dv_ref)
    finished(*first)
    tokens = x_ref.shape[0]
    inverse_ref[...], normed_ref[...] = rms_parts(x_ref[...].astype(F32))
    hidden = (normed_ref[...] * gain_ref[...]).astype(BF16)
    hidden_t = transposed(hidden)
    finished(*later)
    cot = cot_ref[...]
    q, k, v, g = project(hidden, cot, w_ref, wo_ref)
    kt, vt, gt = transposed(k), transposed(v), transposed(g)
    step = math.gcd(tokens, QUERY_BLOCK)
    query = lax.broadcasted_iota(jnp.int32, (step, 2 * step), 1) % step
    mask = query >= lax.broadcasted_iota(jnp.int32, (step, 2 * step), 0)
    pairs = [slice(i * 2 * HD, (i + 1) * 2 * HD) for i in range(HH // 2)]
    att_blocks, dq_blocks = [], []
    for start in range(0, tokens, step):
        rows, keys = slice(start, start + step), slice(0, start + step)
        items = [
            (
                head_pair(q[rows, lanes]), head_pair(g[rows, lanes]), gt[lanes, rows],
                k[keys, lanes], v[keys, lanes], kt[lanes, keys], vt[lanes, keys],
            )
            for lanes in pairs
        ]
        results = pair_steps(items, step, mask)
        for lanes, (_, _, dk, dv) in zip(pairs, results):
            dk_ref[keys, lanes] += dk
            dv_ref[keys, lanes] += dv
        att_blocks.append(jnp.concatenate([result[0] for result in results], 0))
        dq_blocks.append(jnp.concatenate([result[1] for result in results], 0))
    grads_ref[:, :HW] = transposed(jnp.concatenate(dq_blocks, 1))
    grads_ref[:, HW : 2 * HW] = dk_ref[...].astype(BF16)
    grads_ref[:, 2 * HW :] = dv_ref[...].astype(BF16)
    term_qkv = dot_nn(hidden_t, grads_ref[...]).astype(BF16)
    out_ref[...] = dot_nn(jnp.concatenate(att_blocks, 1), cot).astype(BF16)
    grad_normed = dot_nt(grads_ref[...], w_ref[...]) * gain_ref[...]
    base_ref[...] = input_grad(
        cot_ref[...].astype(F32), normed_ref[...], inverse_ref[...], grad_normed
    )
    return term_qkv


def row_kernel(x_any, cot_any, gain_any, wqkv_any, wout_any, qkv_ref, *refs):
    qkv_ref[...] = row_part(x_any, cot_any, gain_any, wqkv_any, wout_any, *refs)


def row_chip_kernel(
    x_any, cot_any, gain_any, wqkv_any, wout_any,
    send_1, send_2, keep_1, keep_2, rows_ref, col_w_ref, col_wo_ref, *refs,
):
    chip, core, _ = here()
    sems, rows = refs[-1], rows_ref.shape[0]
    at = pl.multiple_of((chip * 2 + core) * rows, rows)
    handed = started(
        pltpu.make_async_copy(wqkv_any.at[pl.ds(at, rows), :], rows_ref, sems.at[7]),
        *weight_copies(wqkv_any, wout_any, col_w_ref, col_wo_ref, sems.at[pl.ds(8, 4)], 1),
    )
    term_qkv = row_part(x_any, cot_any, gain_any, wqkv_any, wout_any, *refs)
    chips, cut = send_1.shape[0], keep_1.shape[2]
    pieces = slice(0, chips), slice(0, cut)
    split_cores(term_qkv[:, :cut], send_1, keep_1, *pieces)
    split_cores(term_qkv[:, cut:], send_2, keep_2, *pieces)
    finished(*handed)


def column_part(x, cot, mask, gain, w_ref, wo_ref, weight_waits, grads_ref):
    tokens, block = x.shape[0], mask.shape[0]
    _, normed = rms_parts(x.astype(F32))
    hidden = (normed * gain).astype(BF16)
    hidden_t = transposed(hidden)
    finished(*weight_waits)
    q, k, v, g = project(hidden, cot, w_ref, wo_ref)
    kt, vt, gt = transposed(k), transposed(v), transposed(g)
    pairs = [slice(i * 2 * HD, (i + 1) * 2 * HD) for i in range(HH // 2)]
    blocks = [slice(at, at + block) for at in range(0, tokens, block)]
    items = [
        (
            head_pair(q[rows, lanes]), head_pair(g[rows, lanes]), gt[lanes, rows],
            k[rows, lanes], v[rows, lanes], kt[lanes, rows], vt[lanes, rows],
        )
        for lanes in pairs
        for rows in blocks
    ]
    results = pair_steps(items, block, mask)
    places = [(lanes, rows) for lanes in pairs for rows in blocks]
    for (lanes, rows), (_, _, dk, dv) in zip(places, results):
        grads_ref[rows, HW + lanes.start : HW + lanes.stop] = dk.astype(BF16)
        grads_ref[rows, 2 * HW + lanes.start : 2 * HW + lanes.stop] = dv.astype(BF16)
    by_pair = [results[i * len(blocks) : (i + 1) * len(blocks)] for i in range(len(pairs))]
    attended, grad_q = [
        jnp.concatenate([jnp.concatenate([r[i] for r in some], 1) for some in by_pair], 0)
        for i in range(2)
    ]
    grads_ref[:, :HW] = transposed(grad_q)
    term_qkv = dot_nn(hidden_t, grads_ref[...]).astype(BF16)
    term_out = dot_nn(attended, cot).astype(BF16)
    return term_qkv, term_out


def column_mask(all_rows, group, row_of):
    block = all_rows * group
    shape = (block, 2 * block)
    query = lax.broadcasted_iota(jnp.int32, shape, 1) % block
    key = lax.broadcasted_iota(jnp.int32, shape, 0)
    same_column = query % group == key % group
    return (row_of(query // group) >= row_of(key // group)) & same_column


def column_kernel(
    moved_any, gain_any, wqkv_any, wout_any, row_qkv_ref, row_out_ref,
    terms_ref, grads_ref, w_ref,
    moved_ref, gain_ref, wo_ref, sems,
):
    copies = started(
        pltpu.make_async_copy(moved_any, moved_ref, sems.at[4]),
        pltpu.make_async_copy(gain_any, gain_ref, sems.at[5]),
    )
    weights = started(*weight_copies(wqkv_any, wout_any, w_ref, wo_ref, sems, 1))
    finished(*copies)
    all_rows, _, share, width = moved_ref.shape
    group = math.gcd(share, 16)
    x, cot = [
        jnp.concatenate(
            [
                moved_ref[:, which, at : at + group, :].astype(F32).reshape(all_rows * group, width)
                for at in range(0, share, group)
            ],
            0,
        ).astype(BF16)
        for which in range(2)
    ]
    mask = column_mask(all_rows, group, lambda place: place)
    term_qkv, term_out = column_part(
        x, cot, mask, gain_ref[...], w_ref, wo_ref, weights, grads_ref
    )
    for i in range(3):
        at = i * width
        terms_ref[:, at : at + HW] = row_qkv_ref[:, i * HW : (i + 1) * HW]
        terms_ref[:, at + HW : at + 2 * HW] = term_qkv[:, i * HW : (i + 1) * HW]
    terms_ref[:HW, 3 * width :] = row_out_ref[...]
    terms_ref[HW:, 3 * width :] = term_out


def column_chip_kernel(
    x_ref, cot_ref, near_1, near_2, near_3, far_ref, gain_ref, w_ref, wo_ref, row_out_ref,
    send_ref, keep_ref, grads_ref,
):
    chip, core, _ = here()
    share = far_ref.shape[2]
    half = pl.ds(pl.multiple_of(core * share, share), share)
    at = pl.ds(pl.multiple_of((chip * 2 + core) * share, share), share)
    group = math.gcd(share, 16)

    def tokens(which, mine):
        pieces = [mine[at, :], far_ref[0, which]]
        for i, near in enumerate((near_1, near_2, near_3)):
            pieces += [near[which, half, :], far_ref[i + 1, which]]
        starts = range(0, share, group)
        return jnp.concatenate(
            [piece[start : start + group] for start in starts for piece in pieces], 0
        )

    def row_of(place):
        step = (4 - (place >> 1)) & 3
        return ((step ^ chip) << 1) + ((place & 1) ^ core)

    mask = column_mask(2 * (len(CHIP_STEPS) + 1), group, row_of)
    term_qkv, term_out = column_part(
        tokens(0, x_ref), tokens(1, cot_ref), mask, gain_ref[...], w_ref, wo_ref, (), grads_ref
    )
    chips = send_ref.shape[0]
    refs = send_ref, keep_ref
    out_lanes = slice(3 * HW, send_ref.shape[2])
    split_cores(term_qkv, *refs, slice(0, chips), slice(0, 3 * HW))
    split_cores(row_out_ref[...], *refs, slice(0, chips // 2), out_lanes)
    split_cores(term_out, *refs, slice(chips // 2, chips), out_lanes)


def far_kernel(x_ref, cot_ref, near_1, near_2, near_3, far_ref):
    chip, core, _ = here()
    share = far_ref.shape[2]
    at = pl.ds(pl.multiple_of((chip * 2 + 1 - core) * share, share), share)
    far_ref[0, 0], far_ref[0, 1] = x_ref[at, :], cot_ref[at, :]
    at = pl.ds(pl.multiple_of((1 - core) * share, share), share)
    for i, near in enumerate((near_1, near_2, near_3)):
        far_ref[i + 1] = near[:, at, :]


def back_kernel(grads_ref, w_ref, back_ref):
    grad_hidden = dot_nt(grads_ref[...], w_ref[...])
    all_rows, share, width = back_ref.shape
    group = math.gcd(share, 16)
    block = all_rows * group
    for i in range(share // group):
        piece = grad_hidden[i * block : (i + 1) * block].reshape(all_rows, group, width)
        back_ref[:, i * group : (i + 1) * group, :] = piece.astype(BF16)


def back_chip_kernel(grads_ref, w_ref, send_ref, keep_ref):
    grad_hidden = dot_nt(grads_ref[...], w_ref[...]).astype(BF16)
    chips, share, width = keep_ref.shape
    group = math.gcd(share, 16)
    block = 2 * chips * group
    for i in range(share // group):
        piece = grad_hidden[i * block : (i + 1) * block].reshape(chips, 2, group, width)
        at = slice(i * group, (i + 1) * group)
        keep_ref[:, at, :], send_ref[:, at, :] = piece[:, 0], piece[:, 1]


def back_pack_kernel(keep_ref, got_ref, *targets):
    share = keep_ref.shape[1]
    core = here()[1]
    kept_at = pl.ds(pl.multiple_of(core * share, share), share)
    got_at = pl.ds(pl.multiple_of((1 - core) * share, share), share)
    for i, target in enumerate(targets):
        target[kept_at, :] = keep_ref[i]
        target[got_at, :] = got_ref[i]


def input_kernel(base_ref, normed_ref, inverse_ref, gain_ref, back_ref, grad_ref):
    grad_ref[...] = input_grad(
        base_ref[...], normed_ref[...], inverse_ref[...], back_ref[...].astype(F32) * gain_ref[...]
    ).astype(BF16)


def input_grad(base, normed, inverse_rms, grad_normed):
    projected = jnp.mean(grad_normed * normed, -1, keepdims=True)
    return base + inverse_rms * (grad_normed - normed * projected)


def input_chip_kernel(
    base_ref, normed_ref, inverse_ref, gain_ref, own_ref, got_1, got_2, got_3,
    grad_any, grad_ref, sems,
):
    chip = here()[0]
    count = own_ref.shape[0]
    copies = []
    for i, (step, back_ref) in enumerate(zip((0, *CHIP_STEPS), (own_ref, got_1, got_2, got_3))):
        at = pl.ds(pl.multiple_of((chip ^ step) * count, count), count)
        grad_normed = back_ref[...].astype(F32) * gain_ref[...]
        grad = input_grad(base_ref[at, :], normed_ref[at, :], inverse_ref[at, :], grad_normed)
        grad_ref[i] = grad.astype(BF16)
        copies += started(pltpu.make_async_copy(grad_ref.at[i], grad_any.at[at, :], sems.at[i]))
    finished(*copies)


def pack_kernel(x_any, cot_any, off_1, off_2, off_3, sems):
    chip = here()[0]
    count = off_1.shape[1]
    copies = []
    for i, (step, target) in enumerate(zip(CHIP_STEPS, (off_1, off_2, off_3))):
        at = pl.ds(pl.multiple_of((chip ^ step) * count, count), count)
        for which, source in enumerate((x_any, cot_any)):
            copies.append(
                pltpu.make_async_copy(source.at[at, :], target.at[which], sems.at[2 * i + which])
            )
    finished(*started(*copies))


def chip_sum_kernel(*refs):
    chip = here()[0]
    pieces, targets = refs[:-4], refs[-4:]
    count = len(pieces) // 2
    for step, target in zip((0, *CHIP_STEPS), targets):
        there, at = chip ^ step, 0
        for kept_ref, got_ref in zip(pieces[:count], pieces[count:]):
            to = slice(at, at + kept_ref.shape[2])
            total = kept_ref[there].astype(F32) + got_ref[there].astype(F32)
            target[:, to] = total.astype(target.dtype)
            at = to.stop


def layer_sum_kernel(own_ref, got_1, got_2, got_3, send_ref, keep_ref):
    upper = (here()[2] & 1) == 1
    total = own_ref[...] + (
        (got_1[...].astype(F32) + got_2[...].astype(F32)) + got_3[...].astype(F32)
    )
    half = total.shape[0] // 2
    low, high = total[:half], total[half:]
    send_ref[...] = jnp.where(upper, low, high).astype(BF16)
    keep_ref[...] = jnp.where(upper, high, low)


def join_kernel(kept_ref, got_ref, row_kept, row_got, out_ref):
    cut = kept_ref.shape[1]
    out_ref[:, :cut] = (kept_ref[...] + got_ref[...].astype(F32)).astype(BF16)
    out_ref[:, cut:] = (row_kept[...] + row_got[...].astype(F32)).astype(BF16)


def add_kernel(kept_ref, got_ref, out_ref):
    out_ref[...] = (kept_ref[...].astype(F32) + got_ref[...].astype(F32)).astype(BF16)


def result_kernel(held_ref, got_ref, w_ref, gain_ref, qkv_ref, out_ref, grad_ref):
    rows = qkv_ref.shape[0]
    chip, core, layer = here()
    at = (chip * 2 + core) * rows
    upper = (layer & 1) == 1
    half = rows // 2
    width = out_ref.shape[1]

    def ordered(lanes):
        held, got = held_ref[:, lanes].astype(F32), got_ref[:, lanes].astype(F32)
        return (jnp.where(upper, got, held), jnp.where(upper, held, got))

    row_at = 3 * HW + width
    for i in range(3):
        for at_from, at_to in ((row_at + i * HW, i * width), (i * HW, i * width + HW)):
            to = slice(at_to, at_to + HW)
            qkv_ref[:half, to], qkv_ref[half:, to] = ordered(slice(at_from, at_from + HW))
    out_ref[:half], out_ref[half:] = ordered(slice(3 * HW, row_at))
    total = jnp.sum(qkv_ref[...] * w_ref[...].astype(F32), -1, keepdims=True)
    shape = (rows, gain_ref.shape[1])
    row = lax.broadcasted_iota(jnp.int32, shape, 0)
    feature = lax.broadcasted_iota(jnp.int32, shape, 1)
    gain = jnp.sum(jnp.where(feature == row + at, gain_ref[...], 0.0), -1, keepdims=True)
    shape = (rows, grad_ref.shape[1])
    same = lax.broadcasted_iota(jnp.int32, shape, 0) == lax.broadcasted_iota(jnp.int32, shape, 1)
    grad_ref[...] = jnp.sum(jnp.where(same, total / gain, 0.0), 0, keepdims=True)


def call(kernel, name, ins, outs, scratch=(), vmem=SMALL_VMEM, out_specs=None):
    out_specs = out_specs or [VMEM] * len(outs)
    places = [{id(HBM): pltpu.HBM, id(PINNED): pltpu.VMEM}.get(id(spec)) for spec in out_specs]
    outs = [place(*out) if place else shaped(*out) for place, out in zip(places, outs)]
    args = [
        pltpu.with_memory_space_constraint(array, pltpu.HBM) if spec is HBM else array
        for spec, array in ins
    ]
    return pl.pallas_call(
        kernel,
        out_shape=outs,
        in_specs=[spec for spec, _ in ins],
        out_specs=out_specs,
        scratch_shapes=scratch,
        name=name,
        cost_estimate=pl.CostEstimate(flops=0, bytes_accessed=0, transcendentals=0),
        compiler_params=pltpu.CompilerParams(vmem_limit_bytes=vmem),
    )(*args)


def swap(array, axis, bits):
    count = lax.axis_size(axis)
    return lax.ppermute(array, axis, [(i, i ^ bits) for i in range(count)])


def add_cores(keep, got, name):
    rows, wide = keep[0].shape[1], sum(one.shape[2] for one in keep)
    return call(
        chip_sum_kernel,
        name + "_add_cores",
        [(VMEM, one) for one in (*keep, *got)],
        [((rows, wide), F32)] + [((rows, wide), BF16)] * 3,
        out_specs=[PINNED, VMEM, VMEM, VMEM],
    )


def add_chips(owned, got, name):
    half, wide = owned.shape[0] // 2, owned.shape[1]
    return call(
        layer_sum_kernel,
        name + "_add_chips",
        [(VMEM, one) for one in (owned, *got)],
        [((half, wide), BF16), ((half, wide), F32)],
        out_specs=[VMEM, PINNED],
    )


def cross_chips(*offs):
    return [swap(off, "seq", 2 * step) for off, step in zip(offs, CHIP_STEPS)]


def add_two(kept, got, name):
    (total,) = call(add_kernel, name, [(VMEM, kept), (VMEM, got)], [(kept.shape, BF16)])
    return total


def body(inputs, norm_gain, qkv_weight, out_weight, out_cotan):
    columns, width = inputs.shape[2:]
    n = lax.axis_size("seq")
    m = lax.axis_size("dp")
    share = columns // n
    row_share = width // n
    row_width, col_width = 3 * HW, 3 * HW + width
    x = inputs.reshape(columns, width)
    cot = out_cotan.reshape(columns, width)
    gain = norm_gain.reshape(1, width)
    chips = 4
    layered = n == 2 * chips and m == 4 and row_share == share
    weight_scratch = [
        pltpu.VMEM((1, width), F32),
        pltpu.VMEM((width, 3 * HW), BF16),
        pltpu.VMEM((HW, width), BF16),
    ]
    weights = [(HBM, gain), (HBM, qkv_weight), (HBM, out_weight)]
    col_outs = [((columns, 3 * HW), BF16), ((width, 3 * HW), BF16)]

    if layered:
        packed = call(
            pack_kernel,
            "pack_columns",
            [(HBM, x), (HBM, cot)],
            [((2, 2 * share, width), BF16)] * 3,
            [pltpu.SemaphoreType.DMA((6,))],
            out_specs=[ANY] * 3,
        )
        near = cross_chips(*packed)
        x_first, _ = lax.optimization_barrier((x, packed[0]))
    else:
        outgoing = jnp.stack([x.reshape(n, share, width), cot.reshape(n, share, width)], 1)
        moved = lax.all_to_all(outgoing, "seq", split_axis=0, concat_axis=0, tiled=True)
        x_first = x

    row_outs = [
        ((HW, width), BF16),
        ((columns, width), F32), ((columns, width), F32), ((columns, 1), F32),
        ((columns, width), BF16), ((columns, width), BF16),
    ]
    if layered:
        cut = row_width // 2
        split_outs = [((chips, row_share, cut), BF16)] * 4
        handed_outs = [
            ((row_share, 3 * width), BF16), ((width, 3 * HW), BF16), ((HW, width), BF16),
        ]
        row_outs = [*split_outs, *handed_outs, *row_outs]
        specs = [VMEM] * 4 + [PINNED] * (len(row_outs) - 4)
    else:
        row_outs = [((width, row_width), BF16), *row_outs]
        specs = [VMEM] * len(row_outs)
    *row_terms, row_out, base, normed, inverse_rms, x_near, cot_near = call(
        row_chip_kernel if layered else row_kernel,
        "row_heads",
        [(HBM, x_first), (HBM, cot), *weights],
        row_outs,
        [
            *weight_scratch,
            pltpu.VMEM((columns, HW), F32),
            pltpu.VMEM((columns, HW), F32),
            pltpu.VMEM((columns, 3 * HW), BF16),
            pltpu.SemaphoreType.DMA((12,)),
        ],
        BIG_VMEM,
        specs,
    )
    if layered:
        *row_terms, weight_rows, col_weight, col_out_weight = row_terms
        row_sent = [swap(one, "seq", 1) for one in row_terms[:2]]
        row_owned, *row_off = add_cores(row_terms[2:], row_sent, "row")
        *near, row_owned = lax.optimization_barrier((*near, row_owned))
        (far,) = call(
            far_kernel,
            "pack_other_core",
            [(VMEM, one) for one in (x_near, cot_near, *near)],
            [((chips, 2, share, width), BF16)],
        )
        row_got = cross_chips(*row_off)
        send, keep, col_grads = call(
            column_chip_kernel,
            "column_heads",
            [
                (VMEM, one)
                for one in (
                    x_near, cot_near, *near, swap(far, "seq", 1),
                    gain, col_weight, col_out_weight, row_out,
                )
            ],
            [((chips, row_share, col_width), BF16)] * 2 + [col_outs[0]],
            vmem=BIG_VMEM,
            out_specs=[VMEM, VMEM, PINNED],
        )
        send, *row_got = lax.optimization_barrier((send, *row_got))
        row_next, row_kept = add_chips(row_owned, row_got, "row")
        back_send, back_keep = call(
            back_chip_kernel,
            "column_grad_hidden",
            [(VMEM, col_grads), (VMEM, col_weight)],
            [((chips, share, width), BF16)] * 2,
        )
        keep, row_kept, back_keep = lax.optimization_barrier((keep, row_kept, back_keep))
        owned, *off = add_cores([keep], [swap(send, "seq", 1)], "column")
        got = cross_chips(*off)
        back = call(
            back_pack_kernel,
            "pack_grad_hidden",
            [(VMEM, back_keep), (VMEM, swap(back_send, "seq", 1))],
            [((2 * share, width), BF16)] * 4,
        )
        row_next, _ = lax.optimization_barrier((row_next, owned))
        row_next = swap(row_next, "dp", 1)
        *back, owned, row_next = lax.optimization_barrier((*back, owned, row_next))
        to_next, kept = add_chips(owned, got, "column")
        (pair_sum,) = call(
            join_kernel,
            "add_pair",
            [
                (VMEM, kept), (VMEM, swap(to_next, "dp", 1)),
                (VMEM, row_kept), (VMEM, row_next),
            ],
            [((row_share // 2, col_width + row_width), BF16)],
        )
        *back, pair_sum = lax.optimization_barrier((*back, pair_sum))
        held = add_two(pair_sum, swap(pair_sum, "dp", 2), "add_pairs")
        other = swap(held, "dp", 1)
        (grad,) = call(
            input_chip_kernel,
            "input_grad",
            [
                (VMEM, one)
                for one in (base, normed, inverse_rms, gain, back[0], *cross_chips(*back[1:]))
            ],
            [((columns, width), BF16)],
            [pltpu.VMEM((chips, 2 * share, width), BF16), pltpu.SemaphoreType.DMA((chips,))],
            out_specs=[HBM],
        )
        sum_qkv, sum_out, sum_gain = call(
            result_kernel,
            "result",
            [(VMEM, held), (VMEM, other), (VMEM, weight_rows), (VMEM, gain)],
            [((row_share, 3 * width), F32), ((row_share, width), F32), ((1, row_share), F32)],
        )
        sum_gain = sum_gain.reshape(row_share)
    else:
        terms, *col_grads = call(
            column_kernel,
            "column_heads",
            [(ANY, moved), *weights, (VMEM, row_terms[0]), (VMEM, row_out)],
            [((width, 4 * width), BF16), *col_outs],
            [
                pltpu.VMEM((n, 2, share, width), BF16),
                weight_scratch[0],
                weight_scratch[2],
                pltpu.SemaphoreType.DMA((6,)),
            ],
            BIG_VMEM,
        )
        (back,) = call(
            back_kernel,
            "column_grad_hidden",
            [(VMEM, one) for one in col_grads],
            [((n, share, width), BF16)],
        )
        returned = lax.all_to_all(back, "seq", split_axis=0, concat_axis=0, tiled=True)
        (grad,) = call(
            input_kernel,
            "input_grad",
            [
                (VMEM, base), (VMEM, normed), (VMEM, inverse_rms), (VMEM, gain),
                (VMEM, returned.reshape(columns, width)),
            ],
            [((columns, width), BF16)],
        )
        terms = lax.all_to_all(
            terms.reshape(n, row_share, 4 * width), "seq", split_axis=0, concat_axis=0, tiled=True
        )
        total = jnp.sum(terms.astype(F32), 0)
        for step in range(m.bit_length() - 1):
            sent = total.astype(BF16)
            total = sent.astype(F32) + swap(sent, "dp", 1 << step).astype(F32)
        sum_qkv, sum_out = total[:, : 3 * width], total[:, 3 * width :]
        here_at = lax.axis_index("seq") * row_share
        own_gain = lax.dynamic_slice_in_dim(norm_gain, here_at, row_share, 0)
        own_weight = lax.dynamic_slice_in_dim(qkv_weight, here_at, row_share, 0)
        sum_gain = jnp.sum(sum_qkv * own_weight.astype(F32), -1) / own_gain
    return (grad.reshape(inputs.shape), sum_qkv, sum_out, sum_gain)


def solution(mesh):
    return jax.shard_map(
        body,
        mesh=mesh,
        in_specs=(P("dp", "seq", None, None), P(), P(), P(), P("dp", "seq", None, None)),
        out_specs=(P("dp", "seq", None, None), P("seq", None), P("seq", None), P("seq")),
        check_vma=False,
    )
```

```python
import math

import jax
import jax.numpy as jnp
from jax import lax
from jax.experimental import pallas as pl
from jax.experimental.pallas import tpu as pltpu
from jax.sharding import PartitionSpec as P

H = 8
HD = 64
HH = H // 2
HW = HH * HD
SCALE = HD ** (-0.5)
F32 = jnp.float32
BF16 = jnp.bfloat16
QUERY_BLOCK = 128
BIG_VMEM = 20 * 1024 * 1024
SMALL_VMEM = 8 * 1024 * 1024
ANY = pl.BlockSpec(memory_space=pl.ANY)
VMEM = pl.BlockSpec(memory_space=pltpu.VMEM)
HBM = pl.BlockSpec(memory_space=pltpu.HBM)
CHIP_STEPS = (3, 2, 1)
FIRST_PART = 640
PINNED = pl.BlockSpec(memory_space=pltpu.VMEM)
shaped = jax.ShapeDtypeStruct


def here():
    device = lax.axis_index("seq")
    return device >> 1, device & 1, lax.axis_index("dp")


def dot_nn(a, b):
    return lax.dot_general(a, b, (((1,), (0,)), ((), ())), preferred_element_type=F32)


def dot_nt(a, b):
    return lax.dot_general(a, b, (((1,), (1,)), ((), ())), preferred_element_type=F32)


def rms_parts(x):
    inverse_rms = lax.rsqrt(jnp.mean(x * x, -1, keepdims=True) + 1e-05)
    return inverse_rms, x * inverse_rms


def transposed(x):
    block = math.gcd(x.shape[1], 256)
    eye = (
        lax.broadcasted_iota(jnp.int32, (block, block), 0)
        == lax.broadcasted_iota(jnp.int32, (block, block), 1)
    ).astype(F32).astype(BF16)
    parts = [
        dot_nt(eye, x[:, at : at + block]).astype(BF16) for at in range(0, x.shape[1], block)
    ]
    return parts[0] if len(parts) == 1 else jnp.concatenate(parts, 0)


def head_pair(x):
    lane = lax.broadcasted_iota(jnp.int32, x.shape, 1)
    zero = jnp.zeros_like(x)
    return jnp.concatenate([jnp.where(lane < HD, x, zero), jnp.where(lane < HD, zero, x)], 0)


def both_heads(both, count):
    return jnp.concatenate([both[:HD, :count], both[HD:, count:]], 0)


def pair_steps(items, mask_rows, mask):
    count = items[0][2].shape[1]
    scores = [dot_nt(k, q2) for q2, _, _, k, _, _, _ in items]
    prob_grads = [dot_nt(v, g2) for _, g2, _, _, v, _, _ in items]
    probs = []
    for score in scores:
        first = score.shape[0] - mask_rows
        tail = jnp.where(mask, score[first:], -1e30)
        score = tail if first == 0 else jnp.concatenate([score[:first], tail], 0)
        exponent = jnp.exp(score - jnp.max(score, 0, keepdims=True))
        probs.append(exponent * (1.0 / jnp.sum(exponent, 0, keepdims=True)))
    weights = [prob.astype(BF16) for prob in probs]
    attended = [
        both_heads(dot_nn(item[6], weight), count).astype(BF16)
        for item, weight in zip(items, weights)
    ]
    score_grads = []
    for item, att, prob, prob_grad in zip(items, attended, probs, prob_grads):
        product = item[2].astype(F32) * att.astype(F32)
        delta = [jnp.sum(part, 0, keepdims=True) for part in (product[:HD], product[HD:])]
        score_grads.append((prob * (prob_grad - jnp.concatenate(delta, 1))).astype(BF16))
    grad_q = [
        (both_heads(dot_nn(item[5], score_grad), count) * SCALE).astype(BF16)
        for item, score_grad in zip(items, score_grads)
    ]
    grad_k = [dot_nn(score_grad, item[0]) for item, score_grad in zip(items, score_grads)]
    grad_v = [dot_nn(weight, item[1]) for item, weight in zip(items, weights)]
    return list(zip(attended, grad_q, grad_k, grad_v))


def split_cores(piece, send_ref, keep_ref, chips, lanes):
    rows = send_ref.shape[1]
    parts = piece.reshape(chips.stop - chips.start, 2, rows, piece.shape[1])
    even, odd = parts[:, 0], parts[:, 1]
    first = here()[1] == 0
    send_ref[chips, :, lanes] = jnp.where(first, odd, even)
    keep_ref[chips, :, lanes] = jnp.where(first, even, odd)


def qkv_copies(wqkv_ref, w_ref, sems, second):
    width = wqkv_ref.shape[0]
    return [
        pltpu.make_async_copy(
            wqkv_ref.at[:, pl.ds(i * width + second * HW, HW)],
            w_ref.at[:, pl.ds(i * HW, HW)],
            sems.at[i],
        )
        for i in range(3)
    ]


def weight_copies(wqkv_ref, wout_ref, w_ref, wo_ref, sems, second):
    out_rows = wout_ref.at[pl.ds(second * HW, HW), :]
    return [
        *qkv_copies(wqkv_ref, w_ref, sems, second),
        pltpu.make_async_copy(out_rows, wo_ref, sems.at[3]),
    ]


def started(*copies):
    for copy in copies:
        copy.start()
    return copies


def finished(*copies):
    for copy in copies:
        copy.wait()


def project(hidden, cot, w_ref, wo_ref):
    projected = dot_nn(hidden, w_ref[...]).astype(BF16)
    q, k, v = [projected[:, i * HW : (i + 1) * HW] for i in range(3)]
    g = dot_nt(cot, wo_ref[...]).astype(BF16)
    return q * jnp.asarray(SCALE, BF16), k, v, g


def row_part(
    x_any, cot_any, gain_any, wqkv_any, wout_any,
    out_ref, base_ref, normed_ref, inverse_ref, x_ref, cot_ref,
    gain_ref, w_ref, wo_ref, dk_ref, dv_ref, grads_ref, sems,
):
    first = started(
        pltpu.make_async_copy(x_any, x_ref, sems.at[4]),
        pltpu.make_async_copy(gain_any, gain_ref, sems.at[5]),
    )
    later = started(
        *weight_copies(wqkv_any, wout_any, w_ref, wo_ref, sems, 0),
        pltpu.make_async_copy(cot_any, cot_ref, sems.at[6]),
    )
    dk_ref[...] = jnp.zeros_like(dk_ref)
    dv_ref[...] = jnp.zeros_like(dv_ref)
    finished(*first)
    tokens = x_ref.shape[0]
    inverse_ref[...], normed_ref[...] = rms_parts(x_ref[...].astype(F32))
    hidden = (normed_ref[...] * gain_ref[...]).astype(BF16)
    hidden_t = transposed(hidden)
    finished(*later)
    cot = cot_ref[...]
    q, k, v, g = project(hidden, cot, w_ref, wo_ref)
    kt, vt, gt = transposed(k), transposed(v), transposed(g)
    step = math.gcd(tokens, QUERY_BLOCK)
    query = lax.broadcasted_iota(jnp.int32, (step, 2 * step), 1) % step
    mask = query >= lax.broadcasted_iota(jnp.int32, (step, 2 * step), 0)
    pairs = [slice(i * 2 * HD, (i + 1) * 2 * HD) for i in range(HH // 2)]
    att_blocks, dq_blocks = [], []
    for start in range(0, tokens, step):
        rows, keys = slice(start, start + step), slice(0, start + step)
        items = [
            (
                head_pair(q[rows, lanes]), head_pair(g[rows, lanes]), gt[lanes, rows],
                k[keys, lanes], v[keys, lanes], kt[lanes, keys], vt[lanes, keys],
            )
            for lanes in pairs
        ]
        results = pair_steps(items, step, mask)
        for lanes, (_, _, dk, dv) in zip(pairs, results):
            dk_ref[keys, lanes] += dk
            dv_ref[keys, lanes] += dv
        att_blocks.append(jnp.concatenate([result[0] for result in results], 0))
        dq_blocks.append(jnp.concatenate([result[1] for result in results], 0))
    grads_ref[:, :HW] = transposed(jnp.concatenate(dq_blocks, 1))
    grads_ref[:, HW : 2 * HW] = dk_ref[...].astype(BF16)
    grads_ref[:, 2 * HW :] = dv_ref[...].astype(BF16)
    term_qkv = dot_nn(hidden_t, grads_ref[...]).astype(BF16)
    out_ref[...] = dot_nn(jnp.concatenate(att_blocks, 1), cot).astype(BF16)
    grad_normed = dot_nt(grads_ref[...], w_ref[...]) * gain_ref[...]
    base_ref[...] = input_grad(
        cot_ref[...].astype(F32), normed_ref[...], inverse_ref[...], grad_normed
    )
    return term_qkv


def row_kernel(x_any, cot_any, gain_any, wqkv_any, wout_any, qkv_ref, *refs):
    qkv_ref[...] = row_part(x_any, cot_any, gain_any, wqkv_any, wout_any, *refs)


def row_chip_kernel(
    x_any, cot_any, gain_any, wqkv_any, wout_any,
    send_1, send_2, keep_1, keep_2, rows_ref, col_w_ref, col_wo_ref, *refs,
):
    chip, core, _ = here()
    sems, rows = refs[-1], rows_ref.shape[0]
    at = pl.multiple_of((chip * 2 + core) * rows, rows)
    handed = started(
        pltpu.make_async_copy(wqkv_any.at[pl.ds(at, rows), :], rows_ref, sems.at[7]),
        *weight_copies(wqkv_any, wout_any, col_w_ref, col_wo_ref, sems.at[pl.ds(8, 4)], 1),
    )
    term_qkv = row_part(x_any, cot_any, gain_any, wqkv_any, wout_any, *refs)
    chips, cut = send_1.shape[0], keep_1.shape[2]
    pieces = slice(0, chips), slice(0, cut)
    split_cores(term_qkv[:, :cut], send_1, keep_1, *pieces)
    split_cores(term_qkv[:, cut:], send_2, keep_2, *pieces)
    finished(*handed)


def column_part(x, cot, mask, gain, w_ref, wo_ref, weight_waits, grads_ref):
    tokens, block = x.shape[0], mask.shape[0]
    _, normed = rms_parts(x.astype(F32))
    hidden = (normed * gain).astype(BF16)
    hidden_t = transposed(hidden)
    finished(*weight_waits)
    q, k, v, g = project(hidden, cot, w_ref, wo_ref)
    kt, vt, gt = transposed(k), transposed(v), transposed(g)
    pairs = [slice(i * 2 * HD, (i + 1) * 2 * HD) for i in range(HH // 2)]
    blocks = [slice(at, at + block) for at in range(0, tokens, block)]
    items = [
        (
            head_pair(q[rows, lanes]), head_pair(g[rows, lanes]), gt[lanes, rows],
            k[rows, lanes], v[rows, lanes], kt[lanes, rows], vt[lanes, rows],
        )
        for lanes in pairs
        for rows in blocks
    ]
    results = pair_steps(items, block, mask)
    places = [(lanes, rows) for lanes in pairs for rows in blocks]
    for (lanes, rows), (_, _, dk, dv) in zip(places, results):
        grads_ref[rows, HW + lanes.start : HW + lanes.stop] = dk.astype(BF16)
        grads_ref[rows, 2 * HW + lanes.start : 2 * HW + lanes.stop] = dv.astype(BF16)
    by_pair = [results[i * len(blocks) : (i + 1) * len(blocks)] for i in range(len(pairs))]
    attended, grad_q = [
        jnp.concatenate([jnp.concatenate([r[i] for r in some], 1) for some in by_pair], 0)
        for i in range(2)
    ]
    grads_ref[:, :HW] = transposed(grad_q)
    term_qkv = dot_nn(hidden_t, grads_ref[...]).astype(BF16)
    term_out = dot_nn(attended, cot).astype(BF16)
    return term_qkv, term_out


def column_mask(all_rows, group, row_of):
    block = all_rows * group
    shape = (block, 2 * block)
    query = lax.broadcasted_iota(jnp.int32, shape, 1) % block
    key = lax.broadcasted_iota(jnp.int32, shape, 0)
    same_column = query % group == key % group
    return (row_of(query // group) >= row_of(key // group)) & same_column


def column_kernel(
    moved_any, gain_any, wqkv_any, wout_any, row_qkv_ref, row_out_ref,
    terms_ref, grads_ref, w_ref,
    moved_ref, gain_ref, wo_ref, sems,
):
    copies = started(
        pltpu.make_async_copy(moved_any, moved_ref, sems.at[4]),
        pltpu.make_async_copy(gain_any, gain_ref, sems.at[5]),
    )
    weights = started(*weight_copies(wqkv_any, wout_any, w_ref, wo_ref, sems, 1))
    finished(*copies)
    all_rows, _, share, width = moved_ref.shape
    group = math.gcd(share, 16)
    x, cot = [
        jnp.concatenate(
            [
                moved_ref[:, which, at : at + group, :].astype(F32).reshape(all_rows * group, width)
                for at in range(0, share, group)
            ],
            0,
        ).astype(BF16)
        for which in range(2)
    ]
    mask = column_mask(all_rows, group, lambda place: place)
    term_qkv, term_out = column_part(
        x, cot, mask, gain_ref[...], w_ref, wo_ref, weights, grads_ref
    )
    for i in range(3):
        at = i * width
        terms_ref[:, at : at + HW] = row_qkv_ref[:, i * HW : (i + 1) * HW]
        terms_ref[:, at + HW : at + 2 * HW] = term_qkv[:, i * HW : (i + 1) * HW]
    terms_ref[:HW, 3 * width :] = row_out_ref[...]
    terms_ref[HW:, 3 * width :] = term_out


def column_chip_kernel(
    x_ref, cot_ref, near_1, near_2, near_3, far_ref, gain_ref, w_ref, wo_ref, row_out_ref,
    send_ref, keep_ref, grads_ref,
):
    chip, core, _ = here()
    share = far_ref.shape[2]
    half = pl.ds(pl.multiple_of(core * share, share), share)
    at = pl.ds(pl.multiple_of((chip * 2 + core) * share, share), share)
    group = math.gcd(share, 16)

    def tokens(which, mine):
        pieces = [mine[at, :], far_ref[0, which]]
        for i, near in enumerate((near_1, near_2, near_3)):
            pieces += [near[which, half, :], far_ref[i + 1, which]]
        starts = range(0, share, group)
        return jnp.concatenate(
            [piece[start : start + group] for start in starts for piece in pieces], 0
        )

    def row_of(place):
        step = (4 - (place >> 1)) & 3
        return ((step ^ chip) << 1) + ((place & 1) ^ core)

    mask = column_mask(2 * (len(CHIP_STEPS) + 1), group, row_of)
    term_qkv, term_out = column_part(
        tokens(0, x_ref), tokens(1, cot_ref), mask, gain_ref[...], w_ref, wo_ref, (), grads_ref
    )
    chips = send_ref.shape[0]
    refs = send_ref, keep_ref
    out_lanes = slice(3 * HW, send_ref.shape[2])
    split_cores(term_qkv, *refs, slice(0, chips), slice(0, 3 * HW))
    split_cores(row_out_ref[...], *refs, slice(0, chips // 2), out_lanes)
    split_cores(term_out, *refs, slice(chips // 2, chips), out_lanes)


def far_kernel(x_ref, cot_ref, near_1, near_2, near_3, far_ref):
    chip, core, _ = here()
    share = far_ref.shape[2]
    at = pl.ds(pl.multiple_of((chip * 2 + 1 - core) * share, share), share)
    far_ref[0, 0], far_ref[0, 1] = x_ref[at, :], cot_ref[at, :]
    at = pl.ds(pl.multiple_of((1 - core) * share, share), share)
    for i, near in enumerate((near_1, near_2, near_3)):
        far_ref[i + 1] = near[:, at, :]


def back_kernel(grads_ref, w_ref, back_ref):
    grad_hidden = dot_nt(grads_ref[...], w_ref[...])
    all_rows, share, width = back_ref.shape
    group = math.gcd(share, 16)
    block = all_rows * group
    for i in range(share // group):
        piece = grad_hidden[i * block : (i + 1) * block].reshape(all_rows, group, width)
        back_ref[:, i * group : (i + 1) * group, :] = piece.astype(BF16)


def back_chip_kernel(grads_ref, w_ref, send_ref, keep_ref):
    grad_hidden = dot_nt(grads_ref[...], w_ref[...]).astype(BF16)
    chips, share, width = keep_ref.shape
    group = math.gcd(share, 16)
    block = 2 * chips * group
    for i in range(share // group):
        piece = grad_hidden[i * block : (i + 1) * block].reshape(chips, 2, group, width)
        at = slice(i * group, (i + 1) * group)
        keep_ref[:, at, :], send_ref[:, at, :] = piece[:, 0], piece[:, 1]


def back_pack_kernel(keep_ref, got_ref, *targets):
    share = keep_ref.shape[1]
    core = here()[1]
    kept_at = pl.ds(pl.multiple_of(core * share, share), share)
    got_at = pl.ds(pl.multiple_of((1 - core) * share, share), share)
    for i, target in enumerate(targets):
        target[kept_at, :] = keep_ref[i]
        target[got_at, :] = got_ref[i]


def input_kernel(base_ref, normed_ref, inverse_ref, gain_ref, back_ref, grad_ref):
    grad_ref[...] = input_grad(
        base_ref[...], normed_ref[...], inverse_ref[...], back_ref[...].astype(F32) * gain_ref[...]
    ).astype(BF16)


def input_grad(base, normed, inverse_rms, grad_normed):
    projected = jnp.mean(grad_normed * normed, -1, keepdims=True)
    return base + inverse_rms * (grad_normed - normed * projected)


def input_chip_kernel(
    base_ref, normed_ref, inverse_ref, gain_ref, own_ref, got_1, got_2, got_3,
    grad_any, grad_ref, sems,
):
    chip = here()[0]
    count = own_ref.shape[0]
    copies = []
    for i, (step, back_ref) in enumerate(zip((0, *CHIP_STEPS), (own_ref, got_1, got_2, got_3))):
        at = pl.ds(pl.multiple_of((chip ^ step) * count, count), count)
        grad_normed = back_ref[...].astype(F32) * gain_ref[...]
        grad = input_grad(base_ref[at, :], normed_ref[at, :], inverse_ref[at, :], grad_normed)
        grad_ref[i] = grad.astype(BF16)
        copies += started(pltpu.make_async_copy(grad_ref.at[i], grad_any.at[at, :], sems.at[i]))
    finished(*copies)


def pack_kernel(x_any, cot_any, off_1, off_2, off_3, sems):
    chip = here()[0]
    count = off_1.shape[1]
    copies = []
    for i, (step, target) in enumerate(zip(CHIP_STEPS, (off_1, off_2, off_3))):
        at = pl.ds(pl.multiple_of((chip ^ step) * count, count), count)
        for which, source in enumerate((x_any, cot_any)):
            copies.append(
                pltpu.make_async_copy(source.at[at, :], target.at[which], sems.at[2 * i + which])
            )
    finished(*started(*copies))


def split_rows(total, axis, send_ref, kept_ref):
    upper = (here()[2] & 1) == 1
    low, high = jnp.split(total, 2, axis)
    send_ref[...] = jnp.where(upper, low, high).astype(BF16)
    kept_ref[...] = jnp.where(upper, high, low)


def row_cores_kernel(keep_1, keep_2, got_1, got_2, send_ref, kept_ref):
    total = [
        keep_ref[...].astype(F32) + got_ref[...].astype(F32)
        for keep_ref, got_ref in ((keep_1, got_1), (keep_2, got_2))
    ]
    split_rows(jnp.concatenate(total, 2), 1, send_ref, kept_ref)


def cores_kernel(keep_ref, got_ref, send_ref, kept_ref, *targets):
    chip, cut = here()[0], kept_ref.shape[2]
    first = keep_ref[:, :, :cut].astype(F32) + got_ref[:, :, :cut].astype(F32)
    split_rows(first, 1, send_ref, kept_ref)
    for step, target in zip((0, *CHIP_STEPS), targets):
        there = chip ^ step
        total = keep_ref[there, :, cut:].astype(F32) + got_ref[there, :, cut:].astype(F32)
        target[...] = total.astype(target.dtype)


def pair_kernel(kept_ref, got_ref, row_kept, row_got, *targets):
    chip, cut = here()[0], kept_ref.shape[2]
    for step, target in zip((0, *CHIP_STEPS), targets):
        there = chip ^ step
        total = kept_ref[there] + got_ref[there].astype(F32)
        target[:, :cut] = total.astype(target.dtype)
        total = row_kept[there] + row_got[there].astype(F32)
        target[:, cut:] = total.astype(target.dtype)


def layer_sum(own_ref, got_1, got_2, got_3):
    return own_ref[...] + (
        (got_1[...].astype(F32) + got_2[...].astype(F32)) + got_3[...].astype(F32)
    )


def layer_kernel(own_ref, got_1, got_2, got_3, send_ref, kept_ref):
    split_rows(layer_sum(own_ref, got_1, got_2, got_3), 0, send_ref, kept_ref)


def join_kernel(own_ref, got_1, got_2, got_3, kept_ref, got_ref, out_ref):
    total = layer_sum(own_ref, got_1, got_2, got_3).astype(BF16)
    cut, width = FIRST_PART, kept_ref.shape[1]
    out_ref[:, :cut] = total[:, :cut]
    out_ref[:, cut : cut + width] = (kept_ref[...] + got_ref[...].astype(F32)).astype(BF16)
    out_ref[:, cut + width :] = total[:, cut:]


def add_kernel(kept_ref, got_ref, out_ref):
    out_ref[...] = (kept_ref[...].astype(F32) + got_ref[...].astype(F32)).astype(BF16)


def result_kernel(held_ref, got_ref, w_ref, gain_ref, qkv_ref, out_ref, grad_ref):
    rows = qkv_ref.shape[0]
    chip, core, layer = here()
    at = (chip * 2 + core) * rows
    upper = (layer & 1) == 1
    half = rows // 2
    width = out_ref.shape[1]

    def ordered(lanes):
        held, got = held_ref[:, lanes].astype(F32), got_ref[:, lanes].astype(F32)
        return (jnp.where(upper, got, held), jnp.where(upper, held, got))

    row_at = 3 * HW + width
    for i in range(3):
        for at_from, at_to in ((row_at + i * HW, i * width), (i * HW, i * width + HW)):
            to = slice(at_to, at_to + HW)
            qkv_ref[:half, to], qkv_ref[half:, to] = ordered(slice(at_from, at_from + HW))
    out_ref[:half], out_ref[half:] = ordered(slice(3 * HW, row_at))
    total = jnp.sum(qkv_ref[...] * w_ref[...].astype(F32), -1, keepdims=True)
    shape = (rows, gain_ref.shape[1])
    row = lax.broadcasted_iota(jnp.int32, shape, 0)
    feature = lax.broadcasted_iota(jnp.int32, shape, 1)
    gain = jnp.sum(jnp.where(feature == row + at, gain_ref[...], 0.0), -1, keepdims=True)
    shape = (rows, grad_ref.shape[1])
    same = lax.broadcasted_iota(jnp.int32, shape, 0) == lax.broadcasted_iota(jnp.int32, shape, 1)
    grad_ref[...] = jnp.sum(jnp.where(same, total / gain, 0.0), 0, keepdims=True)


def call(kernel, name, ins, outs, scratch=(), vmem=SMALL_VMEM, out_specs=None):
    out_specs = out_specs or [VMEM] * len(outs)
    places = [{id(HBM): pltpu.HBM, id(PINNED): pltpu.VMEM}.get(id(spec)) for spec in out_specs]
    outs = [place(*out) if place else shaped(*out) for place, out in zip(places, outs)]
    args = [
        pltpu.with_memory_space_constraint(array, pltpu.HBM) if spec is HBM else array
        for spec, array in ins
    ]
    return pl.pallas_call(
        kernel,
        out_shape=outs,
        in_specs=[spec for spec, _ in ins],
        out_specs=out_specs,
        scratch_shapes=scratch,
        name=name,
        cost_estimate=pl.CostEstimate(flops=0, bytes_accessed=0, transcendentals=0),
        compiler_params=pltpu.CompilerParams(vmem_limit_bytes=vmem),
    )(*args)


def swap(array, axis, bits):
    count = lax.axis_size(axis)
    return lax.ppermute(array, axis, [(i, i ^ bits) for i in range(count)])


def cross_chips(*offs):
    return [swap(off, "seq", 2 * step) for off, step in zip(offs, CHIP_STEPS)]


def add_two(kept, got, name):
    (total,) = call(add_kernel, name, [(VMEM, kept), (VMEM, got)], [(kept.shape, BF16)])
    return total


def body(inputs, norm_gain, qkv_weight, out_weight, out_cotan):
    columns, width = inputs.shape[2:]
    n = lax.axis_size("seq")
    m = lax.axis_size("dp")
    share = columns // n
    row_share = width // n
    row_width, col_width = 3 * HW, 3 * HW + width
    x = inputs.reshape(columns, width)
    cot = out_cotan.reshape(columns, width)
    gain = norm_gain.reshape(1, width)
    chips = 4
    layered = n == 2 * chips and m == 4 and row_share == share
    weight_scratch = [
        pltpu.VMEM((1, width), F32),
        pltpu.VMEM((width, 3 * HW), BF16),
        pltpu.VMEM((HW, width), BF16),
    ]
    weights = [(HBM, gain), (HBM, qkv_weight), (HBM, out_weight)]
    col_outs = [((columns, 3 * HW), BF16), ((width, 3 * HW), BF16)]

    if layered:
        packed = call(
            pack_kernel,
            "pack_columns",
            [(HBM, x), (HBM, cot)],
            [((2, 2 * share, width), BF16)] * 3,
            [pltpu.SemaphoreType.DMA((6,))],
            out_specs=[ANY] * 3,
        )
        near = cross_chips(*packed)
        x_first, _ = lax.optimization_barrier((x, packed[0]))
    else:
        outgoing = jnp.stack([x.reshape(n, share, width), cot.reshape(n, share, width)], 1)
        moved = lax.all_to_all(outgoing, "seq", split_axis=0, concat_axis=0, tiled=True)
        x_first = x

    row_outs = [
        ((HW, width), BF16),
        ((columns, width), F32), ((columns, width), F32), ((columns, 1), F32),
        ((columns, width), BF16), ((columns, width), BF16),
    ]
    if layered:
        cut = row_width // 2
        split_outs = [((chips, row_share, cut), BF16)] * 4
        handed_outs = [
            ((row_share, 3 * width), BF16), ((width, 3 * HW), BF16), ((HW, width), BF16),
        ]
        row_outs = [*split_outs, *handed_outs, *row_outs]
        specs = [VMEM] * 4 + [PINNED] * (len(row_outs) - 4)
    else:
        row_outs = [((width, row_width), BF16), *row_outs]
        specs = [VMEM] * len(row_outs)
    *row_terms, row_out, base, normed, inverse_rms, x_near, cot_near = call(
        row_chip_kernel if layered else row_kernel,
        "row_heads",
        [(HBM, x_first), (HBM, cot), *weights],
        row_outs,
        [
            *weight_scratch,
            pltpu.VMEM((columns, HW), F32),
            pltpu.VMEM((columns, HW), F32),
            pltpu.VMEM((columns, 3 * HW), BF16),
            pltpu.SemaphoreType.DMA((12,)),
        ],
        BIG_VMEM,
        specs,
    )
    if layered:
        *row_terms, weight_rows, col_weight, col_out_weight = row_terms
        row_sent = [swap(one, "seq", 1) for one in row_terms[:2]]
        half_block = (chips, row_share // 2, row_width)
        row_next, row_kept = call(
            row_cores_kernel,
            "row_add_cores",
            [(VMEM, one) for one in (*row_terms[2:], *row_sent)],
            [(half_block, BF16), (half_block, F32)],
            out_specs=[VMEM, PINNED],
        )
        *near, row_kept = lax.optimization_barrier((*near, row_kept))
        (far,) = call(
            far_kernel,
            "pack_other_core",
            [(VMEM, one) for one in (x_near, cot_near, *near)],
            [((chips, 2, share, width), BF16)],
        )
        row_got = swap(row_next, "dp", 1)
        send, keep, col_grads = call(
            column_chip_kernel,
            "column_heads",
            [
                (VMEM, one)
                for one in (
                    x_near, cot_near, *near, swap(far, "seq", 1),
                    gain, col_weight, col_out_weight, row_out,
                )
            ],
            [((chips, row_share, col_width), BF16)] * 2 + [col_outs[0]],
            vmem=BIG_VMEM,
            out_specs=[VMEM, VMEM, PINNED],
        )
        back_send, back_keep = call(
            back_chip_kernel,
            "column_grad_hidden",
            [(VMEM, col_grads), (VMEM, col_weight)],
            [((chips, share, width), BF16)] * 2,
        )
        send, row_got, back_keep = lax.optimization_barrier((send, row_got, back_keep))
        first_half = (chips, row_share // 2, FIRST_PART)
        second = (row_share, col_width - FIRST_PART)
        to_next, kept, *parts = call(
            cores_kernel,
            "column_add_cores",
            [(VMEM, keep), (VMEM, swap(send, "seq", 1))],
            [(first_half, BF16), (first_half, F32), (second, F32)] + [(second, BF16)] * 3,
            out_specs=[VMEM, PINNED, PINNED, VMEM, VMEM, VMEM],
        )
        layer_got = cross_chips(*parts[1:])
        back = call(
            back_pack_kernel,
            "pack_grad_hidden",
            [(VMEM, back_keep), (VMEM, swap(back_send, "seq", 1))],
            [((2 * share, width), BF16)] * 4,
        )
        row_kept, *back = lax.optimization_barrier((row_kept, *back))
        joint = (row_share // 2, FIRST_PART + row_width)
        owned, *off = call(
            pair_kernel,
            "first_add_pair",
            [(VMEM, one) for one in (kept, swap(to_next, "dp", 1), row_kept, row_got)],
            [(joint, F32)] + [(joint, BF16)] * 3,
            out_specs=[PINNED, VMEM, VMEM, VMEM],
        )
        got = cross_chips(*off)
        half_second = (row_share // 2, second[1])
        to_next, kept = call(
            layer_kernel,
            "second_add_chips",
            [(VMEM, one) for one in (parts[0], *layer_got)],
            [(half_second, BF16), (half_second, F32)],
            out_specs=[VMEM, PINNED],
        )
        (pair_sum,) = call(
            join_kernel,
            "join_terms",
            [(VMEM, one) for one in (owned, *got, kept, swap(to_next, "dp", 1))],
            [((row_share // 2, col_width + row_width), BF16)],
        )
        *back, pair_sum = lax.optimization_barrier((*back, pair_sum))
        held = add_two(pair_sum, swap(pair_sum, "dp", 2), "add_pairs")
        other = swap(held, "dp", 1)
        (grad,) = call(
            input_chip_kernel,
            "input_grad",
            [
                (VMEM, one)
                for one in (base, normed, inverse_rms, gain, back[0], *cross_chips(*back[1:]))
            ],
            [((columns, width), BF16)],
            [pltpu.VMEM((chips, 2 * share, width), BF16), pltpu.SemaphoreType.DMA((chips,))],
            out_specs=[HBM],
        )
        sum_qkv, sum_out, sum_gain = call(
            result_kernel,
            "result",
            [(VMEM, held), (VMEM, other), (VMEM, weight_rows), (VMEM, gain)],
            [((row_share, 3 * width), F32), ((row_share, width), F32), ((1, row_share), F32)],
        )
        sum_gain = sum_gain.reshape(row_share)
    else:
        terms, *col_grads = call(
            column_kernel,
            "column_heads",
            [(ANY, moved), *weights, (VMEM, row_terms[0]), (VMEM, row_out)],
            [((width, 4 * width), BF16), *col_outs],
            [
                pltpu.VMEM((n, 2, share, width), BF16),
                weight_scratch[0],
                weight_scratch[2],
                pltpu.SemaphoreType.DMA((6,)),
            ],
            BIG_VMEM,
        )
        (back,) = call(
            back_kernel,
            "column_grad_hidden",
            [(VMEM, one) for one in col_grads],
            [((n, share, width), BF16)],
        )
        returned = lax.all_to_all(back, "seq", split_axis=0, concat_axis=0, tiled=True)
        (grad,) = call(
            input_kernel,
            "input_grad",
            [
                (VMEM, base), (VMEM, normed), (VMEM, inverse_rms), (VMEM, gain),
                (VMEM, returned.reshape(columns, width)),
            ],
            [((columns, width), BF16)],
        )
        terms = lax.all_to_all(
            terms.reshape(n, row_share, 4 * width), "seq", split_axis=0, concat_axis=0, tiled=True
        )
        total = jnp.sum(terms.astype(F32), 0)
        for step in range(m.bit_length() - 1):
            sent = total.astype(BF16)
            total = sent.astype(F32) + swap(sent, "dp", 1 << step).astype(F32)
        sum_qkv, sum_out = total[:, : 3 * width], total[:, 3 * width :]
        here_at = lax.axis_index("seq") * row_share
        own_gain = lax.dynamic_slice_in_dim(norm_gain, here_at, row_share, 0)
        own_weight = lax.dynamic_slice_in_dim(qkv_weight, here_at, row_share, 0)
        sum_gain = jnp.sum(sum_qkv * own_weight.astype(F32), -1) / own_gain
    return (grad.reshape(inputs.shape), sum_qkv, sum_out, sum_gain)


def solution(mesh):
    return jax.shard_map(
        body,
        mesh=mesh,
        in_specs=(P("dp", "seq", None, None), P(), P(), P(), P("dp", "seq", None, None)),
        out_specs=(P("dp", "seq", None, None), P("seq", None), P("seq", None), P("seq")),
        check_vma=False,
    )
```

```python
import math

import jax
import jax.numpy as jnp
from jax import lax
from jax.experimental import pallas as pl
from jax.experimental.pallas import tpu as pltpu
from jax.sharding import PartitionSpec as P

H = 8
HD = 64
HH = H // 2
HW = HH * HD
SCALE = HD ** (-0.5)
F32 = jnp.float32
BF16 = jnp.bfloat16
QUERY_BLOCK = 128
BIG_VMEM = 20 * 1024 * 1024
SMALL_VMEM = 8 * 1024 * 1024
ANY = pl.BlockSpec(memory_space=pl.ANY)
VMEM = pl.BlockSpec(memory_space=pltpu.VMEM)
HBM = pl.BlockSpec(memory_space=pltpu.HBM)
CHIP_STEPS = (3, 2, 1)
PINNED = pl.BlockSpec(memory_space=pltpu.VMEM)
shaped = jax.ShapeDtypeStruct


def here():
    device = lax.axis_index("seq")
    return device >> 1, device & 1, lax.axis_index("dp")


def dot_nn(a, b):
    return lax.dot_general(a, b, (((1,), (0,)), ((), ())), preferred_element_type=F32)


def dot_nt(a, b):
    return lax.dot_general(a, b, (((1,), (1,)), ((), ())), preferred_element_type=F32)


def rms_parts(x):
    inverse_rms = lax.rsqrt(jnp.mean(x * x, -1, keepdims=True) + 1e-05)
    return inverse_rms, x * inverse_rms


def transposed(x):
    block = math.gcd(x.shape[1], 256)
    eye = (
        lax.broadcasted_iota(jnp.int32, (block, block), 0)
        == lax.broadcasted_iota(jnp.int32, (block, block), 1)
    ).astype(F32).astype(BF16)
    parts = [
        dot_nt(eye, x[:, at : at + block]).astype(BF16) for at in range(0, x.shape[1], block)
    ]
    return parts[0] if len(parts) == 1 else jnp.concatenate(parts, 0)


def head_pair(x):
    lane = lax.broadcasted_iota(jnp.int32, x.shape, 1)
    zero = jnp.zeros_like(x)
    return jnp.concatenate([jnp.where(lane < HD, x, zero), jnp.where(lane < HD, zero, x)], 0)


def both_heads(both, count):
    return jnp.concatenate([both[:HD, :count], both[HD:, count:]], 0)


def pair_steps(items, mask_rows, mask):
    count = items[0][2].shape[1]
    scores = [dot_nt(k, q2) for q2, _, _, k, _, _, _ in items]
    prob_grads = [dot_nt(v, g2) for _, g2, _, _, v, _, _ in items]
    probs = []
    for score in scores:
        first = score.shape[0] - mask_rows
        tail = jnp.where(mask, score[first:], -1e30)
        score = tail if first == 0 else jnp.concatenate([score[:first], tail], 0)
        exponent = jnp.exp(score - jnp.max(score, 0, keepdims=True))
        probs.append(exponent * (1.0 / jnp.sum(exponent, 0, keepdims=True)))
    weights = [prob.astype(BF16) for prob in probs]
    attended = [
        both_heads(dot_nn(item[6], weight), count).astype(BF16)
        for item, weight in zip(items, weights)
    ]
    score_grads = []
    for item, att, prob, prob_grad in zip(items, attended, probs, prob_grads):
        product = item[2].astype(F32) * att.astype(F32)
        delta = [jnp.sum(part, 0, keepdims=True) for part in (product[:HD], product[HD:])]
        score_grads.append((prob * (prob_grad - jnp.concatenate(delta, 1))).astype(BF16))
    grad_q = [
        (both_heads(dot_nn(item[5], score_grad), count) * SCALE).astype(BF16)
        for item, score_grad in zip(items, score_grads)
    ]
    grad_k = [dot_nn(score_grad, item[0]) for item, score_grad in zip(items, score_grads)]
    grad_v = [dot_nn(weight, item[1]) for item, weight in zip(items, weights)]
    return list(zip(attended, grad_q, grad_k, grad_v))


def split_cores(piece, send_ref, keep_ref, chips, lanes):
    rows = send_ref.shape[1]
    parts = piece.reshape(chips.stop - chips.start, 2, rows, piece.shape[1])
    even, odd = parts[:, 0], parts[:, 1]
    first = here()[1] == 0
    send_ref[chips, :, lanes] = jnp.where(first, odd, even)
    keep_ref[chips, :, lanes] = jnp.where(first, even, odd)


def qkv_copies(wqkv_ref, w_ref, sems, second):
    width = wqkv_ref.shape[0]
    return [
        pltpu.make_async_copy(
            wqkv_ref.at[:, pl.ds(i * width + second * HW, HW)],
            w_ref.at[:, pl.ds(i * HW, HW)],
            sems.at[i],
        )
        for i in range(3)
    ]


def weight_copies(wqkv_ref, wout_ref, w_ref, wo_ref, sems, second):
    out_rows = wout_ref.at[pl.ds(second * HW, HW), :]
    return [
        *qkv_copies(wqkv_ref, w_ref, sems, second),
        pltpu.make_async_copy(out_rows, wo_ref, sems.at[3]),
    ]


def started(*copies):
    for copy in copies:
        copy.start()
    return copies


def finished(*copies):
    for copy in copies:
        copy.wait()


def project(hidden, cot, w_ref, wo_ref):
    projected = dot_nn(hidden, w_ref[...]).astype(BF16)
    q, k, v = [projected[:, i * HW : (i + 1) * HW] for i in range(3)]
    g = dot_nt(cot, wo_ref[...]).astype(BF16)
    return q * jnp.asarray(SCALE, BF16), k, v, g


def row_part(
    x_any, cot_any, gain_any, wqkv_any, wout_any,
    out_ref, base_ref, normed_ref, inverse_ref, x_ref, cot_ref,
    gain_ref, w_ref, wo_ref, dk_ref, dv_ref, grads_ref, sems,
):
    first = started(
        pltpu.make_async_copy(x_any, x_ref, sems.at[4]),
        pltpu.make_async_copy(gain_any, gain_ref, sems.at[5]),
    )
    later = started(
        *weight_copies(wqkv_any, wout_any, w_ref, wo_ref, sems, 0),
        pltpu.make_async_copy(cot_any, cot_ref, sems.at[6]),
    )
    dk_ref[...] = jnp.zeros_like(dk_ref)
    dv_ref[...] = jnp.zeros_like(dv_ref)
    finished(*first)
    tokens = x_ref.shape[0]
    inverse_ref[...], normed_ref[...] = rms_parts(x_ref[...].astype(F32))
    hidden = (normed_ref[...] * gain_ref[...]).astype(BF16)
    hidden_t = transposed(hidden)
    finished(*later)
    cot = cot_ref[...]
    q, k, v, g = project(hidden, cot, w_ref, wo_ref)
    kt, vt, gt = transposed(k), transposed(v), transposed(g)
    step = math.gcd(tokens, QUERY_BLOCK)
    query = lax.broadcasted_iota(jnp.int32, (step, 2 * step), 1) % step
    mask = query >= lax.broadcasted_iota(jnp.int32, (step, 2 * step), 0)
    pairs = [slice(i * 2 * HD, (i + 1) * 2 * HD) for i in range(HH // 2)]
    att_blocks, dq_blocks = [], []
    for start in range(0, tokens, step):
        rows, keys = slice(start, start + step), slice(0, start + step)
        items = [
            (
                head_pair(q[rows, lanes]), head_pair(g[rows, lanes]), gt[lanes, rows],
                k[keys, lanes], v[keys, lanes], kt[lanes, keys], vt[lanes, keys],
            )
            for lanes in pairs
        ]
        results = pair_steps(items, step, mask)
        for lanes, (_, _, dk, dv) in zip(pairs, results):
            dk_ref[keys, lanes] += dk
            dv_ref[keys, lanes] += dv
        att_blocks.append(jnp.concatenate([result[0] for result in results], 0))
        dq_blocks.append(jnp.concatenate([result[1] for result in results], 0))
    grads_ref[:, :HW] = transposed(jnp.concatenate(dq_blocks, 1))
    grads_ref[:, HW : 2 * HW] = dk_ref[...].astype(BF16)
    grads_ref[:, 2 * HW :] = dv_ref[...].astype(BF16)
    term_qkv = dot_nn(hidden_t, grads_ref[...]).astype(BF16)
    out_ref[...] = dot_nn(jnp.concatenate(att_blocks, 1), cot).astype(BF16)
    grad_normed = dot_nt(grads_ref[...], w_ref[...]) * gain_ref[...]
    base_ref[...] = input_grad(
        cot_ref[...].astype(F32), normed_ref[...], inverse_ref[...], grad_normed
    )
    return term_qkv


def row_kernel(x_any, cot_any, gain_any, wqkv_any, wout_any, qkv_ref, *refs):
    qkv_ref[...] = row_part(x_any, cot_any, gain_any, wqkv_any, wout_any, *refs)


def row_chip_kernel(
    x_any, cot_any, gain_any, wqkv_any, wout_any,
    send_1, send_2, keep_1, keep_2, rows_ref, col_w_ref, col_wo_ref, *refs,
):
    chip, core, _ = here()
    sems, rows = refs[-1], rows_ref.shape[0]
    at = pl.multiple_of((chip * 2 + core) * rows, rows)
    handed = started(
        pltpu.make_async_copy(wqkv_any.at[pl.ds(at, rows), :], rows_ref, sems.at[7]),
        *weight_copies(wqkv_any, wout_any, col_w_ref, col_wo_ref, sems.at[pl.ds(8, 4)], 1),
    )
    term_qkv = row_part(x_any, cot_any, gain_any, wqkv_any, wout_any, *refs)
    chips, cut = send_1.shape[0], keep_1.shape[2]
    pieces = slice(0, chips), slice(0, cut)
    split_cores(term_qkv[:, :cut], send_1, keep_1, *pieces)
    split_cores(term_qkv[:, cut:], send_2, keep_2, *pieces)
    finished(*handed)


def column_part(x, cot, mask, gain, w_ref, wo_ref, weight_waits, grads_ref):
    tokens, block = x.shape[0], mask.shape[0]
    _, normed = rms_parts(x.astype(F32))
    hidden = (normed * gain).astype(BF16)
    hidden_t = transposed(hidden)
    finished(*weight_waits)
    q, k, v, g = project(hidden, cot, w_ref, wo_ref)
    kt, vt, gt = transposed(k), transposed(v), transposed(g)
    pairs = [slice(i * 2 * HD, (i + 1) * 2 * HD) for i in range(HH // 2)]
    blocks = [slice(at, at + block) for at in range(0, tokens, block)]
    items = [
        (
            head_pair(q[rows, lanes]), head_pair(g[rows, lanes]), gt[lanes, rows],
            k[rows, lanes], v[rows, lanes], kt[lanes, rows], vt[lanes, rows],
        )
        for lanes in pairs
        for rows in blocks
    ]
    results = pair_steps(items, block, mask)
    places = [(lanes, rows) for lanes in pairs for rows in blocks]
    for (lanes, rows), (_, _, dk, dv) in zip(places, results):
        grads_ref[rows, HW + lanes.start : HW + lanes.stop] = dk.astype(BF16)
        grads_ref[rows, 2 * HW + lanes.start : 2 * HW + lanes.stop] = dv.astype(BF16)
    by_pair = [results[i * len(blocks) : (i + 1) * len(blocks)] for i in range(len(pairs))]
    attended, grad_q = [
        jnp.concatenate([jnp.concatenate([r[i] for r in some], 1) for some in by_pair], 0)
        for i in range(2)
    ]
    grads_ref[:, :HW] = transposed(grad_q)
    term_qkv = dot_nn(hidden_t, grads_ref[...]).astype(BF16)
    term_out = dot_nn(attended, cot).astype(BF16)
    return term_qkv, term_out


def column_mask(all_rows, group, row_of):
    block = all_rows * group
    shape = (block, 2 * block)
    query = lax.broadcasted_iota(jnp.int32, shape, 1) % block
    key = lax.broadcasted_iota(jnp.int32, shape, 0)
    same_column = query % group == key % group
    return (row_of(query // group) >= row_of(key // group)) & same_column


def column_kernel(
    moved_any, gain_any, wqkv_any, wout_any, row_qkv_ref, row_out_ref,
    terms_ref, grads_ref, w_ref,
    moved_ref, gain_ref, wo_ref, sems,
):
    copies = started(
        pltpu.make_async_copy(moved_any, moved_ref, sems.at[4]),
        pltpu.make_async_copy(gain_any, gain_ref, sems.at[5]),
    )
    weights = started(*weight_copies(wqkv_any, wout_any, w_ref, wo_ref, sems, 1))
    finished(*copies)
    all_rows, _, share, width = moved_ref.shape
    group = math.gcd(share, 16)
    x, cot = [
        jnp.concatenate(
            [
                moved_ref[:, which, at : at + group, :].astype(F32).reshape(all_rows * group, width)
                for at in range(0, share, group)
            ],
            0,
        ).astype(BF16)
        for which in range(2)
    ]
    mask = column_mask(all_rows, group, lambda place: place)
    term_qkv, term_out = column_part(
        x, cot, mask, gain_ref[...], w_ref, wo_ref, weights, grads_ref
    )
    for i in range(3):
        at = i * width
        terms_ref[:, at : at + HW] = row_qkv_ref[:, i * HW : (i + 1) * HW]
        terms_ref[:, at + HW : at + 2 * HW] = term_qkv[:, i * HW : (i + 1) * HW]
    terms_ref[:HW, 3 * width :] = row_out_ref[...]
    terms_ref[HW:, 3 * width :] = term_out


def column_chip_kernel(
    x_ref, cot_ref, near_1, near_2, near_3, far_ref, gain_ref, w_ref, wo_ref, row_out_ref,
    send_ref, keep_ref, grads_ref,
):
    chip, core, _ = here()
    share = far_ref.shape[2]
    half = pl.ds(pl.multiple_of(core * share, share), share)
    at = pl.ds(pl.multiple_of((chip * 2 + core) * share, share), share)
    group = math.gcd(share, 16)

    def tokens(which, mine):
        pieces = [mine[at, :], far_ref[0, which]]
        for i, near in enumerate((near_1, near_2, near_3)):
            pieces += [near[which, half, :], far_ref[i + 1, which]]
        starts = range(0, share, group)
        return jnp.concatenate(
            [piece[start : start + group] for start in starts for piece in pieces], 0
        )

    def row_of(place):
        step = (4 - (place >> 1)) & 3
        return ((step ^ chip) << 1) + ((place & 1) ^ core)

    mask = column_mask(2 * (len(CHIP_STEPS) + 1), group, row_of)
    term_qkv, term_out = column_part(
        tokens(0, x_ref), tokens(1, cot_ref), mask, gain_ref[...], w_ref, wo_ref, (), grads_ref
    )
    chips = send_ref.shape[0]
    refs = send_ref, keep_ref
    out_lanes = slice(3 * HW, send_ref.shape[2])
    split_cores(term_qkv, *refs, slice(0, chips), slice(0, 3 * HW))
    split_cores(row_out_ref[...], *refs, slice(0, chips // 2), out_lanes)
    split_cores(term_out, *refs, slice(chips // 2, chips), out_lanes)


def far_kernel(x_ref, cot_ref, near_1, near_2, near_3, far_ref):
    chip, core, _ = here()
    share = far_ref.shape[2]
    at = pl.ds(pl.multiple_of((chip * 2 + 1 - core) * share, share), share)
    far_ref[0, 0], far_ref[0, 1] = x_ref[at, :], cot_ref[at, :]
    at = pl.ds(pl.multiple_of((1 - core) * share, share), share)
    for i, near in enumerate((near_1, near_2, near_3)):
        far_ref[i + 1] = near[:, at, :]


def back_kernel(grads_ref, w_ref, back_ref):
    grad_hidden = dot_nt(grads_ref[...], w_ref[...])
    all_rows, share, width = back_ref.shape
    group = math.gcd(share, 16)
    block = all_rows * group
    for i in range(share // group):
        piece = grad_hidden[i * block : (i + 1) * block].reshape(all_rows, group, width)
        back_ref[:, i * group : (i + 1) * group, :] = piece.astype(BF16)


def back_chip_kernel(grads_ref, w_ref, send_ref, keep_ref):
    grad_hidden = dot_nt(grads_ref[...], w_ref[...]).astype(BF16)
    chips, share, width = keep_ref.shape
    group = math.gcd(share, 16)
    block = 2 * chips * group
    for i in range(share // group):
        piece = grad_hidden[i * block : (i + 1) * block].reshape(chips, 2, group, width)
        at = slice(i * group, (i + 1) * group)
        keep_ref[:, at, :], send_ref[:, at, :] = piece[:, 0], piece[:, 1]


def back_pack_kernel(keep_ref, got_ref, *targets):
    share = keep_ref.shape[1]
    core = here()[1]
    kept_at = pl.ds(pl.multiple_of(core * share, share), share)
    got_at = pl.ds(pl.multiple_of((1 - core) * share, share), share)
    for i, target in enumerate(targets):
        target[kept_at, :] = keep_ref[i]
        target[got_at, :] = got_ref[i]


def input_kernel(base_ref, normed_ref, inverse_ref, gain_ref, back_ref, grad_ref):
    grad_ref[...] = input_grad(
        base_ref[...], normed_ref[...], inverse_ref[...], back_ref[...].astype(F32) * gain_ref[...]
    ).astype(BF16)


def input_grad(base, normed, inverse_rms, grad_normed):
    projected = jnp.mean(grad_normed * normed, -1, keepdims=True)
    return base + inverse_rms * (grad_normed - normed * projected)


def input_chip_kernel(
    base_ref, normed_ref, inverse_ref, gain_ref, own_ref, got_1, got_2, got_3,
    grad_any, grad_ref, sems,
):
    chip = here()[0]
    count = own_ref.shape[0]
    copies = []
    for i, (step, back_ref) in enumerate(zip((0, *CHIP_STEPS), (own_ref, got_1, got_2, got_3))):
        at = pl.ds(pl.multiple_of((chip ^ step) * count, count), count)
        grad_normed = back_ref[...].astype(F32) * gain_ref[...]
        grad = input_grad(base_ref[at, :], normed_ref[at, :], inverse_ref[at, :], grad_normed)
        grad_ref[i] = grad.astype(BF16)
        copies += started(pltpu.make_async_copy(grad_ref.at[i], grad_any.at[at, :], sems.at[i]))
    finished(*copies)


def pack_kernel(x_any, cot_any, off_1, off_2, off_3, sems):
    chip = here()[0]
    count = off_1.shape[1]
    copies = []
    for i, (step, target) in enumerate(zip(CHIP_STEPS, (off_1, off_2, off_3))):
        at = pl.ds(pl.multiple_of((chip ^ step) * count, count), count)
        for which, source in enumerate((x_any, cot_any)):
            copies.append(
                pltpu.make_async_copy(source.at[at, :], target.at[which], sems.at[2 * i + which])
            )
    finished(*started(*copies))


def split_rows(total, axis):
    upper = (here()[2] & 1) == 1
    low, high = jnp.split(total, 2, axis)
    return jnp.where(upper, low, high).astype(BF16), jnp.where(upper, high, low)


def row_cores_kernel(keep_1, keep_2, got_1, got_2, send_ref, kept_ref):
    total = [
        keep_ref[...].astype(F32) + got_ref[...].astype(F32)
        for keep_ref, got_ref in ((keep_1, got_1), (keep_2, got_2))
    ]
    send_ref[...], kept_ref[...] = split_rows(jnp.concatenate(total, 2), 1)


def cores_kernel(keep_ref, got_ref, *targets):
    chip = here()[0]
    for step, target in zip((0, *CHIP_STEPS), targets):
        there = chip ^ step
        total = keep_ref[there].astype(F32) + got_ref[there].astype(F32)
        target[...] = total.astype(target.dtype)


def layer_sum(own_ref, got_1, got_2, got_3):
    return own_ref[...] + (
        (got_1[...].astype(F32) + got_2[...].astype(F32)) + got_3[...].astype(F32)
    )


def layer_kernel(own_ref, got_1, got_2, got_3, send_1, send_2, kept_ref):
    sent, kept_ref[...] = split_rows(layer_sum(own_ref, got_1, got_2, got_3), 0)
    cut = send_1.shape[1]
    send_1[...], send_2[...] = sent[:, :cut], sent[:, cut:]


def join_kernel(own_ref, got_1, got_2, got_3, kept_ref, pair_1, pair_2, out_ref):
    cut = kept_ref.shape[1]
    got = jnp.concatenate([pair_1[...], pair_2[...]], 1).astype(F32)
    out_ref[:, :cut] = (kept_ref[...] + got).astype(BF16)
    out_ref[:, cut:] = layer_sum(own_ref, got_1, got_2, got_3).astype(BF16)


def add_kernel(kept_ref, got_ref, out_ref):
    out_ref[...] = (kept_ref[...].astype(F32) + got_ref[...].astype(F32)).astype(BF16)


def result_kernel(held_ref, got_ref, w_ref, gain_ref, qkv_ref, out_ref, grad_ref):
    rows = qkv_ref.shape[0]
    chip, core, layer = here()
    at = (chip * 2 + core) * rows
    upper = (layer & 1) == 1
    half = rows // 2
    width = out_ref.shape[1]

    def ordered(lanes):
        held, got = held_ref[:, lanes].astype(F32), got_ref[:, lanes].astype(F32)
        return (jnp.where(upper, got, held), jnp.where(upper, held, got))

    row_at = 3 * HW + width
    for i in range(3):
        for at_from, at_to in ((row_at + i * HW, i * width), (i * HW, i * width + HW)):
            to = slice(at_to, at_to + HW)
            qkv_ref[:half, to], qkv_ref[half:, to] = ordered(slice(at_from, at_from + HW))
    out_ref[:half], out_ref[half:] = ordered(slice(3 * HW, row_at))
    total = jnp.sum(qkv_ref[...] * w_ref[...].astype(F32), -1, keepdims=True)
    shape = (rows, gain_ref.shape[1])
    row = lax.broadcasted_iota(jnp.int32, shape, 0)
    feature = lax.broadcasted_iota(jnp.int32, shape, 1)
    gain = jnp.sum(jnp.where(feature == row + at, gain_ref[...], 0.0), -1, keepdims=True)
    shape = (rows, grad_ref.shape[1])
    same = lax.broadcasted_iota(jnp.int32, shape, 0) == lax.broadcasted_iota(jnp.int32, shape, 1)
    grad_ref[...] = jnp.sum(jnp.where(same, total / gain, 0.0), 0, keepdims=True)


def call(kernel, name, ins, outs, scratch=(), vmem=SMALL_VMEM, out_specs=None):
    out_specs = out_specs or [VMEM] * len(outs)
    places = [{id(HBM): pltpu.HBM, id(PINNED): pltpu.VMEM}.get(id(spec)) for spec in out_specs]
    outs = [place(*out) if place else shaped(*out) for place, out in zip(places, outs)]
    args = [
        pltpu.with_memory_space_constraint(array, pltpu.HBM) if spec is HBM else array
        for spec, array in ins
    ]
    return pl.pallas_call(
        kernel,
        out_shape=outs,
        in_specs=[spec for spec, _ in ins],
        out_specs=out_specs,
        scratch_shapes=scratch,
        name=name,
        cost_estimate=pl.CostEstimate(flops=0, bytes_accessed=0, transcendentals=0),
        compiler_params=pltpu.CompilerParams(vmem_limit_bytes=vmem),
    )(*args)


def swap(array, axis, bits):
    count = lax.axis_size(axis)
    return lax.ppermute(array, axis, [(i, i ^ bits) for i in range(count)])


def add_by_chip(keep, got, name):
    shape = keep.shape[1:]
    return call(
        cores_kernel,
        name,
        [(VMEM, keep), (VMEM, got)],
        [(shape, F32)] + [(shape, BF16)] * 3,
        out_specs=[PINNED, VMEM, VMEM, VMEM],
    )


def cross_chips(*offs):
    return [swap(off, "seq", 2 * step) for off, step in zip(offs, CHIP_STEPS)]


def add_two(kept, got, name):
    (total,) = call(add_kernel, name, [(VMEM, kept), (VMEM, got)], [(kept.shape, BF16)])
    return total


def body(inputs, norm_gain, qkv_weight, out_weight, out_cotan):
    columns, width = inputs.shape[2:]
    n = lax.axis_size("seq")
    m = lax.axis_size("dp")
    share = columns // n
    row_share = width // n
    row_width, col_width = 3 * HW, 3 * HW + width
    x = inputs.reshape(columns, width)
    cot = out_cotan.reshape(columns, width)
    gain = norm_gain.reshape(1, width)
    chips = 4
    layered = n == 2 * chips and m == 4 and row_share == share
    weight_scratch = [
        pltpu.VMEM((1, width), F32),
        pltpu.VMEM((width, 3 * HW), BF16),
        pltpu.VMEM((HW, width), BF16),
    ]
    weights = [(HBM, gain), (HBM, qkv_weight), (HBM, out_weight)]
    col_outs = [((columns, 3 * HW), BF16), ((width, 3 * HW), BF16)]

    if layered:
        packed = call(
            pack_kernel,
            "pack_columns",
            [(HBM, x), (HBM, cot)],
            [((2, 2 * share, width), BF16)] * 3,
            [pltpu.SemaphoreType.DMA((6,))],
            out_specs=[ANY] * 3,
        )
        near = cross_chips(*packed)
        x_first, _ = lax.optimization_barrier((x, packed[0]))
    else:
        outgoing = jnp.stack([x.reshape(n, share, width), cot.reshape(n, share, width)], 1)
        moved = lax.all_to_all(outgoing, "seq", split_axis=0, concat_axis=0, tiled=True)
        x_first = x

    row_outs = [
        ((HW, width), BF16),
        ((columns, width), F32), ((columns, width), F32), ((columns, 1), F32),
        ((columns, width), BF16), ((columns, width), BF16),
    ]
    if layered:
        cut = row_width // 2
        split_outs = [((chips, row_share, cut), BF16)] * 4
        handed_outs = [
            ((row_share, 3 * width), BF16), ((width, 3 * HW), BF16), ((HW, width), BF16),
        ]
        row_outs = [*split_outs, *handed_outs, *row_outs]
        specs = [VMEM] * 4 + [PINNED] * (len(row_outs) - 4)
    else:
        row_outs = [((width, row_width), BF16), *row_outs]
        specs = [VMEM] * len(row_outs)
    *row_terms, row_out, base, normed, inverse_rms, x_near, cot_near = call(
        row_chip_kernel if layered else row_kernel,
        "row_heads",
        [(HBM, x_first), (HBM, cot), *weights],
        row_outs,
        [
            *weight_scratch,
            pltpu.VMEM((columns, HW), F32),
            pltpu.VMEM((columns, HW), F32),
            pltpu.VMEM((columns, 3 * HW), BF16),
            pltpu.SemaphoreType.DMA((12,)),
        ],
        BIG_VMEM,
        specs,
    )
    if layered:
        *row_terms, weight_rows, col_weight, col_out_weight = row_terms
        row_sent = [swap(one, "seq", 1) for one in row_terms[:2]]
        half_block = (chips, row_share // 2, row_width)
        row_next, row_kept = call(
            row_cores_kernel,
            "row_add_cores",
            [(VMEM, one) for one in (*row_terms[2:], *row_sent)],
            [(half_block, BF16), (half_block, F32)],
            out_specs=[VMEM, PINNED],
        )
        *near, row_kept = lax.optimization_barrier((*near, row_kept))
        (far,) = call(
            far_kernel,
            "pack_other_core",
            [(VMEM, one) for one in (x_near, cot_near, *near)],
            [((chips, 2, share, width), BF16)],
        )
        send, keep, col_grads = call(
            column_chip_kernel,
            "column_heads",
            [
                (VMEM, one)
                for one in (
                    x_near, cot_near, *near, swap(far, "seq", 1),
                    gain, col_weight, col_out_weight, row_out,
                )
            ],
            [((chips, row_share, col_width), BF16)] * 2 + [col_outs[0]],
            vmem=BIG_VMEM,
            out_specs=[VMEM, VMEM, PINNED],
        )
        back_send, back_keep = call(
            back_chip_kernel,
            "column_grad_hidden",
            [(VMEM, col_grads), (VMEM, col_weight)],
            [((chips, share, width), BF16)] * 2,
        )
        row_next, _ = lax.optimization_barrier((row_next, send))
        keep, back_keep = lax.optimization_barrier((keep, back_keep))
        owned, *off = add_by_chip(keep, swap(send, "seq", 1), "column_add_cores")
        got = cross_chips(*off)
        back = call(
            back_pack_kernel,
            "pack_grad_hidden",
            [(VMEM, back_keep), (VMEM, swap(back_send, "seq", 1))],
            [((2 * share, width), BF16)] * 4,
        )
        row_kept, *back = lax.optimization_barrier((row_kept, *back))
        row_owned, *row_off = add_by_chip(row_kept, swap(row_next, "dp", 1), "row_add_pair")
        row_got = cross_chips(*row_off)
        half_rows = row_share // 2
        *to_next, kept = call(
            layer_kernel,
            "column_add_chips",
            [(VMEM, one) for one in (owned, *got)],
            [((half_rows, col_width // 2), BF16)] * 2 + [((half_rows, col_width), F32)],
            out_specs=[VMEM, VMEM, PINNED],
        )
        pair_got = [swap(one, "dp", 1) for one in to_next]
        (pair_sum,) = call(
            join_kernel,
            "join_terms",
            [(VMEM, one) for one in (row_owned, *row_got, kept, *pair_got)],
            [((row_share // 2, col_width + row_width), BF16)],
        )
        *back, pair_sum = lax.optimization_barrier((*back, pair_sum))
        held = add_two(pair_sum, swap(pair_sum, "dp", 2), "add_pairs")
        other = swap(held, "dp", 1)
        (grad,) = call(
            input_chip_kernel,
            "input_grad",
            [
                (VMEM, one)
                for one in (base, normed, inverse_rms, gain, back[0], *cross_chips(*back[1:]))
            ],
            [((columns, width), BF16)],
            [pltpu.VMEM((chips, 2 * share, width), BF16), pltpu.SemaphoreType.DMA((chips,))],
            out_specs=[HBM],
        )
        sum_qkv, sum_out, sum_gain = call(
            result_kernel,
            "result",
            [(VMEM, held), (VMEM, other), (VMEM, weight_rows), (VMEM, gain)],
            [((row_share, 3 * width), F32), ((row_share, width), F32), ((1, row_share), F32)],
        )
        sum_gain = sum_gain.reshape(row_share)
    else:
        terms, *col_grads = call(
            column_kernel,
            "column_heads",
            [(ANY, moved), *weights, (VMEM, row_terms[0]), (VMEM, row_out)],
            [((width, 4 * width), BF16), *col_outs],
            [
                pltpu.VMEM((n, 2, share, width), BF16),
                weight_scratch[0],
                weight_scratch[2],
                pltpu.SemaphoreType.DMA((6,)),
            ],
            BIG_VMEM,
        )
        (back,) = call(
            back_kernel,
            "column_grad_hidden",
            [(VMEM, one) for one in col_grads],
            [((n, share, width), BF16)],
        )
        returned = lax.all_to_all(back, "seq", split_axis=0, concat_axis=0, tiled=True)
        (grad,) = call(
            input_kernel,
            "input_grad",
            [
                (VMEM, base), (VMEM, normed), (VMEM, inverse_rms), (VMEM, gain),
                (VMEM, returned.reshape(columns, width)),
            ],
            [((columns, width), BF16)],
        )
        terms = lax.all_to_all(
            terms.reshape(n, row_share, 4 * width), "seq", split_axis=0, concat_axis=0, tiled=True
        )
        total = jnp.sum(terms.astype(F32), 0)
        for step in range(m.bit_length() - 1):
            sent = total.astype(BF16)
            total = sent.astype(F32) + swap(sent, "dp", 1 << step).astype(F32)
        sum_qkv, sum_out = total[:, : 3 * width], total[:, 3 * width :]
        here_at = lax.axis_index("seq") * row_share
        own_gain = lax.dynamic_slice_in_dim(norm_gain, here_at, row_share, 0)
        own_weight = lax.dynamic_slice_in_dim(qkv_weight, here_at, row_share, 0)
        sum_gain = jnp.sum(sum_qkv * own_weight.astype(F32), -1) / own_gain
    return (grad.reshape(inputs.shape), sum_qkv, sum_out, sum_gain)


def solution(mesh):
    return jax.shard_map(
        body,
        mesh=mesh,
        in_specs=(P("dp", "seq", None, None), P(), P(), P(), P("dp", "seq", None, None)),
        out_specs=(P("dp", "seq", None, None), P("seq", None), P("seq", None), P("seq")),
        check_vma=False,
    )
```

```python
import math

import jax
import jax.numpy as jnp
from jax import lax
from jax.experimental import pallas as pl
from jax.experimental.pallas import tpu as pltpu
from jax.sharding import PartitionSpec as P

H = 8
HD = 64
HH = H // 2
HW = HH * HD
SCALE = HD ** (-0.5)
F32 = jnp.float32
BF16 = jnp.bfloat16
QUERY_BLOCK = 128
BIG_VMEM = 20 * 1024 * 1024
SMALL_VMEM = 8 * 1024 * 1024
ANY = pl.BlockSpec(memory_space=pl.ANY)
VMEM = pl.BlockSpec(memory_space=pltpu.VMEM)
HBM = pl.BlockSpec(memory_space=pltpu.HBM)
CHIP_STEPS = (3, 2, 1)
FIRST_PART = 384
PINNED = pl.BlockSpec(memory_space=pltpu.VMEM)
shaped = jax.ShapeDtypeStruct


def here():
    device = lax.axis_index("seq")
    return device >> 1, device & 1, lax.axis_index("dp")


def dot_nn(a, b):
    return lax.dot_general(a, b, (((1,), (0,)), ((), ())), preferred_element_type=F32)


def dot_nt(a, b):
    return lax.dot_general(a, b, (((1,), (1,)), ((), ())), preferred_element_type=F32)


def rms_parts(x):
    inverse_rms = lax.rsqrt(jnp.mean(x * x, -1, keepdims=True) + 1e-05)
    return inverse_rms, x * inverse_rms


def transposed(x):
    block = math.gcd(x.shape[1], 256)
    eye = (
        lax.broadcasted_iota(jnp.int32, (block, block), 0)
        == lax.broadcasted_iota(jnp.int32, (block, block), 1)
    ).astype(F32).astype(BF16)
    parts = [
        dot_nt(eye, x[:, at : at + block]).astype(BF16) for at in range(0, x.shape[1], block)
    ]
    return parts[0] if len(parts) == 1 else jnp.concatenate(parts, 0)


def head_pair(x):
    lane = lax.broadcasted_iota(jnp.int32, x.shape, 1)
    zero = jnp.zeros_like(x)
    return jnp.concatenate([jnp.where(lane < HD, x, zero), jnp.where(lane < HD, zero, x)], 0)


def both_heads(both, count):
    return jnp.concatenate([both[:HD, :count], both[HD:, count:]], 0)


def pair_steps(items, mask_rows, mask):
    count = items[0][2].shape[1]
    scores = [dot_nt(k, q2) for q2, _, _, k, _, _, _ in items]
    prob_grads = [dot_nt(v, g2) for _, g2, _, _, v, _, _ in items]
    probs = []
    for score in scores:
        first = score.shape[0] - mask_rows
        tail = jnp.where(mask, score[first:], -1e30)
        score = tail if first == 0 else jnp.concatenate([score[:first], tail], 0)
        exponent = jnp.exp(score - jnp.max(score, 0, keepdims=True))
        probs.append(exponent * (1.0 / jnp.sum(exponent, 0, keepdims=True)))
    weights = [prob.astype(BF16) for prob in probs]
    attended = [
        both_heads(dot_nn(item[6], weight), count).astype(BF16)
        for item, weight in zip(items, weights)
    ]
    score_grads = []
    for item, att, prob, prob_grad in zip(items, attended, probs, prob_grads):
        product = item[2].astype(F32) * att.astype(F32)
        delta = [jnp.sum(part, 0, keepdims=True) for part in (product[:HD], product[HD:])]
        score_grads.append((prob * (prob_grad - jnp.concatenate(delta, 1))).astype(BF16))
    grad_q = [
        (both_heads(dot_nn(item[5], score_grad), count) * SCALE).astype(BF16)
        for item, score_grad in zip(items, score_grads)
    ]
    grad_k = [dot_nn(score_grad, item[0]) for item, score_grad in zip(items, score_grads)]
    grad_v = [dot_nn(weight, item[1]) for item, weight in zip(items, weights)]
    return list(zip(attended, grad_q, grad_k, grad_v))


def split_cores(piece, send_ref, keep_ref, chips, lanes):
    rows = send_ref.shape[1]
    parts = piece.reshape(chips.stop - chips.start, 2, rows, piece.shape[1])
    even, odd = parts[:, 0], parts[:, 1]
    first = here()[1] == 0
    send_ref[chips, :, lanes] = jnp.where(first, odd, even)
    keep_ref[chips, :, lanes] = jnp.where(first, even, odd)


def qkv_copies(wqkv_ref, w_ref, sems, second):
    width = wqkv_ref.shape[0]
    return [
        pltpu.make_async_copy(
            wqkv_ref.at[:, pl.ds(i * width + second * HW, HW)],
            w_ref.at[:, pl.ds(i * HW, HW)],
            sems.at[i],
        )
        for i in range(3)
    ]


def weight_copies(wqkv_ref, wout_ref, w_ref, wo_ref, sems, second):
    out_rows = wout_ref.at[pl.ds(second * HW, HW), :]
    return [
        *qkv_copies(wqkv_ref, w_ref, sems, second),
        pltpu.make_async_copy(out_rows, wo_ref, sems.at[3]),
    ]


def started(*copies):
    for copy in copies:
        copy.start()
    return copies


def finished(*copies):
    for copy in copies:
        copy.wait()


def project(hidden, cot, w_ref, wo_ref):
    projected = dot_nn(hidden, w_ref[...]).astype(BF16)
    q, k, v = [projected[:, i * HW : (i + 1) * HW] for i in range(3)]
    g = dot_nt(cot, wo_ref[...]).astype(BF16)
    return q * jnp.asarray(SCALE, BF16), k, v, g


def row_part(
    x_any, cot_any, gain_any, wqkv_any, wout_any,
    out_ref, base_ref, normed_ref, inverse_ref, x_ref, cot_ref,
    gain_ref, w_ref, wo_ref, dk_ref, dv_ref, grads_ref, sems,
):
    first = started(
        pltpu.make_async_copy(x_any, x_ref, sems.at[4]),
        pltpu.make_async_copy(gain_any, gain_ref, sems.at[5]),
    )
    later = started(
        *weight_copies(wqkv_any, wout_any, w_ref, wo_ref, sems, 0),
        pltpu.make_async_copy(cot_any, cot_ref, sems.at[6]),
    )
    dk_ref[...] = jnp.zeros_like(dk_ref)
    dv_ref[...] = jnp.zeros_like(dv_ref)
    finished(*first)
    tokens = x_ref.shape[0]
    inverse_ref[...], normed_ref[...] = rms_parts(x_ref[...].astype(F32))
    hidden = (normed_ref[...] * gain_ref[...]).astype(BF16)
    hidden_t = transposed(hidden)
    finished(*later)
    cot = cot_ref[...]
    q, k, v, g = project(hidden, cot, w_ref, wo_ref)
    kt, vt, gt = transposed(k), transposed(v), transposed(g)
    step = math.gcd(tokens, QUERY_BLOCK)
    query = lax.broadcasted_iota(jnp.int32, (step, 2 * step), 1) % step
    mask = query >= lax.broadcasted_iota(jnp.int32, (step, 2 * step), 0)
    pairs = [slice(i * 2 * HD, (i + 1) * 2 * HD) for i in range(HH // 2)]
    att_blocks, dq_blocks = [], []
    for start in range(0, tokens, step):
        rows, keys = slice(start, start + step), slice(0, start + step)
        items = [
            (
                head_pair(q[rows, lanes]), head_pair(g[rows, lanes]), gt[lanes, rows],
                k[keys, lanes], v[keys, lanes], kt[lanes, keys], vt[lanes, keys],
            )
            for lanes in pairs
        ]
        results = pair_steps(items, step, mask)
        for lanes, (_, _, dk, dv) in zip(pairs, results):
            dk_ref[keys, lanes] += dk
            dv_ref[keys, lanes] += dv
        att_blocks.append(jnp.concatenate([result[0] for result in results], 0))
        dq_blocks.append(jnp.concatenate([result[1] for result in results], 0))
    grads_ref[:, :HW] = transposed(jnp.concatenate(dq_blocks, 1))
    grads_ref[:, HW : 2 * HW] = dk_ref[...].astype(BF16)
    grads_ref[:, 2 * HW :] = dv_ref[...].astype(BF16)
    term_qkv = dot_nn(hidden_t, grads_ref[...]).astype(BF16)
    out_ref[...] = dot_nn(jnp.concatenate(att_blocks, 1), cot).astype(BF16)
    grad_normed = dot_nt(grads_ref[...], w_ref[...]) * gain_ref[...]
    base_ref[...] = input_grad(
        cot_ref[...].astype(F32), normed_ref[...], inverse_ref[...], grad_normed
    )
    return term_qkv


def row_kernel(x_any, cot_any, gain_any, wqkv_any, wout_any, qkv_ref, *refs):
    qkv_ref[...] = row_part(x_any, cot_any, gain_any, wqkv_any, wout_any, *refs)


def row_chip_kernel(
    x_any, cot_any, gain_any, wqkv_any, wout_any,
    send_1, send_2, keep_1, keep_2, rows_ref, col_w_ref, col_wo_ref, *refs,
):
    chip, core, _ = here()
    sems, rows = refs[-1], rows_ref.shape[0]
    at = pl.multiple_of((chip * 2 + core) * rows, rows)
    handed = started(
        pltpu.make_async_copy(wqkv_any.at[pl.ds(at, rows), :], rows_ref, sems.at[7]),
        *weight_copies(wqkv_any, wout_any, col_w_ref, col_wo_ref, sems.at[pl.ds(8, 4)], 1),
    )
    term_qkv = row_part(x_any, cot_any, gain_any, wqkv_any, wout_any, *refs)
    chips, cut = send_1.shape[0], keep_1.shape[2]
    pieces = slice(0, chips), slice(0, cut)
    split_cores(term_qkv[:, :cut], send_1, keep_1, *pieces)
    split_cores(term_qkv[:, cut:], send_2, keep_2, *pieces)
    finished(*handed)


def column_part(x, cot, mask, gain, w_ref, wo_ref, weight_waits, grads_ref):
    tokens, block = x.shape[0], mask.shape[0]
    _, normed = rms_parts(x.astype(F32))
    hidden = (normed * gain).astype(BF16)
    hidden_t = transposed(hidden)
    finished(*weight_waits)
    q, k, v, g = project(hidden, cot, w_ref, wo_ref)
    kt, vt, gt = transposed(k), transposed(v), transposed(g)
    pairs = [slice(i * 2 * HD, (i + 1) * 2 * HD) for i in range(HH // 2)]
    blocks = [slice(at, at + block) for at in range(0, tokens, block)]
    items = [
        (
            head_pair(q[rows, lanes]), head_pair(g[rows, lanes]), gt[lanes, rows],
            k[rows, lanes], v[rows, lanes], kt[lanes, rows], vt[lanes, rows],
        )
        for lanes in pairs
        for rows in blocks
    ]
    results = pair_steps(items, block, mask)
    places = [(lanes, rows) for lanes in pairs for rows in blocks]
    for (lanes, rows), (_, _, dk, dv) in zip(places, results):
        grads_ref[rows, HW + lanes.start : HW + lanes.stop] = dk.astype(BF16)
        grads_ref[rows, 2 * HW + lanes.start : 2 * HW + lanes.stop] = dv.astype(BF16)
    by_pair = [results[i * len(blocks) : (i + 1) * len(blocks)] for i in range(len(pairs))]
    attended, grad_q = [
        jnp.concatenate([jnp.concatenate([r[i] for r in some], 1) for some in by_pair], 0)
        for i in range(2)
    ]
    grads_ref[:, :HW] = transposed(grad_q)
    term_qkv = dot_nn(hidden_t, grads_ref[...]).astype(BF16)
    term_out = dot_nn(attended, cot).astype(BF16)
    return term_qkv, term_out


def column_mask(all_rows, group, row_of):
    block = all_rows * group
    shape = (block, 2 * block)
    query = lax.broadcasted_iota(jnp.int32, shape, 1) % block
    key = lax.broadcasted_iota(jnp.int32, shape, 0)
    same_column = query % group == key % group
    return (row_of(query // group) >= row_of(key // group)) & same_column


def column_kernel(
    moved_any, gain_any, wqkv_any, wout_any, row_qkv_ref, row_out_ref,
    terms_ref, grads_ref, w_ref,
    moved_ref, gain_ref, wo_ref, sems,
):
    copies = started(
        pltpu.make_async_copy(moved_any, moved_ref, sems.at[4]),
        pltpu.make_async_copy(gain_any, gain_ref, sems.at[5]),
    )
    weights = started(*weight_copies(wqkv_any, wout_any, w_ref, wo_ref, sems, 1))
    finished(*copies)
    all_rows, _, share, width = moved_ref.shape
    group = math.gcd(share, 16)
    x, cot = [
        jnp.concatenate(
            [
                moved_ref[:, which, at : at + group, :].astype(F32).reshape(all_rows * group, width)
                for at in range(0, share, group)
            ],
            0,
        ).astype(BF16)
        for which in range(2)
    ]
    mask = column_mask(all_rows, group, lambda place: place)
    term_qkv, term_out = column_part(
        x, cot, mask, gain_ref[...], w_ref, wo_ref, weights, grads_ref
    )
    for i in range(3):
        at = i * width
        terms_ref[:, at : at + HW] = row_qkv_ref[:, i * HW : (i + 1) * HW]
        terms_ref[:, at + HW : at + 2 * HW] = term_qkv[:, i * HW : (i + 1) * HW]
    terms_ref[:HW, 3 * width :] = row_out_ref[...]
    terms_ref[HW:, 3 * width :] = term_out


def column_chip_kernel(
    x_ref, cot_ref, near_1, near_2, near_3, far_ref, gain_ref, w_ref, wo_ref, row_out_ref,
    send_ref, keep_ref, grads_ref,
):
    chip, core, _ = here()
    share = far_ref.shape[2]
    half = pl.ds(pl.multiple_of(core * share, share), share)
    at = pl.ds(pl.multiple_of((chip * 2 + core) * share, share), share)
    group = math.gcd(share, 16)

    def tokens(which, mine):
        pieces = [mine[at, :], far_ref[0, which]]
        for i, near in enumerate((near_1, near_2, near_3)):
            pieces += [near[which, half, :], far_ref[i + 1, which]]
        starts = range(0, share, group)
        return jnp.concatenate(
            [piece[start : start + group] for start in starts for piece in pieces], 0
        )

    def row_of(place):
        step = (4 - (place >> 1)) & 3
        return ((step ^ chip) << 1) + ((place & 1) ^ core)

    mask = column_mask(2 * (len(CHIP_STEPS) + 1), group, row_of)
    term_qkv, term_out = column_part(
        tokens(0, x_ref), tokens(1, cot_ref), mask, gain_ref[...], w_ref, wo_ref, (), grads_ref
    )
    chips = send_ref.shape[0]
    refs = send_ref, keep_ref
    out_lanes = slice(3 * HW, send_ref.shape[2])
    split_cores(term_qkv, *refs, slice(0, chips), slice(0, 3 * HW))
    split_cores(row_out_ref[...], *refs, slice(0, chips // 2), out_lanes)
    split_cores(term_out, *refs, slice(chips // 2, chips), out_lanes)


def far_kernel(x_ref, cot_ref, near_1, near_2, near_3, far_ref):
    chip, core, _ = here()
    share = far_ref.shape[2]
    at = pl.ds(pl.multiple_of((chip * 2 + 1 - core) * share, share), share)
    far_ref[0, 0], far_ref[0, 1] = x_ref[at, :], cot_ref[at, :]
    at = pl.ds(pl.multiple_of((1 - core) * share, share), share)
    for i, near in enumerate((near_1, near_2, near_3)):
        far_ref[i + 1] = near[:, at, :]


def back_kernel(grads_ref, w_ref, back_ref):
    grad_hidden = dot_nt(grads_ref[...], w_ref[...])
    all_rows, share, width = back_ref.shape
    group = math.gcd(share, 16)
    block = all_rows * group
    for i in range(share // group):
        piece = grad_hidden[i * block : (i + 1) * block].reshape(all_rows, group, width)
        back_ref[:, i * group : (i + 1) * group, :] = piece.astype(BF16)


def back_chip_kernel(grads_ref, w_ref, send_ref, keep_ref):
    grad_hidden = dot_nt(grads_ref[...], w_ref[...]).astype(BF16)
    chips, share, width = keep_ref.shape
    group = math.gcd(share, 16)
    block = 2 * chips * group
    for i in range(share // group):
        piece = grad_hidden[i * block : (i + 1) * block].reshape(chips, 2, group, width)
        at = slice(i * group, (i + 1) * group)
        keep_ref[:, at, :], send_ref[:, at, :] = piece[:, 0], piece[:, 1]


def back_pack_kernel(keep_ref, got_ref, *targets):
    share = keep_ref.shape[1]
    core = here()[1]
    kept_at = pl.ds(pl.multiple_of(core * share, share), share)
    got_at = pl.ds(pl.multiple_of((1 - core) * share, share), share)
    for i, target in enumerate(targets):
        target[kept_at, :] = keep_ref[i]
        target[got_at, :] = got_ref[i]


def input_kernel(base_ref, normed_ref, inverse_ref, gain_ref, back_ref, grad_ref):
    grad_ref[...] = input_grad(
        base_ref[...], normed_ref[...], inverse_ref[...], back_ref[...].astype(F32) * gain_ref[...]
    ).astype(BF16)


def input_grad(base, normed, inverse_rms, grad_normed):
    projected = jnp.mean(grad_normed * normed, -1, keepdims=True)
    return base + inverse_rms * (grad_normed - normed * projected)


def input_chip_kernel(
    base_ref, normed_ref, inverse_ref, gain_ref, own_ref, got_1, got_2, got_3,
    grad_any, grad_ref, sems,
):
    chip = here()[0]
    count = own_ref.shape[0]
    copies = []
    for i, (step, back_ref) in enumerate(zip((0, *CHIP_STEPS), (own_ref, got_1, got_2, got_3))):
        at = pl.ds(pl.multiple_of((chip ^ step) * count, count), count)
        grad_normed = back_ref[...].astype(F32) * gain_ref[...]
        grad = input_grad(base_ref[at, :], normed_ref[at, :], inverse_ref[at, :], grad_normed)
        grad_ref[i] = grad.astype(BF16)
        copies += started(pltpu.make_async_copy(grad_ref.at[i], grad_any.at[at, :], sems.at[i]))
    finished(*copies)


def pack_kernel(x_any, cot_any, off_1, off_2, off_3, sems):
    chip = here()[0]
    count = off_1.shape[1]
    copies = []
    for i, (step, target) in enumerate(zip(CHIP_STEPS, (off_1, off_2, off_3))):
        at = pl.ds(pl.multiple_of((chip ^ step) * count, count), count)
        for which, source in enumerate((x_any, cot_any)):
            copies.append(
                pltpu.make_async_copy(source.at[at, :], target.at[which], sems.at[2 * i + which])
            )
    finished(*started(*copies))


def split_rows(total, axis):
    upper = (here()[2] & 1) == 1
    low, high = jnp.split(total, 2, axis)
    return jnp.where(upper, low, high).astype(BF16), jnp.where(upper, high, low)


def row_cores_kernel(keep_1, keep_2, got_1, got_2, send_ref, kept_ref):
    total = [
        keep_ref[...].astype(F32) + got_ref[...].astype(F32)
        for keep_ref, got_ref in ((keep_1, got_1), (keep_2, got_2))
    ]
    send_ref[...], kept_ref[...] = split_rows(jnp.concatenate(total, 2), 1)


def cores_kernel(keep_ref, got_ref, send_ref, kept_ref, *targets):
    chip, cut = here()[0], kept_ref.shape[2]
    first = keep_ref[:, :, :cut].astype(F32) + got_ref[:, :, :cut].astype(F32)
    send_ref[...], kept_ref[...] = split_rows(first, 1)
    for step, target in zip((0, *CHIP_STEPS), targets):
        there = chip ^ step
        total = keep_ref[there, :, cut:].astype(F32) + got_ref[there, :, cut:].astype(F32)
        target[...] = total.astype(target.dtype)


def pair_kernel(kept_ref, got_ref, row_kept, row_got, *targets):
    chip, cut = here()[0], kept_ref.shape[2]
    for step, target in zip((0, *CHIP_STEPS), targets):
        there = chip ^ step
        total = kept_ref[there] + got_ref[there].astype(F32)
        target[:, :cut] = total.astype(target.dtype)
        total = row_kept[there] + row_got[there].astype(F32)
        target[:, cut:] = total.astype(target.dtype)


def layer_sum(own_ref, got_1, got_2, got_3):
    return own_ref[...] + (
        (got_1[...].astype(F32) + got_2[...].astype(F32)) + got_3[...].astype(F32)
    )


def layer_kernel(own_ref, got_1, got_2, got_3, send_ref, kept_ref):
    send_ref[...], kept_ref[...] = split_rows(layer_sum(own_ref, got_1, got_2, got_3), 0)


def join_kernel(own_ref, got_1, got_2, got_3, kept_ref, got_ref, out_ref):
    total = layer_sum(own_ref, got_1, got_2, got_3).astype(BF16)
    cut, width = FIRST_PART, kept_ref.shape[1]
    out_ref[:, :cut] = total[:, :cut]
    out_ref[:, cut : cut + width] = (kept_ref[...] + got_ref[...].astype(F32)).astype(BF16)
    out_ref[:, cut + width :] = total[:, cut:]


def add_kernel(kept_ref, got_ref, out_ref):
    out_ref[...] = (kept_ref[...].astype(F32) + got_ref[...].astype(F32)).astype(BF16)


def result_kernel(held_ref, got_ref, w_ref, gain_ref, qkv_ref, out_ref, grad_ref):
    rows = qkv_ref.shape[0]
    chip, core, layer = here()
    at = (chip * 2 + core) * rows
    upper = (layer & 1) == 1
    half = rows // 2
    width = out_ref.shape[1]

    def ordered(lanes):
        held, got = held_ref[:, lanes].astype(F32), got_ref[:, lanes].astype(F32)
        return (jnp.where(upper, got, held), jnp.where(upper, held, got))

    row_at = 3 * HW + width
    for i in range(3):
        for at_from, at_to in ((row_at + i * HW, i * width), (i * HW, i * width + HW)):
            to = slice(at_to, at_to + HW)
            qkv_ref[:half, to], qkv_ref[half:, to] = ordered(slice(at_from, at_from + HW))
    out_ref[:half], out_ref[half:] = ordered(slice(3 * HW, row_at))
    total = jnp.sum(qkv_ref[...] * w_ref[...].astype(F32), -1, keepdims=True)
    shape = (rows, gain_ref.shape[1])
    row = lax.broadcasted_iota(jnp.int32, shape, 0)
    feature = lax.broadcasted_iota(jnp.int32, shape, 1)
    gain = jnp.sum(jnp.where(feature == row + at, gain_ref[...], 0.0), -1, keepdims=True)
    shape = (rows, grad_ref.shape[1])
    same = lax.broadcasted_iota(jnp.int32, shape, 0) == lax.broadcasted_iota(jnp.int32, shape, 1)
    grad_ref[...] = jnp.sum(jnp.where(same, total / gain, 0.0), 0, keepdims=True)


def call(kernel, name, ins, outs, scratch=(), vmem=SMALL_VMEM, out_specs=None):
    out_specs = out_specs or [VMEM] * len(outs)
    places = [{id(HBM): pltpu.HBM, id(PINNED): pltpu.VMEM}.get(id(spec)) for spec in out_specs]
    outs = [place(*out) if place else shaped(*out) for place, out in zip(places, outs)]
    args = [
        pltpu.with_memory_space_constraint(array, pltpu.HBM) if spec is HBM else array
        for spec, array in ins
    ]
    return pl.pallas_call(
        kernel,
        out_shape=outs,
        in_specs=[spec for spec, _ in ins],
        out_specs=out_specs,
        scratch_shapes=scratch,
        name=name,
        cost_estimate=pl.CostEstimate(flops=0, bytes_accessed=0, transcendentals=0),
        compiler_params=pltpu.CompilerParams(vmem_limit_bytes=vmem),
    )(*args)


def swap(array, axis, bits):
    count = lax.axis_size(axis)
    return lax.ppermute(array, axis, [(i, i ^ bits) for i in range(count)])


def cross_chips(*offs):
    return [swap(off, "seq", 2 * step) for off, step in zip(offs, CHIP_STEPS)]


def add_two(kept, got, name):
    (total,) = call(add_kernel, name, [(VMEM, kept), (VMEM, got)], [(kept.shape, BF16)])
    return total


def body(inputs, norm_gain, qkv_weight, out_weight, out_cotan):
    columns, width = inputs.shape[2:]
    n = lax.axis_size("seq")
    m = lax.axis_size("dp")
    share = columns // n
    row_share = width // n
    row_width, col_width = 3 * HW, 3 * HW + width
    x = inputs.reshape(columns, width)
    cot = out_cotan.reshape(columns, width)
    gain = norm_gain.reshape(1, width)
    chips = 4
    layered = n == 2 * chips and m == 4 and row_share == share
    weight_scratch = [
        pltpu.VMEM((1, width), F32),
        pltpu.VMEM((width, 3 * HW), BF16),
        pltpu.VMEM((HW, width), BF16),
    ]
    weights = [(HBM, gain), (HBM, qkv_weight), (HBM, out_weight)]
    col_outs = [((columns, 3 * HW), BF16), ((width, 3 * HW), BF16)]

    if layered:
        packed = call(
            pack_kernel,
            "pack_columns",
            [(HBM, x), (HBM, cot)],
            [((2, 2 * share, width), BF16)] * 3,
            [pltpu.SemaphoreType.DMA((6,))],
            out_specs=[ANY] * 3,
        )
        near = cross_chips(*packed)
        x_first, _ = lax.optimization_barrier((x, packed[0]))
    else:
        outgoing = jnp.stack([x.reshape(n, share, width), cot.reshape(n, share, width)], 1)
        moved = lax.all_to_all(outgoing, "seq", split_axis=0, concat_axis=0, tiled=True)
        x_first = x

    row_outs = [
        ((HW, width), BF16),
        ((columns, width), F32), ((columns, width), F32), ((columns, 1), F32),
        ((columns, width), BF16), ((columns, width), BF16),
    ]
    if layered:
        cut = row_width // 2
        split_outs = [((chips, row_share, cut), BF16)] * 4
        handed_outs = [
            ((row_share, 3 * width), BF16), ((width, 3 * HW), BF16), ((HW, width), BF16),
        ]
        row_outs = [*split_outs, *handed_outs, *row_outs]
        specs = [VMEM] * 4 + [PINNED] * (len(row_outs) - 4)
    else:
        row_outs = [((width, row_width), BF16), *row_outs]
        specs = [VMEM] * len(row_outs)
    *row_terms, row_out, base, normed, inverse_rms, x_near, cot_near = call(
        row_chip_kernel if layered else row_kernel,
        "row_heads",
        [(HBM, x_first), (HBM, cot), *weights],
        row_outs,
        [
            *weight_scratch,
            pltpu.VMEM((columns, HW), F32),
            pltpu.VMEM((columns, HW), F32),
            pltpu.VMEM((columns, 3 * HW), BF16),
            pltpu.SemaphoreType.DMA((12,)),
        ],
        BIG_VMEM,
        specs,
    )
    if layered:
        *row_terms, weight_rows, col_weight, col_out_weight = row_terms
        row_sent = [swap(one, "seq", 1) for one in row_terms[:2]]
        half_block = (chips, row_share // 2, row_width)
        row_next, row_kept = call(
            row_cores_kernel,
            "row_add_cores",
            [(VMEM, one) for one in (*row_terms[2:], *row_sent)],
            [(half_block, BF16), (half_block, F32)],
            out_specs=[VMEM, PINNED],
        )
        *near, row_kept = lax.optimization_barrier((*near, row_kept))
        (far,) = call(
            far_kernel,
            "pack_other_core",
            [(VMEM, one) for one in (x_near, cot_near, *near)],
            [((chips, 2, share, width), BF16)],
        )
        send, keep, col_grads = call(
            column_chip_kernel,
            "column_heads",
            [
                (VMEM, one)
                for one in (
                    x_near, cot_near, *near, swap(far, "seq", 1),
                    gain, col_weight, col_out_weight, row_out,
                )
            ],
            [((chips, row_share, col_width), BF16)] * 2 + [col_outs[0]],
            vmem=BIG_VMEM,
            out_specs=[VMEM, VMEM, PINNED],
        )
        back_send, back_keep = call(
            back_chip_kernel,
            "column_grad_hidden",
            [(VMEM, col_grads), (VMEM, col_weight)],
            [((chips, share, width), BF16)] * 2,
        )
        row_next, _ = lax.optimization_barrier((row_next, send))
        keep, back_keep = lax.optimization_barrier((keep, back_keep))
        first_half = (chips, row_share // 2, FIRST_PART)
        second = (row_share, col_width - FIRST_PART)
        to_next, kept, owned, *off = call(
            cores_kernel,
            "column_add_cores",
            [(VMEM, keep), (VMEM, swap(send, "seq", 1))],
            [(first_half, BF16), (first_half, F32), (second, F32)] + [(second, BF16)] * 3,
            out_specs=[VMEM, PINNED, PINNED, VMEM, VMEM, VMEM],
        )
        got = cross_chips(*off)
        back = call(
            back_pack_kernel,
            "pack_grad_hidden",
            [(VMEM, back_keep), (VMEM, swap(back_send, "seq", 1))],
            [((2 * share, width), BF16)] * 4,
        )
        row_kept, *back = lax.optimization_barrier((row_kept, *back))
        joint = (row_share // 2, FIRST_PART + row_width)
        first_owned, *off = call(
            pair_kernel,
            "first_add_pair",
            [
                (VMEM, one)
                for one in (kept, swap(to_next, "dp", 1), row_kept, swap(row_next, "dp", 1))
            ],
            [(joint, F32)] + [(joint, BF16)] * 3,
            out_specs=[PINNED, VMEM, VMEM, VMEM],
        )
        first_got = cross_chips(*off)
        second_half = (row_share // 2, second[1])
        to_next, kept = call(
            layer_kernel,
            "second_add_chips",
            [(VMEM, one) for one in (owned, *got)],
            [(second_half, BF16), (second_half, F32)],
            out_specs=[VMEM, PINNED],
        )
        (pair_sum,) = call(
            join_kernel,
            "join_terms",
            [(VMEM, one) for one in (first_owned, *first_got, kept, swap(to_next, "dp", 1))],
            [((row_share // 2, col_width + row_width), BF16)],
        )
        *back, pair_sum = lax.optimization_barrier((*back, pair_sum))
        held = add_two(pair_sum, swap(pair_sum, "dp", 2), "add_pairs")
        other = swap(held, "dp", 1)
        (grad,) = call(
            input_chip_kernel,
            "input_grad",
            [
                (VMEM, one)
                for one in (base, normed, inverse_rms, gain, back[0], *cross_chips(*back[1:]))
            ],
            [((columns, width), BF16)],
            [pltpu.VMEM((chips, 2 * share, width), BF16), pltpu.SemaphoreType.DMA((chips,))],
            out_specs=[HBM],
        )
        sum_qkv, sum_out, sum_gain = call(
            result_kernel,
            "result",
            [(VMEM, held), (VMEM, other), (VMEM, weight_rows), (VMEM, gain)],
            [((row_share, 3 * width), F32), ((row_share, width), F32), ((1, row_share), F32)],
        )
        sum_gain = sum_gain.reshape(row_share)
    else:
        terms, *col_grads = call(
            column_kernel,
            "column_heads",
            [(ANY, moved), *weights, (VMEM, row_terms[0]), (VMEM, row_out)],
            [((width, 4 * width), BF16), *col_outs],
            [
                pltpu.VMEM((n, 2, share, width), BF16),
                weight_scratch[0],
                weight_scratch[2],
                pltpu.SemaphoreType.DMA((6,)),
            ],
            BIG_VMEM,
        )
        (back,) = call(
            back_kernel,
            "column_grad_hidden",
            [(VMEM, one) for one in col_grads],
            [((n, share, width), BF16)],
        )
        returned = lax.all_to_all(back, "seq", split_axis=0, concat_axis=0, tiled=True)
        (grad,) = call(
            input_kernel,
            "input_grad",
            [
                (VMEM, base), (VMEM, normed), (VMEM, inverse_rms), (VMEM, gain),
                (VMEM, returned.reshape(columns, width)),
            ],
            [((columns, width), BF16)],
        )
        terms = lax.all_to_all(
            terms.reshape(n, row_share, 4 * width), "seq", split_axis=0, concat_axis=0, tiled=True
        )
        total = jnp.sum(terms.astype(F32), 0)
        for step in range(m.bit_length() - 1):
            sent = total.astype(BF16)
            total = sent.astype(F32) + swap(sent, "dp", 1 << step).astype(F32)
        sum_qkv, sum_out = total[:, : 3 * width], total[:, 3 * width :]
        here_at = lax.axis_index("seq") * row_share
        own_gain = lax.dynamic_slice_in_dim(norm_gain, here_at, row_share, 0)
        own_weight = lax.dynamic_slice_in_dim(qkv_weight, here_at, row_share, 0)
        sum_gain = jnp.sum(sum_qkv * own_weight.astype(F32), -1) / own_gain
    return (grad.reshape(inputs.shape), sum_qkv, sum_out, sum_gain)


def solution(mesh):
    return jax.shard_map(
        body,
        mesh=mesh,
        in_specs=(P("dp", "seq", None, None), P(), P(), P(), P("dp", "seq", None, None)),
        out_specs=(P("dp", "seq", None, None), P("seq", None), P("seq", None), P("seq")),
        check_vma=False,
    )
```

```python
import math

import jax
import jax.numpy as jnp
from jax import lax
from jax.experimental import pallas as pl
from jax.experimental.pallas import tpu as pltpu
from jax.sharding import PartitionSpec as P

H = 8
HD = 64
HH = H // 2
HW = HH * HD
SCALE = HD ** (-0.5)
F32 = jnp.float32
BF16 = jnp.bfloat16
QUERY_BLOCK = 128
BIG_VMEM = 20 * 1024 * 1024
SMALL_VMEM = 8 * 1024 * 1024
ANY = pl.BlockSpec(memory_space=pl.ANY)
VMEM = pl.BlockSpec(memory_space=pltpu.VMEM)
HBM = pl.BlockSpec(memory_space=pltpu.HBM)
CHIP_STEPS = (3, 2, 1)
FIRST_PART = 384
SWAP_PIECES = (384, 384, 256, 256)
PINNED = pl.BlockSpec(memory_space=pltpu.VMEM)
shaped = jax.ShapeDtypeStruct


def here():
    device = lax.axis_index("seq")
    return device >> 1, device & 1, lax.axis_index("dp")


def dot_nn(a, b):
    return lax.dot_general(a, b, (((1,), (0,)), ((), ())), preferred_element_type=F32)


def dot_nt(a, b):
    return lax.dot_general(a, b, (((1,), (1,)), ((), ())), preferred_element_type=F32)


def rms_parts(x):
    inverse_rms = lax.rsqrt(jnp.mean(x * x, -1, keepdims=True) + 1e-05)
    return inverse_rms, x * inverse_rms


def transposed(x):
    block = math.gcd(x.shape[1], 256)
    eye = (
        lax.broadcasted_iota(jnp.int32, (block, block), 0)
        == lax.broadcasted_iota(jnp.int32, (block, block), 1)
    ).astype(F32).astype(BF16)
    parts = [
        dot_nt(eye, x[:, at : at + block]).astype(BF16) for at in range(0, x.shape[1], block)
    ]
    return parts[0] if len(parts) == 1 else jnp.concatenate(parts, 0)


def head_pair(x):
    lane = lax.broadcasted_iota(jnp.int32, x.shape, 1)
    zero = jnp.zeros_like(x)
    return jnp.concatenate([jnp.where(lane < HD, x, zero), jnp.where(lane < HD, zero, x)], 0)


def both_heads(both, count):
    return jnp.concatenate([both[:HD, :count], both[HD:, count:]], 0)


def pair_steps(items, mask_rows, mask):
    count = items[0][2].shape[1]
    scores = [dot_nt(k, q2) for q2, _, _, k, _, _, _ in items]
    prob_grads = [dot_nt(v, g2) for _, g2, _, _, v, _, _ in items]
    probs = []
    for score in scores:
        first = score.shape[0] - mask_rows
        tail = jnp.where(mask, score[first:], -1e30)
        score = tail if first == 0 else jnp.concatenate([score[:first], tail], 0)
        exponent = jnp.exp(score - jnp.max(score, 0, keepdims=True))
        probs.append(exponent * (1.0 / jnp.sum(exponent, 0, keepdims=True)))
    weights = [prob.astype(BF16) for prob in probs]
    attended = [
        both_heads(dot_nn(item[6], weight), count).astype(BF16)
        for item, weight in zip(items, weights)
    ]
    score_grads = []
    for item, att, prob, prob_grad in zip(items, attended, probs, prob_grads):
        product = item[2].astype(F32) * att.astype(F32)
        delta = [jnp.sum(part, 0, keepdims=True) for part in (product[:HD], product[HD:])]
        score_grads.append((prob * (prob_grad - jnp.concatenate(delta, 1))).astype(BF16))
    grad_q = [
        (both_heads(dot_nn(item[5], score_grad), count) * SCALE).astype(BF16)
        for item, score_grad in zip(items, score_grads)
    ]
    grad_k = [dot_nn(score_grad, item[0]) for item, score_grad in zip(items, score_grads)]
    grad_v = [dot_nn(weight, item[1]) for item, weight in zip(items, weights)]
    return list(zip(attended, grad_q, grad_k, grad_v))


def split_cores(piece, send_ref, keep_ref, chips, lanes):
    rows = send_ref.shape[1]
    parts = piece.reshape(chips.stop - chips.start, 2, rows, piece.shape[1])
    even, odd = parts[:, 0], parts[:, 1]
    first = here()[1] == 0
    send_ref[chips, :, lanes] = jnp.where(first, odd, even)
    keep_ref[chips, :, lanes] = jnp.where(first, even, odd)


def qkv_copies(wqkv_ref, w_ref, sems, second):
    width = wqkv_ref.shape[0]
    return [
        pltpu.make_async_copy(
            wqkv_ref.at[:, pl.ds(i * width + second * HW, HW)],
            w_ref.at[:, pl.ds(i * HW, HW)],
            sems.at[i],
        )
        for i in range(3)
    ]


def weight_copies(wqkv_ref, wout_ref, w_ref, wo_ref, sems, second):
    out_rows = wout_ref.at[pl.ds(second * HW, HW), :]
    return [
        *qkv_copies(wqkv_ref, w_ref, sems, second),
        pltpu.make_async_copy(out_rows, wo_ref, sems.at[3]),
    ]


def started(*copies):
    for copy in copies:
        copy.start()
    return copies


def finished(*copies):
    for copy in copies:
        copy.wait()


def project(hidden, cot, w_ref, wo_ref):
    projected = dot_nn(hidden, w_ref[...]).astype(BF16)
    q, k, v = [projected[:, i * HW : (i + 1) * HW] for i in range(3)]
    g = dot_nt(cot, wo_ref[...]).astype(BF16)
    return q * jnp.asarray(SCALE, BF16), k, v, g


def row_part(
    x_any, cot_any, gain_any, wqkv_any, wout_any,
    out_ref, base_ref, normed_ref, inverse_ref, x_ref, cot_ref,
    gain_ref, w_ref, wo_ref, dk_ref, dv_ref, grads_ref, sems,
):
    first = started(
        pltpu.make_async_copy(x_any, x_ref, sems.at[4]),
        pltpu.make_async_copy(gain_any, gain_ref, sems.at[5]),
    )
    later = started(
        *weight_copies(wqkv_any, wout_any, w_ref, wo_ref, sems, 0),
        pltpu.make_async_copy(cot_any, cot_ref, sems.at[6]),
    )
    dk_ref[...] = jnp.zeros_like(dk_ref)
    dv_ref[...] = jnp.zeros_like(dv_ref)
    finished(*first)
    tokens = x_ref.shape[0]
    inverse_ref[...], normed_ref[...] = rms_parts(x_ref[...].astype(F32))
    hidden = (normed_ref[...] * gain_ref[...]).astype(BF16)
    hidden_t = transposed(hidden)
    finished(*later)
    cot = cot_ref[...]
    q, k, v, g = project(hidden, cot, w_ref, wo_ref)
    kt, vt, gt = transposed(k), transposed(v), transposed(g)
    step = math.gcd(tokens, QUERY_BLOCK)
    query = lax.broadcasted_iota(jnp.int32, (step, 2 * step), 1) % step
    mask = query >= lax.broadcasted_iota(jnp.int32, (step, 2 * step), 0)
    pairs = [slice(i * 2 * HD, (i + 1) * 2 * HD) for i in range(HH // 2)]
    att_blocks, dq_blocks = [], []
    for start in range(0, tokens, step):
        rows, keys = slice(start, start + step), slice(0, start + step)
        items = [
            (
                head_pair(q[rows, lanes]), head_pair(g[rows, lanes]), gt[lanes, rows],
                k[keys, lanes], v[keys, lanes], kt[lanes, keys], vt[lanes, keys],
            )
            for lanes in pairs
        ]
        results = pair_steps(items, step, mask)
        for lanes, (_, _, dk, dv) in zip(pairs, results):
            dk_ref[keys, lanes] += dk
            dv_ref[keys, lanes] += dv
        att_blocks.append(jnp.concatenate([result[0] for result in results], 0))
        dq_blocks.append(jnp.concatenate([result[1] for result in results], 0))
    grads_ref[:, :HW] = transposed(jnp.concatenate(dq_blocks, 1))
    grads_ref[:, HW : 2 * HW] = dk_ref[...].astype(BF16)
    grads_ref[:, 2 * HW :] = dv_ref[...].astype(BF16)
    term_qkv = dot_nn(hidden_t, grads_ref[...]).astype(BF16)
    out_ref[...] = dot_nn(jnp.concatenate(att_blocks, 1), cot).astype(BF16)
    grad_normed = dot_nt(grads_ref[...], w_ref[...]) * gain_ref[...]
    base_ref[...] = input_grad(
        cot_ref[...].astype(F32), normed_ref[...], inverse_ref[...], grad_normed
    )
    return term_qkv


def row_kernel(x_any, cot_any, gain_any, wqkv_any, wout_any, qkv_ref, *refs):
    qkv_ref[...] = row_part(x_any, cot_any, gain_any, wqkv_any, wout_any, *refs)


def row_chip_kernel(
    x_any, cot_any, gain_any, wqkv_any, wout_any,
    send_1, send_2, keep_1, keep_2, rows_ref, col_w_ref, col_wo_ref, *refs,
):
    chip, core, _ = here()
    sems, rows = refs[-1], rows_ref.shape[0]
    at = pl.multiple_of((chip * 2 + core) * rows, rows)
    handed = started(
        pltpu.make_async_copy(wqkv_any.at[pl.ds(at, rows), :], rows_ref, sems.at[7]),
        *weight_copies(wqkv_any, wout_any, col_w_ref, col_wo_ref, sems.at[pl.ds(8, 4)], 1),
    )
    term_qkv = row_part(x_any, cot_any, gain_any, wqkv_any, wout_any, *refs)
    chips, cut = send_1.shape[0], keep_1.shape[2]
    pieces = slice(0, chips), slice(0, cut)
    split_cores(term_qkv[:, :cut], send_1, keep_1, *pieces)
    split_cores(term_qkv[:, cut:], send_2, keep_2, *pieces)
    finished(*handed)


def column_part(x, cot, mask, gain, w_ref, wo_ref, weight_waits, grads_ref):
    tokens, block = x.shape[0], mask.shape[0]
    _, normed = rms_parts(x.astype(F32))
    hidden = (normed * gain).astype(BF16)
    hidden_t = transposed(hidden)
    finished(*weight_waits)
    q, k, v, g = project(hidden, cot, w_ref, wo_ref)
    kt, vt, gt = transposed(k), transposed(v), transposed(g)
    pairs = [slice(i * 2 * HD, (i + 1) * 2 * HD) for i in range(HH // 2)]
    blocks = [slice(at, at + block) for at in range(0, tokens, block)]
    items = [
        (
            head_pair(q[rows, lanes]), head_pair(g[rows, lanes]), gt[lanes, rows],
            k[rows, lanes], v[rows, lanes], kt[lanes, rows], vt[lanes, rows],
        )
        for lanes in pairs
        for rows in blocks
    ]
    results = pair_steps(items, block, mask)
    places = [(lanes, rows) for lanes in pairs for rows in blocks]
    for (lanes, rows), (_, _, dk, dv) in zip(places, results):
        grads_ref[rows, HW + lanes.start : HW + lanes.stop] = dk.astype(BF16)
        grads_ref[rows, 2 * HW + lanes.start : 2 * HW + lanes.stop] = dv.astype(BF16)
    by_pair = [results[i * len(blocks) : (i + 1) * len(blocks)] for i in range(len(pairs))]
    attended, grad_q = [
        jnp.concatenate([jnp.concatenate([r[i] for r in some], 1) for some in by_pair], 0)
        for i in range(2)
    ]
    grads_ref[:, :HW] = transposed(grad_q)
    term_qkv = dot_nn(hidden_t, grads_ref[...]).astype(BF16)
    term_out = dot_nn(attended, cot).astype(BF16)
    return term_qkv, term_out


def column_mask(all_rows, group, row_of):
    block = all_rows * group
    shape = (block, 2 * block)
    query = lax.broadcasted_iota(jnp.int32, shape, 1) % block
    key = lax.broadcasted_iota(jnp.int32, shape, 0)
    same_column = query % group == key % group
    return (row_of(query // group) >= row_of(key // group)) & same_column


def column_kernel(
    moved_any, gain_any, wqkv_any, wout_any, row_qkv_ref, row_out_ref,
    terms_ref, grads_ref, w_ref,
    moved_ref, gain_ref, wo_ref, sems,
):
    copies = started(
        pltpu.make_async_copy(moved_any, moved_ref, sems.at[4]),
        pltpu.make_async_copy(gain_any, gain_ref, sems.at[5]),
    )
    weights = started(*weight_copies(wqkv_any, wout_any, w_ref, wo_ref, sems, 1))
    finished(*copies)
    all_rows, _, share, width = moved_ref.shape
    group = math.gcd(share, 16)
    x, cot = [
        jnp.concatenate(
            [
                moved_ref[:, which, at : at + group, :].astype(F32).reshape(all_rows * group, width)
                for at in range(0, share, group)
            ],
            0,
        ).astype(BF16)
        for which in range(2)
    ]
    mask = column_mask(all_rows, group, lambda place: place)
    term_qkv, term_out = column_part(
        x, cot, mask, gain_ref[...], w_ref, wo_ref, weights, grads_ref
    )
    for i in range(3):
        at = i * width
        terms_ref[:, at : at + HW] = row_qkv_ref[:, i * HW : (i + 1) * HW]
        terms_ref[:, at + HW : at + 2 * HW] = term_qkv[:, i * HW : (i + 1) * HW]
    terms_ref[:HW, 3 * width :] = row_out_ref[...]
    terms_ref[HW:, 3 * width :] = term_out


def column_chip_kernel(
    x_ref, cot_ref, near_1, near_2, near_3, far_ref, gain_ref, w_ref, wo_ref, row_out_ref,
    keep_ref, grads_ref, *refs,
):
    chip, core, _ = here()
    share = far_ref.shape[2]
    half = pl.ds(pl.multiple_of(core * share, share), share)
    at = pl.ds(pl.multiple_of((chip * 2 + core) * share, share), share)
    group = math.gcd(share, 16)

    def tokens(which, mine):
        pieces = [mine[at, :], far_ref[0, which]]
        for i, near in enumerate((near_1, near_2, near_3)):
            pieces += [near[which, half, :], far_ref[i + 1, which]]
        starts = range(0, share, group)
        return jnp.concatenate(
            [piece[start : start + group] for start in starts for piece in pieces], 0
        )

    def row_of(place):
        step = (4 - (place >> 1)) & 3
        return ((step ^ chip) << 1) + ((place & 1) ^ core)

    mask = column_mask(2 * (len(CHIP_STEPS) + 1), group, row_of)
    term_qkv, term_out = column_part(
        tokens(0, x_ref), tokens(1, cot_ref), mask, gain_ref[...], w_ref, wo_ref, (), grads_ref
    )
    *pieces, send_ref = refs
    chips = send_ref.shape[0]
    both = send_ref, keep_ref
    out_lanes = slice(3 * HW, send_ref.shape[2])
    split_cores(term_qkv, *both, slice(0, chips), slice(0, 3 * HW))
    split_cores(row_out_ref[...], *both, slice(0, chips // 2), out_lanes)
    split_cores(term_out, *both, slice(chips // 2, chips), out_lanes)
    at = 0
    for piece in pieces:
        piece[...] = send_ref[:, :, at : at + piece.shape[2]]
        at += piece.shape[2]


def far_kernel(x_ref, cot_ref, near_1, near_2, near_3, far_ref):
    chip, core, _ = here()
    share = far_ref.shape[2]
    at = pl.ds(pl.multiple_of((chip * 2 + 1 - core) * share, share), share)
    far_ref[0, 0], far_ref[0, 1] = x_ref[at, :], cot_ref[at, :]
    at = pl.ds(pl.multiple_of((1 - core) * share, share), share)
    for i, near in enumerate((near_1, near_2, near_3)):
        far_ref[i + 1] = near[:, at, :]


def back_kernel(grads_ref, w_ref, back_ref):
    grad_hidden = dot_nt(grads_ref[...], w_ref[...])
    all_rows, share, width = back_ref.shape
    group = math.gcd(share, 16)
    block = all_rows * group
    for i in range(share // group):
        piece = grad_hidden[i * block : (i + 1) * block].reshape(all_rows, group, width)
        back_ref[:, i * group : (i + 1) * group, :] = piece.astype(BF16)


def back_chip_kernel(grads_ref, w_ref, send_ref, keep_ref):
    grad_hidden = dot_nt(grads_ref[...], w_ref[...]).astype(BF16)
    chips, share, width = keep_ref.shape
    group = math.gcd(share, 16)
    block = 2 * chips * group
    for i in range(share // group):
        piece = grad_hidden[i * block : (i + 1) * block].reshape(chips, 2, group, width)
        at = slice(i * group, (i + 1) * group)
        keep_ref[:, at, :], send_ref[:, at, :] = piece[:, 0], piece[:, 1]


def back_pack_kernel(keep_ref, got_ref, *targets):
    share = keep_ref.shape[1]
    core = here()[1]
    kept_at = pl.ds(pl.multiple_of(core * share, share), share)
    got_at = pl.ds(pl.multiple_of((1 - core) * share, share), share)
    for i, target in enumerate(targets):
        target[kept_at, :] = keep_ref[i]
        target[got_at, :] = got_ref[i]


def input_kernel(base_ref, normed_ref, inverse_ref, gain_ref, back_ref, grad_ref):
    grad_ref[...] = input_grad(
        base_ref[...], normed_ref[...], inverse_ref[...], back_ref[...].astype(F32) * gain_ref[...]
    ).astype(BF16)


def input_grad(base, normed, inverse_rms, grad_normed):
    projected = jnp.mean(grad_normed * normed, -1, keepdims=True)
    return base + inverse_rms * (grad_normed - normed * projected)


def input_chip_kernel(
    base_ref, normed_ref, inverse_ref, gain_ref, own_ref, got_1, got_2, got_3,
    grad_any, grad_ref, sems,
):
    chip = here()[0]
    count = own_ref.shape[0]
    copies = []
    for i, (step, back_ref) in enumerate(zip((0, *CHIP_STEPS), (own_ref, got_1, got_2, got_3))):
        at = pl.ds(pl.multiple_of((chip ^ step) * count, count), count)
        grad_normed = back_ref[...].astype(F32) * gain_ref[...]
        grad = input_grad(base_ref[at, :], normed_ref[at, :], inverse_ref[at, :], grad_normed)
        grad_ref[i] = grad.astype(BF16)
        copies += started(pltpu.make_async_copy(grad_ref.at[i], grad_any.at[at, :], sems.at[i]))
    finished(*copies)


def pack_kernel(x_any, cot_any, off_1, off_2, off_3, sems):
    chip = here()[0]
    count = off_1.shape[1]
    copies = []
    for i, (step, target) in enumerate(zip(CHIP_STEPS, (off_1, off_2, off_3))):
        at = pl.ds(pl.multiple_of((chip ^ step) * count, count), count)
        for which, source in enumerate((x_any, cot_any)):
            copies.append(
                pltpu.make_async_copy(source.at[at, :], target.at[which], sems.at[2 * i + which])
            )
    finished(*started(*copies))


def split_rows(total, axis):
    upper = (here()[2] & 1) == 1
    low, high = jnp.split(total, 2, axis)
    return jnp.where(upper, low, high).astype(BF16), jnp.where(upper, high, low)


def row_cores_kernel(keep_1, keep_2, got_1, got_2, send_ref, kept_ref):
    total = [
        keep_ref[...].astype(F32) + got_ref[...].astype(F32)
        for keep_ref, got_ref in ((keep_1, got_1), (keep_2, got_2))
    ]
    send_ref[...], kept_ref[...] = split_rows(jnp.concatenate(total, 2), 1)


def cores_kernel(keep_ref, got_1, got_2, got_3, got_4, send_ref, kept_ref, *targets):
    chip, cut = here()[0], kept_ref.shape[2]
    first = keep_ref[:, :, :cut].astype(F32) + got_1[...].astype(F32)
    send_ref[...], kept_ref[...] = split_rows(first, 1)
    for step, target in zip((0, *CHIP_STEPS), targets):
        there = chip ^ step
        got = jnp.concatenate([ref[there] for ref in (got_2, got_3, got_4)], 1)
        total = keep_ref[there, :, cut:].astype(F32) + got.astype(F32)
        target[...] = total.astype(target.dtype)


def pair_kernel(kept_ref, got_ref, row_kept, row_got, *targets):
    chip, cut = here()[0], kept_ref.shape[2]
    for step, target in zip((0, *CHIP_STEPS), targets):
        there = chip ^ step
        total = kept_ref[there] + got_ref[there].astype(F32)
        target[:, :cut] = total.astype(target.dtype)
        total = row_kept[there] + row_got[there].astype(F32)
        target[:, cut:] = total.astype(target.dtype)


def layer_sum(own_ref, got_1, got_2, got_3):
    return own_ref[...] + (
        (got_1[...].astype(F32) + got_2[...].astype(F32)) + got_3[...].astype(F32)
    )


def layer_kernel(own_ref, got_1, got_2, got_3, send_ref, kept_ref):
    send_ref[...], kept_ref[...] = split_rows(layer_sum(own_ref, got_1, got_2, got_3), 0)


def join_kernel(own_ref, got_1, got_2, got_3, kept_ref, got_ref, out_ref):
    total = layer_sum(own_ref, got_1, got_2, got_3).astype(BF16)
    cut, width = FIRST_PART, kept_ref.shape[1]
    out_ref[:, :cut] = total[:, :cut]
    out_ref[:, cut : cut + width] = (kept_ref[...] + got_ref[...].astype(F32)).astype(BF16)
    out_ref[:, cut + width :] = total[:, cut:]


def add_kernel(kept_ref, got_ref, out_ref):
    out_ref[...] = (kept_ref[...].astype(F32) + got_ref[...].astype(F32)).astype(BF16)


def result_kernel(held_ref, got_ref, w_ref, gain_ref, qkv_ref, out_ref, grad_ref):
    rows = qkv_ref.shape[0]
    chip, core, layer = here()
    at = (chip * 2 + core) * rows
    upper = (layer & 1) == 1
    half = rows // 2
    width = out_ref.shape[1]

    def ordered(lanes):
        held, got = held_ref[:, lanes].astype(F32), got_ref[:, lanes].astype(F32)
        return (jnp.where(upper, got, held), jnp.where(upper, held, got))

    row_at = 3 * HW + width
    for i in range(3):
        for at_from, at_to in ((row_at + i * HW, i * width), (i * HW, i * width + HW)):
            to = slice(at_to, at_to + HW)
            qkv_ref[:half, to], qkv_ref[half:, to] = ordered(slice(at_from, at_from + HW))
    out_ref[:half], out_ref[half:] = ordered(slice(3 * HW, row_at))
    total = jnp.sum(qkv_ref[...] * w_ref[...].astype(F32), -1, keepdims=True)
    shape = (rows, gain_ref.shape[1])
    row = lax.broadcasted_iota(jnp.int32, shape, 0)
    feature = lax.broadcasted_iota(jnp.int32, shape, 1)
    gain = jnp.sum(jnp.where(feature == row + at, gain_ref[...], 0.0), -1, keepdims=True)
    shape = (rows, grad_ref.shape[1])
    same = lax.broadcasted_iota(jnp.int32, shape, 0) == lax.broadcasted_iota(jnp.int32, shape, 1)
    grad_ref[...] = jnp.sum(jnp.where(same, total / gain, 0.0), 0, keepdims=True)


def call(kernel, name, ins, outs, scratch=(), vmem=SMALL_VMEM, out_specs=None):
    out_specs = out_specs or [VMEM] * len(outs)
    places = [{id(HBM): pltpu.HBM, id(PINNED): pltpu.VMEM}.get(id(spec)) for spec in out_specs]
    outs = [place(*out) if place else shaped(*out) for place, out in zip(places, outs)]
    args = [
        pltpu.with_memory_space_constraint(array, pltpu.HBM) if spec is HBM else array
        for spec, array in ins
    ]
    return pl.pallas_call(
        kernel,
        out_shape=outs,
        in_specs=[spec for spec, _ in ins],
        out_specs=out_specs,
        scratch_shapes=scratch,
        name=name,
        cost_estimate=pl.CostEstimate(flops=0, bytes_accessed=0, transcendentals=0),
        compiler_params=pltpu.CompilerParams(vmem_limit_bytes=vmem),
    )(*args)


def swap(array, axis, bits):
    count = lax.axis_size(axis)
    return lax.ppermute(array, axis, [(i, i ^ bits) for i in range(count)])


def cross_chips(*offs):
    return [swap(off, "seq", 2 * step) for off, step in zip(offs, CHIP_STEPS)]


def add_two(kept, got, name):
    (total,) = call(add_kernel, name, [(VMEM, kept), (VMEM, got)], [(kept.shape, BF16)])
    return total


def body(inputs, norm_gain, qkv_weight, out_weight, out_cotan):
    columns, width = inputs.shape[2:]
    n = lax.axis_size("seq")
    m = lax.axis_size("dp")
    share = columns // n
    row_share = width // n
    row_width, col_width = 3 * HW, 3 * HW + width
    x = inputs.reshape(columns, width)
    cot = out_cotan.reshape(columns, width)
    gain = norm_gain.reshape(1, width)
    chips = 4
    layered = n == 2 * chips and m == 4 and row_share == share
    weight_scratch = [
        pltpu.VMEM((1, width), F32),
        pltpu.VMEM((width, 3 * HW), BF16),
        pltpu.VMEM((HW, width), BF16),
    ]
    weights = [(HBM, gain), (HBM, qkv_weight), (HBM, out_weight)]
    col_outs = [((columns, 3 * HW), BF16), ((width, 3 * HW), BF16)]

    if layered:
        packed = call(
            pack_kernel,
            "pack_columns",
            [(HBM, x), (HBM, cot)],
            [((2, 2 * share, width), BF16)] * 3,
            [pltpu.SemaphoreType.DMA((6,))],
            out_specs=[ANY] * 3,
        )
        near = cross_chips(*packed)
        x_first, _ = lax.optimization_barrier((x, packed[0]))
    else:
        outgoing = jnp.stack([x.reshape(n, share, width), cot.reshape(n, share, width)], 1)
        moved = lax.all_to_all(outgoing, "seq", split_axis=0, concat_axis=0, tiled=True)
        x_first = x

    row_outs = [
        ((HW, width), BF16),
        ((columns, width), F32), ((columns, width), F32), ((columns, 1), F32),
        ((columns, width), BF16), ((columns, width), BF16),
    ]
    if layered:
        cut = row_width // 2
        split_outs = [((chips, row_share, cut), BF16)] * 4
        handed_outs = [
            ((row_share, 3 * width), BF16), ((width, 3 * HW), BF16), ((HW, width), BF16),
        ]
        row_outs = [*split_outs, *handed_outs, *row_outs]
        specs = [VMEM] * 4 + [PINNED] * (len(row_outs) - 4)
    else:
        row_outs = [((width, row_width), BF16), *row_outs]
        specs = [VMEM] * len(row_outs)
    *row_terms, row_out, base, normed, inverse_rms, x_near, cot_near = call(
        row_chip_kernel if layered else row_kernel,
        "row_heads",
        [(HBM, x_first), (HBM, cot), *weights],
        row_outs,
        [
            *weight_scratch,
            pltpu.VMEM((columns, HW), F32),
            pltpu.VMEM((columns, HW), F32),
            pltpu.VMEM((columns, 3 * HW), BF16),
            pltpu.SemaphoreType.DMA((12,)),
        ],
        BIG_VMEM,
        specs,
    )
    if layered:
        *row_terms, weight_rows, col_weight, col_out_weight = row_terms
        row_sent = [swap(one, "seq", 1) for one in row_terms[:2]]
        half_block = (chips, row_share // 2, row_width)
        row_next, row_kept = call(
            row_cores_kernel,
            "row_add_cores",
            [(VMEM, one) for one in (*row_terms[2:], *row_sent)],
            [(half_block, BF16), (half_block, F32)],
            out_specs=[VMEM, PINNED],
        )
        *near, row_kept = lax.optimization_barrier((*near, row_kept))
        (far,) = call(
            far_kernel,
            "pack_other_core",
            [(VMEM, one) for one in (x_near, cot_near, *near)],
            [((chips, 2, share, width), BF16)],
        )
        row_got = swap(row_next, "dp", 1)
        keep, col_grads, *pieces = call(
            column_chip_kernel,
            "column_heads",
            [
                (VMEM, one)
                for one in (
                    x_near, cot_near, *near, swap(far, "seq", 1),
                    gain, col_weight, col_out_weight, row_out,
                )
            ],
            [((chips, row_share, col_width), BF16), col_outs[0]]
            + [((chips, row_share, wide), BF16) for wide in SWAP_PIECES],
            [pltpu.VMEM((chips, row_share, col_width), BF16)],
            BIG_VMEM,
            [VMEM, PINNED] + [VMEM] * len(SWAP_PIECES),
        )
        back_send, back_keep = call(
            back_chip_kernel,
            "column_grad_hidden",
            [(VMEM, col_grads), (VMEM, col_weight)],
            [((chips, share, width), BF16)] * 2,
        )
        keep, back_keep, row_got = lax.optimization_barrier((keep, back_keep, row_got))
        first_half = (chips, row_share // 2, FIRST_PART)
        second = (row_share, col_width - FIRST_PART)
        to_next, kept, owned, *off = call(
            cores_kernel,
            "column_add_cores",
            [(VMEM, keep), *[(VMEM, swap(piece, "seq", 1)) for piece in pieces]],
            [(first_half, BF16), (first_half, F32), (second, F32)] + [(second, BF16)] * 3,
            out_specs=[VMEM, PINNED, PINNED, VMEM, VMEM, VMEM],
        )
        got = cross_chips(*off)
        back = call(
            back_pack_kernel,
            "pack_grad_hidden",
            [(VMEM, back_keep), (VMEM, swap(back_send, "seq", 1))],
            [((2 * share, width), BF16)] * 4,
        )
        row_kept, *back = lax.optimization_barrier((row_kept, *back))
        joint = (row_share // 2, FIRST_PART + row_width)
        first_owned, *off = call(
            pair_kernel,
            "first_add_pair",
            [
                (VMEM, one)
                for one in (kept, swap(to_next, "dp", 1), row_kept, row_got)
            ],
            [(joint, F32)] + [(joint, BF16)] * 3,
            out_specs=[PINNED, VMEM, VMEM, VMEM],
        )
        first_got = cross_chips(*off)
        second_half = (row_share // 2, second[1])
        to_next, kept = call(
            layer_kernel,
            "second_add_chips",
            [(VMEM, one) for one in (owned, *got)],
            [(second_half, BF16), (second_half, F32)],
            out_specs=[VMEM, PINNED],
        )
        (pair_sum,) = call(
            join_kernel,
            "join_terms",
            [(VMEM, one) for one in (first_owned, *first_got, kept, swap(to_next, "dp", 1))],
            [((row_share // 2, col_width + row_width), BF16)],
        )
        *back, pair_sum = lax.optimization_barrier((*back, pair_sum))
        held = add_two(pair_sum, swap(pair_sum, "dp", 2), "add_pairs")
        other = swap(held, "dp", 1)
        (grad,) = call(
            input_chip_kernel,
            "input_grad",
            [
                (VMEM, one)
                for one in (base, normed, inverse_rms, gain, back[0], *cross_chips(*back[1:]))
            ],
            [((columns, width), BF16)],
            [pltpu.VMEM((chips, 2 * share, width), BF16), pltpu.SemaphoreType.DMA((chips,))],
            out_specs=[HBM],
        )
        sum_qkv, sum_out, sum_gain = call(
            result_kernel,
            "result",
            [(VMEM, held), (VMEM, other), (VMEM, weight_rows), (VMEM, gain)],
            [((row_share, 3 * width), F32), ((row_share, width), F32), ((1, row_share), F32)],
        )
        sum_gain = sum_gain.reshape(row_share)
    else:
        terms, *col_grads = call(
            column_kernel,
            "column_heads",
            [(ANY, moved), *weights, (VMEM, row_terms[0]), (VMEM, row_out)],
            [((width, 4 * width), BF16), *col_outs],
            [
                pltpu.VMEM((n, 2, share, width), BF16),
                weight_scratch[0],
                weight_scratch[2],
                pltpu.SemaphoreType.DMA((6,)),
            ],
            BIG_VMEM,
        )
        (back,) = call(
            back_kernel,
            "column_grad_hidden",
            [(VMEM, one) for one in col_grads],
            [((n, share, width), BF16)],
        )
        returned = lax.all_to_all(back, "seq", split_axis=0, concat_axis=0, tiled=True)
        (grad,) = call(
            input_kernel,
            "input_grad",
            [
                (VMEM, base), (VMEM, normed), (VMEM, inverse_rms), (VMEM, gain),
                (VMEM, returned.reshape(columns, width)),
            ],
            [((columns, width), BF16)],
        )
        terms = lax.all_to_all(
            terms.reshape(n, row_share, 4 * width), "seq", split_axis=0, concat_axis=0, tiled=True
        )
        total = jnp.sum(terms.astype(F32), 0)
        for step in range(m.bit_length() - 1):
            sent = total.astype(BF16)
            total = sent.astype(F32) + swap(sent, "dp", 1 << step).astype(F32)
        sum_qkv, sum_out = total[:, : 3 * width], total[:, 3 * width :]
        here_at = lax.axis_index("seq") * row_share
        own_gain = lax.dynamic_slice_in_dim(norm_gain, here_at, row_share, 0)
        own_weight = lax.dynamic_slice_in_dim(qkv_weight, here_at, row_share, 0)
        sum_gain = jnp.sum(sum_qkv * own_weight.astype(F32), -1) / own_gain
    return (grad.reshape(inputs.shape), sum_qkv, sum_out, sum_gain)


def solution(mesh):
    return jax.shard_map(
        body,
        mesh=mesh,
        in_specs=(P("dp", "seq", None, None), P(), P(), P(), P("dp", "seq", None, None)),
        out_specs=(P("dp", "seq", None, None), P("seq", None), P("seq", None), P("seq")),
        check_vma=False,
    )
```

```python
import math

import jax
import jax.numpy as jnp
from jax import lax
from jax.experimental import pallas as pl
from jax.experimental.pallas import tpu as pltpu
from jax.sharding import PartitionSpec as P

H = 8
HD = 64
HH = H // 2
HW = HH * HD
SCALE = HD ** (-0.5)
F32 = jnp.float32
BF16 = jnp.bfloat16
QUERY_BLOCK = 128
BIG_VMEM = 20 * 1024 * 1024
SMALL_VMEM = 8 * 1024 * 1024
ANY = pl.BlockSpec(memory_space=pl.ANY)
VMEM = pl.BlockSpec(memory_space=pltpu.VMEM)
HBM = pl.BlockSpec(memory_space=pltpu.HBM)
CHIP_STEPS = (3, 2, 1)
FIRST_PART = 384
PINNED = pl.BlockSpec(memory_space=pltpu.VMEM)
shaped = jax.ShapeDtypeStruct


def here():
    device = lax.axis_index("seq")
    return device >> 1, device & 1, lax.axis_index("dp")


def dot_nn(a, b):
    return lax.dot_general(a, b, (((1,), (0,)), ((), ())), preferred_element_type=F32)


def dot_nt(a, b):
    return lax.dot_general(a, b, (((1,), (1,)), ((), ())), preferred_element_type=F32)


def rms_parts(x):
    inverse_rms = lax.rsqrt(jnp.mean(x * x, -1, keepdims=True) + 1e-05)
    return inverse_rms, x * inverse_rms


def transposed(x):
    block = math.gcd(x.shape[1], 256)
    eye = (
        lax.broadcasted_iota(jnp.int32, (block, block), 0)
        == lax.broadcasted_iota(jnp.int32, (block, block), 1)
    ).astype(F32).astype(BF16)
    parts = [
        dot_nt(eye, x[:, at : at + block]).astype(BF16) for at in range(0, x.shape[1], block)
    ]
    return parts[0] if len(parts) == 1 else jnp.concatenate(parts, 0)


def head_pair(x):
    lane = lax.broadcasted_iota(jnp.int32, x.shape, 1)
    zero = jnp.zeros_like(x)
    return jnp.concatenate([jnp.where(lane < HD, x, zero), jnp.where(lane < HD, zero, x)], 0)


def both_heads(both, count):
    return jnp.concatenate([both[:HD, :count], both[HD:, count:]], 0)


def pair_steps(items, mask_rows, mask):
    count = items[0][2].shape[1]
    scores = [dot_nt(k, q2) for q2, _, _, k, _, _, _ in items]
    prob_grads = [dot_nt(v, g2) for _, g2, _, _, v, _, _ in items]
    probs = []
    for score in scores:
        first = score.shape[0] - mask_rows
        tail = jnp.where(mask, score[first:], -1e30)
        score = tail if first == 0 else jnp.concatenate([score[:first], tail], 0)
        exponent = jnp.exp(score - jnp.max(score, 0, keepdims=True))
        probs.append(exponent * (1.0 / jnp.sum(exponent, 0, keepdims=True)))
    weights = [prob.astype(BF16) for prob in probs]
    attended = [
        both_heads(dot_nn(item[6], weight), count).astype(BF16)
        for item, weight in zip(items, weights)
    ]
    score_grads = []
    for item, att, prob, prob_grad in zip(items, attended, probs, prob_grads):
        product = item[2].astype(F32) * att.astype(F32)
        delta = [jnp.sum(part, 0, keepdims=True) for part in (product[:HD], product[HD:])]
        score_grads.append((prob * (prob_grad - jnp.concatenate(delta, 1))).astype(BF16))
    grad_q = [
        (both_heads(dot_nn(item[5], score_grad), count) * SCALE).astype(BF16)
        for item, score_grad in zip(items, score_grads)
    ]
    grad_k = [dot_nn(score_grad, item[0]) for item, score_grad in zip(items, score_grads)]
    grad_v = [dot_nn(weight, item[1]) for item, weight in zip(items, weights)]
    return list(zip(attended, grad_q, grad_k, grad_v))


def split_cores(piece, send_ref, keep_ref, chips, lanes):
    rows = send_ref.shape[1]
    parts = piece.reshape(chips.stop - chips.start, 2, rows, piece.shape[1])
    even, odd = parts[:, 0], parts[:, 1]
    first = here()[1] == 0
    send_ref[chips, :, lanes] = jnp.where(first, odd, even)
    keep_ref[chips, :, lanes] = jnp.where(first, even, odd)


def qkv_copies(wqkv_ref, w_ref, sems, second):
    width = wqkv_ref.shape[0]
    return [
        pltpu.make_async_copy(
            wqkv_ref.at[:, pl.ds(i * width + second * HW, HW)],
            w_ref.at[:, pl.ds(i * HW, HW)],
            sems.at[i],
        )
        for i in range(3)
    ]


def weight_copies(wqkv_ref, wout_ref, w_ref, wo_ref, sems, second):
    out_rows = wout_ref.at[pl.ds(second * HW, HW), :]
    return [
        *qkv_copies(wqkv_ref, w_ref, sems, second),
        pltpu.make_async_copy(out_rows, wo_ref, sems.at[3]),
    ]


def started(*copies):
    for copy in copies:
        copy.start()
    return copies


def finished(*copies):
    for copy in copies:
        copy.wait()


def project(hidden, cot, w_ref, wo_ref):
    projected = dot_nn(hidden, w_ref[...]).astype(BF16)
    q, k, v = [projected[:, i * HW : (i + 1) * HW] for i in range(3)]
    g = dot_nt(cot, wo_ref[...]).astype(BF16)
    return q * jnp.asarray(SCALE, BF16), k, v, g


def row_part(
    x_any, cot_any, gain_any, wqkv_any, wout_any,
    out_ref, base_ref, normed_ref, inverse_ref, x_ref, cot_ref,
    gain_ref, w_ref, wo_ref, dk_ref, dv_ref, grads_ref, sems,
):
    first = started(
        pltpu.make_async_copy(x_any, x_ref, sems.at[4]),
        pltpu.make_async_copy(gain_any, gain_ref, sems.at[5]),
    )
    later = started(
        *weight_copies(wqkv_any, wout_any, w_ref, wo_ref, sems, 0),
        pltpu.make_async_copy(cot_any, cot_ref, sems.at[6]),
    )
    dk_ref[...] = jnp.zeros_like(dk_ref)
    dv_ref[...] = jnp.zeros_like(dv_ref)
    finished(*first)
    tokens = x_ref.shape[0]
    inverse_ref[...], normed_ref[...] = rms_parts(x_ref[...].astype(F32))
    hidden = (normed_ref[...] * gain_ref[...]).astype(BF16)
    hidden_t = transposed(hidden)
    finished(*later)
    cot = cot_ref[...]
    q, k, v, g = project(hidden, cot, w_ref, wo_ref)
    kt, vt, gt = transposed(k), transposed(v), transposed(g)
    step = math.gcd(tokens, QUERY_BLOCK)
    query = lax.broadcasted_iota(jnp.int32, (step, 2 * step), 1) % step
    mask = query >= lax.broadcasted_iota(jnp.int32, (step, 2 * step), 0)
    pairs = [slice(i * 2 * HD, (i + 1) * 2 * HD) for i in range(HH // 2)]
    att_blocks, dq_blocks = [], []
    for start in range(0, tokens, step):
        rows, keys = slice(start, start + step), slice(0, start + step)
        items = [
            (
                head_pair(q[rows, lanes]), head_pair(g[rows, lanes]), gt[lanes, rows],
                k[keys, lanes], v[keys, lanes], kt[lanes, keys], vt[lanes, keys],
            )
            for lanes in pairs
        ]
        results = pair_steps(items, step, mask)
        for lanes, (_, _, dk, dv) in zip(pairs, results):
            dk_ref[keys, lanes] += dk
            dv_ref[keys, lanes] += dv
        att_blocks.append(jnp.concatenate([result[0] for result in results], 0))
        dq_blocks.append(jnp.concatenate([result[1] for result in results], 0))
    grads_ref[:, :HW] = transposed(jnp.concatenate(dq_blocks, 1))
    grads_ref[:, HW : 2 * HW] = dk_ref[...].astype(BF16)
    grads_ref[:, 2 * HW :] = dv_ref[...].astype(BF16)
    term_qkv = dot_nn(hidden_t, grads_ref[...]).astype(BF16)
    out_ref[...] = dot_nn(jnp.concatenate(att_blocks, 1), cot).astype(BF16)
    grad_normed = dot_nt(grads_ref[...], w_ref[...]) * gain_ref[...]
    base_ref[...] = input_grad(
        cot_ref[...].astype(F32), normed_ref[...], inverse_ref[...], grad_normed
    )
    return term_qkv


def row_kernel(x_any, cot_any, gain_any, wqkv_any, wout_any, qkv_ref, *refs):
    qkv_ref[...] = row_part(x_any, cot_any, gain_any, wqkv_any, wout_any, *refs)


def row_chip_kernel(
    x_any, cot_any, gain_any, wqkv_any, wout_any,
    send_1, send_2, keep_1, keep_2, rows_ref, col_w_ref, col_wo_ref, *refs,
):
    chip, core, _ = here()
    sems, rows = refs[-1], rows_ref.shape[0]
    at = pl.multiple_of((chip * 2 + core) * rows, rows)
    handed = started(
        pltpu.make_async_copy(wqkv_any.at[pl.ds(at, rows), :], rows_ref, sems.at[7]),
        *weight_copies(wqkv_any, wout_any, col_w_ref, col_wo_ref, sems.at[pl.ds(8, 4)], 1),
    )
    term_qkv = row_part(x_any, cot_any, gain_any, wqkv_any, wout_any, *refs)
    chips, cut = send_1.shape[0], keep_1.shape[2]
    pieces = slice(0, chips), slice(0, cut)
    split_cores(term_qkv[:, :cut], send_1, keep_1, *pieces)
    split_cores(term_qkv[:, cut:], send_2, keep_2, *pieces)
    finished(*handed)


def column_part(x, cot, mask, gain, w_ref, wo_ref, weight_waits, grads_ref):
    tokens, block = x.shape[0], mask.shape[0]
    _, normed = rms_parts(x.astype(F32))
    hidden = (normed * gain).astype(BF16)
    hidden_t = transposed(hidden)
    finished(*weight_waits)
    q, k, v, g = project(hidden, cot, w_ref, wo_ref)
    kt, vt, gt = transposed(k), transposed(v), transposed(g)
    pairs = [slice(i * 2 * HD, (i + 1) * 2 * HD) for i in range(HH // 2)]
    blocks = [slice(at, at + block) for at in range(0, tokens, block)]
    items = [
        (
            head_pair(q[rows, lanes]), head_pair(g[rows, lanes]), gt[lanes, rows],
            k[rows, lanes], v[rows, lanes], kt[lanes, rows], vt[lanes, rows],
        )
        for lanes in pairs
        for rows in blocks
    ]
    results = pair_steps(items, block, mask)
    places = [(lanes, rows) for lanes in pairs for rows in blocks]
    for (lanes, rows), (_, _, dk, dv) in zip(places, results):
        grads_ref[rows, HW + lanes.start : HW + lanes.stop] = dk.astype(BF16)
        grads_ref[rows, 2 * HW + lanes.start : 2 * HW + lanes.stop] = dv.astype(BF16)
    by_pair = [results[i * len(blocks) : (i + 1) * len(blocks)] for i in range(len(pairs))]
    attended, grad_q = [
        jnp.concatenate([jnp.concatenate([r[i] for r in some], 1) for some in by_pair], 0)
        for i in range(2)
    ]
    grads_ref[:, :HW] = transposed(grad_q)
    term_qkv = dot_nn(hidden_t, grads_ref[...]).astype(BF16)
    term_out = dot_nn(attended, cot).astype(BF16)
    return term_qkv, term_out


def column_mask(all_rows, group, row_of):
    block = all_rows * group
    shape = (block, 2 * block)
    query = lax.broadcasted_iota(jnp.int32, shape, 1) % block
    key = lax.broadcasted_iota(jnp.int32, shape, 0)
    same_column = query % group == key % group
    return (row_of(query // group) >= row_of(key // group)) & same_column


def column_kernel(
    moved_any, gain_any, wqkv_any, wout_any, row_qkv_ref, row_out_ref,
    terms_ref, grads_ref, w_ref,
    moved_ref, gain_ref, wo_ref, sems,
):
    copies = started(
        pltpu.make_async_copy(moved_any, moved_ref, sems.at[4]),
        pltpu.make_async_copy(gain_any, gain_ref, sems.at[5]),
    )
    weights = started(*weight_copies(wqkv_any, wout_any, w_ref, wo_ref, sems, 1))
    finished(*copies)
    all_rows, _, share, width = moved_ref.shape
    group = math.gcd(share, 16)
    x, cot = [
        jnp.concatenate(
            [
                moved_ref[:, which, at : at + group, :].astype(F32).reshape(all_rows * group, width)
                for at in range(0, share, group)
            ],
            0,
        ).astype(BF16)
        for which in range(2)
    ]
    mask = column_mask(all_rows, group, lambda place: place)
    term_qkv, term_out = column_part(
        x, cot, mask, gain_ref[...], w_ref, wo_ref, weights, grads_ref
    )
    for i in range(3):
        at = i * width
        terms_ref[:, at : at + HW] = row_qkv_ref[:, i * HW : (i + 1) * HW]
        terms_ref[:, at + HW : at + 2 * HW] = term_qkv[:, i * HW : (i + 1) * HW]
    terms_ref[:HW, 3 * width :] = row_out_ref[...]
    terms_ref[HW:, 3 * width :] = term_out


def column_chip_kernel(
    x_ref, cot_ref, near_1, near_2, near_3, far_ref, gain_ref, w_ref, wo_ref, row_out_ref,
    send_ref, keep_ref, grads_ref,
):
    chip, core, _ = here()
    share = far_ref.shape[2]
    half = pl.ds(pl.multiple_of(core * share, share), share)
    at = pl.ds(pl.multiple_of((chip * 2 + core) * share, share), share)
    group = math.gcd(share, 16)

    def tokens(which, mine):
        pieces = [mine[at, :], far_ref[0, which]]
        for i, near in enumerate((near_1, near_2, near_3)):
            pieces += [near[which, half, :], far_ref[i + 1, which]]
        starts = range(0, share, group)
        return jnp.concatenate(
            [piece[start : start + group] for start in starts for piece in pieces], 0
        )

    def row_of(place):
        step = (4 - (place >> 1)) & 3
        return ((step ^ chip) << 1) + ((place & 1) ^ core)

    mask = column_mask(2 * (len(CHIP_STEPS) + 1), group, row_of)
    term_qkv, term_out = column_part(
        tokens(0, x_ref), tokens(1, cot_ref), mask, gain_ref[...], w_ref, wo_ref, (), grads_ref
    )
    chips = send_ref.shape[0]
    refs = send_ref, keep_ref
    out_lanes = slice(3 * HW, send_ref.shape[2])
    split_cores(term_qkv, *refs, slice(0, chips), slice(0, 3 * HW))
    split_cores(row_out_ref[...], *refs, slice(0, chips // 2), out_lanes)
    split_cores(term_out, *refs, slice(chips // 2, chips), out_lanes)


def far_kernel(x_ref, cot_ref, near_1, near_2, near_3, far_ref):
    chip, core, _ = here()
    share = far_ref.shape[2]
    at = pl.ds(pl.multiple_of((chip * 2 + 1 - core) * share, share), share)
    far_ref[0, 0], far_ref[0, 1] = x_ref[at, :], cot_ref[at, :]
    at = pl.ds(pl.multiple_of((1 - core) * share, share), share)
    for i, near in enumerate((near_1, near_2, near_3)):
        far_ref[i + 1] = near[:, at, :]


def back_kernel(grads_ref, w_ref, back_ref):
    grad_hidden = dot_nt(grads_ref[...], w_ref[...])
    all_rows, share, width = back_ref.shape
    group = math.gcd(share, 16)
    block = all_rows * group
    for i in range(share // group):
        piece = grad_hidden[i * block : (i + 1) * block].reshape(all_rows, group, width)
        back_ref[:, i * group : (i + 1) * group, :] = piece.astype(BF16)


def back_chip_kernel(grads_ref, w_ref, send_ref, keep_ref):
    grad_hidden = dot_nt(grads_ref[...], w_ref[...]).astype(BF16)
    chips, share, width = keep_ref.shape
    group = math.gcd(share, 16)
    block = 2 * chips * group
    for i in range(share // group):
        piece = grad_hidden[i * block : (i + 1) * block].reshape(chips, 2, group, width)
        at = slice(i * group, (i + 1) * group)
        keep_ref[:, at, :], send_ref[:, at, :] = piece[:, 0], piece[:, 1]


def back_pack_kernel(keep_ref, got_ref, *targets):
    share = keep_ref.shape[1]
    core = here()[1]
    kept_at = pl.ds(pl.multiple_of(core * share, share), share)
    got_at = pl.ds(pl.multiple_of((1 - core) * share, share), share)
    for i, target in enumerate(targets):
        target[kept_at, :] = keep_ref[i]
        target[got_at, :] = got_ref[i]


def input_kernel(base_ref, normed_ref, inverse_ref, gain_ref, back_ref, grad_ref):
    grad_ref[...] = input_grad(
        base_ref[...], normed_ref[...], inverse_ref[...], back_ref[...].astype(F32) * gain_ref[...]
    ).astype(BF16)


def input_grad(base, normed, inverse_rms, grad_normed):
    projected = jnp.mean(grad_normed * normed, -1, keepdims=True)
    return base + inverse_rms * (grad_normed - normed * projected)


def input_chip_kernel(
    base_ref, normed_ref, inverse_ref, gain_ref, own_ref, got_1, got_2, got_3,
    grad_any, grad_ref, sems,
):
    chip = here()[0]
    count = own_ref.shape[0]
    copies = []
    for i, (step, back_ref) in enumerate(zip((0, *CHIP_STEPS), (own_ref, got_1, got_2, got_3))):
        at = pl.ds(pl.multiple_of((chip ^ step) * count, count), count)
        grad_normed = back_ref[...].astype(F32) * gain_ref[...]
        grad = input_grad(base_ref[at, :], normed_ref[at, :], inverse_ref[at, :], grad_normed)
        grad_ref[i] = grad.astype(BF16)
        copies += started(pltpu.make_async_copy(grad_ref.at[i], grad_any.at[at, :], sems.at[i]))
    finished(*copies)


def pack_kernel(x_any, cot_any, off_1, off_2, off_3, sems):
    chip = here()[0]
    count = off_1.shape[1]
    copies = []
    for i, (step, target) in enumerate(zip(CHIP_STEPS, (off_1, off_2, off_3))):
        at = pl.ds(pl.multiple_of((chip ^ step) * count, count), count)
        for which, source in enumerate((x_any, cot_any)):
            copies.append(
                pltpu.make_async_copy(source.at[at, :], target.at[which], sems.at[2 * i + which])
            )
    finished(*started(*copies))


def split_rows(total, axis):
    upper = (here()[2] & 1) == 1
    low, high = jnp.split(total, 2, axis)
    return jnp.where(upper, low, high).astype(BF16), jnp.where(upper, high, low)


def row_cores_kernel(keep_1, keep_2, got_1, got_2, send_ref, kept_ref):
    total = [
        keep_ref[...].astype(F32) + got_ref[...].astype(F32)
        for keep_ref, got_ref in ((keep_1, got_1), (keep_2, got_2))
    ]
    send_ref[...], kept_ref[...] = split_rows(jnp.concatenate(total, 2), 1)


def cores_kernel(keep_ref, got_ref, send_ref, kept_ref, *targets):
    chip, cut = here()[0], kept_ref.shape[2]
    first = keep_ref[:, :, :cut].astype(F32) + got_ref[:, :, :cut].astype(F32)
    send_ref[...], kept_ref[...] = split_rows(first, 1)
    for step, target in zip((0, *CHIP_STEPS), targets):
        there = chip ^ step
        total = keep_ref[there, :, cut:].astype(F32) + got_ref[there, :, cut:].astype(F32)
        target[...] = total.astype(target.dtype)


def pair_kernel(kept_ref, got_ref, row_kept, row_got, *targets):
    chip, cut = here()[0], kept_ref.shape[2]
    for step, target in zip((0, *CHIP_STEPS), targets):
        there = chip ^ step
        total = kept_ref[there] + got_ref[there].astype(F32)
        target[:, :cut] = total.astype(target.dtype)
        total = row_kept[there] + row_got[there].astype(F32)
        target[:, cut:] = total.astype(target.dtype)


def layer_sum(own_ref, got_1, got_2, got_3):
    return own_ref[...] + (
        (got_1[...].astype(F32) + got_2[...].astype(F32)) + got_3[...].astype(F32)
    )


def layer_kernel(own_ref, got_1, got_2, got_3, send_ref, kept_ref):
    send_ref[...], kept_ref[...] = split_rows(layer_sum(own_ref, got_1, got_2, got_3), 0)


def layer_total_kernel(own_ref, got_1, got_2, got_3, out_ref):
    out_ref[...] = layer_sum(own_ref, got_1, got_2, got_3).astype(BF16)


def add_kernel(kept_ref, got_ref, out_ref):
    out_ref[...] = (kept_ref[...].astype(F32) + got_ref[...].astype(F32)).astype(BF16)


def result_kernel(
    first_held, first_got, held_ref, got_ref, w_ref, gain_ref, qkv_ref, out_ref, grad_ref
):
    rows = qkv_ref.shape[0]
    chip, core, layer = here()
    at = (chip * 2 + core) * rows
    upper = (layer & 1) == 1
    half = rows // 2
    width = out_ref.shape[1]

    def place(target, to, first, lanes):
        held, got = (first_held, first_got) if first else (held_ref, got_ref)
        held, got = held[:, lanes].astype(F32), got[:, lanes].astype(F32)
        to = slice(to, to + held.shape[1])
        target[:half, to], target[half:, to] = jnp.where(upper, got, held), jnp.where(upper, held, got)

    def place_column(target, to, at, count):
        in_first = max(0, min(count, FIRST_PART - at))
        if in_first:
            place(target, to, True, slice(at, at + in_first))
        if in_first < count:
            at -= FIRST_PART
            place(target, to + in_first, False, slice(at + in_first, at + count))

    for i in range(3):
        row_at = FIRST_PART + i * HW
        place(qkv_ref, i * width, True, slice(row_at, row_at + HW))
        place_column(qkv_ref, i * width + HW, i * HW, HW)
    place_column(out_ref, 0, 3 * HW, width)
    total = jnp.sum(qkv_ref[...] * w_ref[...].astype(F32), -1, keepdims=True)
    shape = (rows, gain_ref.shape[1])
    row = lax.broadcasted_iota(jnp.int32, shape, 0)
    feature = lax.broadcasted_iota(jnp.int32, shape, 1)
    gain = jnp.sum(jnp.where(feature == row + at, gain_ref[...], 0.0), -1, keepdims=True)
    shape = (rows, grad_ref.shape[1])
    same = lax.broadcasted_iota(jnp.int32, shape, 0) == lax.broadcasted_iota(jnp.int32, shape, 1)
    grad_ref[...] = jnp.sum(jnp.where(same, total / gain, 0.0), 0, keepdims=True)


def call(kernel, name, ins, outs, scratch=(), vmem=SMALL_VMEM, out_specs=None):
    out_specs = out_specs or [VMEM] * len(outs)
    places = [{id(HBM): pltpu.HBM, id(PINNED): pltpu.VMEM}.get(id(spec)) for spec in out_specs]
    outs = [place(*out) if place else shaped(*out) for place, out in zip(places, outs)]
    args = [
        pltpu.with_memory_space_constraint(array, pltpu.HBM) if spec is HBM else array
        for spec, array in ins
    ]
    return pl.pallas_call(
        kernel,
        out_shape=outs,
        in_specs=[spec for spec, _ in ins],
        out_specs=out_specs,
        scratch_shapes=scratch,
        name=name,
        cost_estimate=pl.CostEstimate(flops=0, bytes_accessed=0, transcendentals=0),
        compiler_params=pltpu.CompilerParams(vmem_limit_bytes=vmem),
    )(*args)


def swap(array, axis, bits):
    count = lax.axis_size(axis)
    return lax.ppermute(array, axis, [(i, i ^ bits) for i in range(count)])


def cross_chips(*offs):
    return [swap(off, "seq", 2 * step) for off, step in zip(offs, CHIP_STEPS)]


def add_two(kept, got, name):
    (total,) = call(add_kernel, name, [(VMEM, kept), (VMEM, got)], [(kept.shape, BF16)])
    return total


def body(inputs, norm_gain, qkv_weight, out_weight, out_cotan):
    columns, width = inputs.shape[2:]
    n = lax.axis_size("seq")
    m = lax.axis_size("dp")
    share = columns // n
    row_share = width // n
    row_width, col_width = 3 * HW, 3 * HW + width
    x = inputs.reshape(columns, width)
    cot = out_cotan.reshape(columns, width)
    gain = norm_gain.reshape(1, width)
    chips = 4
    layered = n == 2 * chips and m == 4 and row_share == share
    weight_scratch = [
        pltpu.VMEM((1, width), F32),
        pltpu.VMEM((width, 3 * HW), BF16),
        pltpu.VMEM((HW, width), BF16),
    ]
    weights = [(HBM, gain), (HBM, qkv_weight), (HBM, out_weight)]
    col_outs = [((columns, 3 * HW), BF16), ((width, 3 * HW), BF16)]

    if layered:
        packed = call(
            pack_kernel,
            "pack_columns",
            [(HBM, x), (HBM, cot)],
            [((2, 2 * share, width), BF16)] * 3,
            [pltpu.SemaphoreType.DMA((6,))],
            out_specs=[ANY] * 3,
        )
        near = cross_chips(*packed)
        x_first, _ = lax.optimization_barrier((x, packed[0]))
    else:
        outgoing = jnp.stack([x.reshape(n, share, width), cot.reshape(n, share, width)], 1)
        moved = lax.all_to_all(outgoing, "seq", split_axis=0, concat_axis=0, tiled=True)
        x_first = x

    row_outs = [
        ((HW, width), BF16),
        ((columns, width), F32), ((columns, width), F32), ((columns, 1), F32),
        ((columns, width), BF16), ((columns, width), BF16),
    ]
    if layered:
        cut = row_width // 2
        split_outs = [((chips, row_share, cut), BF16)] * 4
        handed_outs = [
            ((row_share, 3 * width), BF16), ((width, 3 * HW), BF16), ((HW, width), BF16),
        ]
        row_outs = [*split_outs, *handed_outs, *row_outs]
        specs = [VMEM] * 4 + [PINNED] * (len(row_outs) - 4)
    else:
        row_outs = [((width, row_width), BF16), *row_outs]
        specs = [VMEM] * len(row_outs)
    *row_terms, row_out, base, normed, inverse_rms, x_near, cot_near = call(
        row_chip_kernel if layered else row_kernel,
        "row_heads",
        [(HBM, x_first), (HBM, cot), *weights],
        row_outs,
        [
            *weight_scratch,
            pltpu.VMEM((columns, HW), F32),
            pltpu.VMEM((columns, HW), F32),
            pltpu.VMEM((columns, 3 * HW), BF16),
            pltpu.SemaphoreType.DMA((12,)),
        ],
        BIG_VMEM,
        specs,
    )
    if layered:
        *row_terms, weight_rows, col_weight, col_out_weight = row_terms
        row_sent = [swap(one, "seq", 1) for one in row_terms[:2]]
        half_block = (chips, row_share // 2, row_width)
        row_next, row_kept = call(
            row_cores_kernel,
            "row_add_cores",
            [(VMEM, one) for one in (*row_terms[2:], *row_sent)],
            [(half_block, BF16), (half_block, F32)],
            out_specs=[VMEM, PINNED],
        )
        *near, row_kept = lax.optimization_barrier((*near, row_kept))
        (far,) = call(
            far_kernel,
            "pack_other_core",
            [(VMEM, one) for one in (x_near, cot_near, *near)],
            [((chips, 2, share, width), BF16)],
        )
        send, keep, col_grads = call(
            column_chip_kernel,
            "column_heads",
            [
                (VMEM, one)
                for one in (
                    x_near, cot_near, *near, swap(far, "seq", 1),
                    gain, col_weight, col_out_weight, row_out,
                )
            ],
            [((chips, row_share, col_width), BF16)] * 2 + [col_outs[0]],
            vmem=BIG_VMEM,
            out_specs=[VMEM, VMEM, PINNED],
        )
        back_send, back_keep = call(
            back_chip_kernel,
            "column_grad_hidden",
            [(VMEM, col_grads), (VMEM, col_weight)],
            [((chips, share, width), BF16)] * 2,
        )
        row_next, _ = lax.optimization_barrier((row_next, send))
        keep, back_keep = lax.optimization_barrier((keep, back_keep))
        first_half = (chips, row_share // 2, FIRST_PART)
        second = (row_share, col_width - FIRST_PART)
        to_next, kept, owned, *off = call(
            cores_kernel,
            "column_add_cores",
            [(VMEM, keep), (VMEM, swap(send, "seq", 1))],
            [(first_half, BF16), (first_half, F32), (second, F32)] + [(second, BF16)] * 3,
            out_specs=[VMEM, PINNED, PINNED, VMEM, VMEM, VMEM],
        )
        got = cross_chips(*off)
        back = call(
            back_pack_kernel,
            "pack_grad_hidden",
            [(VMEM, back_keep), (VMEM, swap(back_send, "seq", 1))],
            [((2 * share, width), BF16)] * 4,
        )
        row_kept, *back = lax.optimization_barrier((row_kept, *back))
        joint = (row_share // 2, FIRST_PART + row_width)
        first_owned, *off = call(
            pair_kernel,
            "first_add_pair",
            [
                (VMEM, one)
                for one in (kept, swap(to_next, "dp", 1), row_kept, swap(row_next, "dp", 1))
            ],
            [(joint, F32)] + [(joint, BF16)] * 3,
            out_specs=[PINNED, VMEM, VMEM, VMEM],
        )
        first_got = cross_chips(*off)
        second_half = (row_share // 2, second[1])
        to_next, kept = call(
            layer_kernel,
            "second_add_chips",
            [(VMEM, one) for one in (owned, *got)],
            [(second_half, BF16), (second_half, F32)],
            out_specs=[VMEM, PINNED],
        )
        (first_sum,) = call(
            layer_total_kernel,
            "first_add_chips",
            [(VMEM, one) for one in (first_owned, *first_got)],
            [(joint, BF16)],
        )
        first_held = add_two(first_sum, swap(first_sum, "dp", 2), "first_add_pairs")
        first_other = swap(first_held, "dp", 1)
        pair_sum = add_two(kept, swap(to_next, "dp", 1), "second_add_pair")
        *back, pair_sum = lax.optimization_barrier((*back, pair_sum))
        held = add_two(pair_sum, swap(pair_sum, "dp", 2), "second_add_pairs")
        other = swap(held, "dp", 1)
        (grad,) = call(
            input_chip_kernel,
            "input_grad",
            [
                (VMEM, one)
                for one in (base, normed, inverse_rms, gain, back[0], *cross_chips(*back[1:]))
            ],
            [((columns, width), BF16)],
            [pltpu.VMEM((chips, 2 * share, width), BF16), pltpu.SemaphoreType.DMA((chips,))],
            out_specs=[HBM],
        )
        sum_qkv, sum_out, sum_gain = call(
            result_kernel,
            "result",
            [
                (VMEM, one)
                for one in (first_held, first_other, held, other, weight_rows, gain)
            ],
            [((row_share, 3 * width), F32), ((row_share, width), F32), ((1, row_share), F32)],
        )
        sum_gain = sum_gain.reshape(row_share)
    else:
        terms, *col_grads = call(
            column_kernel,
            "column_heads",
            [(ANY, moved), *weights, (VMEM, row_terms[0]), (VMEM, row_out)],
            [((width, 4 * width), BF16), *col_outs],
            [
                pltpu.VMEM((n, 2, share, width), BF16),
                weight_scratch[0],
                weight_scratch[2],
                pltpu.SemaphoreType.DMA((6,)),
            ],
            BIG_VMEM,
        )
        (back,) = call(
            back_kernel,
            "column_grad_hidden",
            [(VMEM, one) for one in col_grads],
            [((n, share, width), BF16)],
        )
        returned = lax.all_to_all(back, "seq", split_axis=0, concat_axis=0, tiled=True)
        (grad,) = call(
            input_kernel,
            "input_grad",
            [
                (VMEM, base), (VMEM, normed), (VMEM, inverse_rms), (VMEM, gain),
                (VMEM, returned.reshape(columns, width)),
            ],
            [((columns, width), BF16)],
        )
        terms = lax.all_to_all(
            terms.reshape(n, row_share, 4 * width), "seq", split_axis=0, concat_axis=0, tiled=True
        )
        total = jnp.sum(terms.astype(F32), 0)
        for step in range(m.bit_length() - 1):
            sent = total.astype(BF16)
            total = sent.astype(F32) + swap(sent, "dp", 1 << step).astype(F32)
        sum_qkv, sum_out = total[:, : 3 * width], total[:, 3 * width :]
        here_at = lax.axis_index("seq") * row_share
        own_gain = lax.dynamic_slice_in_dim(norm_gain, here_at, row_share, 0)
        own_weight = lax.dynamic_slice_in_dim(qkv_weight, here_at, row_share, 0)
        sum_gain = jnp.sum(sum_qkv * own_weight.astype(F32), -1) / own_gain
    return (grad.reshape(inputs.shape), sum_qkv, sum_out, sum_gain)


def solution(mesh):
    return jax.shard_map(
        body,
        mesh=mesh,
        in_specs=(P("dp", "seq", None, None), P(), P(), P(), P("dp", "seq", None, None)),
        out_specs=(P("dp", "seq", None, None), P("seq", None), P("seq", None), P("seq")),
        check_vma=False,
    )
```

```python
import math

import jax
import jax.numpy as jnp
from jax import lax
from jax.experimental import pallas as pl
from jax.experimental.pallas import tpu as pltpu
from jax.sharding import PartitionSpec as P

H = 8
HD = 64
HH = H // 2
HW = HH * HD
SCALE = HD ** (-0.5)
F32 = jnp.float32
BF16 = jnp.bfloat16
QUERY_BLOCK = 128
BIG_VMEM = 20 * 1024 * 1024
SMALL_VMEM = 8 * 1024 * 1024
ANY = pl.BlockSpec(memory_space=pl.ANY)
VMEM = pl.BlockSpec(memory_space=pltpu.VMEM)
HBM = pl.BlockSpec(memory_space=pltpu.HBM)
CHIP_STEPS = (3, 2, 1)
FIRST_PART = 384
PINNED = pl.BlockSpec(memory_space=pltpu.VMEM)
shaped = jax.ShapeDtypeStruct


def here():
    device = lax.axis_index("seq")
    return device >> 1, device & 1, lax.axis_index("dp")


def dot_nn(a, b):
    return lax.dot_general(a, b, (((1,), (0,)), ((), ())), preferred_element_type=F32)


def dot_nt(a, b):
    return lax.dot_general(a, b, (((1,), (1,)), ((), ())), preferred_element_type=F32)


def rms_parts(x):
    inverse_rms = lax.rsqrt(jnp.mean(x * x, -1, keepdims=True) + 1e-05)
    return inverse_rms, x * inverse_rms


def transposed(x):
    block = math.gcd(x.shape[1], 256)
    eye = (
        lax.broadcasted_iota(jnp.int32, (block, block), 0)
        == lax.broadcasted_iota(jnp.int32, (block, block), 1)
    ).astype(F32).astype(BF16)
    parts = [
        dot_nt(eye, x[:, at : at + block]).astype(BF16) for at in range(0, x.shape[1], block)
    ]
    return parts[0] if len(parts) == 1 else jnp.concatenate(parts, 0)


def head_pair(x):
    lane = lax.broadcasted_iota(jnp.int32, x.shape, 1)
    zero = jnp.zeros_like(x)
    return jnp.concatenate([jnp.where(lane < HD, x, zero), jnp.where(lane < HD, zero, x)], 0)


def both_heads(both, count):
    return jnp.concatenate([both[:HD, :count], both[HD:, count:]], 0)


def pair_steps(items, mask_rows, mask):
    count = items[0][2].shape[1]
    scores = [dot_nt(k, q2) for q2, _, _, k, _, _, _ in items]
    prob_grads = [dot_nt(v, g2) for _, g2, _, _, v, _, _ in items]
    probs = []
    for score in scores:
        first = score.shape[0] - mask_rows
        tail = jnp.where(mask, score[first:], -1e30)
        score = tail if first == 0 else jnp.concatenate([score[:first], tail], 0)
        exponent = jnp.exp(score - jnp.max(score, 0, keepdims=True))
        probs.append(exponent * (1.0 / jnp.sum(exponent, 0, keepdims=True)))
    weights = [prob.astype(BF16) for prob in probs]
    attended = [
        both_heads(dot_nn(item[6], weight), count).astype(BF16)
        for item, weight in zip(items, weights)
    ]
    score_grads = []
    for item, att, prob, prob_grad in zip(items, attended, probs, prob_grads):
        product = item[2].astype(F32) * att.astype(F32)
        delta = [jnp.sum(part, 0, keepdims=True) for part in (product[:HD], product[HD:])]
        score_grads.append((prob * (prob_grad - jnp.concatenate(delta, 1))).astype(BF16))
    grad_q = [
        (both_heads(dot_nn(item[5], score_grad), count) * SCALE).astype(BF16)
        for item, score_grad in zip(items, score_grads)
    ]
    grad_k = [dot_nn(score_grad, item[0]) for item, score_grad in zip(items, score_grads)]
    grad_v = [dot_nn(weight, item[1]) for item, weight in zip(items, weights)]
    return list(zip(attended, grad_q, grad_k, grad_v))


def split_cores(piece, send_ref, keep_ref, chips, lanes):
    rows = send_ref.shape[1]
    parts = piece.reshape(chips.stop - chips.start, 2, rows, piece.shape[1])
    even, odd = parts[:, 0], parts[:, 1]
    first = here()[1] == 0
    send_ref[chips, :, lanes] = jnp.where(first, odd, even)
    keep_ref[chips, :, lanes] = jnp.where(first, even, odd)


def qkv_copies(wqkv_ref, w_ref, sems, second):
    width = wqkv_ref.shape[0]
    return [
        pltpu.make_async_copy(
            wqkv_ref.at[:, pl.ds(i * width + second * HW, HW)],
            w_ref.at[:, pl.ds(i * HW, HW)],
            sems.at[i],
        )
        for i in range(3)
    ]


def weight_copies(wqkv_ref, wout_ref, w_ref, wo_ref, sems, second):
    out_rows = wout_ref.at[pl.ds(second * HW, HW), :]
    return [
        *qkv_copies(wqkv_ref, w_ref, sems, second),
        pltpu.make_async_copy(out_rows, wo_ref, sems.at[3]),
    ]


def started(*copies):
    for copy in copies:
        copy.start()
    return copies


def finished(*copies):
    for copy in copies:
        copy.wait()


def project(hidden, cot, w_ref, wo_ref):
    projected = dot_nn(hidden, w_ref[...]).astype(BF16)
    q, k, v = [projected[:, i * HW : (i + 1) * HW] for i in range(3)]
    g = dot_nt(cot, wo_ref[...]).astype(BF16)
    return q * jnp.asarray(SCALE, BF16), k, v, g


def row_part(
    x_any, cot_any, gain_any, wqkv_any, wout_any,
    out_ref, base_ref, normed_ref, inverse_ref, x_ref, cot_ref,
    gain_ref, w_ref, wo_ref, dk_ref, dv_ref, grads_ref, sems,
):
    first = started(
        pltpu.make_async_copy(x_any, x_ref, sems.at[4]),
        pltpu.make_async_copy(gain_any, gain_ref, sems.at[5]),
    )
    later = started(
        *weight_copies(wqkv_any, wout_any, w_ref, wo_ref, sems, 0),
        pltpu.make_async_copy(cot_any, cot_ref, sems.at[6]),
    )
    dk_ref[...] = jnp.zeros_like(dk_ref)
    dv_ref[...] = jnp.zeros_like(dv_ref)
    finished(*first)
    tokens = x_ref.shape[0]
    inverse_ref[...], normed_ref[...] = rms_parts(x_ref[...].astype(F32))
    hidden = (normed_ref[...] * gain_ref[...]).astype(BF16)
    hidden_t = transposed(hidden)
    finished(*later)
    cot = cot_ref[...]
    q, k, v, g = project(hidden, cot, w_ref, wo_ref)
    kt, vt, gt = transposed(k), transposed(v), transposed(g)
    step = math.gcd(tokens, QUERY_BLOCK)
    query = lax.broadcasted_iota(jnp.int32, (step, 2 * step), 1) % step
    mask = query >= lax.broadcasted_iota(jnp.int32, (step, 2 * step), 0)
    pairs = [slice(i * 2 * HD, (i + 1) * 2 * HD) for i in range(HH // 2)]
    att_blocks, dq_blocks = [], []
    for start in range(0, tokens, step):
        rows, keys = slice(start, start + step), slice(0, start + step)
        items = [
            (
                head_pair(q[rows, lanes]), head_pair(g[rows, lanes]), gt[lanes, rows],
                k[keys, lanes], v[keys, lanes], kt[lanes, keys], vt[lanes, keys],
            )
            for lanes in pairs
        ]
        results = pair_steps(items, step, mask)
        for lanes, (_, _, dk, dv) in zip(pairs, results):
            dk_ref[keys, lanes] += dk
            dv_ref[keys, lanes] += dv
        att_blocks.append(jnp.concatenate([result[0] for result in results], 0))
        dq_blocks.append(jnp.concatenate([result[1] for result in results], 0))
    grads_ref[:, :HW] = transposed(jnp.concatenate(dq_blocks, 1))
    grads_ref[:, HW : 2 * HW] = dk_ref[...].astype(BF16)
    grads_ref[:, 2 * HW :] = dv_ref[...].astype(BF16)
    term_qkv = dot_nn(hidden_t, grads_ref[...]).astype(BF16)
    out_ref[...] = dot_nn(jnp.concatenate(att_blocks, 1), cot).astype(BF16)
    grad_normed = dot_nt(grads_ref[...], w_ref[...]) * gain_ref[...]
    base_ref[...] = input_grad(
        cot_ref[...].astype(F32), normed_ref[...], inverse_ref[...], grad_normed
    )
    return term_qkv


def row_kernel(x_any, cot_any, gain_any, wqkv_any, wout_any, qkv_ref, *refs):
    qkv_ref[...] = row_part(x_any, cot_any, gain_any, wqkv_any, wout_any, *refs)


def row_chip_kernel(
    x_any, cot_any, gain_any, wqkv_any, wout_any,
    send_1, send_2, keep_1, keep_2, rows_ref, col_w_ref, col_wo_ref, *refs,
):
    chip, core, _ = here()
    sems, rows = refs[-1], rows_ref.shape[0]
    at = pl.multiple_of((chip * 2 + core) * rows, rows)
    handed = started(
        pltpu.make_async_copy(wqkv_any.at[pl.ds(at, rows), :], rows_ref, sems.at[7]),
        *weight_copies(wqkv_any, wout_any, col_w_ref, col_wo_ref, sems.at[pl.ds(8, 4)], 1),
    )
    term_qkv = row_part(x_any, cot_any, gain_any, wqkv_any, wout_any, *refs)
    chips, cut = send_1.shape[0], keep_1.shape[2]
    pieces = slice(0, chips), slice(0, cut)
    split_cores(term_qkv[:, :cut], send_1, keep_1, *pieces)
    split_cores(term_qkv[:, cut:], send_2, keep_2, *pieces)
    finished(*handed)


def column_part(x, cot, mask, gain, w_ref, wo_ref, weight_waits, grads_ref):
    tokens, block = x.shape[0], mask.shape[0]
    _, normed = rms_parts(x.astype(F32))
    hidden = (normed * gain).astype(BF16)
    hidden_t = transposed(hidden)
    finished(*weight_waits)
    q, k, v, g = project(hidden, cot, w_ref, wo_ref)
    kt, vt, gt = transposed(k), transposed(v), transposed(g)
    pairs = [slice(i * 2 * HD, (i + 1) * 2 * HD) for i in range(HH // 2)]
    blocks = [slice(at, at + block) for at in range(0, tokens, block)]
    items = [
        (
            head_pair(q[rows, lanes]), head_pair(g[rows, lanes]), gt[lanes, rows],
            k[rows, lanes], v[rows, lanes], kt[lanes, rows], vt[lanes, rows],
        )
        for lanes in pairs
        for rows in blocks
    ]
    results = pair_steps(items, block, mask)
    places = [(lanes, rows) for lanes in pairs for rows in blocks]
    for (lanes, rows), (_, _, dk, dv) in zip(places, results):
        grads_ref[rows, HW + lanes.start : HW + lanes.stop] = dk.astype(BF16)
        grads_ref[rows, 2 * HW + lanes.start : 2 * HW + lanes.stop] = dv.astype(BF16)
    by_pair = [results[i * len(blocks) : (i + 1) * len(blocks)] for i in range(len(pairs))]
    attended, grad_q = [
        jnp.concatenate([jnp.concatenate([r[i] for r in some], 1) for some in by_pair], 0)
        for i in range(2)
    ]
    grads_ref[:, :HW] = transposed(grad_q)
    term_qkv = dot_nn(hidden_t, grads_ref[...]).astype(BF16)
    term_out = dot_nn(attended, cot).astype(BF16)
    return term_qkv, term_out


def column_mask(all_rows, group, row_of):
    block = all_rows * group
    shape = (block, 2 * block)
    query = lax.broadcasted_iota(jnp.int32, shape, 1) % block
    key = lax.broadcasted_iota(jnp.int32, shape, 0)
    same_column = query % group == key % group
    return (row_of(query // group) >= row_of(key // group)) & same_column


def column_kernel(
    moved_any, gain_any, wqkv_any, wout_any, row_qkv_ref, row_out_ref,
    terms_ref, grads_ref, w_ref,
    moved_ref, gain_ref, wo_ref, sems,
):
    copies = started(
        pltpu.make_async_copy(moved_any, moved_ref, sems.at[4]),
        pltpu.make_async_copy(gain_any, gain_ref, sems.at[5]),
    )
    weights = started(*weight_copies(wqkv_any, wout_any, w_ref, wo_ref, sems, 1))
    finished(*copies)
    all_rows, _, share, width = moved_ref.shape
    group = math.gcd(share, 16)
    x, cot = [
        jnp.concatenate(
            [
                moved_ref[:, which, at : at + group, :].astype(F32).reshape(all_rows * group, width)
                for at in range(0, share, group)
            ],
            0,
        ).astype(BF16)
        for which in range(2)
    ]
    mask = column_mask(all_rows, group, lambda place: place)
    term_qkv, term_out = column_part(
        x, cot, mask, gain_ref[...], w_ref, wo_ref, weights, grads_ref
    )
    for i in range(3):
        at = i * width
        terms_ref[:, at : at + HW] = row_qkv_ref[:, i * HW : (i + 1) * HW]
        terms_ref[:, at + HW : at + 2 * HW] = term_qkv[:, i * HW : (i + 1) * HW]
    terms_ref[:HW, 3 * width :] = row_out_ref[...]
    terms_ref[HW:, 3 * width :] = term_out


def column_chip_kernel(
    x_ref, cot_ref, near_1, near_2, near_3, far_ref, last_ref, gain_ref, w_ref, wo_ref, row_out_ref,
    send_ref, keep_ref, grads_ref,
):
    chip, core, _ = here()
    share = far_ref.shape[2]
    half = pl.ds(pl.multiple_of(core * share, share), share)
    at = pl.ds(pl.multiple_of((chip * 2 + core) * share, share), share)
    group = math.gcd(share, 16)

    def tokens(which, mine):
        pieces = [mine[at, :], far_ref[0, which]]
        fars = last_ref[which], far_ref[1, which], far_ref[2, which]
        for near, far in zip((near_1, near_2, near_3), fars):
            pieces += [near[which, half, :], far]
        starts = range(0, share, group)
        return jnp.concatenate(
            [piece[start : start + group] for start in starts for piece in pieces], 0
        )

    def row_of(place):
        step = (4 - (place >> 1)) & 3
        return ((step ^ chip) << 1) + ((place & 1) ^ core)

    mask = column_mask(2 * (len(CHIP_STEPS) + 1), group, row_of)
    term_qkv, term_out = column_part(
        tokens(0, x_ref), tokens(1, cot_ref), mask, gain_ref[...], w_ref, wo_ref, (), grads_ref
    )
    chips = send_ref.shape[0]
    refs = send_ref, keep_ref
    out_lanes = slice(3 * HW, send_ref.shape[2])
    split_cores(term_qkv, *refs, slice(0, chips), slice(0, 3 * HW))
    split_cores(row_out_ref[...], *refs, slice(0, chips // 2), out_lanes)
    split_cores(term_out, *refs, slice(chips // 2, chips), out_lanes)


def other_core(near, share):
    at = pl.ds(pl.multiple_of((1 - here()[1]) * share, share), share)
    return near[:, at, :]


def far_kernel(x_ref, cot_ref, near_2, near_3, far_ref):
    chip, core, _ = here()
    share = far_ref.shape[2]
    at = pl.ds(pl.multiple_of((chip * 2 + 1 - core) * share, share), share)
    far_ref[0, 0], far_ref[0, 1] = x_ref[at, :], cot_ref[at, :]
    for i, near in enumerate((near_2, near_3)):
        far_ref[i + 1] = other_core(near, share)


def last_far_kernel(near_1, far_ref):
    far_ref[...] = other_core(near_1, far_ref.shape[1])


def back_kernel(grads_ref, w_ref, back_ref):
    grad_hidden = dot_nt(grads_ref[...], w_ref[...])
    all_rows, share, width = back_ref.shape
    group = math.gcd(share, 16)
    block = all_rows * group
    for i in range(share // group):
        piece = grad_hidden[i * block : (i + 1) * block].reshape(all_rows, group, width)
        back_ref[:, i * group : (i + 1) * group, :] = piece.astype(BF16)


def back_chip_kernel(grads_ref, w_ref, send_ref, keep_ref):
    grad_hidden = dot_nt(grads_ref[...], w_ref[...]).astype(BF16)
    chips, share, width = keep_ref.shape
    group = math.gcd(share, 16)
    block = 2 * chips * group
    for i in range(share // group):
        piece = grad_hidden[i * block : (i + 1) * block].reshape(chips, 2, group, width)
        at = slice(i * group, (i + 1) * group)
        keep_ref[:, at, :], send_ref[:, at, :] = piece[:, 0], piece[:, 1]


def back_pack_kernel(keep_ref, got_ref, *targets):
    share = keep_ref.shape[1]
    core = here()[1]
    kept_at = pl.ds(pl.multiple_of(core * share, share), share)
    got_at = pl.ds(pl.multiple_of((1 - core) * share, share), share)
    for i, target in enumerate(targets):
        target[kept_at, :] = keep_ref[i]
        target[got_at, :] = got_ref[i]


def input_kernel(base_ref, normed_ref, inverse_ref, gain_ref, back_ref, grad_ref):
    grad_ref[...] = input_grad(
        base_ref[...], normed_ref[...], inverse_ref[...], back_ref[...].astype(F32) * gain_ref[...]
    ).astype(BF16)


def input_grad(base, normed, inverse_rms, grad_normed):
    projected = jnp.mean(grad_normed * normed, -1, keepdims=True)
    return base + inverse_rms * (grad_normed - normed * projected)


def input_chip_kernel(
    base_ref, normed_ref, inverse_ref, gain_ref, own_ref, got_1, got_2, got_3,
    grad_any, grad_ref, sems,
):
    chip = here()[0]
    count = own_ref.shape[0]
    copies = []
    for i, (step, back_ref) in enumerate(zip((0, *CHIP_STEPS), (own_ref, got_1, got_2, got_3))):
        at = pl.ds(pl.multiple_of((chip ^ step) * count, count), count)
        grad_normed = back_ref[...].astype(F32) * gain_ref[...]
        grad = input_grad(base_ref[at, :], normed_ref[at, :], inverse_ref[at, :], grad_normed)
        grad_ref[i] = grad.astype(BF16)
        copies += started(pltpu.make_async_copy(grad_ref.at[i], grad_any.at[at, :], sems.at[i]))
    finished(*copies)


def pack_kernel(x_any, cot_any, off_1, off_2, off_3, sems):
    chip = here()[0]
    count = off_1.shape[1]
    copies = []
    for i, (step, target) in enumerate(zip(CHIP_STEPS, (off_1, off_2, off_3))):
        at = pl.ds(pl.multiple_of((chip ^ step) * count, count), count)
        for which, source in enumerate((x_any, cot_any)):
            copies.append(
                pltpu.make_async_copy(source.at[at, :], target.at[which], sems.at[2 * i + which])
            )
    finished(*started(*copies))


def split_rows(total, axis):
    upper = (here()[2] & 1) == 1
    low, high = jnp.split(total, 2, axis)
    return jnp.where(upper, low, high).astype(BF16), jnp.where(upper, high, low)


def row_cores_kernel(keep_1, keep_2, got_1, got_2, send_ref, kept_ref):
    total = [
        keep_ref[...].astype(F32) + got_ref[...].astype(F32)
        for keep_ref, got_ref in ((keep_1, got_1), (keep_2, got_2))
    ]
    send_ref[...], kept_ref[...] = split_rows(jnp.concatenate(total, 2), 1)


def cores_kernel(keep_ref, got_ref, send_ref, kept_ref, *targets):
    chip, cut = here()[0], kept_ref.shape[2]
    first = keep_ref[:, :, :cut].astype(F32) + got_ref[:, :, :cut].astype(F32)
    send_ref[...], kept_ref[...] = split_rows(first, 1)
    for step, target in zip((0, *CHIP_STEPS), targets):
        there = chip ^ step
        total = keep_ref[there, :, cut:].astype(F32) + got_ref[there, :, cut:].astype(F32)
        target[...] = total.astype(target.dtype)


def pair_kernel(kept_ref, got_ref, row_kept, row_got, *targets):
    chip, cut = here()[0], kept_ref.shape[2]
    for step, target in zip((0, *CHIP_STEPS), targets):
        there = chip ^ step
        total = kept_ref[there] + got_ref[there].astype(F32)
        target[:, :cut] = total.astype(target.dtype)
        total = row_kept[there] + row_got[there].astype(F32)
        target[:, cut:] = total.astype(target.dtype)


def layer_sum(own_ref, got_1, got_2, got_3):
    return own_ref[...] + (
        (got_1[...].astype(F32) + got_2[...].astype(F32)) + got_3[...].astype(F32)
    )


def layer_kernel(own_ref, got_1, got_2, got_3, send_ref, kept_ref):
    send_ref[...], kept_ref[...] = split_rows(layer_sum(own_ref, got_1, got_2, got_3), 0)


def join_kernel(own_ref, got_1, got_2, got_3, kept_ref, got_ref, out_ref):
    total = layer_sum(own_ref, got_1, got_2, got_3).astype(BF16)
    cut, width = FIRST_PART, kept_ref.shape[1]
    out_ref[:, :cut] = total[:, :cut]
    out_ref[:, cut : cut + width] = (kept_ref[...] + got_ref[...].astype(F32)).astype(BF16)
    out_ref[:, cut + width :] = total[:, cut:]


def add_kernel(kept_ref, got_ref, out_ref):
    out_ref[...] = (kept_ref[...].astype(F32) + got_ref[...].astype(F32)).astype(BF16)


def result_kernel(held_ref, got_ref, w_ref, gain_ref, qkv_ref, out_ref, grad_ref):
    rows = qkv_ref.shape[0]
    chip, core, layer = here()
    at = (chip * 2 + core) * rows
    upper = (layer & 1) == 1
    half = rows // 2
    width = out_ref.shape[1]

    def ordered(lanes):
        held, got = held_ref[:, lanes].astype(F32), got_ref[:, lanes].astype(F32)
        return (jnp.where(upper, got, held), jnp.where(upper, held, got))

    row_at = 3 * HW + width
    for i in range(3):
        for at_from, at_to in ((row_at + i * HW, i * width), (i * HW, i * width + HW)):
            to = slice(at_to, at_to + HW)
            qkv_ref[:half, to], qkv_ref[half:, to] = ordered(slice(at_from, at_from + HW))
    out_ref[:half], out_ref[half:] = ordered(slice(3 * HW, row_at))
    total = jnp.sum(qkv_ref[...] * w_ref[...].astype(F32), -1, keepdims=True)
    shape = (rows, gain_ref.shape[1])
    row = lax.broadcasted_iota(jnp.int32, shape, 0)
    feature = lax.broadcasted_iota(jnp.int32, shape, 1)
    gain = jnp.sum(jnp.where(feature == row + at, gain_ref[...], 0.0), -1, keepdims=True)
    shape = (rows, grad_ref.shape[1])
    same = lax.broadcasted_iota(jnp.int32, shape, 0) == lax.broadcasted_iota(jnp.int32, shape, 1)
    grad_ref[...] = jnp.sum(jnp.where(same, total / gain, 0.0), 0, keepdims=True)


def call(kernel, name, ins, outs, scratch=(), vmem=SMALL_VMEM, out_specs=None):
    out_specs = out_specs or [VMEM] * len(outs)
    places = [{id(HBM): pltpu.HBM, id(PINNED): pltpu.VMEM}.get(id(spec)) for spec in out_specs]
    outs = [place(*out) if place else shaped(*out) for place, out in zip(places, outs)]
    args = [
        pltpu.with_memory_space_constraint(array, pltpu.HBM) if spec is HBM else array
        for spec, array in ins
    ]
    return pl.pallas_call(
        kernel,
        out_shape=outs,
        in_specs=[spec for spec, _ in ins],
        out_specs=out_specs,
        scratch_shapes=scratch,
        name=name,
        cost_estimate=pl.CostEstimate(flops=0, bytes_accessed=0, transcendentals=0),
        compiler_params=pltpu.CompilerParams(vmem_limit_bytes=vmem),
    )(*args)


def swap(array, axis, bits):
    count = lax.axis_size(axis)
    return lax.ppermute(array, axis, [(i, i ^ bits) for i in range(count)])


def cross_chips(*offs):
    return [swap(off, "seq", 2 * step) for off, step in zip(offs, CHIP_STEPS)]


def add_two(kept, got, name):
    (total,) = call(add_kernel, name, [(VMEM, kept), (VMEM, got)], [(kept.shape, BF16)])
    return total


def body(inputs, norm_gain, qkv_weight, out_weight, out_cotan):
    columns, width = inputs.shape[2:]
    n = lax.axis_size("seq")
    m = lax.axis_size("dp")
    share = columns // n
    row_share = width // n
    row_width, col_width = 3 * HW, 3 * HW + width
    x = inputs.reshape(columns, width)
    cot = out_cotan.reshape(columns, width)
    gain = norm_gain.reshape(1, width)
    chips = 4
    layered = n == 2 * chips and m == 4 and row_share == share
    weight_scratch = [
        pltpu.VMEM((1, width), F32),
        pltpu.VMEM((width, 3 * HW), BF16),
        pltpu.VMEM((HW, width), BF16),
    ]
    weights = [(HBM, gain), (HBM, qkv_weight), (HBM, out_weight)]
    col_outs = [((columns, 3 * HW), BF16), ((width, 3 * HW), BF16)]

    if layered:
        packed = call(
            pack_kernel,
            "pack_columns",
            [(HBM, x), (HBM, cot)],
            [((2, 2 * share, width), BF16)] * 3,
            [pltpu.SemaphoreType.DMA((6,))],
            out_specs=[ANY] * 3,
        )
        near = cross_chips(*packed)
        x_first, _ = lax.optimization_barrier((x, packed[0]))
    else:
        outgoing = jnp.stack([x.reshape(n, share, width), cot.reshape(n, share, width)], 1)
        moved = lax.all_to_all(outgoing, "seq", split_axis=0, concat_axis=0, tiled=True)
        x_first = x

    row_outs = [
        ((HW, width), BF16),
        ((columns, width), F32), ((columns, width), F32), ((columns, 1), F32),
        ((columns, width), BF16), ((columns, width), BF16),
    ]
    if layered:
        cut = row_width // 2
        split_outs = [((chips, row_share, cut), BF16)] * 4
        handed_outs = [
            ((row_share, 3 * width), BF16), ((width, 3 * HW), BF16), ((HW, width), BF16),
        ]
        row_outs = [*split_outs, *handed_outs, *row_outs]
        specs = [VMEM] * 4 + [PINNED] * (len(row_outs) - 4)
    else:
        row_outs = [((width, row_width), BF16), *row_outs]
        specs = [VMEM] * len(row_outs)
    *row_terms, row_out, base, normed, inverse_rms, x_near, cot_near = call(
        row_chip_kernel if layered else row_kernel,
        "row_heads",
        [(HBM, x_first), (HBM, cot), *weights],
        row_outs,
        [
            *weight_scratch,
            pltpu.VMEM((columns, HW), F32),
            pltpu.VMEM((columns, HW), F32),
            pltpu.VMEM((columns, 3 * HW), BF16),
            pltpu.SemaphoreType.DMA((12,)),
        ],
        BIG_VMEM,
        specs,
    )
    if layered:
        *row_terms, weight_rows, col_weight, col_out_weight = row_terms
        row_sent = [swap(one, "seq", 1) for one in row_terms[:2]]
        half_block = (chips, row_share // 2, row_width)
        row_next, row_kept = call(
            row_cores_kernel,
            "row_add_cores",
            [(VMEM, one) for one in (*row_terms[2:], *row_sent)],
            [(half_block, BF16), (half_block, F32)],
            out_specs=[VMEM, PINNED],
        )
        col_weight, row_kept = lax.optimization_barrier((col_weight, row_kept))
        (far,) = call(
            far_kernel,
            "pack_other_core",
            [(VMEM, one) for one in (x_near, cot_near, *near[1:])],
            [((3, 2, share, width), BF16)],
        )
        near[0], _ = lax.optimization_barrier((near[0], far))
        (last,) = call(
            last_far_kernel,
            "pack_other_core_last",
            [(VMEM, near[0])],
            [((2, share, width), BF16)],
        )
        send, keep, col_grads = call(
            column_chip_kernel,
            "column_heads",
            [
                (VMEM, one)
                for one in (
                    x_near, cot_near, *near, swap(far, "seq", 1), swap(last, "seq", 1),
                    gain, col_weight, col_out_weight, row_out,
                )
            ],
            [((chips, row_share, col_width), BF16)] * 2 + [col_outs[0]],
            vmem=BIG_VMEM,
            out_specs=[VMEM, VMEM, PINNED],
        )
        back_send, back_keep = call(
            back_chip_kernel,
            "column_grad_hidden",
            [(VMEM, col_grads), (VMEM, col_weight)],
            [((chips, share, width), BF16)] * 2,
        )
        row_next, _ = lax.optimization_barrier((row_next, send))
        keep, back_keep = lax.optimization_barrier((keep, back_keep))
        first_half = (chips, row_share // 2, FIRST_PART)
        second = (row_share, col_width - FIRST_PART)
        to_next, kept, owned, *off = call(
            cores_kernel,
            "column_add_cores",
            [(VMEM, keep), (VMEM, swap(send, "seq", 1))],
            [(first_half, BF16), (first_half, F32), (second, F32)] + [(second, BF16)] * 3,
            out_specs=[VMEM, PINNED, PINNED, VMEM, VMEM, VMEM],
        )
        got = cross_chips(*off)
        back = call(
            back_pack_kernel,
            "pack_grad_hidden",
            [(VMEM, back_keep), (VMEM, swap(back_send, "seq", 1))],
            [((2 * share, width), BF16)] * 4,
        )
        row_kept, *back = lax.optimization_barrier((row_kept, *back))
        joint = (row_share // 2, FIRST_PART + row_width)
        first_owned, *off = call(
            pair_kernel,
            "first_add_pair",
            [
                (VMEM, one)
                for one in (kept, swap(to_next, "dp", 1), row_kept, swap(row_next, "dp", 1))
            ],
            [(joint, F32)] + [(joint, BF16)] * 3,
            out_specs=[PINNED, VMEM, VMEM, VMEM],
        )
        first_got = cross_chips(*off)
        second_half = (row_share // 2, second[1])
        to_next, kept = call(
            layer_kernel,
            "second_add_chips",
            [(VMEM, one) for one in (owned, *got)],
            [(second_half, BF16), (second_half, F32)],
            out_specs=[VMEM, PINNED],
        )
        (pair_sum,) = call(
            join_kernel,
            "join_terms",
            [(VMEM, one) for one in (first_owned, *first_got, kept, swap(to_next, "dp", 1))],
            [((row_share // 2, col_width + row_width), BF16)],
        )
        *back, pair_sum = lax.optimization_barrier((*back, pair_sum))
        held = add_two(pair_sum, swap(pair_sum, "dp", 2), "add_pairs")
        other = swap(held, "dp", 1)
        (grad,) = call(
            input_chip_kernel,
            "input_grad",
            [
                (VMEM, one)
                for one in (base, normed, inverse_rms, gain, back[0], *cross_chips(*back[1:]))
            ],
            [((columns, width), BF16)],
            [pltpu.VMEM((chips, 2 * share, width), BF16), pltpu.SemaphoreType.DMA((chips,))],
            out_specs=[HBM],
        )
        sum_qkv, sum_out, sum_gain = call(
            result_kernel,
            "result",
            [(VMEM, held), (VMEM, other), (VMEM, weight_rows), (VMEM, gain)],
            [((row_share, 3 * width), F32), ((row_share, width), F32), ((1, row_share), F32)],
        )
        sum_gain = sum_gain.reshape(row_share)
    else:
        terms, *col_grads = call(
            column_kernel,
            "column_heads",
            [(ANY, moved), *weights, (VMEM, row_terms[0]), (VMEM, row_out)],
            [((width, 4 * width), BF16), *col_outs],
            [
                pltpu.VMEM((n, 2, share, width), BF16),
                weight_scratch[0],
                weight_scratch[2],
                pltpu.SemaphoreType.DMA((6,)),
            ],
            BIG_VMEM,
        )
        (back,) = call(
            back_kernel,
            "column_grad_hidden",
            [(VMEM, one) for one in col_grads],
            [((n, share, width), BF16)],
        )
        returned = lax.all_to_all(back, "seq", split_axis=0, concat_axis=0, tiled=True)
        (grad,) = call(
            input_kernel,
            "input_grad",
            [
                (VMEM, base), (VMEM, normed), (VMEM, inverse_rms), (VMEM, gain),
                (VMEM, returned.reshape(columns, width)),
            ],
            [((columns, width), BF16)],
        )
        terms = lax.all_to_all(
            terms.reshape(n, row_share, 4 * width), "seq", split_axis=0, concat_axis=0, tiled=True
        )
        total = jnp.sum(terms.astype(F32), 0)
        for step in range(m.bit_length() - 1):
            sent = total.astype(BF16)
            total = sent.astype(F32) + swap(sent, "dp", 1 << step).astype(F32)
        sum_qkv, sum_out = total[:, : 3 * width], total[:, 3 * width :]
        here_at = lax.axis_index("seq") * row_share
        own_gain = lax.dynamic_slice_in_dim(norm_gain, here_at, row_share, 0)
        own_weight = lax.dynamic_slice_in_dim(qkv_weight, here_at, row_share, 0)
        sum_gain = jnp.sum(sum_qkv * own_weight.astype(F32), -1) / own_gain
    return (grad.reshape(inputs.shape), sum_qkv, sum_out, sum_gain)


def solution(mesh):
    return jax.shard_map(
        body,
        mesh=mesh,
        in_specs=(P("dp", "seq", None, None), P(), P(), P(), P("dp", "seq", None, None)),
        out_specs=(P("dp", "seq", None, None), P("seq", None), P("seq", None), P("seq")),
        check_vma=False,
    )
```

```python
import math

import jax
import jax.numpy as jnp
from jax import lax
from jax.experimental import pallas as pl
from jax.experimental.pallas import tpu as pltpu
from jax.sharding import PartitionSpec as P

H = 8
HD = 64
HH = H // 2
HW = HH * HD
SCALE = HD ** (-0.5)
F32 = jnp.float32
BF16 = jnp.bfloat16
QUERY_BLOCK = 128
BIG_VMEM = 20 * 1024 * 1024
SMALL_VMEM = 8 * 1024 * 1024
ANY = pl.BlockSpec(memory_space=pl.ANY)
VMEM = pl.BlockSpec(memory_space=pltpu.VMEM)
HBM = pl.BlockSpec(memory_space=pltpu.HBM)
CHIP_STEPS = (3, 2, 1)
FIRST_PART = 256
PINNED = pl.BlockSpec(memory_space=pltpu.VMEM)
shaped = jax.ShapeDtypeStruct


def here():
    device = lax.axis_index("seq")
    return device >> 1, device & 1, lax.axis_index("dp")


def dot_nn(a, b):
    return lax.dot_general(a, b, (((1,), (0,)), ((), ())), preferred_element_type=F32)


def dot_nt(a, b):
    return lax.dot_general(a, b, (((1,), (1,)), ((), ())), preferred_element_type=F32)


def rms_parts(x):
    inverse_rms = lax.rsqrt(jnp.mean(x * x, -1, keepdims=True) + 1e-05)
    return inverse_rms, x * inverse_rms


def transposed(x):
    block = math.gcd(x.shape[1], 256)
    eye = (
        lax.broadcasted_iota(jnp.int32, (block, block), 0)
        == lax.broadcasted_iota(jnp.int32, (block, block), 1)
    ).astype(F32).astype(BF16)
    parts = [
        dot_nt(eye, x[:, at : at + block]).astype(BF16) for at in range(0, x.shape[1], block)
    ]
    return parts[0] if len(parts) == 1 else jnp.concatenate(parts, 0)


def head_pair(x):
    lane = lax.broadcasted_iota(jnp.int32, x.shape, 1)
    zero = jnp.zeros_like(x)
    return jnp.concatenate([jnp.where(lane < HD, x, zero), jnp.where(lane < HD, zero, x)], 0)


def both_heads(both, count):
    return jnp.concatenate([both[:HD, :count], both[HD:, count:]], 0)


def pair_steps(items, mask_rows, mask):
    count = items[0][2].shape[1]
    scores = [dot_nt(k, q2) for q2, _, _, k, _, _, _ in items]
    prob_grads = [dot_nt(v, g2) for _, g2, _, _, v, _, _ in items]
    probs = []
    for score in scores:
        first = score.shape[0] - mask_rows
        tail = jnp.where(mask, score[first:], -1e30)
        score = tail if first == 0 else jnp.concatenate([score[:first], tail], 0)
        exponent = jnp.exp(score - jnp.max(score, 0, keepdims=True))
        probs.append(exponent * (1.0 / jnp.sum(exponent, 0, keepdims=True)))
    weights = [prob.astype(BF16) for prob in probs]
    attended = [
        both_heads(dot_nn(item[6], weight), count).astype(BF16)
        for item, weight in zip(items, weights)
    ]
    score_grads = []
    for item, att, prob, prob_grad in zip(items, attended, probs, prob_grads):
        product = item[2].astype(F32) * att.astype(F32)
        delta = [jnp.sum(part, 0, keepdims=True) for part in (product[:HD], product[HD:])]
        score_grads.append((prob * (prob_grad - jnp.concatenate(delta, 1))).astype(BF16))
    grad_q = [
        (both_heads(dot_nn(item[5], score_grad), count) * SCALE).astype(BF16)
        for item, score_grad in zip(items, score_grads)
    ]
    grad_k = [dot_nn(score_grad, item[0]) for item, score_grad in zip(items, score_grads)]
    grad_v = [dot_nn(weight, item[1]) for item, weight in zip(items, weights)]
    return list(zip(attended, grad_q, grad_k, grad_v))


def split_cores(piece, send_ref, keep_ref, chips, lanes):
    rows = send_ref.shape[1]
    parts = piece.reshape(chips.stop - chips.start, 2, rows, piece.shape[1])
    even, odd = parts[:, 0], parts[:, 1]
    first = here()[1] == 0
    send_ref[chips, :, lanes] = jnp.where(first, odd, even)
    keep_ref[chips, :, lanes] = jnp.where(first, even, odd)


def qkv_copies(wqkv_ref, w_ref, sems, second):
    width = wqkv_ref.shape[0]
    return [
        pltpu.make_async_copy(
            wqkv_ref.at[:, pl.ds(i * width + second * HW, HW)],
            w_ref.at[:, pl.ds(i * HW, HW)],
            sems.at[i],
        )
        for i in range(3)
    ]


def weight_copies(wqkv_ref, wout_ref, w_ref, wo_ref, sems, second):
    out_rows = wout_ref.at[pl.ds(second * HW, HW), :]
    return [
        *qkv_copies(wqkv_ref, w_ref, sems, second),
        pltpu.make_async_copy(out_rows, wo_ref, sems.at[3]),
    ]


def started(*copies):
    for copy in copies:
        copy.start()
    return copies


def finished(*copies):
    for copy in copies:
        copy.wait()


def project(hidden, cot, w_ref, wo_ref):
    projected = dot_nn(hidden, w_ref[...]).astype(BF16)
    q, k, v = [projected[:, i * HW : (i + 1) * HW] for i in range(3)]
    g = dot_nt(cot, wo_ref[...]).astype(BF16)
    return q * jnp.asarray(SCALE, BF16), k, v, g


def row_part(
    x_any, cot_any, gain_any, wqkv_any, wout_any,
    out_ref, base_ref, normed_ref, inverse_ref, x_ref, cot_ref,
    gain_ref, w_ref, wo_ref, dk_ref, dv_ref, grads_ref, sems,
):
    first = started(
        pltpu.make_async_copy(x_any, x_ref, sems.at[4]),
        pltpu.make_async_copy(gain_any, gain_ref, sems.at[5]),
    )
    later = started(
        *weight_copies(wqkv_any, wout_any, w_ref, wo_ref, sems, 0),
        pltpu.make_async_copy(cot_any, cot_ref, sems.at[6]),
    )
    dk_ref[...] = jnp.zeros_like(dk_ref)
    dv_ref[...] = jnp.zeros_like(dv_ref)
    finished(*first)
    tokens = x_ref.shape[0]
    inverse_ref[...], normed_ref[...] = rms_parts(x_ref[...].astype(F32))
    hidden = (normed_ref[...] * gain_ref[...]).astype(BF16)
    hidden_t = transposed(hidden)
    finished(*later)
    cot = cot_ref[...]
    q, k, v, g = project(hidden, cot, w_ref, wo_ref)
    kt, vt, gt = transposed(k), transposed(v), transposed(g)
    step = math.gcd(tokens, QUERY_BLOCK)
    query = lax.broadcasted_iota(jnp.int32, (step, 2 * step), 1) % step
    mask = query >= lax.broadcasted_iota(jnp.int32, (step, 2 * step), 0)
    pairs = [slice(i * 2 * HD, (i + 1) * 2 * HD) for i in range(HH // 2)]
    att_blocks, dq_blocks = [], []
    for start in range(0, tokens, step):
        rows, keys = slice(start, start + step), slice(0, start + step)
        items = [
            (
                head_pair(q[rows, lanes]), head_pair(g[rows, lanes]), gt[lanes, rows],
                k[keys, lanes], v[keys, lanes], kt[lanes, keys], vt[lanes, keys],
            )
            for lanes in pairs
        ]
        results = pair_steps(items, step, mask)
        for lanes, (_, _, dk, dv) in zip(pairs, results):
            dk_ref[keys, lanes] += dk
            dv_ref[keys, lanes] += dv
        att_blocks.append(jnp.concatenate([result[0] for result in results], 0))
        dq_blocks.append(jnp.concatenate([result[1] for result in results], 0))
    grads_ref[:, :HW] = transposed(jnp.concatenate(dq_blocks, 1))
    grads_ref[:, HW : 2 * HW] = dk_ref[...].astype(BF16)
    grads_ref[:, 2 * HW :] = dv_ref[...].astype(BF16)
    term_qkv = dot_nn(hidden_t, grads_ref[...]).astype(BF16)
    out_ref[...] = dot_nn(jnp.concatenate(att_blocks, 1), cot).astype(BF16)
    grad_normed = dot_nt(grads_ref[...], w_ref[...]) * gain_ref[...]
    base_ref[...] = input_grad(
        cot_ref[...].astype(F32), normed_ref[...], inverse_ref[...], grad_normed
    )
    return term_qkv


def row_kernel(x_any, cot_any, gain_any, wqkv_any, wout_any, qkv_ref, *refs):
    qkv_ref[...] = row_part(x_any, cot_any, gain_any, wqkv_any, wout_any, *refs)


def row_chip_kernel(
    x_any, cot_any, gain_any, wqkv_any, wout_any,
    send_1, send_2, keep_1, keep_2, rows_ref, col_w_ref, col_wo_ref, *refs,
):
    chip, core, _ = here()
    sems, rows = refs[-1], rows_ref.shape[0]
    at = pl.multiple_of((chip * 2 + core) * rows, rows)
    handed = started(
        pltpu.make_async_copy(wqkv_any.at[pl.ds(at, rows), :], rows_ref, sems.at[7]),
        *weight_copies(wqkv_any, wout_any, col_w_ref, col_wo_ref, sems.at[pl.ds(8, 4)], 1),
    )
    term_qkv = row_part(x_any, cot_any, gain_any, wqkv_any, wout_any, *refs)
    chips, cut = send_1.shape[0], keep_1.shape[2]
    pieces = slice(0, chips), slice(0, cut)
    split_cores(term_qkv[:, :cut], send_1, keep_1, *pieces)
    split_cores(term_qkv[:, cut:], send_2, keep_2, *pieces)
    finished(*handed)


def column_part(x, cot, mask, gain, w_ref, wo_ref, weight_waits, grads_ref):
    tokens, block = x.shape[0], mask.shape[0]
    _, normed = rms_parts(x.astype(F32))
    hidden = (normed * gain).astype(BF16)
    hidden_t = transposed(hidden)
    finished(*weight_waits)
    q, k, v, g = project(hidden, cot, w_ref, wo_ref)
    kt, vt, gt = transposed(k), transposed(v), transposed(g)
    pairs = [slice(i * 2 * HD, (i + 1) * 2 * HD) for i in range(HH // 2)]
    blocks = [slice(at, at + block) for at in range(0, tokens, block)]
    items = [
        (
            head_pair(q[rows, lanes]), head_pair(g[rows, lanes]), gt[lanes, rows],
            k[rows, lanes], v[rows, lanes], kt[lanes, rows], vt[lanes, rows],
        )
        for lanes in pairs
        for rows in blocks
    ]
    results = pair_steps(items, block, mask)
    places = [(lanes, rows) for lanes in pairs for rows in blocks]
    for (lanes, rows), (_, _, dk, dv) in zip(places, results):
        grads_ref[rows, HW + lanes.start : HW + lanes.stop] = dk.astype(BF16)
        grads_ref[rows, 2 * HW + lanes.start : 2 * HW + lanes.stop] = dv.astype(BF16)
    by_pair = [results[i * len(blocks) : (i + 1) * len(blocks)] for i in range(len(pairs))]
    attended, grad_q = [
        jnp.concatenate([jnp.concatenate([r[i] for r in some], 1) for some in by_pair], 0)
        for i in range(2)
    ]
    grads_ref[:, :HW] = transposed(grad_q)
    term_qkv = dot_nn(hidden_t, grads_ref[...]).astype(BF16)
    term_out = dot_nn(attended, cot).astype(BF16)
    return term_qkv, term_out


def column_mask(all_rows, group, row_of):
    block = all_rows * group
    shape = (block, 2 * block)
    query = lax.broadcasted_iota(jnp.int32, shape, 1) % block
    key = lax.broadcasted_iota(jnp.int32, shape, 0)
    same_column = query % group == key % group
    return (row_of(query // group) >= row_of(key // group)) & same_column


def column_kernel(
    moved_any, gain_any, wqkv_any, wout_any, row_qkv_ref, row_out_ref,
    terms_ref, grads_ref, w_ref,
    moved_ref, gain_ref, wo_ref, sems,
):
    copies = started(
        pltpu.make_async_copy(moved_any, moved_ref, sems.at[4]),
        pltpu.make_async_copy(gain_any, gain_ref, sems.at[5]),
    )
    weights = started(*weight_copies(wqkv_any, wout_any, w_ref, wo_ref, sems, 1))
    finished(*copies)
    all_rows, _, share, width = moved_ref.shape
    group = math.gcd(share, 16)
    x, cot = [
        jnp.concatenate(
            [
                moved_ref[:, which, at : at + group, :].astype(F32).reshape(all_rows * group, width)
                for at in range(0, share, group)
            ],
            0,
        ).astype(BF16)
        for which in range(2)
    ]
    mask = column_mask(all_rows, group, lambda place: place)
    term_qkv, term_out = column_part(
        x, cot, mask, gain_ref[...], w_ref, wo_ref, weights, grads_ref
    )
    for i in range(3):
        at = i * width
        terms_ref[:, at : at + HW] = row_qkv_ref[:, i * HW : (i + 1) * HW]
        terms_ref[:, at + HW : at + 2 * HW] = term_qkv[:, i * HW : (i + 1) * HW]
    terms_ref[:HW, 3 * width :] = row_out_ref[...]
    terms_ref[HW:, 3 * width :] = term_out


def column_chip_kernel(
    x_ref, cot_ref, near_1, near_2, near_3, far_ref, last_ref, gain_ref, w_ref, wo_ref, row_out_ref,
    send_ref, keep_ref, grads_ref,
):
    chip, core, _ = here()
    share = far_ref.shape[2]
    half = pl.ds(pl.multiple_of(core * share, share), share)
    at = pl.ds(pl.multiple_of((chip * 2 + core) * share, share), share)
    group = math.gcd(share, 16)

    def tokens(which, mine):
        pieces = [mine[at, :], far_ref[0, which]]
        fars = last_ref[which], far_ref[1, which], far_ref[2, which]
        for near, far in zip((near_1, near_2, near_3), fars):
            pieces += [near[which, half, :], far]
        starts = range(0, share, group)
        return jnp.concatenate(
            [piece[start : start + group] for start in starts for piece in pieces], 0
        )

    def row_of(place):
        step = (4 - (place >> 1)) & 3
        return ((step ^ chip) << 1) + ((place & 1) ^ core)

    mask = column_mask(2 * (len(CHIP_STEPS) + 1), group, row_of)
    term_qkv, term_out = column_part(
        tokens(0, x_ref), tokens(1, cot_ref), mask, gain_ref[...], w_ref, wo_ref, (), grads_ref
    )
    chips = send_ref.shape[0]
    refs = send_ref, keep_ref
    out_lanes = slice(3 * HW, send_ref.shape[2])
    split_cores(term_qkv, *refs, slice(0, chips), slice(0, 3 * HW))
    split_cores(row_out_ref[...], *refs, slice(0, chips // 2), out_lanes)
    split_cores(term_out, *refs, slice(chips // 2, chips), out_lanes)


def other_core(near, share):
    at = pl.ds(pl.multiple_of((1 - here()[1]) * share, share), share)
    return near[:, at, :]


def far_kernel(x_ref, cot_ref, near_2, near_3, far_ref):
    chip, core, _ = here()
    share = far_ref.shape[2]
    at = pl.ds(pl.multiple_of((chip * 2 + 1 - core) * share, share), share)
    far_ref[0, 0], far_ref[0, 1] = x_ref[at, :], cot_ref[at, :]
    for i, near in enumerate((near_2, near_3)):
        far_ref[i + 1] = other_core(near, share)


def last_far_kernel(near_1, far_ref):
    far_ref[...] = other_core(near_1, far_ref.shape[1])


def back_kernel(grads_ref, w_ref, back_ref):
    grad_hidden = dot_nt(grads_ref[...], w_ref[...])
    all_rows, share, width = back_ref.shape
    group = math.gcd(share, 16)
    block = all_rows * group
    for i in range(share // group):
        piece = grad_hidden[i * block : (i + 1) * block].reshape(all_rows, group, width)
        back_ref[:, i * group : (i + 1) * group, :] = piece.astype(BF16)


def back_chip_kernel(grads_ref, w_ref, send_ref, keep_ref):
    grad_hidden = dot_nt(grads_ref[...], w_ref[...]).astype(BF16)
    chips, share, width = keep_ref.shape
    group = math.gcd(share, 16)
    block = 2 * chips * group
    for i in range(share // group):
        piece = grad_hidden[i * block : (i + 1) * block].reshape(chips, 2, group, width)
        at = slice(i * group, (i + 1) * group)
        keep_ref[:, at, :], send_ref[:, at, :] = piece[:, 0], piece[:, 1]


def back_pack_kernel(keep_ref, got_ref, *targets):
    share = keep_ref.shape[1]
    core = here()[1]
    kept_at = pl.ds(pl.multiple_of(core * share, share), share)
    got_at = pl.ds(pl.multiple_of((1 - core) * share, share), share)
    for i, target in enumerate(targets):
        target[kept_at, :] = keep_ref[i]
        target[got_at, :] = got_ref[i]


def input_kernel(base_ref, normed_ref, inverse_ref, gain_ref, back_ref, grad_ref):
    grad_ref[...] = input_grad(
        base_ref[...], normed_ref[...], inverse_ref[...], back_ref[...].astype(F32) * gain_ref[...]
    ).astype(BF16)


def input_grad(base, normed, inverse_rms, grad_normed):
    projected = jnp.mean(grad_normed * normed, -1, keepdims=True)
    return base + inverse_rms * (grad_normed - normed * projected)


def input_chip_kernel(
    base_ref, normed_ref, inverse_ref, gain_ref, own_ref, got_1, got_2, got_3,
    grad_any, grad_ref, sems,
):
    chip = here()[0]
    count = own_ref.shape[0]
    copies = []
    for i, (step, back_ref) in enumerate(zip((0, *CHIP_STEPS), (own_ref, got_1, got_2, got_3))):
        at = pl.ds(pl.multiple_of((chip ^ step) * count, count), count)
        grad_normed = back_ref[...].astype(F32) * gain_ref[...]
        grad = input_grad(base_ref[at, :], normed_ref[at, :], inverse_ref[at, :], grad_normed)
        grad_ref[i] = grad.astype(BF16)
        copies += started(pltpu.make_async_copy(grad_ref.at[i], grad_any.at[at, :], sems.at[i]))
    finished(*copies)


def pack_kernel(x_any, cot_any, off_1, off_2, off_3, sems):
    chip = here()[0]
    count = off_1.shape[1]
    copies = []
    for i, (step, target) in enumerate(zip(CHIP_STEPS, (off_1, off_2, off_3))):
        at = pl.ds(pl.multiple_of((chip ^ step) * count, count), count)
        for which, source in enumerate((x_any, cot_any)):
            copies.append(
                pltpu.make_async_copy(source.at[at, :], target.at[which], sems.at[2 * i + which])
            )
    finished(*started(*copies))


def split_rows(total, axis):
    upper = (here()[2] & 1) == 1
    low, high = jnp.split(total, 2, axis)
    return jnp.where(upper, low, high).astype(BF16), jnp.where(upper, high, low)


def row_cores_kernel(keep_1, keep_2, got_1, got_2, send_ref, kept_ref):
    total = [
        keep_ref[...].astype(F32) + got_ref[...].astype(F32)
        for keep_ref, got_ref in ((keep_1, got_1), (keep_2, got_2))
    ]
    send_ref[...], kept_ref[...] = split_rows(jnp.concatenate(total, 2), 1)


def cores_kernel(keep_ref, got_ref, send_ref, kept_ref, *targets):
    chip, cut = here()[0], kept_ref.shape[2]
    first = keep_ref[:, :, :cut].astype(F32) + got_ref[:, :, :cut].astype(F32)
    send_ref[...], kept_ref[...] = split_rows(first, 1)
    for step, target in zip((0, *CHIP_STEPS), targets):
        there = chip ^ step
        total = keep_ref[there, :, cut:].astype(F32) + got_ref[there, :, cut:].astype(F32)
        target[...] = total.astype(target.dtype)


def pair_kernel(kept_ref, got_ref, row_kept, row_got, *targets):
    chip, cut = here()[0], kept_ref.shape[2]
    for step, target in zip((0, *CHIP_STEPS), targets):
        there = chip ^ step
        total = kept_ref[there] + got_ref[there].astype(F32)
        target[:, :cut] = total.astype(target.dtype)
        total = row_kept[there] + row_got[there].astype(F32)
        target[:, cut:] = total.astype(target.dtype)


def layer_sum(own_ref, got_1, got_2, got_3):
    return own_ref[...] + (
        (got_1[...].astype(F32) + got_2[...].astype(F32)) + got_3[...].astype(F32)
    )


def layer_kernel(own_ref, got_1, got_2, got_3, send_ref, kept_ref):
    send_ref[...], kept_ref[...] = split_rows(layer_sum(own_ref, got_1, got_2, got_3), 0)


def join_kernel(own_ref, got_1, got_2, got_3, kept_ref, got_ref, out_ref):
    total = layer_sum(own_ref, got_1, got_2, got_3).astype(BF16)
    cut, width = FIRST_PART, kept_ref.shape[1]
    out_ref[:, :cut] = total[:, :cut]
    out_ref[:, cut : cut + width] = (kept_ref[...] + got_ref[...].astype(F32)).astype(BF16)
    out_ref[:, cut + width :] = total[:, cut:]


def add_kernel(kept_ref, got_ref, out_ref):
    out_ref[...] = (kept_ref[...].astype(F32) + got_ref[...].astype(F32)).astype(BF16)


def result_kernel(held_ref, got_ref, w_ref, gain_ref, qkv_ref, out_ref, grad_ref):
    rows = qkv_ref.shape[0]
    chip, core, layer = here()
    at = (chip * 2 + core) * rows
    upper = (layer & 1) == 1
    half = rows // 2
    width = out_ref.shape[1]

    def ordered(lanes):
        held, got = held_ref[:, lanes].astype(F32), got_ref[:, lanes].astype(F32)
        return (jnp.where(upper, got, held), jnp.where(upper, held, got))

    row_at = 3 * HW + width
    for i in range(3):
        for at_from, at_to in ((row_at + i * HW, i * width), (i * HW, i * width + HW)):
            to = slice(at_to, at_to + HW)
            qkv_ref[:half, to], qkv_ref[half:, to] = ordered(slice(at_from, at_from + HW))
    out_ref[:half], out_ref[half:] = ordered(slice(3 * HW, row_at))
    total = jnp.sum(qkv_ref[...] * w_ref[...].astype(F32), -1, keepdims=True)
    shape = (rows, gain_ref.shape[1])
    row = lax.broadcasted_iota(jnp.int32, shape, 0)
    feature = lax.broadcasted_iota(jnp.int32, shape, 1)
    gain = jnp.sum(jnp.where(feature == row + at, gain_ref[...], 0.0), -1, keepdims=True)
    shape = (rows, grad_ref.shape[1])
    same = lax.broadcasted_iota(jnp.int32, shape, 0) == lax.broadcasted_iota(jnp.int32, shape, 1)
    grad_ref[...] = jnp.sum(jnp.where(same, total / gain, 0.0), 0, keepdims=True)


def call(kernel, name, ins, outs, scratch=(), vmem=SMALL_VMEM, out_specs=None):
    out_specs = out_specs or [VMEM] * len(outs)
    places = [{id(HBM): pltpu.HBM, id(PINNED): pltpu.VMEM}.get(id(spec)) for spec in out_specs]
    outs = [place(*out) if place else shaped(*out) for place, out in zip(places, outs)]
    args = [
        pltpu.with_memory_space_constraint(array, pltpu.HBM) if spec is HBM else array
        for spec, array in ins
    ]
    return pl.pallas_call(
        kernel,
        out_shape=outs,
        in_specs=[spec for spec, _ in ins],
        out_specs=out_specs,
        scratch_shapes=scratch,
        name=name,
        cost_estimate=pl.CostEstimate(flops=0, bytes_accessed=0, transcendentals=0),
        compiler_params=pltpu.CompilerParams(vmem_limit_bytes=vmem),
    )(*args)


def swap(array, axis, bits):
    count = lax.axis_size(axis)
    return lax.ppermute(array, axis, [(i, i ^ bits) for i in range(count)])


def cross_chips(*offs):
    return [swap(off, "seq", 2 * step) for off, step in zip(offs, CHIP_STEPS)]


def add_two(kept, got, name):
    (total,) = call(add_kernel, name, [(VMEM, kept), (VMEM, got)], [(kept.shape, BF16)])
    return total


def body(inputs, norm_gain, qkv_weight, out_weight, out_cotan):
    columns, width = inputs.shape[2:]
    n = lax.axis_size("seq")
    m = lax.axis_size("dp")
    share = columns // n
    row_share = width // n
    row_width, col_width = 3 * HW, 3 * HW + width
    x = inputs.reshape(columns, width)
    cot = out_cotan.reshape(columns, width)
    gain = norm_gain.reshape(1, width)
    chips = 4
    layered = n == 2 * chips and m == 4 and row_share == share
    weight_scratch = [
        pltpu.VMEM((1, width), F32),
        pltpu.VMEM((width, 3 * HW), BF16),
        pltpu.VMEM((HW, width), BF16),
    ]
    weights = [(HBM, gain), (HBM, qkv_weight), (HBM, out_weight)]
    col_outs = [((columns, 3 * HW), BF16), ((width, 3 * HW), BF16)]

    if layered:
        packed = call(
            pack_kernel,
            "pack_columns",
            [(HBM, x), (HBM, cot)],
            [((2, 2 * share, width), BF16)] * 3,
            [pltpu.SemaphoreType.DMA((6,))],
            out_specs=[ANY] * 3,
        )
        near = cross_chips(*packed)
        x_first, _ = lax.optimization_barrier((x, packed[0]))
    else:
        outgoing = jnp.stack([x.reshape(n, share, width), cot.reshape(n, share, width)], 1)
        moved = lax.all_to_all(outgoing, "seq", split_axis=0, concat_axis=0, tiled=True)
        x_first = x

    row_outs = [
        ((HW, width), BF16),
        ((columns, width), F32), ((columns, width), F32), ((columns, 1), F32),
        ((columns, width), BF16), ((columns, width), BF16),
    ]
    if layered:
        cut = row_width // 2
        split_outs = [((chips, row_share, cut), BF16)] * 4
        handed_outs = [
            ((row_share, 3 * width), BF16), ((width, 3 * HW), BF16), ((HW, width), BF16),
        ]
        row_outs = [*split_outs, *handed_outs, *row_outs]
        specs = [VMEM] * 4 + [PINNED] * (len(row_outs) - 4)
    else:
        row_outs = [((width, row_width), BF16), *row_outs]
        specs = [VMEM] * len(row_outs)
    *row_terms, row_out, base, normed, inverse_rms, x_near, cot_near = call(
        row_chip_kernel if layered else row_kernel,
        "row_heads",
        [(HBM, x_first), (HBM, cot), *weights],
        row_outs,
        [
            *weight_scratch,
            pltpu.VMEM((columns, HW), F32),
            pltpu.VMEM((columns, HW), F32),
            pltpu.VMEM((columns, 3 * HW), BF16),
            pltpu.SemaphoreType.DMA((12,)),
        ],
        BIG_VMEM,
        specs,
    )
    if layered:
        *row_terms, weight_rows, col_weight, col_out_weight = row_terms
        row_sent = [swap(one, "seq", 1) for one in row_terms[:2]]
        half_block = (chips, row_share // 2, row_width)
        row_next, row_kept = call(
            row_cores_kernel,
            "row_add_cores",
            [(VMEM, one) for one in (*row_terms[2:], *row_sent)],
            [(half_block, BF16), (half_block, F32)],
            out_specs=[VMEM, PINNED],
        )
        col_weight, row_kept = lax.optimization_barrier((col_weight, row_kept))
        (far,) = call(
            far_kernel,
            "pack_other_core",
            [(VMEM, one) for one in (x_near, cot_near, *near[1:])],
            [((3, 2, share, width), BF16)],
        )
        near[0], _ = lax.optimization_barrier((near[0], far))
        (last,) = call(
            last_far_kernel,
            "pack_other_core_last",
            [(VMEM, near[0])],
            [((2, share, width), BF16)],
        )
        send, keep, col_grads = call(
            column_chip_kernel,
            "column_heads",
            [
                (VMEM, one)
                for one in (
                    x_near, cot_near, *near, swap(far, "seq", 1), swap(last, "seq", 1),
                    gain, col_weight, col_out_weight, row_out,
                )
            ],
            [((chips, row_share, col_width), BF16)] * 2 + [col_outs[0]],
            vmem=BIG_VMEM,
            out_specs=[VMEM, VMEM, PINNED],
        )
        back_send, back_keep = call(
            back_chip_kernel,
            "column_grad_hidden",
            [(VMEM, col_grads), (VMEM, col_weight)],
            [((chips, share, width), BF16)] * 2,
        )
        row_next, _ = lax.optimization_barrier((row_next, send))
        keep, back_keep = lax.optimization_barrier((keep, back_keep))
        first_half = (chips, row_share // 2, FIRST_PART)
        second = (row_share, col_width - FIRST_PART)
        to_next, kept, owned, *off = call(
            cores_kernel,
            "column_add_cores",
            [(VMEM, keep), (VMEM, swap(send, "seq", 1))],
            [(first_half, BF16), (first_half, F32), (second, F32)] + [(second, BF16)] * 3,
            out_specs=[VMEM, PINNED, PINNED, VMEM, VMEM, VMEM],
        )
        got = cross_chips(*off)
        back = call(
            back_pack_kernel,
            "pack_grad_hidden",
            [(VMEM, back_keep), (VMEM, swap(back_send, "seq", 1))],
            [((2 * share, width), BF16)] * 4,
        )
        row_kept, *back = lax.optimization_barrier((row_kept, *back))
        joint = (row_share // 2, FIRST_PART + row_width)
        first_owned, *off = call(
            pair_kernel,
            "first_add_pair",
            [
                (VMEM, one)
                for one in (kept, swap(to_next, "dp", 1), row_kept, swap(row_next, "dp", 1))
            ],
            [(joint, F32)] + [(joint, BF16)] * 3,
            out_specs=[PINNED, VMEM, VMEM, VMEM],
        )
        first_got = cross_chips(*off)
        second_half = (row_share // 2, second[1])
        to_next, kept = call(
            layer_kernel,
            "second_add_chips",
            [(VMEM, one) for one in (owned, *got)],
            [(second_half, BF16), (second_half, F32)],
            out_specs=[VMEM, PINNED],
        )
        (pair_sum,) = call(
            join_kernel,
            "join_terms",
            [(VMEM, one) for one in (first_owned, *first_got, kept, swap(to_next, "dp", 1))],
            [((row_share // 2, col_width + row_width), BF16)],
        )
        *back, pair_sum = lax.optimization_barrier((*back, pair_sum))
        held = add_two(pair_sum, swap(pair_sum, "dp", 2), "add_pairs")
        other = swap(held, "dp", 1)
        (grad,) = call(
            input_chip_kernel,
            "input_grad",
            [
                (VMEM, one)
                for one in (base, normed, inverse_rms, gain, back[0], *cross_chips(*back[1:]))
            ],
            [((columns, width), BF16)],
            [pltpu.VMEM((chips, 2 * share, width), BF16), pltpu.SemaphoreType.DMA((chips,))],
            out_specs=[HBM],
        )
        sum_qkv, sum_out, sum_gain = call(
            result_kernel,
            "result",
            [(VMEM, held), (VMEM, other), (VMEM, weight_rows), (VMEM, gain)],
            [((row_share, 3 * width), F32), ((row_share, width), F32), ((1, row_share), F32)],
        )
        sum_gain = sum_gain.reshape(row_share)
    else:
        terms, *col_grads = call(
            column_kernel,
            "column_heads",
            [(ANY, moved), *weights, (VMEM, row_terms[0]), (VMEM, row_out)],
            [((width, 4 * width), BF16), *col_outs],
            [
                pltpu.VMEM((n, 2, share, width), BF16),
                weight_scratch[0],
                weight_scratch[2],
                pltpu.SemaphoreType.DMA((6,)),
            ],
            BIG_VMEM,
        )
        (back,) = call(
            back_kernel,
            "column_grad_hidden",
            [(VMEM, one) for one in col_grads],
            [((n, share, width), BF16)],
        )
        returned = lax.all_to_all(back, "seq", split_axis=0, concat_axis=0, tiled=True)
        (grad,) = call(
            input_kernel,
            "input_grad",
            [
                (VMEM, base), (VMEM, normed), (VMEM, inverse_rms), (VMEM, gain),
                (VMEM, returned.reshape(columns, width)),
            ],
            [((columns, width), BF16)],
        )
        terms = lax.all_to_all(
            terms.reshape(n, row_share, 4 * width), "seq", split_axis=0, concat_axis=0, tiled=True
        )
        total = jnp.sum(terms.astype(F32), 0)
        for step in range(m.bit_length() - 1):
            sent = total.astype(BF16)
            total = sent.astype(F32) + swap(sent, "dp", 1 << step).astype(F32)
        sum_qkv, sum_out = total[:, : 3 * width], total[:, 3 * width :]
        here_at = lax.axis_index("seq") * row_share
        own_gain = lax.dynamic_slice_in_dim(norm_gain, here_at, row_share, 0)
        own_weight = lax.dynamic_slice_in_dim(qkv_weight, here_at, row_share, 0)
        sum_gain = jnp.sum(sum_qkv * own_weight.astype(F32), -1) / own_gain
    return (grad.reshape(inputs.shape), sum_qkv, sum_out, sum_gain)


def solution(mesh):
    return jax.shard_map(
        body,
        mesh=mesh,
        in_specs=(P("dp", "seq", None, None), P(), P(), P(), P("dp", "seq", None, None)),
        out_specs=(P("dp", "seq", None, None), P("seq", None), P("seq", None), P("seq")),
        check_vma=False,
    )
```

```python
import math

import jax
import jax.numpy as jnp
from jax import lax
from jax.experimental import pallas as pl
from jax.experimental.pallas import tpu as pltpu
from jax.sharding import PartitionSpec as P

H = 8
HD = 64
HH = H // 2
HW = HH * HD
SCALE = HD ** (-0.5)
F32 = jnp.float32
BF16 = jnp.bfloat16
QUERY_BLOCK = 128
BIG_VMEM = 20 * 1024 * 1024
SMALL_VMEM = 8 * 1024 * 1024
ANY = pl.BlockSpec(memory_space=pl.ANY)
VMEM = pl.BlockSpec(memory_space=pltpu.VMEM)
HBM = pl.BlockSpec(memory_space=pltpu.HBM)
CHIP_STEPS = (3, 2, 1)
FIRST_PART = 512
SWAP_PIECES = (384, 384, 256, 256)
PINNED = pl.BlockSpec(memory_space=pltpu.VMEM)
shaped = jax.ShapeDtypeStruct


def here():
    device = lax.axis_index("seq")
    return device >> 1, device & 1, lax.axis_index("dp")


def dot_nn(a, b):
    return lax.dot_general(a, b, (((1,), (0,)), ((), ())), preferred_element_type=F32)


def dot_nt(a, b):
    return lax.dot_general(a, b, (((1,), (1,)), ((), ())), preferred_element_type=F32)


def rms_parts(x):
    inverse_rms = lax.rsqrt(jnp.mean(x * x, -1, keepdims=True) + 1e-05)
    return inverse_rms, x * inverse_rms


def transposed(x):
    block = math.gcd(x.shape[1], 256)
    eye = (
        lax.broadcasted_iota(jnp.int32, (block, block), 0)
        == lax.broadcasted_iota(jnp.int32, (block, block), 1)
    ).astype(F32).astype(BF16)
    parts = [
        dot_nt(eye, x[:, at : at + block]).astype(BF16) for at in range(0, x.shape[1], block)
    ]
    return parts[0] if len(parts) == 1 else jnp.concatenate(parts, 0)


def head_pair(x):
    lane = lax.broadcasted_iota(jnp.int32, x.shape, 1)
    zero = jnp.zeros_like(x)
    return jnp.concatenate([jnp.where(lane < HD, x, zero), jnp.where(lane < HD, zero, x)], 0)


def both_heads(both, count):
    return jnp.concatenate([both[:HD, :count], both[HD:, count:]], 0)


def pair_steps(items, mask_rows, mask):
    count = items[0][2].shape[1]
    scores = [dot_nt(k, q2) for q2, _, _, k, _, _, _ in items]
    prob_grads = [dot_nt(v, g2) for _, g2, _, _, v, _, _ in items]
    probs = []
    for score in scores:
        first = score.shape[0] - mask_rows
        tail = jnp.where(mask, score[first:], -1e30)
        score = tail if first == 0 else jnp.concatenate([score[:first], tail], 0)
        exponent = jnp.exp(score - jnp.max(score, 0, keepdims=True))
        probs.append(exponent * (1.0 / jnp.sum(exponent, 0, keepdims=True)))
    weights = [prob.astype(BF16) for prob in probs]
    attended = [
        both_heads(dot_nn(item[6], weight), count).astype(BF16)
        for item, weight in zip(items, weights)
    ]
    score_grads = []
    for item, att, prob, prob_grad in zip(items, attended, probs, prob_grads):
        product = item[2].astype(F32) * att.astype(F32)
        delta = [jnp.sum(part, 0, keepdims=True) for part in (product[:HD], product[HD:])]
        score_grads.append((prob * (prob_grad - jnp.concatenate(delta, 1))).astype(BF16))
    grad_q = [
        (both_heads(dot_nn(item[5], score_grad), count) * SCALE).astype(BF16)
        for item, score_grad in zip(items, score_grads)
    ]
    grad_k = [dot_nn(score_grad, item[0]) for item, score_grad in zip(items, score_grads)]
    grad_v = [dot_nn(weight, item[1]) for item, weight in zip(items, weights)]
    return list(zip(attended, grad_q, grad_k, grad_v))


def split_cores(piece, send_ref, keep_ref, chips, lanes):
    rows = send_ref.shape[1]
    parts = piece.reshape(chips.stop - chips.start, 2, rows, piece.shape[1])
    even, odd = parts[:, 0], parts[:, 1]
    first = here()[1] == 0
    send_ref[chips, :, lanes] = jnp.where(first, odd, even)
    keep_ref[chips, :, lanes] = jnp.where(first, even, odd)


def qkv_copies(wqkv_ref, w_ref, sems, second):
    width = wqkv_ref.shape[0]
    return [
        pltpu.make_async_copy(
            wqkv_ref.at[:, pl.ds(i * width + second * HW, HW)],
            w_ref.at[:, pl.ds(i * HW, HW)],
            sems.at[i],
        )
        for i in range(3)
    ]


def weight_copies(wqkv_ref, wout_ref, w_ref, wo_ref, sems, second):
    out_rows = wout_ref.at[pl.ds(second * HW, HW), :]
    return [
        *qkv_copies(wqkv_ref, w_ref, sems, second),
        pltpu.make_async_copy(out_rows, wo_ref, sems.at[3]),
    ]


def started(*copies):
    for copy in copies:
        copy.start()
    return copies


def finished(*copies):
    for copy in copies:
        copy.wait()


def project(hidden, cot, w_ref, wo_ref):
    projected = dot_nn(hidden, w_ref[...]).astype(BF16)
    q, k, v = [projected[:, i * HW : (i + 1) * HW] for i in range(3)]
    g = dot_nt(cot, wo_ref[...]).astype(BF16)
    return q * jnp.asarray(SCALE, BF16), k, v, g


def row_part(
    x_any, cot_any, gain_any, wqkv_any, wout_any,
    out_ref, base_ref, normed_ref, inverse_ref, x_ref, cot_ref,
    gain_ref, w_ref, wo_ref, dk_ref, dv_ref, grads_ref, sems,
):
    first = started(
        pltpu.make_async_copy(x_any, x_ref, sems.at[4]),
        pltpu.make_async_copy(gain_any, gain_ref, sems.at[5]),
    )
    later = started(
        *weight_copies(wqkv_any, wout_any, w_ref, wo_ref, sems, 0),
        pltpu.make_async_copy(cot_any, cot_ref, sems.at[6]),
    )
    dk_ref[...] = jnp.zeros_like(dk_ref)
    dv_ref[...] = jnp.zeros_like(dv_ref)
    finished(*first)
    tokens = x_ref.shape[0]
    inverse_ref[...], normed_ref[...] = rms_parts(x_ref[...].astype(F32))
    hidden = (normed_ref[...] * gain_ref[...]).astype(BF16)
    hidden_t = transposed(hidden)
    finished(*later)
    cot = cot_ref[...]
    q, k, v, g = project(hidden, cot, w_ref, wo_ref)
    kt, vt, gt = transposed(k), transposed(v), transposed(g)
    step = math.gcd(tokens, QUERY_BLOCK)
    query = lax.broadcasted_iota(jnp.int32, (step, 2 * step), 1) % step
    mask = query >= lax.broadcasted_iota(jnp.int32, (step, 2 * step), 0)
    pairs = [slice(i * 2 * HD, (i + 1) * 2 * HD) for i in range(HH // 2)]
    att_blocks, dq_blocks = [], []
    for start in range(0, tokens, step):
        rows, keys = slice(start, start + step), slice(0, start + step)
        items = [
            (
                head_pair(q[rows, lanes]), head_pair(g[rows, lanes]), gt[lanes, rows],
                k[keys, lanes], v[keys, lanes], kt[lanes, keys], vt[lanes, keys],
            )
            for lanes in pairs
        ]
        results = pair_steps(items, step, mask)
        for lanes, (_, _, dk, dv) in zip(pairs, results):
            dk_ref[keys, lanes] += dk
            dv_ref[keys, lanes] += dv
        att_blocks.append(jnp.concatenate([result[0] for result in results], 0))
        dq_blocks.append(jnp.concatenate([result[1] for result in results], 0))
    grads_ref[:, :HW] = transposed(jnp.concatenate(dq_blocks, 1))
    grads_ref[:, HW : 2 * HW] = dk_ref[...].astype(BF16)
    grads_ref[:, 2 * HW :] = dv_ref[...].astype(BF16)
    term_qkv = dot_nn(hidden_t, grads_ref[...]).astype(BF16)
    out_ref[...] = dot_nn(jnp.concatenate(att_blocks, 1), cot).astype(BF16)
    grad_normed = dot_nt(grads_ref[...], w_ref[...]) * gain_ref[...]
    base_ref[...] = input_grad(
        cot_ref[...].astype(F32), normed_ref[...], inverse_ref[...], grad_normed
    )
    return term_qkv


def row_kernel(x_any, cot_any, gain_any, wqkv_any, wout_any, qkv_ref, *refs):
    qkv_ref[...] = row_part(x_any, cot_any, gain_any, wqkv_any, wout_any, *refs)


def row_chip_kernel(
    x_any, cot_any, gain_any, wqkv_any, wout_any,
    send_1, send_2, keep_1, keep_2, rows_ref, col_w_ref, col_wo_ref, *refs,
):
    chip, core, _ = here()
    sems, rows = refs[-1], rows_ref.shape[0]
    at = pl.multiple_of((chip * 2 + core) * rows, rows)
    handed = started(
        pltpu.make_async_copy(wqkv_any.at[pl.ds(at, rows), :], rows_ref, sems.at[7]),
        *weight_copies(wqkv_any, wout_any, col_w_ref, col_wo_ref, sems.at[pl.ds(8, 4)], 1),
    )
    term_qkv = row_part(x_any, cot_any, gain_any, wqkv_any, wout_any, *refs)
    chips, cut = send_1.shape[0], keep_1.shape[2]
    pieces = slice(0, chips), slice(0, cut)
    split_cores(term_qkv[:, :cut], send_1, keep_1, *pieces)
    split_cores(term_qkv[:, cut:], send_2, keep_2, *pieces)
    finished(*handed)


def column_part(x, cot, mask, gain, w_ref, wo_ref, weight_waits, grads_ref):
    tokens, block = x.shape[0], mask.shape[0]
    _, normed = rms_parts(x.astype(F32))
    hidden = (normed * gain).astype(BF16)
    hidden_t = transposed(hidden)
    finished(*weight_waits)
    q, k, v, g = project(hidden, cot, w_ref, wo_ref)
    kt, vt, gt = transposed(k), transposed(v), transposed(g)
    pairs = [slice(i * 2 * HD, (i + 1) * 2 * HD) for i in range(HH // 2)]
    blocks = [slice(at, at + block) for at in range(0, tokens, block)]
    items = [
        (
            head_pair(q[rows, lanes]), head_pair(g[rows, lanes]), gt[lanes, rows],
            k[rows, lanes], v[rows, lanes], kt[lanes, rows], vt[lanes, rows],
        )
        for lanes in pairs
        for rows in blocks
    ]
    results = pair_steps(items, block, mask)
    places = [(lanes, rows) for lanes in pairs for rows in blocks]
    for (lanes, rows), (_, _, dk, dv) in zip(places, results):
        grads_ref[rows, HW + lanes.start : HW + lanes.stop] = dk.astype(BF16)
        grads_ref[rows, 2 * HW + lanes.start : 2 * HW + lanes.stop] = dv.astype(BF16)
    by_pair = [results[i * len(blocks) : (i + 1) * len(blocks)] for i in range(len(pairs))]
    attended, grad_q = [
        jnp.concatenate([jnp.concatenate([r[i] for r in some], 1) for some in by_pair], 0)
        for i in range(2)
    ]
    grads_ref[:, :HW] = transposed(grad_q)
    term_qkv = dot_nn(hidden_t, grads_ref[...]).astype(BF16)
    term_out = dot_nn(attended, cot).astype(BF16)
    return term_qkv, term_out


def column_mask(all_rows, group, row_of):
    block = all_rows * group
    shape = (block, 2 * block)
    query = lax.broadcasted_iota(jnp.int32, shape, 1) % block
    key = lax.broadcasted_iota(jnp.int32, shape, 0)
    same_column = query % group == key % group
    return (row_of(query // group) >= row_of(key // group)) & same_column


def column_kernel(
    moved_any, gain_any, wqkv_any, wout_any, row_qkv_ref, row_out_ref,
    terms_ref, grads_ref, w_ref,
    moved_ref, gain_ref, wo_ref, sems,
):
    copies = started(
        pltpu.make_async_copy(moved_any, moved_ref, sems.at[4]),
        pltpu.make_async_copy(gain_any, gain_ref, sems.at[5]),
    )
    weights = started(*weight_copies(wqkv_any, wout_any, w_ref, wo_ref, sems, 1))
    finished(*copies)
    all_rows, _, share, width = moved_ref.shape
    group = math.gcd(share, 16)
    x, cot = [
        jnp.concatenate(
            [
                moved_ref[:, which, at : at + group, :].astype(F32).reshape(all_rows * group, width)
                for at in range(0, share, group)
            ],
            0,
        ).astype(BF16)
        for which in range(2)
    ]
    mask = column_mask(all_rows, group, lambda place: place)
    term_qkv, term_out = column_part(
        x, cot, mask, gain_ref[...], w_ref, wo_ref, weights, grads_ref
    )
    for i in range(3):
        at = i * width
        terms_ref[:, at : at + HW] = row_qkv_ref[:, i * HW : (i + 1) * HW]
        terms_ref[:, at + HW : at + 2 * HW] = term_qkv[:, i * HW : (i + 1) * HW]
    terms_ref[:HW, 3 * width :] = row_out_ref[...]
    terms_ref[HW:, 3 * width :] = term_out


def column_chip_kernel(
    x_ref, cot_ref, near_1, near_2, near_3, far_ref, last_ref, gain_ref, w_ref, wo_ref, row_out_ref,
    keep_ref, grads_ref, *refs,
):
    chip, core, _ = here()
    share = far_ref.shape[2]
    half = pl.ds(pl.multiple_of(core * share, share), share)
    at = pl.ds(pl.multiple_of((chip * 2 + core) * share, share), share)
    group = math.gcd(share, 16)

    def tokens(which, mine):
        pieces = [mine[at, :], far_ref[0, which]]
        fars = last_ref[which], far_ref[1, which], far_ref[2, which]
        for near, far in zip((near_1, near_2, near_3), fars):
            pieces += [near[which, half, :], far]
        starts = range(0, share, group)
        return jnp.concatenate(
            [piece[start : start + group] for start in starts for piece in pieces], 0
        )

    def row_of(place):
        step = (4 - (place >> 1)) & 3
        return ((step ^ chip) << 1) + ((place & 1) ^ core)

    mask = column_mask(2 * (len(CHIP_STEPS) + 1), group, row_of)
    term_qkv, term_out = column_part(
        tokens(0, x_ref), tokens(1, cot_ref), mask, gain_ref[...], w_ref, wo_ref, (), grads_ref
    )
    *pieces, send_ref = refs
    chips = send_ref.shape[0]
    both = send_ref, keep_ref
    out_lanes = slice(3 * HW, send_ref.shape[2])
    split_cores(term_qkv, *both, slice(0, chips), slice(0, 3 * HW))
    split_cores(row_out_ref[...], *both, slice(0, chips // 2), out_lanes)
    split_cores(term_out, *both, slice(chips // 2, chips), out_lanes)
    at = 0
    for piece in pieces:
        piece[...] = send_ref[:, :, at : at + piece.shape[2]]
        at += piece.shape[2]


def other_core(near, share):
    at = pl.ds(pl.multiple_of((1 - here()[1]) * share, share), share)
    return near[:, at, :]


def far_kernel(x_ref, cot_ref, near_2, near_3, far_ref):
    chip, core, _ = here()
    share = far_ref.shape[2]
    at = pl.ds(pl.multiple_of((chip * 2 + 1 - core) * share, share), share)
    far_ref[0, 0], far_ref[0, 1] = x_ref[at, :], cot_ref[at, :]
    for i, near in enumerate((near_2, near_3)):
        far_ref[i + 1] = other_core(near, share)


def last_far_kernel(near_1, far_ref):
    far_ref[...] = other_core(near_1, far_ref.shape[1])


def back_kernel(grads_ref, w_ref, back_ref):
    grad_hidden = dot_nt(grads_ref[...], w_ref[...])
    all_rows, share, width = back_ref.shape
    group = math.gcd(share, 16)
    block = all_rows * group
    for i in range(share // group):
        piece = grad_hidden[i * block : (i + 1) * block].reshape(all_rows, group, width)
        back_ref[:, i * group : (i + 1) * group, :] = piece.astype(BF16)


def back_chip_kernel(grads_ref, w_ref, send_ref, keep_ref):
    grad_hidden = dot_nt(grads_ref[...], w_ref[...]).astype(BF16)
    chips, share, width = keep_ref.shape
    group = math.gcd(share, 16)
    block = 2 * chips * group
    for i in range(share // group):
        piece = grad_hidden[i * block : (i + 1) * block].reshape(chips, 2, group, width)
        at = slice(i * group, (i + 1) * group)
        keep_ref[:, at, :], send_ref[:, at, :] = piece[:, 0], piece[:, 1]


def back_pack_kernel(keep_ref, got_ref, *targets):
    share = keep_ref.shape[1]
    core = here()[1]
    kept_at = pl.ds(pl.multiple_of(core * share, share), share)
    got_at = pl.ds(pl.multiple_of((1 - core) * share, share), share)
    for i, target in enumerate(targets):
        target[kept_at, :] = keep_ref[i]
        target[got_at, :] = got_ref[i]


def input_kernel(base_ref, normed_ref, inverse_ref, gain_ref, back_ref, grad_ref):
    grad_ref[...] = input_grad(
        base_ref[...], normed_ref[...], inverse_ref[...], back_ref[...].astype(F32) * gain_ref[...]
    ).astype(BF16)


def input_grad(base, normed, inverse_rms, grad_normed):
    projected = jnp.mean(grad_normed * normed, -1, keepdims=True)
    return base + inverse_rms * (grad_normed - normed * projected)


def input_chip_kernel(
    base_ref, normed_ref, inverse_ref, gain_ref, own_ref, got_1, got_2, got_3,
    grad_any, grad_ref, sems,
):
    chip = here()[0]
    count = own_ref.shape[0]
    copies = []
    for i, (step, back_ref) in enumerate(zip((0, *CHIP_STEPS), (own_ref, got_1, got_2, got_3))):
        at = pl.ds(pl.multiple_of((chip ^ step) * count, count), count)
        grad_normed = back_ref[...].astype(F32) * gain_ref[...]
        grad = input_grad(base_ref[at, :], normed_ref[at, :], inverse_ref[at, :], grad_normed)
        grad_ref[i] = grad.astype(BF16)
        copies += started(pltpu.make_async_copy(grad_ref.at[i], grad_any.at[at, :], sems.at[i]))
    finished(*copies)


def pack_kernel(x_any, cot_any, off_1, off_2, off_3, sems):
    chip = here()[0]
    count = off_1.shape[1]
    copies = []
    for i, (step, target) in enumerate(zip(CHIP_STEPS, (off_1, off_2, off_3))):
        at = pl.ds(pl.multiple_of((chip ^ step) * count, count), count)
        for which, source in enumerate((x_any, cot_any)):
            copies.append(
                pltpu.make_async_copy(source.at[at, :], target.at[which], sems.at[2 * i + which])
            )
    finished(*started(*copies))


def split_rows(total, axis):
    upper = (here()[2] & 1) == 1
    low, high = jnp.split(total, 2, axis)
    return jnp.where(upper, low, high).astype(BF16), jnp.where(upper, high, low)


def row_cores_kernel(keep_1, keep_2, got_1, got_2, send_ref, kept_ref):
    total = [
        keep_ref[...].astype(F32) + got_ref[...].astype(F32)
        for keep_ref, got_ref in ((keep_1, got_1), (keep_2, got_2))
    ]
    send_ref[...], kept_ref[...] = split_rows(jnp.concatenate(total, 2), 1)


def cores_kernel(keep_ref, got_1, got_2, got_3, got_4, send_ref, kept_ref, *targets):
    chip, cut = here()[0], kept_ref.shape[2]
    got = jnp.concatenate([ref[...] for ref in (got_1, got_2)], 2)
    first = keep_ref[:, :, :cut].astype(F32) + got[:, :, :cut].astype(F32)
    send_ref[...], kept_ref[...] = split_rows(first, 1)
    for step, target in zip((0, *CHIP_STEPS), targets):
        there = chip ^ step
        got = jnp.concatenate([ref[there] for ref in (got_1, got_2, got_3, got_4)], 1)
        total = keep_ref[there, :, cut:].astype(F32) + got[:, cut:].astype(F32)
        target[...] = total.astype(target.dtype)


def pair_kernel(kept_ref, got_ref, row_kept, row_got, *targets):
    chip, cut = here()[0], kept_ref.shape[2]
    for step, target in zip((0, *CHIP_STEPS), targets):
        there = chip ^ step
        total = kept_ref[there] + got_ref[there].astype(F32)
        target[:, :cut] = total.astype(target.dtype)
        total = row_kept[there] + row_got[there].astype(F32)
        target[:, cut:] = total.astype(target.dtype)


def layer_sum(own_ref, got_1, got_2, got_3):
    return own_ref[...] + (
        (got_1[...].astype(F32) + got_2[...].astype(F32)) + got_3[...].astype(F32)
    )


def layer_kernel(own_ref, got_1, got_2, got_3, send_ref, kept_ref):
    send_ref[...], kept_ref[...] = split_rows(layer_sum(own_ref, got_1, got_2, got_3), 0)


def join_kernel(own_ref, got_1, got_2, got_3, kept_ref, got_ref, out_ref):
    total = layer_sum(own_ref, got_1, got_2, got_3).astype(BF16)
    cut, width = FIRST_PART, kept_ref.shape[1]
    out_ref[:, :cut] = total[:, :cut]
    out_ref[:, cut : cut + width] = (kept_ref[...] + got_ref[...].astype(F32)).astype(BF16)
    out_ref[:, cut + width :] = total[:, cut:]


def add_kernel(kept_ref, got_ref, out_ref):
    out_ref[...] = (kept_ref[...].astype(F32) + got_ref[...].astype(F32)).astype(BF16)


def result_kernel(held_ref, got_ref, w_ref, gain_ref, qkv_ref, out_ref, grad_ref):
    rows = qkv_ref.shape[0]
    chip, core, layer = here()
    at = (chip * 2 + core) * rows
    upper = (layer & 1) == 1
    half = rows // 2
    width = out_ref.shape[1]

    def ordered(lanes):
        held, got = held_ref[:, lanes].astype(F32), got_ref[:, lanes].astype(F32)
        return (jnp.where(upper, got, held), jnp.where(upper, held, got))

    row_at = 3 * HW + width
    for i in range(3):
        for at_from, at_to in ((row_at + i * HW, i * width), (i * HW, i * width + HW)):
            to = slice(at_to, at_to + HW)
            qkv_ref[:half, to], qkv_ref[half:, to] = ordered(slice(at_from, at_from + HW))
    out_ref[:half], out_ref[half:] = ordered(slice(3 * HW, row_at))
    total = jnp.sum(qkv_ref[...] * w_ref[...].astype(F32), -1, keepdims=True)
    shape = (rows, gain_ref.shape[1])
    row = lax.broadcasted_iota(jnp.int32, shape, 0)
    feature = lax.broadcasted_iota(jnp.int32, shape, 1)
    gain = jnp.sum(jnp.where(feature == row + at, gain_ref[...], 0.0), -1, keepdims=True)
    shape = (rows, grad_ref.shape[1])
    same = lax.broadcasted_iota(jnp.int32, shape, 0) == lax.broadcasted_iota(jnp.int32, shape, 1)
    grad_ref[...] = jnp.sum(jnp.where(same, total / gain, 0.0), 0, keepdims=True)


def call(kernel, name, ins, outs, scratch=(), vmem=SMALL_VMEM, out_specs=None):
    out_specs = out_specs or [VMEM] * len(outs)
    places = [{id(HBM): pltpu.HBM, id(PINNED): pltpu.VMEM}.get(id(spec)) for spec in out_specs]
    outs = [place(*out) if place else shaped(*out) for place, out in zip(places, outs)]
    args = [
        pltpu.with_memory_space_constraint(array, pltpu.HBM) if spec is HBM else array
        for spec, array in ins
    ]
    return pl.pallas_call(
        kernel,
        out_shape=outs,
        in_specs=[spec for spec, _ in ins],
        out_specs=out_specs,
        scratch_shapes=scratch,
        name=name,
        cost_estimate=pl.CostEstimate(flops=0, bytes_accessed=0, transcendentals=0),
        compiler_params=pltpu.CompilerParams(vmem_limit_bytes=vmem),
    )(*args)


def swap(array, axis, bits):
    count = lax.axis_size(axis)
    return lax.ppermute(array, axis, [(i, i ^ bits) for i in range(count)])


def cross_chips(*offs):
    return [swap(off, "seq", 2 * step) for off, step in zip(offs, CHIP_STEPS)]


def add_two(kept, got, name):
    (total,) = call(add_kernel, name, [(VMEM, kept), (VMEM, got)], [(kept.shape, BF16)])
    return total


def body(inputs, norm_gain, qkv_weight, out_weight, out_cotan):
    columns, width = inputs.shape[2:]
    n = lax.axis_size("seq")
    m = lax.axis_size("dp")
    share = columns // n
    row_share = width // n
    row_width, col_width = 3 * HW, 3 * HW + width
    x = inputs.reshape(columns, width)
    cot = out_cotan.reshape(columns, width)
    gain = norm_gain.reshape(1, width)
    chips = 4
    layered = n == 2 * chips and m == 4 and row_share == share
    weight_scratch = [
        pltpu.VMEM((1, width), F32),
        pltpu.VMEM((width, 3 * HW), BF16),
        pltpu.VMEM((HW, width), BF16),
    ]
    weights = [(HBM, gain), (HBM, qkv_weight), (HBM, out_weight)]
    col_outs = [((columns, 3 * HW), BF16), ((width, 3 * HW), BF16)]

    if layered:
        packed = call(
            pack_kernel,
            "pack_columns",
            [(HBM, x), (HBM, cot)],
            [((2, 2 * share, width), BF16)] * 3,
            [pltpu.SemaphoreType.DMA((6,))],
            out_specs=[ANY] * 3,
        )
        near = cross_chips(*packed)
        x_first, _ = lax.optimization_barrier((x, packed[0]))
    else:
        outgoing = jnp.stack([x.reshape(n, share, width), cot.reshape(n, share, width)], 1)
        moved = lax.all_to_all(outgoing, "seq", split_axis=0, concat_axis=0, tiled=True)
        x_first = x

    row_outs = [
        ((HW, width), BF16),
        ((columns, width), F32), ((columns, width), F32), ((columns, 1), F32),
        ((columns, width), BF16), ((columns, width), BF16),
    ]
    if layered:
        cut = row_width // 2
        split_outs = [((chips, row_share, cut), BF16)] * 4
        handed_outs = [
            ((row_share, 3 * width), BF16), ((width, 3 * HW), BF16), ((HW, width), BF16),
        ]
        row_outs = [*split_outs, *handed_outs, *row_outs]
        specs = [VMEM] * 4 + [PINNED] * (len(row_outs) - 4)
    else:
        row_outs = [((width, row_width), BF16), *row_outs]
        specs = [VMEM] * len(row_outs)
    *row_terms, row_out, base, normed, inverse_rms, x_near, cot_near = call(
        row_chip_kernel if layered else row_kernel,
        "row_heads",
        [(HBM, x_first), (HBM, cot), *weights],
        row_outs,
        [
            *weight_scratch,
            pltpu.VMEM((columns, HW), F32),
            pltpu.VMEM((columns, HW), F32),
            pltpu.VMEM((columns, 3 * HW), BF16),
            pltpu.SemaphoreType.DMA((12,)),
        ],
        BIG_VMEM,
        specs,
    )
    if layered:
        *row_terms, weight_rows, col_weight, col_out_weight = row_terms
        row_sent = [swap(one, "seq", 1) for one in row_terms[:2]]
        half_block = (chips, row_share // 2, row_width)
        row_next, row_kept = call(
            row_cores_kernel,
            "row_add_cores",
            [(VMEM, one) for one in (*row_terms[2:], *row_sent)],
            [(half_block, BF16), (half_block, F32)],
            out_specs=[VMEM, PINNED],
        )
        col_weight, row_kept = lax.optimization_barrier((col_weight, row_kept))
        (far,) = call(
            far_kernel,
            "pack_other_core",
            [(VMEM, one) for one in (x_near, cot_near, *near[1:])],
            [((3, 2, share, width), BF16)],
        )
        near[0], _ = lax.optimization_barrier((near[0], far))
        (last,) = call(
            last_far_kernel,
            "pack_other_core_last",
            [(VMEM, near[0])],
            [((2, share, width), BF16)],
        )
        row_got = swap(row_next, "dp", 1)
        keep, col_grads, *pieces = call(
            column_chip_kernel,
            "column_heads",
            [
                (VMEM, one)
                for one in (
                    x_near, cot_near, *near, swap(far, "seq", 1), swap(last, "seq", 1),
                    gain, col_weight, col_out_weight, row_out,
                )
            ],
            [((chips, row_share, col_width), BF16), col_outs[0]]
            + [((chips, row_share, wide), BF16) for wide in SWAP_PIECES],
            [pltpu.VMEM((chips, row_share, col_width), BF16)],
            BIG_VMEM,
            [VMEM, PINNED] + [VMEM] * len(SWAP_PIECES),
        )
        back_send, back_keep = call(
            back_chip_kernel,
            "column_grad_hidden",
            [(VMEM, col_grads), (VMEM, col_weight)],
            [((chips, share, width), BF16)] * 2,
        )
        keep, back_keep, row_got = lax.optimization_barrier((keep, back_keep, row_got))
        first_half = (chips, row_share // 2, FIRST_PART)
        second = (row_share, col_width - FIRST_PART)
        to_next, kept, owned, *off = call(
            cores_kernel,
            "column_add_cores",
            [(VMEM, keep), *[(VMEM, swap(piece, "seq", 1)) for piece in pieces]],
            [(first_half, BF16), (first_half, F32), (second, F32)] + [(second, BF16)] * 3,
            out_specs=[VMEM, PINNED, PINNED, VMEM, VMEM, VMEM],
        )
        got = cross_chips(*off)
        back = call(
            back_pack_kernel,
            "pack_grad_hidden",
            [(VMEM, back_keep), (VMEM, swap(back_send, "seq", 1))],
            [((2 * share, width), BF16)] * 4,
        )
        row_kept, *back = lax.optimization_barrier((row_kept, *back))
        joint = (row_share // 2, FIRST_PART + row_width)
        first_owned, *off = call(
            pair_kernel,
            "first_add_pair",
            [
                (VMEM, one)
                for one in (kept, swap(to_next, "dp", 1), row_kept, row_got)
            ],
            [(joint, F32)] + [(joint, BF16)] * 3,
            out_specs=[PINNED, VMEM, VMEM, VMEM],
        )
        first_got = cross_chips(*off)
        second_half = (row_share // 2, second[1])
        to_next, kept = call(
            layer_kernel,
            "second_add_chips",
            [(VMEM, one) for one in (owned, *got)],
            [(second_half, BF16), (second_half, F32)],
            out_specs=[VMEM, PINNED],
        )
        (pair_sum,) = call(
            join_kernel,
            "join_terms",
            [(VMEM, one) for one in (first_owned, *first_got, kept, swap(to_next, "dp", 1))],
            [((row_share // 2, col_width + row_width), BF16)],
        )
        *back, pair_sum = lax.optimization_barrier((*back, pair_sum))
        held = add_two(pair_sum, swap(pair_sum, "dp", 2), "add_pairs")
        other = swap(held, "dp", 1)
        (grad,) = call(
            input_chip_kernel,
            "input_grad",
            [
                (VMEM, one)
                for one in (base, normed, inverse_rms, gain, back[0], *cross_chips(*back[1:]))
            ],
            [((columns, width), BF16)],
            [pltpu.VMEM((chips, 2 * share, width), BF16), pltpu.SemaphoreType.DMA((chips,))],
            out_specs=[HBM],
        )
        sum_qkv, sum_out, sum_gain = call(
            result_kernel,
            "result",
            [(VMEM, held), (VMEM, other), (VMEM, weight_rows), (VMEM, gain)],
            [((row_share, 3 * width), F32), ((row_share, width), F32), ((1, row_share), F32)],
        )
        sum_gain = sum_gain.reshape(row_share)
    else:
        terms, *col_grads = call(
            column_kernel,
            "column_heads",
            [(ANY, moved), *weights, (VMEM, row_terms[0]), (VMEM, row_out)],
            [((width, 4 * width), BF16), *col_outs],
            [
                pltpu.VMEM((n, 2, share, width), BF16),
                weight_scratch[0],
                weight_scratch[2],
                pltpu.SemaphoreType.DMA((6,)),
            ],
            BIG_VMEM,
        )
        (back,) = call(
            back_kernel,
            "column_grad_hidden",
            [(VMEM, one) for one in col_grads],
            [((n, share, width), BF16)],
        )
        returned = lax.all_to_all(back, "seq", split_axis=0, concat_axis=0, tiled=True)
        (grad,) = call(
            input_kernel,
            "input_grad",
            [
                (VMEM, base), (VMEM, normed), (VMEM, inverse_rms), (VMEM, gain),
                (VMEM, returned.reshape(columns, width)),
            ],
            [((columns, width), BF16)],
        )
        terms = lax.all_to_all(
            terms.reshape(n, row_share, 4 * width), "seq", split_axis=0, concat_axis=0, tiled=True
        )
        total = jnp.sum(terms.astype(F32), 0)
        for step in range(m.bit_length() - 1):
            sent = total.astype(BF16)
            total = sent.astype(F32) + swap(sent, "dp", 1 << step).astype(F32)
        sum_qkv, sum_out = total[:, : 3 * width], total[:, 3 * width :]
        here_at = lax.axis_index("seq") * row_share
        own_gain = lax.dynamic_slice_in_dim(norm_gain, here_at, row_share, 0)
        own_weight = lax.dynamic_slice_in_dim(qkv_weight, here_at, row_share, 0)
        sum_gain = jnp.sum(sum_qkv * own_weight.astype(F32), -1) / own_gain
    return (grad.reshape(inputs.shape), sum_qkv, sum_out, sum_gain)


def solution(mesh):
    return jax.shard_map(
        body,
        mesh=mesh,
        in_specs=(P("dp", "seq", None, None), P(), P(), P(), P("dp", "seq", None, None)),
        out_specs=(P("dp", "seq", None, None), P("seq", None), P("seq", None), P("seq")),
        check_vma=False,
    )
```

```python
import math

import jax
import jax.numpy as jnp
from jax import lax
from jax.experimental import pallas as pl
from jax.experimental.pallas import tpu as pltpu
from jax.sharding import PartitionSpec as P

H = 8
HD = 64
HH = H // 2
HW = HH * HD
SCALE = HD ** (-0.5)
F32 = jnp.float32
BF16 = jnp.bfloat16
QUERY_BLOCK = 128
BIG_VMEM = 20 * 1024 * 1024
SMALL_VMEM = 8 * 1024 * 1024
ANY = pl.BlockSpec(memory_space=pl.ANY)
VMEM = pl.BlockSpec(memory_space=pltpu.VMEM)
HBM = pl.BlockSpec(memory_space=pltpu.HBM)
CHIP_STEPS = ((3, 2, 1), (3, 1, 2))
FIRST_PART = 384
PINNED = pl.BlockSpec(memory_space=pltpu.VMEM)
shaped = jax.ShapeDtypeStruct


def here():
    device = lax.axis_index("seq")
    return device >> 1, device & 1, lax.axis_index("dp")


def chip_steps():
    core = here()[1]
    return [0] + [jnp.where(core == 0, even, odd) for even, odd in zip(*CHIP_STEPS)]


def dot_nn(a, b):
    return lax.dot_general(a, b, (((1,), (0,)), ((), ())), preferred_element_type=F32)


def dot_nt(a, b):
    return lax.dot_general(a, b, (((1,), (1,)), ((), ())), preferred_element_type=F32)


def rms_parts(x):
    inverse_rms = lax.rsqrt(jnp.mean(x * x, -1, keepdims=True) + 1e-05)
    return inverse_rms, x * inverse_rms


def transposed(x):
    block = math.gcd(x.shape[1], 256)
    eye = (
        lax.broadcasted_iota(jnp.int32, (block, block), 0)
        == lax.broadcasted_iota(jnp.int32, (block, block), 1)
    ).astype(F32).astype(BF16)
    parts = [
        dot_nt(eye, x[:, at : at + block]).astype(BF16) for at in range(0, x.shape[1], block)
    ]
    return parts[0] if len(parts) == 1 else jnp.concatenate(parts, 0)


def head_pair(x):
    lane = lax.broadcasted_iota(jnp.int32, x.shape, 1)
    zero = jnp.zeros_like(x)
    return jnp.concatenate([jnp.where(lane < HD, x, zero), jnp.where(lane < HD, zero, x)], 0)


def both_heads(both, count):
    return jnp.concatenate([both[:HD, :count], both[HD:, count:]], 0)


def pair_steps(items, mask_rows, mask):
    count = items[0][2].shape[1]
    scores = [dot_nt(k, q2) for q2, _, _, k, _, _, _ in items]
    prob_grads = [dot_nt(v, g2) for _, g2, _, _, v, _, _ in items]
    probs = []
    for score in scores:
        first = score.shape[0] - mask_rows
        tail = jnp.where(mask, score[first:], -1e30)
        score = tail if first == 0 else jnp.concatenate([score[:first], tail], 0)
        exponent = jnp.exp(score - jnp.max(score, 0, keepdims=True))
        probs.append(exponent * (1.0 / jnp.sum(exponent, 0, keepdims=True)))
    weights = [prob.astype(BF16) for prob in probs]
    attended = [
        both_heads(dot_nn(item[6], weight), count).astype(BF16)
        for item, weight in zip(items, weights)
    ]
    score_grads = []
    for item, att, prob, prob_grad in zip(items, attended, probs, prob_grads):
        product = item[2].astype(F32) * att.astype(F32)
        delta = [jnp.sum(part, 0, keepdims=True) for part in (product[:HD], product[HD:])]
        score_grads.append((prob * (prob_grad - jnp.concatenate(delta, 1))).astype(BF16))
    grad_q = [
        (both_heads(dot_nn(item[5], score_grad), count) * SCALE).astype(BF16)
        for item, score_grad in zip(items, score_grads)
    ]
    grad_k = [dot_nn(score_grad, item[0]) for item, score_grad in zip(items, score_grads)]
    grad_v = [dot_nn(weight, item[1]) for item, weight in zip(items, weights)]
    return list(zip(attended, grad_q, grad_k, grad_v))


def split_cores(piece, send_ref, keep_ref, chips, lanes):
    rows = send_ref.shape[1]
    parts = piece.reshape(chips.stop - chips.start, 2, rows, piece.shape[1])
    even, odd = parts[:, 0], parts[:, 1]
    first = here()[1] == 0
    send_ref[chips, :, lanes] = jnp.where(first, odd, even)
    keep_ref[chips, :, lanes] = jnp.where(first, even, odd)


def qkv_copies(wqkv_ref, w_ref, sems, second):
    width = wqkv_ref.shape[0]
    return [
        pltpu.make_async_copy(
            wqkv_ref.at[:, pl.ds(i * width + second * HW, HW)],
            w_ref.at[:, pl.ds(i * HW, HW)],
            sems.at[i],
        )
        for i in range(3)
    ]


def weight_copies(wqkv_ref, wout_ref, w_ref, wo_ref, sems, second):
    out_rows = wout_ref.at[pl.ds(second * HW, HW), :]
    return [
        *qkv_copies(wqkv_ref, w_ref, sems, second),
        pltpu.make_async_copy(out_rows, wo_ref, sems.at[3]),
    ]


def started(*copies):
    for copy in copies:
        copy.start()
    return copies


def finished(*copies):
    for copy in copies:
        copy.wait()


def project(hidden, cot, w_ref, wo_ref):
    projected = dot_nn(hidden, w_ref[...]).astype(BF16)
    q, k, v = [projected[:, i * HW : (i + 1) * HW] for i in range(3)]
    g = dot_nt(cot, wo_ref[...]).astype(BF16)
    return q * jnp.asarray(SCALE, BF16), k, v, g


def row_part(
    x_any, cot_any, gain_any, wqkv_any, wout_any,
    out_ref, base_ref, normed_ref, inverse_ref, x_ref, cot_ref,
    gain_ref, w_ref, wo_ref, dk_ref, dv_ref, grads_ref, sems,
):
    first = started(
        pltpu.make_async_copy(x_any, x_ref, sems.at[4]),
        pltpu.make_async_copy(gain_any, gain_ref, sems.at[5]),
    )
    later = started(
        *weight_copies(wqkv_any, wout_any, w_ref, wo_ref, sems, 0),
        pltpu.make_async_copy(cot_any, cot_ref, sems.at[6]),
    )
    dk_ref[...] = jnp.zeros_like(dk_ref)
    dv_ref[...] = jnp.zeros_like(dv_ref)
    finished(*first)
    tokens = x_ref.shape[0]
    inverse_ref[...], normed_ref[...] = rms_parts(x_ref[...].astype(F32))
    hidden = (normed_ref[...] * gain_ref[...]).astype(BF16)
    hidden_t = transposed(hidden)
    finished(*later)
    cot = cot_ref[...]
    q, k, v, g = project(hidden, cot, w_ref, wo_ref)
    kt, vt, gt = transposed(k), transposed(v), transposed(g)
    step = math.gcd(tokens, QUERY_BLOCK)
    query = lax.broadcasted_iota(jnp.int32, (step, 2 * step), 1) % step
    mask = query >= lax.broadcasted_iota(jnp.int32, (step, 2 * step), 0)
    pairs = [slice(i * 2 * HD, (i + 1) * 2 * HD) for i in range(HH // 2)]
    att_blocks, dq_blocks = [], []
    for start in range(0, tokens, step):
        rows, keys = slice(start, start + step), slice(0, start + step)
        items = [
            (
                head_pair(q[rows, lanes]), head_pair(g[rows, lanes]), gt[lanes, rows],
                k[keys, lanes], v[keys, lanes], kt[lanes, keys], vt[lanes, keys],
            )
            for lanes in pairs
        ]
        results = pair_steps(items, step, mask)
        for lanes, (_, _, dk, dv) in zip(pairs, results):
            dk_ref[keys, lanes] += dk
            dv_ref[keys, lanes] += dv
        att_blocks.append(jnp.concatenate([result[0] for result in results], 0))
        dq_blocks.append(jnp.concatenate([result[1] for result in results], 0))
    grads_ref[:, :HW] = transposed(jnp.concatenate(dq_blocks, 1))
    grads_ref[:, HW : 2 * HW] = dk_ref[...].astype(BF16)
    grads_ref[:, 2 * HW :] = dv_ref[...].astype(BF16)
    term_qkv = dot_nn(hidden_t, grads_ref[...]).astype(BF16)
    out_ref[...] = dot_nn(jnp.concatenate(att_blocks, 1), cot).astype(BF16)
    grad_normed = dot_nt(grads_ref[...], w_ref[...]) * gain_ref[...]
    base_ref[...] = input_grad(
        cot_ref[...].astype(F32), normed_ref[...], inverse_ref[...], grad_normed
    )
    return term_qkv


def row_kernel(x_any, cot_any, gain_any, wqkv_any, wout_any, qkv_ref, *refs):
    qkv_ref[...] = row_part(x_any, cot_any, gain_any, wqkv_any, wout_any, *refs)


def row_chip_kernel(
    x_any, cot_any, gain_any, wqkv_any, wout_any,
    send_1, send_2, keep_1, keep_2, rows_ref, col_w_ref, col_wo_ref, *refs,
):
    chip, core, _ = here()
    sems, rows = refs[-1], rows_ref.shape[0]
    at = pl.multiple_of((chip * 2 + core) * rows, rows)
    handed = started(
        pltpu.make_async_copy(wqkv_any.at[pl.ds(at, rows), :], rows_ref, sems.at[7]),
        *weight_copies(wqkv_any, wout_any, col_w_ref, col_wo_ref, sems.at[pl.ds(8, 4)], 1),
    )
    term_qkv = row_part(x_any, cot_any, gain_any, wqkv_any, wout_any, *refs)
    chips, cut = send_1.shape[0], keep_1.shape[2]
    pieces = slice(0, chips), slice(0, cut)
    split_cores(term_qkv[:, :cut], send_1, keep_1, *pieces)
    split_cores(term_qkv[:, cut:], send_2, keep_2, *pieces)
    finished(*handed)


def column_part(x, cot, mask, gain, w_ref, wo_ref, weight_waits, grads_ref):
    tokens, block = x.shape[0], mask.shape[0]
    _, normed = rms_parts(x.astype(F32))
    hidden = (normed * gain).astype(BF16)
    hidden_t = transposed(hidden)
    finished(*weight_waits)
    q, k, v, g = project(hidden, cot, w_ref, wo_ref)
    kt, vt, gt = transposed(k), transposed(v), transposed(g)
    pairs = [slice(i * 2 * HD, (i + 1) * 2 * HD) for i in range(HH // 2)]
    blocks = [slice(at, at + block) for at in range(0, tokens, block)]
    items = [
        (
            head_pair(q[rows, lanes]), head_pair(g[rows, lanes]), gt[lanes, rows],
            k[rows, lanes], v[rows, lanes], kt[lanes, rows], vt[lanes, rows],
        )
        for lanes in pairs
        for rows in blocks
    ]
    results = pair_steps(items, block, mask)
    places = [(lanes, rows) for lanes in pairs for rows in blocks]
    for (lanes, rows), (_, _, dk, dv) in zip(places, results):
        grads_ref[rows, HW + lanes.start : HW + lanes.stop] = dk.astype(BF16)
        grads_ref[rows, 2 * HW + lanes.start : 2 * HW + lanes.stop] = dv.astype(BF16)
    by_pair = [results[i * len(blocks) : (i + 1) * len(blocks)] for i in range(len(pairs))]
    attended, grad_q = [
        jnp.concatenate([jnp.concatenate([r[i] for r in some], 1) for some in by_pair], 0)
        for i in range(2)
    ]
    grads_ref[:, :HW] = transposed(grad_q)
    term_qkv = dot_nn(hidden_t, grads_ref[...]).astype(BF16)
    term_out = dot_nn(attended, cot).astype(BF16)
    return term_qkv, term_out


def column_mask(all_rows, group, row_of):
    block = all_rows * group
    shape = (block, 2 * block)
    query = lax.broadcasted_iota(jnp.int32, shape, 1) % block
    key = lax.broadcasted_iota(jnp.int32, shape, 0)
    same_column = query % group == key % group
    return (row_of(query // group) >= row_of(key // group)) & same_column


def column_kernel(
    moved_any, gain_any, wqkv_any, wout_any, row_qkv_ref, row_out_ref,
    terms_ref, grads_ref, w_ref,
    moved_ref, gain_ref, wo_ref, sems,
):
    copies = started(
        pltpu.make_async_copy(moved_any, moved_ref, sems.at[4]),
        pltpu.make_async_copy(gain_any, gain_ref, sems.at[5]),
    )
    weights = started(*weight_copies(wqkv_any, wout_any, w_ref, wo_ref, sems, 1))
    finished(*copies)
    all_rows, _, share, width = moved_ref.shape
    group = math.gcd(share, 16)
    x, cot = [
        jnp.concatenate(
            [
                moved_ref[:, which, at : at + group, :].astype(F32).reshape(all_rows * group, width)
                for at in range(0, share, group)
            ],
            0,
        ).astype(BF16)
        for which in range(2)
    ]
    mask = column_mask(all_rows, group, lambda place: place)
    term_qkv, term_out = column_part(
        x, cot, mask, gain_ref[...], w_ref, wo_ref, weights, grads_ref
    )
    for i in range(3):
        at = i * width
        terms_ref[:, at : at + HW] = row_qkv_ref[:, i * HW : (i + 1) * HW]
        terms_ref[:, at + HW : at + 2 * HW] = term_qkv[:, i * HW : (i + 1) * HW]
    terms_ref[:HW, 3 * width :] = row_out_ref[...]
    terms_ref[HW:, 3 * width :] = term_out


def column_chip_kernel(
    x_ref, cot_ref, near_1, near_2, near_3, far_ref, last_ref, gain_ref, w_ref, wo_ref, row_out_ref,
    send_ref, keep_ref, grads_ref,
):
    chip, core, _ = here()
    share = far_ref.shape[2]
    half = pl.ds(pl.multiple_of(core * share, share), share)
    at = pl.ds(pl.multiple_of((chip * 2 + core) * share, share), share)
    group = math.gcd(share, 16)

    def tokens(which, mine):
        pieces = [mine[at, :], far_ref[0, which]]
        fars = last_ref[which], far_ref[1, which], far_ref[2, which]
        for near, far in zip((near_1, near_2, near_3), fars):
            pieces += [near[which, half, :], far]
        starts = range(0, share, group)
        return jnp.concatenate(
            [piece[start : start + group] for start in starts for piece in pieces], 0
        )

    def row_of(place):
        owner, step = (place & 1) ^ core, 0
        for i, (even, odd) in enumerate(zip(*CHIP_STEPS)):
            step = jnp.where(place >> 1 == i + 1, jnp.where(owner == 0, even, odd), step)
        return ((step ^ chip) << 1) + owner

    mask = column_mask(2 * (len(CHIP_STEPS[0]) + 1), group, row_of)
    term_qkv, term_out = column_part(
        tokens(0, x_ref), tokens(1, cot_ref), mask, gain_ref[...], w_ref, wo_ref, (), grads_ref
    )
    chips = send_ref.shape[0]
    refs = send_ref, keep_ref
    out_lanes = slice(3 * HW, send_ref.shape[2])
    split_cores(term_qkv, *refs, slice(0, chips), slice(0, 3 * HW))
    split_cores(row_out_ref[...], *refs, slice(0, chips // 2), out_lanes)
    split_cores(term_out, *refs, slice(chips // 2, chips), out_lanes)


def other_core(near, share):
    at = pl.ds(pl.multiple_of((1 - here()[1]) * share, share), share)
    return near[:, at, :]


def far_kernel(x_ref, cot_ref, near_2, near_3, far_ref):
    chip, core, _ = here()
    share = far_ref.shape[2]
    at = pl.ds(pl.multiple_of((chip * 2 + 1 - core) * share, share), share)
    far_ref[0, 0], far_ref[0, 1] = x_ref[at, :], cot_ref[at, :]
    for i, near in enumerate((near_2, near_3)):
        far_ref[i + 1] = other_core(near, share)


def last_far_kernel(near_1, far_ref):
    far_ref[...] = other_core(near_1, far_ref.shape[1])


def back_kernel(grads_ref, w_ref, back_ref):
    grad_hidden = dot_nt(grads_ref[...], w_ref[...])
    all_rows, share, width = back_ref.shape
    group = math.gcd(share, 16)
    block = all_rows * group
    for i in range(share // group):
        piece = grad_hidden[i * block : (i + 1) * block].reshape(all_rows, group, width)
        back_ref[:, i * group : (i + 1) * group, :] = piece.astype(BF16)


def back_chip_kernel(grads_ref, w_ref, send_ref, keep_ref):
    grad_hidden = dot_nt(grads_ref[...], w_ref[...]).astype(BF16)
    chips, share, width = keep_ref.shape
    group = math.gcd(share, 16)
    block = 2 * chips * group
    for i in range(share // group):
        piece = grad_hidden[i * block : (i + 1) * block].reshape(chips, 2, group, width)
        at = slice(i * group, (i + 1) * group)
        keep_ref[:, at, :], send_ref[:, at, :] = piece[:, 0], piece[:, 1]


def back_pack_kernel(keep_ref, got_ref, *targets):
    share = keep_ref.shape[1]
    core = here()[1]
    kept_at = pl.ds(pl.multiple_of(core * share, share), share)
    got_at = pl.ds(pl.multiple_of((1 - core) * share, share), share)
    for i, target in enumerate(targets):
        target[kept_at, :] = keep_ref[i]
        target[got_at, :] = got_ref[i]


def input_kernel(base_ref, normed_ref, inverse_ref, gain_ref, back_ref, grad_ref):
    grad_ref[...] = input_grad(
        base_ref[...], normed_ref[...], inverse_ref[...], back_ref[...].astype(F32) * gain_ref[...]
    ).astype(BF16)


def input_grad(base, normed, inverse_rms, grad_normed):
    projected = jnp.mean(grad_normed * normed, -1, keepdims=True)
    return base + inverse_rms * (grad_normed - normed * projected)


def input_chip_kernel(
    base_ref, normed_ref, inverse_ref, gain_ref, own_ref, got_1, got_2, got_3,
    grad_any, grad_ref, sems,
):
    chip = here()[0]
    count = own_ref.shape[0]
    copies = []
    for i, (step, back_ref) in enumerate(zip(chip_steps(), (own_ref, got_1, got_2, got_3))):
        at = pl.ds(pl.multiple_of((chip ^ step) * count, count), count)
        grad_normed = back_ref[...].astype(F32) * gain_ref[...]
        grad = input_grad(base_ref[at, :], normed_ref[at, :], inverse_ref[at, :], grad_normed)
        grad_ref[i] = grad.astype(BF16)
        copies += started(pltpu.make_async_copy(grad_ref.at[i], grad_any.at[at, :], sems.at[i]))
    finished(*copies)


def pack_kernel(x_any, cot_any, off_1, off_2, off_3, sems):
    chip = here()[0]
    count = off_1.shape[1]
    copies = []
    for i, (step, target) in enumerate(zip(chip_steps()[1:], (off_1, off_2, off_3))):
        at = pl.ds(pl.multiple_of((chip ^ step) * count, count), count)
        for which, source in enumerate((x_any, cot_any)):
            copies.append(
                pltpu.make_async_copy(source.at[at, :], target.at[which], sems.at[2 * i + which])
            )
    finished(*started(*copies))


def split_rows(total, axis):
    upper = (here()[2] & 1) == 1
    low, high = jnp.split(total, 2, axis)
    return jnp.where(upper, low, high).astype(BF16), jnp.where(upper, high, low)


def row_cores_kernel(keep_1, keep_2, got_1, got_2, send_ref, kept_ref):
    total = [
        keep_ref[...].astype(F32) + got_ref[...].astype(F32)
        for keep_ref, got_ref in ((keep_1, got_1), (keep_2, got_2))
    ]
    send_ref[...], kept_ref[...] = split_rows(jnp.concatenate(total, 2), 1)


def cores_kernel(keep_ref, got_ref, send_ref, kept_ref, *targets):
    chip, cut = here()[0], kept_ref.shape[2]
    first = keep_ref[:, :, :cut].astype(F32) + got_ref[:, :, :cut].astype(F32)
    send_ref[...], kept_ref[...] = split_rows(first, 1)
    for step, target in zip(chip_steps(), targets):
        there = chip ^ step
        total = keep_ref[there, :, cut:].astype(F32) + got_ref[there, :, cut:].astype(F32)
        target[...] = total.astype(target.dtype)


def pair_kernel(kept_ref, got_ref, row_kept, row_got, *targets):
    chip, cut = here()[0], kept_ref.shape[2]
    for step, target in zip(chip_steps(), targets):
        there = chip ^ step
        total = kept_ref[there] + got_ref[there].astype(F32)
        target[:, :cut] = total.astype(target.dtype)
        total = row_kept[there] + row_got[there].astype(F32)
        target[:, cut:] = total.astype(target.dtype)


def layer_sum(own_ref, got_1, got_2, got_3):
    return own_ref[...] + (
        (got_1[...].astype(F32) + got_2[...].astype(F32)) + got_3[...].astype(F32)
    )


def layer_kernel(own_ref, got_1, got_2, got_3, send_ref, kept_ref):
    send_ref[...], kept_ref[...] = split_rows(layer_sum(own_ref, got_1, got_2, got_3), 0)


def join_kernel(own_ref, got_1, got_2, got_3, kept_ref, got_ref, out_ref):
    total = layer_sum(own_ref, got_1, got_2, got_3).astype(BF16)
    cut, width = FIRST_PART, kept_ref.shape[1]
    out_ref[:, :cut] = total[:, :cut]
    out_ref[:, cut : cut + width] = (kept_ref[...] + got_ref[...].astype(F32)).astype(BF16)
    out_ref[:, cut + width :] = total[:, cut:]


def add_kernel(kept_ref, got_ref, out_ref):
    out_ref[...] = (kept_ref[...].astype(F32) + got_ref[...].astype(F32)).astype(BF16)


def result_kernel(held_ref, got_ref, w_ref, gain_ref, qkv_ref, out_ref, grad_ref):
    rows = qkv_ref.shape[0]
    chip, core, layer = here()
    at = (chip * 2 + core) * rows
    upper = (layer & 1) == 1
    half = rows // 2
    width = out_ref.shape[1]

    def ordered(lanes):
        held, got = held_ref[:, lanes].astype(F32), got_ref[:, lanes].astype(F32)
        return (jnp.where(upper, got, held), jnp.where(upper, held, got))

    row_at = 3 * HW + width
    for i in range(3):
        for at_from, at_to in ((row_at + i * HW, i * width), (i * HW, i * width + HW)):
            to = slice(at_to, at_to + HW)
            qkv_ref[:half, to], qkv_ref[half:, to] = ordered(slice(at_from, at_from + HW))
    out_ref[:half], out_ref[half:] = ordered(slice(3 * HW, row_at))
    total = jnp.sum(qkv_ref[...] * w_ref[...].astype(F32), -1, keepdims=True)
    shape = (rows, gain_ref.shape[1])
    row = lax.broadcasted_iota(jnp.int32, shape, 0)
    feature = lax.broadcasted_iota(jnp.int32, shape, 1)
    gain = jnp.sum(jnp.where(feature == row + at, gain_ref[...], 0.0), -1, keepdims=True)
    shape = (rows, grad_ref.shape[1])
    same = lax.broadcasted_iota(jnp.int32, shape, 0) == lax.broadcasted_iota(jnp.int32, shape, 1)
    grad_ref[...] = jnp.sum(jnp.where(same, total / gain, 0.0), 0, keepdims=True)


def call(kernel, name, ins, outs, scratch=(), vmem=SMALL_VMEM, out_specs=None):
    out_specs = out_specs or [VMEM] * len(outs)
    places = [{id(HBM): pltpu.HBM, id(PINNED): pltpu.VMEM}.get(id(spec)) for spec in out_specs]
    outs = [place(*out) if place else shaped(*out) for place, out in zip(places, outs)]
    args = [
        pltpu.with_memory_space_constraint(array, pltpu.HBM) if spec is HBM else array
        for spec, array in ins
    ]
    return pl.pallas_call(
        kernel,
        out_shape=outs,
        in_specs=[spec for spec, _ in ins],
        out_specs=out_specs,
        scratch_shapes=scratch,
        name=name,
        cost_estimate=pl.CostEstimate(flops=0, bytes_accessed=0, transcendentals=0),
        compiler_params=pltpu.CompilerParams(vmem_limit_bytes=vmem),
    )(*args)


def swap(array, axis, bits):
    count = lax.axis_size(axis)
    return lax.ppermute(array, axis, [(i, i ^ bits) for i in range(count)])


def cross_chips(*offs):
    count = lax.axis_size("seq")
    return [
        lax.ppermute(off, "seq", [(d, d ^ 2 * steps[d & 1]) for d in range(count)])
        for off, steps in zip(offs, zip(*CHIP_STEPS))
    ]


def add_two(kept, got, name):
    (total,) = call(add_kernel, name, [(VMEM, kept), (VMEM, got)], [(kept.shape, BF16)])
    return total


def body(inputs, norm_gain, qkv_weight, out_weight, out_cotan):
    columns, width = inputs.shape[2:]
    n = lax.axis_size("seq")
    m = lax.axis_size("dp")
    share = columns // n
    row_share = width // n
    row_width, col_width = 3 * HW, 3 * HW + width
    x = inputs.reshape(columns, width)
    cot = out_cotan.reshape(columns, width)
    gain = norm_gain.reshape(1, width)
    chips = 4
    layered = n == 2 * chips and m == 4 and row_share == share
    weight_scratch = [
        pltpu.VMEM((1, width), F32),
        pltpu.VMEM((width, 3 * HW), BF16),
        pltpu.VMEM((HW, width), BF16),
    ]
    weights = [(HBM, gain), (HBM, qkv_weight), (HBM, out_weight)]
    col_outs = [((columns, 3 * HW), BF16), ((width, 3 * HW), BF16)]

    if layered:
        packed = call(
            pack_kernel,
            "pack_columns",
            [(HBM, x), (HBM, cot)],
            [((2, 2 * share, width), BF16)] * 3,
            [pltpu.SemaphoreType.DMA((6,))],
            out_specs=[ANY] * 3,
        )
        near = cross_chips(*packed)
        x_first, _ = lax.optimization_barrier((x, packed[0]))
    else:
        outgoing = jnp.stack([x.reshape(n, share, width), cot.reshape(n, share, width)], 1)
        moved = lax.all_to_all(outgoing, "seq", split_axis=0, concat_axis=0, tiled=True)
        x_first = x

    row_outs = [
        ((HW, width), BF16),
        ((columns, width), F32), ((columns, width), F32), ((columns, 1), F32),
        ((columns, width), BF16), ((columns, width), BF16),
    ]
    if layered:
        cut = row_width // 2
        split_outs = [((chips, row_share, cut), BF16)] * 4
        handed_outs = [
            ((row_share, 3 * width), BF16), ((width, 3 * HW), BF16), ((HW, width), BF16),
        ]
        row_outs = [*split_outs, *handed_outs, *row_outs]
        specs = [VMEM] * 4 + [PINNED] * (len(row_outs) - 4)
    else:
        row_outs = [((width, row_width), BF16), *row_outs]
        specs = [VMEM] * len(row_outs)
    *row_terms, row_out, base, normed, inverse_rms, x_near, cot_near = call(
        row_chip_kernel if layered else row_kernel,
        "row_heads",
        [(HBM, x_first), (HBM, cot), *weights],
        row_outs,
        [
            *weight_scratch,
            pltpu.VMEM((columns, HW), F32),
            pltpu.VMEM((columns, HW), F32),
            pltpu.VMEM((columns, 3 * HW), BF16),
            pltpu.SemaphoreType.DMA((12,)),
        ],
        BIG_VMEM,
        specs,
    )
    if layered:
        *row_terms, weight_rows, col_weight, col_out_weight = row_terms
        row_sent = [swap(one, "seq", 1) for one in row_terms[:2]]
        half_block = (chips, row_share // 2, row_width)
        row_next, row_kept = call(
            row_cores_kernel,
            "row_add_cores",
            [(VMEM, one) for one in (*row_terms[2:], *row_sent)],
            [(half_block, BF16), (half_block, F32)],
            out_specs=[VMEM, PINNED],
        )
        col_weight, row_kept = lax.optimization_barrier((col_weight, row_kept))
        (far,) = call(
            far_kernel,
            "pack_other_core",
            [(VMEM, one) for one in (x_near, cot_near, *near[1:])],
            [((3, 2, share, width), BF16)],
        )
        near[0], _ = lax.optimization_barrier((near[0], far))
        (last,) = call(
            last_far_kernel,
            "pack_other_core_last",
            [(VMEM, near[0])],
            [((2, share, width), BF16)],
        )
        send, keep, col_grads = call(
            column_chip_kernel,
            "column_heads",
            [
                (VMEM, one)
                for one in (
                    x_near, cot_near, *near, swap(far, "seq", 1), swap(last, "seq", 1),
                    gain, col_weight, col_out_weight, row_out,
                )
            ],
            [((chips, row_share, col_width), BF16)] * 2 + [col_outs[0]],
            vmem=BIG_VMEM,
            out_specs=[VMEM, VMEM, PINNED],
        )
        back_send, back_keep = call(
            back_chip_kernel,
            "column_grad_hidden",
            [(VMEM, col_grads), (VMEM, col_weight)],
            [((chips, share, width), BF16)] * 2,
        )
        row_next, _ = lax.optimization_barrier((row_next, send))
        keep, back_keep = lax.optimization_barrier((keep, back_keep))
        first_half = (chips, row_share // 2, FIRST_PART)
        second = (row_share, col_width - FIRST_PART)
        to_next, kept, owned, *off = call(
            cores_kernel,
            "column_add_cores",
            [(VMEM, keep), (VMEM, swap(send, "seq", 1))],
            [(first_half, BF16), (first_half, F32), (second, F32)] + [(second, BF16)] * 3,
            out_specs=[VMEM, PINNED, PINNED, VMEM, VMEM, VMEM],
        )
        got = cross_chips(*off)
        back = call(
            back_pack_kernel,
            "pack_grad_hidden",
            [(VMEM, back_keep), (VMEM, swap(back_send, "seq", 1))],
            [((2 * share, width), BF16)] * 4,
        )
        row_kept, *back = lax.optimization_barrier((row_kept, *back))
        joint = (row_share // 2, FIRST_PART + row_width)
        first_owned, *off = call(
            pair_kernel,
            "first_add_pair",
            [
                (VMEM, one)
                for one in (kept, swap(to_next, "dp", 1), row_kept, swap(row_next, "dp", 1))
            ],
            [(joint, F32)] + [(joint, BF16)] * 3,
            out_specs=[PINNED, VMEM, VMEM, VMEM],
        )
        first_got = cross_chips(*off)
        second_half = (row_share // 2, second[1])
        to_next, kept = call(
            layer_kernel,
            "second_add_chips",
            [(VMEM, one) for one in (owned, *got)],
            [(second_half, BF16), (second_half, F32)],
            out_specs=[VMEM, PINNED],
        )
        (pair_sum,) = call(
            join_kernel,
            "join_terms",
            [(VMEM, one) for one in (first_owned, *first_got, kept, swap(to_next, "dp", 1))],
            [((row_share // 2, col_width + row_width), BF16)],
        )
        *back, pair_sum = lax.optimization_barrier((*back, pair_sum))
        held = add_two(pair_sum, swap(pair_sum, "dp", 2), "add_pairs")
        other = swap(held, "dp", 1)
        (grad,) = call(
            input_chip_kernel,
            "input_grad",
            [
                (VMEM, one)
                for one in (base, normed, inverse_rms, gain, back[0], *cross_chips(*back[1:]))
            ],
            [((columns, width), BF16)],
            [pltpu.VMEM((chips, 2 * share, width), BF16), pltpu.SemaphoreType.DMA((chips,))],
            out_specs=[HBM],
        )
        sum_qkv, sum_out, sum_gain = call(
            result_kernel,
            "result",
            [(VMEM, held), (VMEM, other), (VMEM, weight_rows), (VMEM, gain)],
            [((row_share, 3 * width), F32), ((row_share, width), F32), ((1, row_share), F32)],
        )
        sum_gain = sum_gain.reshape(row_share)
    else:
        terms, *col_grads = call(
            column_kernel,
            "column_heads",
            [(ANY, moved), *weights, (VMEM, row_terms[0]), (VMEM, row_out)],
            [((width, 4 * width), BF16), *col_outs],
            [
                pltpu.VMEM((n, 2, share, width), BF16),
                weight_scratch[0],
                weight_scratch[2],
                pltpu.SemaphoreType.DMA((6,)),
            ],
            BIG_VMEM,
        )
        (back,) = call(
            back_kernel,
            "column_grad_hidden",
            [(VMEM, one) for one in col_grads],
            [((n, share, width), BF16)],
        )
        returned = lax.all_to_all(back, "seq", split_axis=0, concat_axis=0, tiled=True)
        (grad,) = call(
            input_kernel,
            "input_grad",
            [
                (VMEM, base), (VMEM, normed), (VMEM, inverse_rms), (VMEM, gain),
                (VMEM, returned.reshape(columns, width)),
            ],
            [((columns, width), BF16)],
        )
        terms = lax.all_to_all(
            terms.reshape(n, row_share, 4 * width), "seq", split_axis=0, concat_axis=0, tiled=True
        )
        total = jnp.sum(terms.astype(F32), 0)
        for step in range(m.bit_length() - 1):
            sent = total.astype(BF16)
            total = sent.astype(F32) + swap(sent, "dp", 1 << step).astype(F32)
        sum_qkv, sum_out = total[:, : 3 * width], total[:, 3 * width :]
        here_at = lax.axis_index("seq") * row_share
        own_gain = lax.dynamic_slice_in_dim(norm_gain, here_at, row_share, 0)
        own_weight = lax.dynamic_slice_in_dim(qkv_weight, here_at, row_share, 0)
        sum_gain = jnp.sum(sum_qkv * own_weight.astype(F32), -1) / own_gain
    return (grad.reshape(inputs.shape), sum_qkv, sum_out, sum_gain)


def solution(mesh):
    return jax.shard_map(
        body,
        mesh=mesh,
        in_specs=(P("dp", "seq", None, None), P(), P(), P(), P("dp", "seq", None, None)),
        out_specs=(P("dp", "seq", None, None), P("seq", None), P("seq", None), P("seq")),
        check_vma=False,
    )
```

```python
import math

import jax
import jax.numpy as jnp
from jax import lax
from jax.experimental import pallas as pl
from jax.experimental.pallas import tpu as pltpu
from jax.sharding import PartitionSpec as P

H = 8
HD = 64
HH = H // 2
HW = HH * HD
SCALE = HD ** (-0.5)
F32 = jnp.float32
BF16 = jnp.bfloat16
QUERY_BLOCK = 128
BIG_VMEM = 20 * 1024 * 1024
SMALL_VMEM = 8 * 1024 * 1024
ANY = pl.BlockSpec(memory_space=pl.ANY)
VMEM = pl.BlockSpec(memory_space=pltpu.VMEM)
HBM = pl.BlockSpec(memory_space=pltpu.HBM)
CHIP_STEPS = ((3, 2, 1), (3, 1, 2))
TERM_STEPS = (3, 2, 1)
FIRST_PART = 384
PINNED = pl.BlockSpec(memory_space=pltpu.VMEM)
shaped = jax.ShapeDtypeStruct


def here():
    device = lax.axis_index("seq")
    return device >> 1, device & 1, lax.axis_index("dp")


def chip_steps():
    core = here()[1]
    return [0] + [jnp.where(core == 0, even, odd) for even, odd in zip(*CHIP_STEPS)]


def dot_nn(a, b):
    return lax.dot_general(a, b, (((1,), (0,)), ((), ())), preferred_element_type=F32)


def dot_nt(a, b):
    return lax.dot_general(a, b, (((1,), (1,)), ((), ())), preferred_element_type=F32)


def rms_parts(x):
    inverse_rms = lax.rsqrt(jnp.mean(x * x, -1, keepdims=True) + 1e-05)
    return inverse_rms, x * inverse_rms


def transposed(x):
    block = math.gcd(x.shape[1], 256)
    eye = (
        lax.broadcasted_iota(jnp.int32, (block, block), 0)
        == lax.broadcasted_iota(jnp.int32, (block, block), 1)
    ).astype(F32).astype(BF16)
    parts = [
        dot_nt(eye, x[:, at : at + block]).astype(BF16) for at in range(0, x.shape[1], block)
    ]
    return parts[0] if len(parts) == 1 else jnp.concatenate(parts, 0)


def head_pair(x):
    lane = lax.broadcasted_iota(jnp.int32, x.shape, 1)
    zero = jnp.zeros_like(x)
    return jnp.concatenate([jnp.where(lane < HD, x, zero), jnp.where(lane < HD, zero, x)], 0)


def both_heads(both, count):
    return jnp.concatenate([both[:HD, :count], both[HD:, count:]], 0)


def pair_steps(items, mask_rows, mask):
    count = items[0][2].shape[1]
    scores = [dot_nt(k, q2) for q2, _, _, k, _, _, _ in items]
    prob_grads = [dot_nt(v, g2) for _, g2, _, _, v, _, _ in items]
    probs = []
    for score in scores:
        first = score.shape[0] - mask_rows
        tail = jnp.where(mask, score[first:], -1e30)
        score = tail if first == 0 else jnp.concatenate([score[:first], tail], 0)
        exponent = jnp.exp(score - jnp.max(score, 0, keepdims=True))
        probs.append(exponent * (1.0 / jnp.sum(exponent, 0, keepdims=True)))
    weights = [prob.astype(BF16) for prob in probs]
    attended = [
        both_heads(dot_nn(item[6], weight), count).astype(BF16)
        for item, weight in zip(items, weights)
    ]
    score_grads = []
    for item, att, prob, prob_grad in zip(items, attended, probs, prob_grads):
        product = item[2].astype(F32) * att.astype(F32)
        delta = [jnp.sum(part, 0, keepdims=True) for part in (product[:HD], product[HD:])]
        score_grads.append((prob * (prob_grad - jnp.concatenate(delta, 1))).astype(BF16))
    grad_q = [
        (both_heads(dot_nn(item[5], score_grad), count) * SCALE).astype(BF16)
        for item, score_grad in zip(items, score_grads)
    ]
    grad_k = [dot_nn(score_grad, item[0]) for item, score_grad in zip(items, score_grads)]
    grad_v = [dot_nn(weight, item[1]) for item, weight in zip(items, weights)]
    return list(zip(attended, grad_q, grad_k, grad_v))


def split_cores(piece, send_ref, keep_ref, chips, lanes):
    rows = send_ref.shape[1]
    parts = piece.reshape(chips.stop - chips.start, 2, rows, piece.shape[1])
    even, odd = parts[:, 0], parts[:, 1]
    first = here()[1] == 0
    send_ref[chips, :, lanes] = jnp.where(first, odd, even)
    keep_ref[chips, :, lanes] = jnp.where(first, even, odd)


def qkv_copies(wqkv_ref, w_ref, sems, second):
    width = wqkv_ref.shape[0]
    return [
        pltpu.make_async_copy(
            wqkv_ref.at[:, pl.ds(i * width + second * HW, HW)],
            w_ref.at[:, pl.ds(i * HW, HW)],
            sems.at[i],
        )
        for i in range(3)
    ]


def weight_copies(wqkv_ref, wout_ref, w_ref, wo_ref, sems, second):
    out_rows = wout_ref.at[pl.ds(second * HW, HW), :]
    return [
        *qkv_copies(wqkv_ref, w_ref, sems, second),
        pltpu.make_async_copy(out_rows, wo_ref, sems.at[3]),
    ]


def started(*copies):
    for copy in copies:
        copy.start()
    return copies


def finished(*copies):
    for copy in copies:
        copy.wait()


def project(hidden, cot, w_ref, wo_ref):
    projected = dot_nn(hidden, w_ref[...]).astype(BF16)
    q, k, v = [projected[:, i * HW : (i + 1) * HW] for i in range(3)]
    g = dot_nt(cot, wo_ref[...]).astype(BF16)
    return q * jnp.asarray(SCALE, BF16), k, v, g


def row_part(
    x_any, cot_any, gain_any, wqkv_any, wout_any,
    out_ref, base_ref, normed_ref, inverse_ref, x_ref, cot_ref,
    gain_ref, w_ref, wo_ref, dk_ref, dv_ref, grads_ref, sems,
):
    first = started(
        pltpu.make_async_copy(x_any, x_ref, sems.at[4]),
        pltpu.make_async_copy(gain_any, gain_ref, sems.at[5]),
    )
    later = started(
        *weight_copies(wqkv_any, wout_any, w_ref, wo_ref, sems, 0),
        pltpu.make_async_copy(cot_any, cot_ref, sems.at[6]),
    )
    dk_ref[...] = jnp.zeros_like(dk_ref)
    dv_ref[...] = jnp.zeros_like(dv_ref)
    finished(*first)
    tokens = x_ref.shape[0]
    inverse_ref[...], normed_ref[...] = rms_parts(x_ref[...].astype(F32))
    hidden = (normed_ref[...] * gain_ref[...]).astype(BF16)
    hidden_t = transposed(hidden)
    finished(*later)
    cot = cot_ref[...]
    q, k, v, g = project(hidden, cot, w_ref, wo_ref)
    kt, vt, gt = transposed(k), transposed(v), transposed(g)
    step = math.gcd(tokens, QUERY_BLOCK)
    query = lax.broadcasted_iota(jnp.int32, (step, 2 * step), 1) % step
    mask = query >= lax.broadcasted_iota(jnp.int32, (step, 2 * step), 0)
    pairs = [slice(i * 2 * HD, (i + 1) * 2 * HD) for i in range(HH // 2)]
    att_blocks, dq_blocks = [], []
    for start in range(0, tokens, step):
        rows, keys = slice(start, start + step), slice(0, start + step)
        items = [
            (
                head_pair(q[rows, lanes]), head_pair(g[rows, lanes]), gt[lanes, rows],
                k[keys, lanes], v[keys, lanes], kt[lanes, keys], vt[lanes, keys],
            )
            for lanes in pairs
        ]
        results = pair_steps(items, step, mask)
        for lanes, (_, _, dk, dv) in zip(pairs, results):
            dk_ref[keys, lanes] += dk
            dv_ref[keys, lanes] += dv
        att_blocks.append(jnp.concatenate([result[0] for result in results], 0))
        dq_blocks.append(jnp.concatenate([result[1] for result in results], 0))
    grads_ref[:, :HW] = transposed(jnp.concatenate(dq_blocks, 1))
    grads_ref[:, HW : 2 * HW] = dk_ref[...].astype(BF16)
    grads_ref[:, 2 * HW :] = dv_ref[...].astype(BF16)
    term_qkv = dot_nn(hidden_t, grads_ref[...]).astype(BF16)
    out_ref[...] = dot_nn(jnp.concatenate(att_blocks, 1), cot).astype(BF16)
    grad_normed = dot_nt(grads_ref[...], w_ref[...]) * gain_ref[...]
    base_ref[...] = input_grad(
        cot_ref[...].astype(F32), normed_ref[...], inverse_ref[...], grad_normed
    )
    return term_qkv


def row_kernel(x_any, cot_any, gain_any, wqkv_any, wout_any, qkv_ref, *refs):
    qkv_ref[...] = row_part(x_any, cot_any, gain_any, wqkv_any, wout_any, *refs)


def row_chip_kernel(
    x_any, cot_any, gain_any, wqkv_any, wout_any,
    send_1, send_2, keep_1, keep_2, rows_ref, col_w_ref, col_wo_ref, *refs,
):
    chip, core, _ = here()
    sems, rows = refs[-1], rows_ref.shape[0]
    at = pl.multiple_of((chip * 2 + core) * rows, rows)
    handed = started(
        pltpu.make_async_copy(wqkv_any.at[pl.ds(at, rows), :], rows_ref, sems.at[7]),
        *weight_copies(wqkv_any, wout_any, col_w_ref, col_wo_ref, sems.at[pl.ds(8, 4)], 1),
    )
    term_qkv = row_part(x_any, cot_any, gain_any, wqkv_any, wout_any, *refs)
    chips, cut = send_1.shape[0], keep_1.shape[2]
    pieces = slice(0, chips), slice(0, cut)
    split_cores(term_qkv[:, :cut], send_1, keep_1, *pieces)
    split_cores(term_qkv[:, cut:], send_2, keep_2, *pieces)
    finished(*handed)


def column_part(x, cot, mask, gain, w_ref, wo_ref, weight_waits, grads_ref):
    tokens, block = x.shape[0], mask.shape[0]
    _, normed = rms_parts(x.astype(F32))
    hidden = (normed * gain).astype(BF16)
    hidden_t = transposed(hidden)
    finished(*weight_waits)
    q, k, v, g = project(hidden, cot, w_ref, wo_ref)
    kt, vt, gt = transposed(k), transposed(v), transposed(g)
    pairs = [slice(i * 2 * HD, (i + 1) * 2 * HD) for i in range(HH // 2)]
    blocks = [slice(at, at + block) for at in range(0, tokens, block)]
    items = [
        (
            head_pair(q[rows, lanes]), head_pair(g[rows, lanes]), gt[lanes, rows],
            k[rows, lanes], v[rows, lanes], kt[lanes, rows], vt[lanes, rows],
        )
        for lanes in pairs
        for rows in blocks
    ]
    results = pair_steps(items, block, mask)
    places = [(lanes, rows) for lanes in pairs for rows in blocks]
    for (lanes, rows), (_, _, dk, dv) in zip(places, results):
        grads_ref[rows, HW + lanes.start : HW + lanes.stop] = dk.astype(BF16)
        grads_ref[rows, 2 * HW + lanes.start : 2 * HW + lanes.stop] = dv.astype(BF16)
    by_pair = [results[i * len(blocks) : (i + 1) * len(blocks)] for i in range(len(pairs))]
    attended, grad_q = [
        jnp.concatenate([jnp.concatenate([r[i] for r in some], 1) for some in by_pair], 0)
        for i in range(2)
    ]
    grads_ref[:, :HW] = transposed(grad_q)
    term_qkv = dot_nn(hidden_t, grads_ref[...]).astype(BF16)
    term_out = dot_nn(attended, cot).astype(BF16)
    return term_qkv, term_out


def column_mask(all_rows, group, row_of):
    block = all_rows * group
    shape = (block, 2 * block)
    query = lax.broadcasted_iota(jnp.int32, shape, 1) % block
    key = lax.broadcasted_iota(jnp.int32, shape, 0)
    same_column = query % group == key % group
    return (row_of(query // group) >= row_of(key // group)) & same_column


def column_kernel(
    moved_any, gain_any, wqkv_any, wout_any, row_qkv_ref, row_out_ref,
    terms_ref, grads_ref, w_ref,
    moved_ref, gain_ref, wo_ref, sems,
):
    copies = started(
        pltpu.make_async_copy(moved_any, moved_ref, sems.at[4]),
        pltpu.make_async_copy(gain_any, gain_ref, sems.at[5]),
    )
    weights = started(*weight_copies(wqkv_any, wout_any, w_ref, wo_ref, sems, 1))
    finished(*copies)
    all_rows, _, share, width = moved_ref.shape
    group = math.gcd(share, 16)
    x, cot = [
        jnp.concatenate(
            [
                moved_ref[:, which, at : at + group, :].astype(F32).reshape(all_rows * group, width)
                for at in range(0, share, group)
            ],
            0,
        ).astype(BF16)
        for which in range(2)
    ]
    mask = column_mask(all_rows, group, lambda place: place)
    term_qkv, term_out = column_part(
        x, cot, mask, gain_ref[...], w_ref, wo_ref, weights, grads_ref
    )
    for i in range(3):
        at = i * width
        terms_ref[:, at : at + HW] = row_qkv_ref[:, i * HW : (i + 1) * HW]
        terms_ref[:, at + HW : at + 2 * HW] = term_qkv[:, i * HW : (i + 1) * HW]
    terms_ref[:HW, 3 * width :] = row_out_ref[...]
    terms_ref[HW:, 3 * width :] = term_out


def column_chip_kernel(
    x_ref, cot_ref, near_1, near_2, near_3, far_ref, gain_ref, w_ref, wo_ref, row_out_ref,
    send_ref, keep_ref, grads_ref,
):
    chip, core, _ = here()
    share = far_ref.shape[2]
    half = pl.ds(pl.multiple_of(core * share, share), share)
    at = pl.ds(pl.multiple_of((chip * 2 + core) * share, share), share)
    group = math.gcd(share, 16)

    def tokens(which, mine):
        pieces = [mine[at, :], far_ref[0, which]]
        for i, near in enumerate((near_1, near_2, near_3)):
            pieces += [near[which, half, :], far_ref[i + 1, which]]
        starts = range(0, share, group)
        return jnp.concatenate(
            [piece[start : start + group] for start in starts for piece in pieces], 0
        )

    def row_of(place):
        owner, step = (place & 1) ^ core, 0
        for i, (even, odd) in enumerate(zip(*CHIP_STEPS)):
            step = jnp.where(place >> 1 == i + 1, jnp.where(owner == 0, even, odd), step)
        return ((step ^ chip) << 1) + owner

    mask = column_mask(2 * (len(CHIP_STEPS[0]) + 1), group, row_of)
    term_qkv, term_out = column_part(
        tokens(0, x_ref), tokens(1, cot_ref), mask, gain_ref[...], w_ref, wo_ref, (), grads_ref
    )
    chips = send_ref.shape[0]
    refs = send_ref, keep_ref
    out_lanes = slice(3 * HW, send_ref.shape[2])
    split_cores(term_qkv, *refs, slice(0, chips), slice(0, 3 * HW))
    split_cores(row_out_ref[...], *refs, slice(0, chips // 2), out_lanes)
    split_cores(term_out, *refs, slice(chips // 2, chips), out_lanes)


def far_kernel(x_ref, cot_ref, near_1, near_2, near_3, far_ref):
    chip, core, _ = here()
    share = far_ref.shape[2]
    at = pl.ds(pl.multiple_of((chip * 2 + 1 - core) * share, share), share)
    far_ref[0, 0], far_ref[0, 1] = x_ref[at, :], cot_ref[at, :]
    at = pl.ds(pl.multiple_of((1 - core) * share, share), share)
    for i, near in enumerate((near_1, near_2, near_3)):
        far_ref[i + 1] = near[:, at, :]


def back_kernel(grads_ref, w_ref, back_ref):
    grad_hidden = dot_nt(grads_ref[...], w_ref[...])
    all_rows, share, width = back_ref.shape
    group = math.gcd(share, 16)
    block = all_rows * group
    for i in range(share // group):
        piece = grad_hidden[i * block : (i + 1) * block].reshape(all_rows, group, width)
        back_ref[:, i * group : (i + 1) * group, :] = piece.astype(BF16)


def back_chip_kernel(grads_ref, w_ref, send_ref, keep_ref):
    grad_hidden = dot_nt(grads_ref[...], w_ref[...]).astype(BF16)
    chips, share, width = keep_ref.shape
    group = math.gcd(share, 16)
    block = 2 * chips * group
    for i in range(share // group):
        piece = grad_hidden[i * block : (i + 1) * block].reshape(chips, 2, group, width)
        at = slice(i * group, (i + 1) * group)
        keep_ref[:, at, :], send_ref[:, at, :] = piece[:, 0], piece[:, 1]


def back_pack_kernel(keep_ref, got_ref, *targets):
    share = keep_ref.shape[1]
    core = here()[1]
    kept_at = pl.ds(pl.multiple_of(core * share, share), share)
    got_at = pl.ds(pl.multiple_of((1 - core) * share, share), share)
    for i, target in enumerate(targets):
        target[kept_at, :] = keep_ref[i]
        target[got_at, :] = got_ref[i]


def input_kernel(base_ref, normed_ref, inverse_ref, gain_ref, back_ref, grad_ref):
    grad_ref[...] = input_grad(
        base_ref[...], normed_ref[...], inverse_ref[...], back_ref[...].astype(F32) * gain_ref[...]
    ).astype(BF16)


def input_grad(base, normed, inverse_rms, grad_normed):
    projected = jnp.mean(grad_normed * normed, -1, keepdims=True)
    return base + inverse_rms * (grad_normed - normed * projected)


def input_chip_kernel(
    base_ref, normed_ref, inverse_ref, gain_ref, own_ref, got_1, got_2, got_3,
    grad_any, grad_ref, sems,
):
    chip = here()[0]
    count = own_ref.shape[0]
    copies = []
    for i, (step, back_ref) in enumerate(zip(chip_steps(), (own_ref, got_1, got_2, got_3))):
        at = pl.ds(pl.multiple_of((chip ^ step) * count, count), count)
        grad_normed = back_ref[...].astype(F32) * gain_ref[...]
        grad = input_grad(base_ref[at, :], normed_ref[at, :], inverse_ref[at, :], grad_normed)
        grad_ref[i] = grad.astype(BF16)
        copies += started(pltpu.make_async_copy(grad_ref.at[i], grad_any.at[at, :], sems.at[i]))
    finished(*copies)


def pack_kernel(x_any, cot_any, off_1, off_2, off_3, sems):
    chip = here()[0]
    count = off_1.shape[1]
    copies = []
    for i, (step, target) in enumerate(zip(chip_steps()[1:], (off_1, off_2, off_3))):
        at = pl.ds(pl.multiple_of((chip ^ step) * count, count), count)
        for which, source in enumerate((x_any, cot_any)):
            copies.append(
                pltpu.make_async_copy(source.at[at, :], target.at[which], sems.at[2 * i + which])
            )
    finished(*started(*copies))


def split_rows(total, axis):
    upper = (here()[2] & 1) == 1
    low, high = jnp.split(total, 2, axis)
    return jnp.where(upper, low, high).astype(BF16), jnp.where(upper, high, low)


def row_cores_kernel(keep_1, keep_2, got_1, got_2, send_ref, kept_ref):
    total = [
        keep_ref[...].astype(F32) + got_ref[...].astype(F32)
        for keep_ref, got_ref in ((keep_1, got_1), (keep_2, got_2))
    ]
    send_ref[...], kept_ref[...] = split_rows(jnp.concatenate(total, 2), 1)


def cores_kernel(keep_ref, got_ref, send_ref, kept_ref, *targets):
    chip, cut = here()[0], kept_ref.shape[2]
    first = keep_ref[:, :, :cut].astype(F32) + got_ref[:, :, :cut].astype(F32)
    send_ref[...], kept_ref[...] = split_rows(first, 1)
    for step, target in zip((0, *TERM_STEPS), targets):
        there = chip ^ step
        total = keep_ref[there, :, cut:].astype(F32) + got_ref[there, :, cut:].astype(F32)
        target[...] = total.astype(target.dtype)


def pair_kernel(kept_ref, got_ref, row_kept, row_got, *targets):
    chip, cut = here()[0], kept_ref.shape[2]
    for step, target in zip((0, *TERM_STEPS), targets):
        there = chip ^ step
        total = kept_ref[there] + got_ref[there].astype(F32)
        target[:, :cut] = total.astype(target.dtype)
        total = row_kept[there] + row_got[there].astype(F32)
        target[:, cut:] = total.astype(target.dtype)


def layer_sum(own_ref, got_1, got_2, got_3):
    return own_ref[...] + (
        (got_1[...].astype(F32) + got_2[...].astype(F32)) + got_3[...].astype(F32)
    )


def layer_kernel(own_ref, got_1, got_2, got_3, send_ref, kept_ref):
    send_ref[...], kept_ref[...] = split_rows(layer_sum(own_ref, got_1, got_2, got_3), 0)


def join_kernel(own_ref, got_1, got_2, got_3, kept_ref, got_ref, out_ref):
    total = layer_sum(own_ref, got_1, got_2, got_3).astype(BF16)
    cut, width = FIRST_PART, kept_ref.shape[1]
    out_ref[:, :cut] = total[:, :cut]
    out_ref[:, cut : cut + width] = (kept_ref[...] + got_ref[...].astype(F32)).astype(BF16)
    out_ref[:, cut + width :] = total[:, cut:]


def add_kernel(kept_ref, got_ref, out_ref):
    out_ref[...] = (kept_ref[...].astype(F32) + got_ref[...].astype(F32)).astype(BF16)


def result_kernel(held_ref, got_ref, w_ref, gain_ref, qkv_ref, out_ref, grad_ref):
    rows = qkv_ref.shape[0]
    chip, core, layer = here()
    at = (chip * 2 + core) * rows
    upper = (layer & 1) == 1
    half = rows // 2
    width = out_ref.shape[1]

    def ordered(lanes):
        held, got = held_ref[:, lanes].astype(F32), got_ref[:, lanes].astype(F32)
        return (jnp.where(upper, got, held), jnp.where(upper, held, got))

    row_at = 3 * HW + width
    for i in range(3):
        for at_from, at_to in ((row_at + i * HW, i * width), (i * HW, i * width + HW)):
            to = slice(at_to, at_to + HW)
            qkv_ref[:half, to], qkv_ref[half:, to] = ordered(slice(at_from, at_from + HW))
    out_ref[:half], out_ref[half:] = ordered(slice(3 * HW, row_at))
    total = jnp.sum(qkv_ref[...] * w_ref[...].astype(F32), -1, keepdims=True)
    shape = (rows, gain_ref.shape[1])
    row = lax.broadcasted_iota(jnp.int32, shape, 0)
    feature = lax.broadcasted_iota(jnp.int32, shape, 1)
    gain = jnp.sum(jnp.where(feature == row + at, gain_ref[...], 0.0), -1, keepdims=True)
    shape = (rows, grad_ref.shape[1])
    same = lax.broadcasted_iota(jnp.int32, shape, 0) == lax.broadcasted_iota(jnp.int32, shape, 1)
    grad_ref[...] = jnp.sum(jnp.where(same, total / gain, 0.0), 0, keepdims=True)


def call(kernel, name, ins, outs, scratch=(), vmem=SMALL_VMEM, out_specs=None):
    out_specs = out_specs or [VMEM] * len(outs)
    places = [{id(HBM): pltpu.HBM, id(PINNED): pltpu.VMEM}.get(id(spec)) for spec in out_specs]
    outs = [place(*out) if place else shaped(*out) for place, out in zip(places, outs)]
    args = [
        pltpu.with_memory_space_constraint(array, pltpu.HBM) if spec is HBM else array
        for spec, array in ins
    ]
    return pl.pallas_call(
        kernel,
        out_shape=outs,
        in_specs=[spec for spec, _ in ins],
        out_specs=out_specs,
        scratch_shapes=scratch,
        name=name,
        cost_estimate=pl.CostEstimate(flops=0, bytes_accessed=0, transcendentals=0),
        compiler_params=pltpu.CompilerParams(vmem_limit_bytes=vmem),
    )(*args)


def swap(array, axis, bits):
    count = lax.axis_size(axis)
    return lax.ppermute(array, axis, [(i, i ^ bits) for i in range(count)])


def cross_chips(offs, by_core=CHIP_STEPS):
    count = lax.axis_size("seq")
    return [
        lax.ppermute(off, "seq", [(d, d ^ 2 * steps[d & 1]) for d in range(count)])
        for off, steps in zip(offs, zip(*by_core))
    ]


def add_two(kept, got, name):
    (total,) = call(add_kernel, name, [(VMEM, kept), (VMEM, got)], [(kept.shape, BF16)])
    return total


def body(inputs, norm_gain, qkv_weight, out_weight, out_cotan):
    columns, width = inputs.shape[2:]
    n = lax.axis_size("seq")
    m = lax.axis_size("dp")
    share = columns // n
    row_share = width // n
    row_width, col_width = 3 * HW, 3 * HW + width
    x = inputs.reshape(columns, width)
    cot = out_cotan.reshape(columns, width)
    gain = norm_gain.reshape(1, width)
    chips = 4
    layered = n == 2 * chips and m == 4 and row_share == share
    weight_scratch = [
        pltpu.VMEM((1, width), F32),
        pltpu.VMEM((width, 3 * HW), BF16),
        pltpu.VMEM((HW, width), BF16),
    ]
    weights = [(HBM, gain), (HBM, qkv_weight), (HBM, out_weight)]
    col_outs = [((columns, 3 * HW), BF16), ((width, 3 * HW), BF16)]

    if layered:
        packed = call(
            pack_kernel,
            "pack_columns",
            [(HBM, x), (HBM, cot)],
            [((2, 2 * share, width), BF16)] * 3,
            [pltpu.SemaphoreType.DMA((6,))],
            out_specs=[ANY] * 3,
        )
        near = cross_chips(packed)
        x_first, _ = lax.optimization_barrier((x, packed[0]))
    else:
        outgoing = jnp.stack([x.reshape(n, share, width), cot.reshape(n, share, width)], 1)
        moved = lax.all_to_all(outgoing, "seq", split_axis=0, concat_axis=0, tiled=True)
        x_first = x

    row_outs = [
        ((HW, width), BF16),
        ((columns, width), F32), ((columns, width), F32), ((columns, 1), F32),
        ((columns, width), BF16), ((columns, width), BF16),
    ]
    if layered:
        cut = row_width // 2
        split_outs = [((chips, row_share, cut), BF16)] * 4
        handed_outs = [
            ((row_share, 3 * width), BF16), ((width, 3 * HW), BF16), ((HW, width), BF16),
        ]
        row_outs = [*split_outs, *handed_outs, *row_outs]
        specs = [VMEM] * 4 + [PINNED] * (len(row_outs) - 4)
    else:
        row_outs = [((width, row_width), BF16), *row_outs]
        specs = [VMEM] * len(row_outs)
    *row_terms, row_out, base, normed, inverse_rms, x_near, cot_near = call(
        row_chip_kernel if layered else row_kernel,
        "row_heads",
        [(HBM, x_first), (HBM, cot), *weights],
        row_outs,
        [
            *weight_scratch,
            pltpu.VMEM((columns, HW), F32),
            pltpu.VMEM((columns, HW), F32),
            pltpu.VMEM((columns, 3 * HW), BF16),
            pltpu.SemaphoreType.DMA((12,)),
        ],
        BIG_VMEM,
        specs,
    )
    if layered:
        *row_terms, weight_rows, col_weight, col_out_weight = row_terms
        row_sent = [swap(one, "seq", 1) for one in row_terms[:2]]
        half_block = (chips, row_share // 2, row_width)
        row_next, row_kept = call(
            row_cores_kernel,
            "row_add_cores",
            [(VMEM, one) for one in (*row_terms[2:], *row_sent)],
            [(half_block, BF16), (half_block, F32)],
            out_specs=[VMEM, PINNED],
        )
        *near, row_kept = lax.optimization_barrier((*near, row_kept))
        (far,) = call(
            far_kernel,
            "pack_other_core",
            [(VMEM, one) for one in (x_near, cot_near, *near)],
            [((chips, 2, share, width), BF16)],
        )
        send, keep, col_grads = call(
            column_chip_kernel,
            "column_heads",
            [
                (VMEM, one)
                for one in (
                    x_near, cot_near, *near, swap(far, "seq", 1),
                    gain, col_weight, col_out_weight, row_out,
                )
            ],
            [((chips, row_share, col_width), BF16)] * 2 + [col_outs[0]],
            vmem=BIG_VMEM,
            out_specs=[VMEM, VMEM, PINNED],
        )
        back_send, back_keep = call(
            back_chip_kernel,
            "column_grad_hidden",
            [(VMEM, col_grads), (VMEM, col_weight)],
            [((chips, share, width), BF16)] * 2,
        )
        row_next, _ = lax.optimization_barrier((row_next, send))
        keep, back_keep = lax.optimization_barrier((keep, back_keep))
        first_half = (chips, row_share // 2, FIRST_PART)
        second = (row_share, col_width - FIRST_PART)
        to_next, kept, owned, *off = call(
            cores_kernel,
            "column_add_cores",
            [(VMEM, keep), (VMEM, swap(send, "seq", 1))],
            [(first_half, BF16), (first_half, F32), (second, F32)] + [(second, BF16)] * 3,
            out_specs=[VMEM, PINNED, PINNED, VMEM, VMEM, VMEM],
        )
        got = cross_chips(off, (TERM_STEPS, TERM_STEPS))
        back = call(
            back_pack_kernel,
            "pack_grad_hidden",
            [(VMEM, back_keep), (VMEM, swap(back_send, "seq", 1))],
            [((2 * share, width), BF16)] * 4,
        )
        row_kept, *back = lax.optimization_barrier((row_kept, *back))
        joint = (row_share // 2, FIRST_PART + row_width)
        first_owned, *off = call(
            pair_kernel,
            "first_add_pair",
            [
                (VMEM, one)
                for one in (kept, swap(to_next, "dp", 1), row_kept, swap(row_next, "dp", 1))
            ],
            [(joint, F32)] + [(joint, BF16)] * 3,
            out_specs=[PINNED, VMEM, VMEM, VMEM],
        )
        first_got = cross_chips(off, (TERM_STEPS, TERM_STEPS))
        second_half = (row_share // 2, second[1])
        to_next, kept = call(
            layer_kernel,
            "second_add_chips",
            [(VMEM, one) for one in (owned, *got)],
            [(second_half, BF16), (second_half, F32)],
            out_specs=[VMEM, PINNED],
        )
        (pair_sum,) = call(
            join_kernel,
            "join_terms",
            [(VMEM, one) for one in (first_owned, *first_got, kept, swap(to_next, "dp", 1))],
            [((row_share // 2, col_width + row_width), BF16)],
        )
        *back, pair_sum = lax.optimization_barrier((*back, pair_sum))
        held = add_two(pair_sum, swap(pair_sum, "dp", 2), "add_pairs")
        other = swap(held, "dp", 1)
        (grad,) = call(
            input_chip_kernel,
            "input_grad",
            [
                (VMEM, one)
                for one in (base, normed, inverse_rms, gain, back[0], *cross_chips(back[1:]))
            ],
            [((columns, width), BF16)],
            [pltpu.VMEM((chips, 2 * share, width), BF16), pltpu.SemaphoreType.DMA((chips,))],
            out_specs=[HBM],
        )
        sum_qkv, sum_out, sum_gain = call(
            result_kernel,
            "result",
            [(VMEM, held), (VMEM, other), (VMEM, weight_rows), (VMEM, gain)],
            [((row_share, 3 * width), F32), ((row_share, width), F32), ((1, row_share), F32)],
        )
        sum_gain = sum_gain.reshape(row_share)
    else:
        terms, *col_grads = call(
            column_kernel,
            "column_heads",
            [(ANY, moved), *weights, (VMEM, row_terms[0]), (VMEM, row_out)],
            [((width, 4 * width), BF16), *col_outs],
            [
                pltpu.VMEM((n, 2, share, width), BF16),
                weight_scratch[0],
                weight_scratch[2],
                pltpu.SemaphoreType.DMA((6,)),
            ],
            BIG_VMEM,
        )
        (back,) = call(
            back_kernel,
            "column_grad_hidden",
            [(VMEM, one) for one in col_grads],
            [((n, share, width), BF16)],
        )
        returned = lax.all_to_all(back, "seq", split_axis=0, concat_axis=0, tiled=True)
        (grad,) = call(
            input_kernel,
            "input_grad",
            [
                (VMEM, base), (VMEM, normed), (VMEM, inverse_rms), (VMEM, gain),
                (VMEM, returned.reshape(columns, width)),
            ],
            [((columns, width), BF16)],
        )
        terms = lax.all_to_all(
            terms.reshape(n, row_share, 4 * width), "seq", split_axis=0, concat_axis=0, tiled=True
        )
        total = jnp.sum(terms.astype(F32), 0)
        for step in range(m.bit_length() - 1):
            sent = total.astype(BF16)
            total = sent.astype(F32) + swap(sent, "dp", 1 << step).astype(F32)
        sum_qkv, sum_out = total[:, : 3 * width], total[:, 3 * width :]
        here_at = lax.axis_index("seq") * row_share
        own_gain = lax.dynamic_slice_in_dim(norm_gain, here_at, row_share, 0)
        own_weight = lax.dynamic_slice_in_dim(qkv_weight, here_at, row_share, 0)
        sum_gain = jnp.sum(sum_qkv * own_weight.astype(F32), -1) / own_gain
    return (grad.reshape(inputs.shape), sum_qkv, sum_out, sum_gain)


def solution(mesh):
    return jax.shard_map(
        body,
        mesh=mesh,
        in_specs=(P("dp", "seq", None, None), P(), P(), P(), P("dp", "seq", None, None)),
        out_specs=(P("dp", "seq", None, None), P("seq", None), P("seq", None), P("seq")),
        check_vma=False,
    )
```

```python
import math

import jax
import jax.numpy as jnp
from jax import lax
from jax.experimental import pallas as pl
from jax.experimental.pallas import tpu as pltpu
from jax.sharding import PartitionSpec as P

H = 8
HD = 64
HH = H // 2
HW = HH * HD
SCALE = HD ** (-0.5)
F32 = jnp.float32
BF16 = jnp.bfloat16
QUERY_BLOCK = 128
BIG_VMEM = 20 * 1024 * 1024
SMALL_VMEM = 8 * 1024 * 1024
ANY = pl.BlockSpec(memory_space=pl.ANY)
VMEM = pl.BlockSpec(memory_space=pltpu.VMEM)
HBM = pl.BlockSpec(memory_space=pltpu.HBM)
CHIP_STEPS = (3, 2, 1)
FIRST_PART = 384
PINNED = pl.BlockSpec(memory_space=pltpu.VMEM)
shaped = jax.ShapeDtypeStruct


def here():
    device = lax.axis_index("seq")
    return device >> 1, device & 1, lax.axis_index("dp")


def dot_nn(a, b):
    return lax.dot_general(a, b, (((1,), (0,)), ((), ())), preferred_element_type=F32)


def dot_nt(a, b):
    return lax.dot_general(a, b, (((1,), (1,)), ((), ())), preferred_element_type=F32)


def rms_parts(x):
    inverse_rms = lax.rsqrt(jnp.mean(x * x, -1, keepdims=True) + 1e-05)
    return inverse_rms, x * inverse_rms


def transposed(x):
    block = math.gcd(x.shape[1], 256)
    eye = (
        lax.broadcasted_iota(jnp.int32, (block, block), 0)
        == lax.broadcasted_iota(jnp.int32, (block, block), 1)
    ).astype(F32).astype(BF16)
    parts = [
        dot_nt(eye, x[:, at : at + block]).astype(BF16) for at in range(0, x.shape[1], block)
    ]
    return parts[0] if len(parts) == 1 else jnp.concatenate(parts, 0)


def head_pair(x):
    lane = lax.broadcasted_iota(jnp.int32, x.shape, 1)
    zero = jnp.zeros_like(x)
    return jnp.concatenate([jnp.where(lane < HD, x, zero), jnp.where(lane < HD, zero, x)], 0)


def both_heads(both, count):
    return jnp.concatenate([both[:HD, :count], both[HD:, count:]], 0)


def pair_steps(items, mask_rows, mask):
    count = items[0][2].shape[1]
    scores = [dot_nt(k, q2) for q2, _, _, k, _, _, _ in items]
    prob_grads = [dot_nt(v, g2) for _, g2, _, _, v, _, _ in items]
    probs = []
    for score in scores:
        first = score.shape[0] - mask_rows
        tail = jnp.where(mask, score[first:], -1e30)
        score = tail if first == 0 else jnp.concatenate([score[:first], tail], 0)
        exponent = jnp.exp(score - jnp.max(score, 0, keepdims=True))
        probs.append(exponent * (1.0 / jnp.sum(exponent, 0, keepdims=True)))
    weights = [prob.astype(BF16) for prob in probs]
    attended = [
        both_heads(dot_nn(item[6], weight), count).astype(BF16)
        for item, weight in zip(items, weights)
    ]
    score_grads = []
    for item, att, prob, prob_grad in zip(items, attended, probs, prob_grads):
        product = item[2].astype(F32) * att.astype(F32)
        delta = [jnp.sum(part, 0, keepdims=True) for part in (product[:HD], product[HD:])]
        score_grads.append((prob * (prob_grad - jnp.concatenate(delta, 1))).astype(BF16))
    grad_q = [
        (both_heads(dot_nn(item[5], score_grad), count) * SCALE).astype(BF16)
        for item, score_grad in zip(items, score_grads)
    ]
    grad_k = [dot_nn(score_grad, item[0]) for item, score_grad in zip(items, score_grads)]
    grad_v = [dot_nn(weight, item[1]) for item, weight in zip(items, weights)]
    return list(zip(attended, grad_q, grad_k, grad_v))


def split_cores(piece, send_ref, keep_ref, chips, lanes):
    rows = send_ref.shape[1]
    parts = piece.reshape(chips.stop - chips.start, 2, rows, piece.shape[1])
    even, odd = parts[:, 0], parts[:, 1]
    first = here()[1] == 0
    send_ref[chips, :, lanes] = jnp.where(first, odd, even)
    keep_ref[chips, :, lanes] = jnp.where(first, even, odd)


def qkv_copies(wqkv_ref, w_ref, sems, second):
    width = wqkv_ref.shape[0]
    return [
        pltpu.make_async_copy(
            wqkv_ref.at[:, pl.ds(i * width + second * HW, HW)],
            w_ref.at[:, pl.ds(i * HW, HW)],
            sems.at[i],
        )
        for i in range(3)
    ]


def weight_copies(wqkv_ref, wout_ref, w_ref, wo_ref, sems, second):
    out_rows = wout_ref.at[pl.ds(second * HW, HW), :]
    return [
        *qkv_copies(wqkv_ref, w_ref, sems, second),
        pltpu.make_async_copy(out_rows, wo_ref, sems.at[3]),
    ]


def started(*copies):
    for copy in copies:
        copy.start()
    return copies


def finished(*copies):
    for copy in copies:
        copy.wait()


def project(hidden, cot, w_ref, wo_ref):
    projected = dot_nn(hidden, w_ref[...]).astype(BF16)
    q, k, v = [projected[:, i * HW : (i + 1) * HW] for i in range(3)]
    g = dot_nt(cot, wo_ref[...]).astype(BF16)
    return q * jnp.asarray(SCALE, BF16), k, v, g


def row_part(
    x_any, cot_any, gain_any, wqkv_any, wout_any,
    out_ref, base_ref, normed_ref, inverse_ref, x_ref, cot_ref,
    gain_ref, w_ref, wo_ref, dk_ref, dv_ref, grads_ref, sems,
):
    first = started(
        pltpu.make_async_copy(x_any, x_ref, sems.at[4]),
        pltpu.make_async_copy(gain_any, gain_ref, sems.at[5]),
    )
    later = started(
        *weight_copies(wqkv_any, wout_any, w_ref, wo_ref, sems, 0),
        pltpu.make_async_copy(cot_any, cot_ref, sems.at[6]),
    )
    dk_ref[...] = jnp.zeros_like(dk_ref)
    dv_ref[...] = jnp.zeros_like(dv_ref)
    finished(*first)
    tokens = x_ref.shape[0]
    inverse_ref[...], normed_ref[...] = rms_parts(x_ref[...].astype(F32))
    hidden = (normed_ref[...] * gain_ref[...]).astype(BF16)
    hidden_t = transposed(hidden)
    finished(*later)
    cot = cot_ref[...]
    q, k, v, g = project(hidden, cot, w_ref, wo_ref)
    kt, vt, gt = transposed(k), transposed(v), transposed(g)
    step = math.gcd(tokens, QUERY_BLOCK)
    query = lax.broadcasted_iota(jnp.int32, (step, 2 * step), 1) % step
    mask = query >= lax.broadcasted_iota(jnp.int32, (step, 2 * step), 0)
    pairs = [slice(i * 2 * HD, (i + 1) * 2 * HD) for i in range(HH // 2)]
    att_blocks, dq_blocks = [], []
    for start in range(0, tokens, step):
        rows, keys = slice(start, start + step), slice(0, start + step)
        items = [
            (
                head_pair(q[rows, lanes]), head_pair(g[rows, lanes]), gt[lanes, rows],
                k[keys, lanes], v[keys, lanes], kt[lanes, keys], vt[lanes, keys],
            )
            for lanes in pairs
        ]
        results = pair_steps(items, step, mask)
        for lanes, (_, _, dk, dv) in zip(pairs, results):
            dk_ref[keys, lanes] += dk
            dv_ref[keys, lanes] += dv
        att_blocks.append(jnp.concatenate([result[0] for result in results], 0))
        dq_blocks.append(jnp.concatenate([result[1] for result in results], 0))
    grads_ref[:, :HW] = transposed(jnp.concatenate(dq_blocks, 1))
    grads_ref[:, HW : 2 * HW] = dk_ref[...].astype(BF16)
    grads_ref[:, 2 * HW :] = dv_ref[...].astype(BF16)
    term_qkv = dot_nn(hidden_t, grads_ref[...]).astype(BF16)
    out_ref[...] = dot_nn(jnp.concatenate(att_blocks, 1), cot).astype(BF16)
    grad_normed = dot_nt(grads_ref[...], w_ref[...]) * gain_ref[...]
    base_ref[...] = input_grad(
        cot_ref[...].astype(F32), normed_ref[...], inverse_ref[...], grad_normed
    )
    return term_qkv


def row_kernel(x_any, cot_any, gain_any, wqkv_any, wout_any, qkv_ref, *refs):
    qkv_ref[...] = row_part(x_any, cot_any, gain_any, wqkv_any, wout_any, *refs)


def row_chip_kernel(
    x_any, cot_any, gain_any, wqkv_any, wout_any,
    send_1, send_2, keep_1, keep_2, rows_ref, col_w_ref, col_wo_ref, *refs,
):
    chip, core, _ = here()
    sems, rows = refs[-1], rows_ref.shape[0]
    at = pl.multiple_of((chip * 2 + core) * rows, rows)
    handed = started(
        pltpu.make_async_copy(wqkv_any.at[pl.ds(at, rows), :], rows_ref, sems.at[7]),
        *weight_copies(wqkv_any, wout_any, col_w_ref, col_wo_ref, sems.at[pl.ds(8, 4)], 1),
    )
    term_qkv = row_part(x_any, cot_any, gain_any, wqkv_any, wout_any, *refs)
    chips, cut = send_1.shape[0], keep_1.shape[2]
    pieces = slice(0, chips), slice(0, cut)
    split_cores(term_qkv[:, :cut], send_1, keep_1, *pieces)
    split_cores(term_qkv[:, cut:], send_2, keep_2, *pieces)
    finished(*handed)


def column_part(x, cot, mask, gain, w_ref, wo_ref, weight_waits, grads_ref):
    tokens, block = x.shape[0], mask.shape[0]
    _, normed = rms_parts(x.astype(F32))
    hidden = (normed * gain).astype(BF16)
    hidden_t = transposed(hidden)
    finished(*weight_waits)
    q, k, v, g = project(hidden, cot, w_ref, wo_ref)
    kt, vt, gt = transposed(k), transposed(v), transposed(g)
    pairs = [slice(i * 2 * HD, (i + 1) * 2 * HD) for i in range(HH // 2)]
    blocks = [slice(at, at + block) for at in range(0, tokens, block)]
    items = [
        (
            head_pair(q[rows, lanes]), head_pair(g[rows, lanes]), gt[lanes, rows],
            k[rows, lanes], v[rows, lanes], kt[lanes, rows], vt[lanes, rows],
        )
        for lanes in pairs
        for rows in blocks
    ]
    results = pair_steps(items, block, mask)
    places = [(lanes, rows) for lanes in pairs for rows in blocks]
    for (lanes, rows), (_, _, dk, dv) in zip(places, results):
        grads_ref[rows, HW + lanes.start : HW + lanes.stop] = dk.astype(BF16)
        grads_ref[rows, 2 * HW + lanes.start : 2 * HW + lanes.stop] = dv.astype(BF16)
    by_pair = [results[i * len(blocks) : (i + 1) * len(blocks)] for i in range(len(pairs))]
    attended, grad_q = [
        jnp.concatenate([jnp.concatenate([r[i] for r in some], 1) for some in by_pair], 0)
        for i in range(2)
    ]
    grads_ref[:, :HW] = transposed(grad_q)
    term_qkv = dot_nn(hidden_t, grads_ref[...]).astype(BF16)
    term_out = dot_nn(attended, cot).astype(BF16)
    return term_qkv, term_out


def column_mask(all_rows, group, row_of):
    block = all_rows * group
    shape = (block, 2 * block)
    query = lax.broadcasted_iota(jnp.int32, shape, 1) % block
    key = lax.broadcasted_iota(jnp.int32, shape, 0)
    same_column = query % group == key % group
    return (row_of(query // group) >= row_of(key // group)) & same_column


def column_kernel(
    moved_any, gain_any, wqkv_any, wout_any, row_qkv_ref, row_out_ref,
    terms_ref, grads_ref, w_ref,
    moved_ref, gain_ref, wo_ref, sems,
):
    copies = started(
        pltpu.make_async_copy(moved_any, moved_ref, sems.at[4]),
        pltpu.make_async_copy(gain_any, gain_ref, sems.at[5]),
    )
    weights = started(*weight_copies(wqkv_any, wout_any, w_ref, wo_ref, sems, 1))
    finished(*copies)
    all_rows, _, share, width = moved_ref.shape
    group = math.gcd(share, 16)
    x, cot = [
        jnp.concatenate(
            [
                moved_ref[:, which, at : at + group, :].astype(F32).reshape(all_rows * group, width)
                for at in range(0, share, group)
            ],
            0,
        ).astype(BF16)
        for which in range(2)
    ]
    mask = column_mask(all_rows, group, lambda place: place)
    term_qkv, term_out = column_part(
        x, cot, mask, gain_ref[...], w_ref, wo_ref, weights, grads_ref
    )
    for i in range(3):
        at = i * width
        terms_ref[:, at : at + HW] = row_qkv_ref[:, i * HW : (i + 1) * HW]
        terms_ref[:, at + HW : at + 2 * HW] = term_qkv[:, i * HW : (i + 1) * HW]
    terms_ref[:HW, 3 * width :] = row_out_ref[...]
    terms_ref[HW:, 3 * width :] = term_out


def column_chip_kernel(
    x_ref, cot_ref, swapped_ref, corner_ref, near_2, near_3, far_ref, gain_ref, w_ref, wo_ref, row_out_ref,
    send_ref, keep_ref, grads_ref,
):
    chip, core, _ = here()
    share = far_ref.shape[2]
    half = pl.ds(pl.multiple_of(core * share, share), share)
    at = pl.ds(pl.multiple_of((chip * 2 + core) * share, share), share)
    group = math.gcd(share, 16)

    def tokens(which, mine):
        pieces = [
            mine[at, :], swapped_ref[0, which], corner_ref[0, which], corner_ref[1, which],
        ]
        for i, near in enumerate((near_2, near_3)):
            pieces += [near[which, half, :], far_ref[i, which]]
        starts = range(0, share, group)
        return jnp.concatenate(
            [piece[start : start + group] for start in starts for piece in pieces], 0
        )

    def row_of(place):
        step = (4 - (place >> 1)) & 3
        return ((step ^ chip) << 1) + ((place & 1) ^ core)

    mask = column_mask(2 * (len(CHIP_STEPS) + 1), group, row_of)
    term_qkv, term_out = column_part(
        tokens(0, x_ref), tokens(1, cot_ref), mask, gain_ref[...], w_ref, wo_ref, (), grads_ref
    )
    chips = send_ref.shape[0]
    refs = send_ref, keep_ref
    out_lanes = slice(3 * HW, send_ref.shape[2])
    split_cores(term_qkv, *refs, slice(0, chips), slice(0, 3 * HW))
    split_cores(row_out_ref[...], *refs, slice(0, chips // 2), out_lanes)
    split_cores(term_out, *refs, slice(chips // 2, chips), out_lanes)


def far_kernel(near_2, near_3, far_ref):
    share = far_ref.shape[2]
    at = pl.ds(pl.multiple_of((1 - here()[1]) * share, share), share)
    for i, near in enumerate((near_2, near_3)):
        far_ref[i] = near[:, at, :]


def back_kernel(grads_ref, w_ref, back_ref):
    grad_hidden = dot_nt(grads_ref[...], w_ref[...])
    all_rows, share, width = back_ref.shape
    group = math.gcd(share, 16)
    block = all_rows * group
    for i in range(share // group):
        piece = grad_hidden[i * block : (i + 1) * block].reshape(all_rows, group, width)
        back_ref[:, i * group : (i + 1) * group, :] = piece.astype(BF16)


def back_chip_kernel(grads_ref, w_ref, send_ref, keep_ref):
    grad_hidden = dot_nt(grads_ref[...], w_ref[...]).astype(BF16)
    chips, share, width = keep_ref.shape
    group = math.gcd(share, 16)
    block = 2 * chips * group
    for i in range(share // group):
        piece = grad_hidden[i * block : (i + 1) * block].reshape(chips, 2, group, width)
        at = slice(i * group, (i + 1) * group)
        keep_ref[:, at, :], send_ref[:, at, :] = piece[:, 0], piece[:, 1]


def back_pack_kernel(keep_ref, got_ref, *targets):
    share = keep_ref.shape[1]
    core = here()[1]
    kept_at = pl.ds(pl.multiple_of(core * share, share), share)
    got_at = pl.ds(pl.multiple_of((1 - core) * share, share), share)
    for i, target in enumerate(targets):
        target[kept_at, :] = keep_ref[i]
        target[got_at, :] = got_ref[i]


def input_kernel(base_ref, normed_ref, inverse_ref, gain_ref, back_ref, grad_ref):
    grad_ref[...] = input_grad(
        base_ref[...], normed_ref[...], inverse_ref[...], back_ref[...].astype(F32) * gain_ref[...]
    ).astype(BF16)


def input_grad(base, normed, inverse_rms, grad_normed):
    projected = jnp.mean(grad_normed * normed, -1, keepdims=True)
    return base + inverse_rms * (grad_normed - normed * projected)


def input_chip_kernel(
    base_ref, normed_ref, inverse_ref, gain_ref, own_ref, got_1, got_2, got_3,
    grad_any, grad_ref, sems,
):
    chip = here()[0]
    count = own_ref.shape[0]
    copies = []
    for i, (step, back_ref) in enumerate(zip((0, *CHIP_STEPS), (own_ref, got_1, got_2, got_3))):
        at = pl.ds(pl.multiple_of((chip ^ step) * count, count), count)
        grad_normed = back_ref[...].astype(F32) * gain_ref[...]
        grad = input_grad(base_ref[at, :], normed_ref[at, :], inverse_ref[at, :], grad_normed)
        grad_ref[i] = grad.astype(BF16)
        copies += started(pltpu.make_async_copy(grad_ref.at[i], grad_any.at[at, :], sems.at[i]))
    finished(*copies)


def pack_kernel(x_any, cot_any, swap_ref, corner_ref, off_2, off_3, sems):
    chip, core, _ = here()
    share = corner_ref.shape[1]

    def columns(step, of_core):
        return pl.multiple_of(((chip ^ step) * 2 + of_core) * share, share)

    corner = CHIP_STEPS[0]
    copies = []
    for which, source in enumerate((x_any, cot_any)):
        pieces = [
            (columns(0, 1 - core), share, swap_ref.at[0, which]),
            (columns(corner, 1 - core), share, swap_ref.at[1, which]),
            (columns(corner, core), share, corner_ref.at[which]),
            (columns(CHIP_STEPS[1], 0), 2 * share, off_2.at[which]),
            (columns(CHIP_STEPS[2], 0), 2 * share, off_3.at[which]),
        ]
        for i, (at, count, target) in enumerate(pieces):
            copies.append(
                pltpu.make_async_copy(
                    source.at[pl.ds(at, count), :], target, sems.at[5 * which + i]
                )
            )
    finished(*started(*copies))


def corner_kernel(corner_ref, swapped_ref, out_ref):
    out_ref[0], out_ref[1] = corner_ref[...], swapped_ref[1]


def split_rows(total, axis):
    upper = (here()[2] & 1) == 1
    low, high = jnp.split(total, 2, axis)
    return jnp.where(upper, low, high).astype(BF16), jnp.where(upper, high, low)


def row_cores_kernel(keep_1, keep_2, got_1, got_2, send_ref, kept_ref):
    total = [
        keep_ref[...].astype(F32) + got_ref[...].astype(F32)
        for keep_ref, got_ref in ((keep_1, got_1), (keep_2, got_2))
    ]
    send_ref[...], kept_ref[...] = split_rows(jnp.concatenate(total, 2), 1)


def cores_kernel(keep_ref, got_ref, send_ref, kept_ref, *targets):
    chip, cut = here()[0], kept_ref.shape[2]
    first = keep_ref[:, :, :cut].astype(F32) + got_ref[:, :, :cut].astype(F32)
    send_ref[...], kept_ref[...] = split_rows(first, 1)
    for step, target in zip((0, *CHIP_STEPS), targets):
        there = chip ^ step
        total = keep_ref[there, :, cut:].astype(F32) + got_ref[there, :, cut:].astype(F32)
        target[...] = total.astype(target.dtype)


def pair_kernel(kept_ref, got_ref, row_kept, row_got, *targets):
    chip, cut = here()[0], kept_ref.shape[2]
    for step, target in zip((0, *CHIP_STEPS), targets):
        there = chip ^ step
        total = kept_ref[there] + got_ref[there].astype(F32)
        target[:, :cut] = total.astype(target.dtype)
        total = row_kept[there] + row_got[there].astype(F32)
        target[:, cut:] = total.astype(target.dtype)


def layer_sum(own_ref, got_1, got_2, got_3):
    return own_ref[...] + (
        (got_1[...].astype(F32) + got_2[...].astype(F32)) + got_3[...].astype(F32)
    )


def layer_kernel(own_ref, got_1, got_2, got_3, send_ref, kept_ref):
    send_ref[...], kept_ref[...] = split_rows(layer_sum(own_ref, got_1, got_2, got_3), 0)


def join_kernel(own_ref, got_1, got_2, got_3, kept_ref, got_ref, out_ref):
    total = layer_sum(own_ref, got_1, got_2, got_3).astype(BF16)
    cut, width = FIRST_PART, kept_ref.shape[1]
    out_ref[:, :cut] = total[:, :cut]
    out_ref[:, cut : cut + width] = (kept_ref[...] + got_ref[...].astype(F32)).astype(BF16)
    out_ref[:, cut + width :] = total[:, cut:]


def add_kernel(kept_ref, got_ref, out_ref):
    out_ref[...] = (kept_ref[...].astype(F32) + got_ref[...].astype(F32)).astype(BF16)


def result_kernel(held_ref, got_ref, w_ref, gain_ref, qkv_ref, out_ref, grad_ref):
    rows = qkv_ref.shape[0]
    chip, core, layer = here()
    at = (chip * 2 + core) * rows
    upper = (layer & 1) == 1
    half = rows // 2
    width = out_ref.shape[1]

    def ordered(lanes):
        held, got = held_ref[:, lanes].astype(F32), got_ref[:, lanes].astype(F32)
        return (jnp.where(upper, got, held), jnp.where(upper, held, got))

    row_at = 3 * HW + width
    for i in range(3):
        for at_from, at_to in ((row_at + i * HW, i * width), (i * HW, i * width + HW)):
            to = slice(at_to, at_to + HW)
            qkv_ref[:half, to], qkv_ref[half:, to] = ordered(slice(at_from, at_from + HW))
    out_ref[:half], out_ref[half:] = ordered(slice(3 * HW, row_at))
    total = jnp.sum(qkv_ref[...] * w_ref[...].astype(F32), -1, keepdims=True)
    shape = (rows, gain_ref.shape[1])
    row = lax.broadcasted_iota(jnp.int32, shape, 0)
    feature = lax.broadcasted_iota(jnp.int32, shape, 1)
    gain = jnp.sum(jnp.where(feature == row + at, gain_ref[...], 0.0), -1, keepdims=True)
    shape = (rows, grad_ref.shape[1])
    same = lax.broadcasted_iota(jnp.int32, shape, 0) == lax.broadcasted_iota(jnp.int32, shape, 1)
    grad_ref[...] = jnp.sum(jnp.where(same, total / gain, 0.0), 0, keepdims=True)


def call(kernel, name, ins, outs, scratch=(), vmem=SMALL_VMEM, out_specs=None):
    out_specs = out_specs or [VMEM] * len(outs)
    places = [{id(HBM): pltpu.HBM, id(PINNED): pltpu.VMEM}.get(id(spec)) for spec in out_specs]
    outs = [place(*out) if place else shaped(*out) for place, out in zip(places, outs)]
    args = [
        pltpu.with_memory_space_constraint(array, pltpu.HBM) if spec is HBM else array
        for spec, array in ins
    ]
    return pl.pallas_call(
        kernel,
        out_shape=outs,
        in_specs=[spec for spec, _ in ins],
        out_specs=out_specs,
        scratch_shapes=scratch,
        name=name,
        cost_estimate=pl.CostEstimate(flops=0, bytes_accessed=0, transcendentals=0),
        compiler_params=pltpu.CompilerParams(vmem_limit_bytes=vmem),
    )(*args)


def swap(array, axis, bits):
    count = lax.axis_size(axis)
    return lax.ppermute(array, axis, [(i, i ^ bits) for i in range(count)])


def cross_chips(*offs):
    return [swap(off, "seq", 2 * step) for off, step in zip(offs, CHIP_STEPS)]


def add_two(kept, got, name):
    (total,) = call(add_kernel, name, [(VMEM, kept), (VMEM, got)], [(kept.shape, BF16)])
    return total


def body(inputs, norm_gain, qkv_weight, out_weight, out_cotan):
    columns, width = inputs.shape[2:]
    n = lax.axis_size("seq")
    m = lax.axis_size("dp")
    share = columns // n
    row_share = width // n
    row_width, col_width = 3 * HW, 3 * HW + width
    x = inputs.reshape(columns, width)
    cot = out_cotan.reshape(columns, width)
    gain = norm_gain.reshape(1, width)
    chips = 4
    layered = n == 2 * chips and m == 4 and row_share == share
    weight_scratch = [
        pltpu.VMEM((1, width), F32),
        pltpu.VMEM((width, 3 * HW), BF16),
        pltpu.VMEM((HW, width), BF16),
    ]
    weights = [(HBM, gain), (HBM, qkv_weight), (HBM, out_weight)]
    col_outs = [((columns, 3 * HW), BF16), ((width, 3 * HW), BF16)]

    if layered:
        packed = call(
            pack_kernel,
            "pack_columns",
            [(HBM, x), (HBM, cot)],
            [((2, 2, share, width), BF16), ((2, share, width), BF16)]
            + [((2, 2 * share, width), BF16)] * 2,
            [pltpu.SemaphoreType.DMA((10,))],
            out_specs=[ANY] * 4,
        )
        near = [swap(one, "seq", 2 * step) for one, step in zip(packed[2:], CHIP_STEPS[1:])]
        swapped = swap(packed[0], "seq", 1)
        (corner,) = call(
            corner_kernel,
            "pack_corner",
            [(VMEM, packed[1]), (VMEM, swapped)],
            [((2, 2, share, width), BF16)],
        )
        x_first, _ = lax.optimization_barrier((x, corner))
        corner = swap(corner, "seq", 2 * CHIP_STEPS[0])
    else:
        outgoing = jnp.stack([x.reshape(n, share, width), cot.reshape(n, share, width)], 1)
        moved = lax.all_to_all(outgoing, "seq", split_axis=0, concat_axis=0, tiled=True)
        x_first = x

    row_outs = [
        ((HW, width), BF16),
        ((columns, width), F32), ((columns, width), F32), ((columns, 1), F32),
        ((columns, width), BF16), ((columns, width), BF16),
    ]
    if layered:
        cut = row_width // 2
        split_outs = [((chips, row_share, cut), BF16)] * 4
        handed_outs = [
            ((row_share, 3 * width), BF16), ((width, 3 * HW), BF16), ((HW, width), BF16),
        ]
        row_outs = [*split_outs, *handed_outs, *row_outs]
        specs = [VMEM] * 4 + [PINNED] * (len(row_outs) - 4)
    else:
        row_outs = [((width, row_width), BF16), *row_outs]
        specs = [VMEM] * len(row_outs)
    *row_terms, row_out, base, normed, inverse_rms, x_near, cot_near = call(
        row_chip_kernel if layered else row_kernel,
        "row_heads",
        [(HBM, x_first), (HBM, cot), *weights],
        row_outs,
        [
            *weight_scratch,
            pltpu.VMEM((columns, HW), F32),
            pltpu.VMEM((columns, HW), F32),
            pltpu.VMEM((columns, 3 * HW), BF16),
            pltpu.SemaphoreType.DMA((12,)),
        ],
        BIG_VMEM,
        specs,
    )
    if layered:
        *row_terms, weight_rows, col_weight, col_out_weight = row_terms
        row_sent = [swap(one, "seq", 1) for one in row_terms[:2]]
        half_block = (chips, row_share // 2, row_width)
        row_next, row_kept = call(
            row_cores_kernel,
            "row_add_cores",
            [(VMEM, one) for one in (*row_terms[2:], *row_sent)],
            [(half_block, BF16), (half_block, F32)],
            out_specs=[VMEM, PINNED],
        )
        col_weight, row_kept = lax.optimization_barrier((col_weight, row_kept))
        *near, base = lax.optimization_barrier((*near, base))
        (far,) = call(
            far_kernel,
            "pack_other_core",
            [(VMEM, one) for one in near],
            [((2, 2, share, width), BF16)],
        )
        send, keep, col_grads = call(
            column_chip_kernel,
            "column_heads",
            [
                (VMEM, one)
                for one in (
                    x_near, cot_near, swapped, corner, *near, swap(far, "seq", 1),
                    gain, col_weight, col_out_weight, row_out,
                )
            ],
            [((chips, row_share, col_width), BF16)] * 2 + [col_outs[0]],
            vmem=BIG_VMEM,
            out_specs=[VMEM, VMEM, PINNED],
        )
        back_send, back_keep = call(
            back_chip_kernel,
            "column_grad_hidden",
            [(VMEM, col_grads), (VMEM, col_weight)],
            [((chips, share, width), BF16)] * 2,
        )
        row_next, _ = lax.optimization_barrier((row_next, send))
        keep, back_keep = lax.optimization_barrier((keep, back_keep))
        first_half = (chips, row_share // 2, FIRST_PART)
        second = (row_share, col_width - FIRST_PART)
        to_next, kept, owned, *off = call(
            cores_kernel,
            "column_add_cores",
            [(VMEM, keep), (VMEM, swap(send, "seq", 1))],
            [(first_half, BF16), (first_half, F32), (second, F32)] + [(second, BF16)] * 3,
            out_specs=[VMEM, PINNED, PINNED, VMEM, VMEM, VMEM],
        )
        got = cross_chips(*off)
        back = call(
            back_pack_kernel,
            "pack_grad_hidden",
            [(VMEM, back_keep), (VMEM, swap(back_send, "seq", 1))],
            [((2 * share, width), BF16)] * 4,
        )
        row_kept, *back = lax.optimization_barrier((row_kept, *back))
        joint = (row_share // 2, FIRST_PART + row_width)
        first_owned, *off = call(
            pair_kernel,
            "first_add_pair",
            [
                (VMEM, one)
                for one in (kept, swap(to_next, "dp", 1), row_kept, swap(row_next, "dp", 1))
            ],
            [(joint, F32)] + [(joint, BF16)] * 3,
            out_specs=[PINNED, VMEM, VMEM, VMEM],
        )
        first_got = cross_chips(*off)
        second_half = (row_share // 2, second[1])
        to_next, kept = call(
            layer_kernel,
            "second_add_chips",
            [(VMEM, one) for one in (owned, *got)],
            [(second_half, BF16), (second_half, F32)],
            out_specs=[VMEM, PINNED],
        )
        (pair_sum,) = call(
            join_kernel,
            "join_terms",
            [(VMEM, one) for one in (first_owned, *first_got, kept, swap(to_next, "dp", 1))],
            [((row_share // 2, col_width + row_width), BF16)],
        )
        *back, pair_sum = lax.optimization_barrier((*back, pair_sum))
        held = add_two(pair_sum, swap(pair_sum, "dp", 2), "add_pairs")
        other = swap(held, "dp", 1)
        (grad,) = call(
            input_chip_kernel,
            "input_grad",
            [
                (VMEM, one)
                for one in (base, normed, inverse_rms, gain, back[0], *cross_chips(*back[1:]))
            ],
            [((columns, width), BF16)],
            [pltpu.VMEM((chips, 2 * share, width), BF16), pltpu.SemaphoreType.DMA((chips,))],
            out_specs=[HBM],
        )
        sum_qkv, sum_out, sum_gain = call(
            result_kernel,
            "result",
            [(VMEM, held), (VMEM, other), (VMEM, weight_rows), (VMEM, gain)],
            [((row_share, 3 * width), F32), ((row_share, width), F32), ((1, row_share), F32)],
        )
        sum_gain = sum_gain.reshape(row_share)
    else:
        terms, *col_grads = call(
            column_kernel,
            "column_heads",
            [(ANY, moved), *weights, (VMEM, row_terms[0]), (VMEM, row_out)],
            [((width, 4 * width), BF16), *col_outs],
            [
                pltpu.VMEM((n, 2, share, width), BF16),
                weight_scratch[0],
                weight_scratch[2],
                pltpu.SemaphoreType.DMA((6,)),
            ],
            BIG_VMEM,
        )
        (back,) = call(
            back_kernel,
            "column_grad_hidden",
            [(VMEM, one) for one in col_grads],
            [((n, share, width), BF16)],
        )
        returned = lax.all_to_all(back, "seq", split_axis=0, concat_axis=0, tiled=True)
        (grad,) = call(
            input_kernel,
            "input_grad",
            [
                (VMEM, base), (VMEM, normed), (VMEM, inverse_rms), (VMEM, gain),
                (VMEM, returned.reshape(columns, width)),
            ],
            [((columns, width), BF16)],
        )
        terms = lax.all_to_all(
            terms.reshape(n, row_share, 4 * width), "seq", split_axis=0, concat_axis=0, tiled=True
        )
        total = jnp.sum(terms.astype(F32), 0)
        for step in range(m.bit_length() - 1):
            sent = total.astype(BF16)
            total = sent.astype(F32) + swap(sent, "dp", 1 << step).astype(F32)
        sum_qkv, sum_out = total[:, : 3 * width], total[:, 3 * width :]
        here_at = lax.axis_index("seq") * row_share
        own_gain = lax.dynamic_slice_in_dim(norm_gain, here_at, row_share, 0)
        own_weight = lax.dynamic_slice_in_dim(qkv_weight, here_at, row_share, 0)
        sum_gain = jnp.sum(sum_qkv * own_weight.astype(F32), -1) / own_gain
    return (grad.reshape(inputs.shape), sum_qkv, sum_out, sum_gain)


def solution(mesh):
    return jax.shard_map(
        body,
        mesh=mesh,
        in_specs=(P("dp", "seq", None, None), P(), P(), P(), P("dp", "seq", None, None)),
        out_specs=(P("dp", "seq", None, None), P("seq", None), P("seq", None), P("seq")),
        check_vma=False,
    )
```

```python
import functools
import math

import jax
import jax.numpy as jnp
from jax import lax
from jax.experimental import pallas as pl
from jax.experimental.pallas import tpu as pltpu
from jax.sharding import PartitionSpec as P

H = 8
HD = 64
HH = H // 2
HW = HH * HD
SCALE = HD ** (-0.5)
F32 = jnp.float32
BF16 = jnp.bfloat16
QUERY_BLOCK = 128
BIG_VMEM = 20 * 1024 * 1024
SMALL_VMEM = 8 * 1024 * 1024
ANY = pl.BlockSpec(memory_space=pl.ANY)
VMEM = pl.BlockSpec(memory_space=pltpu.VMEM)
HBM = pl.BlockSpec(memory_space=pltpu.HBM)
CHIP_STEPS = (3, 2, 1)
FIRST_PART = 384
PINNED = pl.BlockSpec(memory_space=pltpu.VMEM)
shaped = jax.ShapeDtypeStruct


def here():
    device = lax.axis_index("seq")
    return device >> 1, device & 1, lax.axis_index("dp")


def dot_nn(a, b):
    return lax.dot_general(a, b, (((1,), (0,)), ((), ())), preferred_element_type=F32)


def dot_nt(a, b):
    return lax.dot_general(a, b, (((1,), (1,)), ((), ())), preferred_element_type=F32)


def rms_parts(x):
    inverse_rms = lax.rsqrt(jnp.mean(x * x, -1, keepdims=True) + 1e-05)
    return inverse_rms, x * inverse_rms


def transposed(x):
    block = math.gcd(x.shape[1], 256)
    eye = (
        lax.broadcasted_iota(jnp.int32, (block, block), 0)
        == lax.broadcasted_iota(jnp.int32, (block, block), 1)
    ).astype(F32).astype(BF16)
    parts = [
        dot_nt(eye, x[:, at : at + block]).astype(BF16) for at in range(0, x.shape[1], block)
    ]
    return parts[0] if len(parts) == 1 else jnp.concatenate(parts, 0)


def head_pair(x):
    lane = lax.broadcasted_iota(jnp.int32, x.shape, 1)
    zero = jnp.zeros_like(x)
    return jnp.concatenate([jnp.where(lane < HD, x, zero), jnp.where(lane < HD, zero, x)], 0)


def both_heads(both, count):
    return jnp.concatenate([both[:HD, :count], both[HD:, count:]], 0)


def pair_steps(items, mask_rows, mask):
    count = items[0][2].shape[1]
    scores = [dot_nt(k, q2) for q2, _, _, k, _, _, _ in items]
    prob_grads = [dot_nt(v, g2) for _, g2, _, _, v, _, _ in items]
    probs = []
    for score in scores:
        first = score.shape[0] - mask_rows
        tail = jnp.where(mask, score[first:], -1e30)
        score = tail if first == 0 else jnp.concatenate([score[:first], tail], 0)
        exponent = jnp.exp(score - jnp.max(score, 0, keepdims=True))
        probs.append(exponent * (1.0 / jnp.sum(exponent, 0, keepdims=True)))
    weights = [prob.astype(BF16) for prob in probs]
    attended = [
        both_heads(dot_nn(item[6], weight), count).astype(BF16)
        for item, weight in zip(items, weights)
    ]
    score_grads = []
    for item, att, prob, prob_grad in zip(items, attended, probs, prob_grads):
        product = item[2].astype(F32) * att.astype(F32)
        delta = [jnp.sum(part, 0, keepdims=True) for part in (product[:HD], product[HD:])]
        score_grads.append((prob * (prob_grad - jnp.concatenate(delta, 1))).astype(BF16))
    grad_q = [
        (both_heads(dot_nn(item[5], score_grad), count) * SCALE).astype(BF16)
        for item, score_grad in zip(items, score_grads)
    ]
    grad_k = [dot_nn(score_grad, item[0]) for item, score_grad in zip(items, score_grads)]
    grad_v = [dot_nn(weight, item[1]) for item, weight in zip(items, weights)]
    return list(zip(attended, grad_q, grad_k, grad_v))


def split_cores(piece, send_ref, keep_ref, chips, lanes):
    rows = send_ref.shape[1]
    parts = piece.reshape(chips.stop - chips.start, 2, rows, piece.shape[1])
    even, odd = parts[:, 0], parts[:, 1]
    first = here()[1] == 0
    send_ref[chips, :, lanes] = jnp.where(first, odd, even)
    keep_ref[chips, :, lanes] = jnp.where(first, even, odd)


def qkv_copies(wqkv_ref, w_ref, sems, second):
    width = wqkv_ref.shape[0]
    return [
        pltpu.make_async_copy(
            wqkv_ref.at[:, pl.ds(i * width + second * HW, HW)],
            w_ref.at[:, pl.ds(i * HW, HW)],
            sems.at[i],
        )
        for i in range(3)
    ]


def weight_copies(wqkv_ref, wout_ref, w_ref, wo_ref, sems, second):
    out_rows = wout_ref.at[pl.ds(second * HW, HW), :]
    return [
        *qkv_copies(wqkv_ref, w_ref, sems, second),
        pltpu.make_async_copy(out_rows, wo_ref, sems.at[3]),
    ]


def started(*copies):
    for copy in copies:
        copy.start()
    return copies


def finished(*copies):
    for copy in copies:
        copy.wait()


def project(hidden, cot, w_ref, wo_ref):
    projected = dot_nn(hidden, w_ref[...]).astype(BF16)
    q, k, v = [projected[:, i * HW : (i + 1) * HW] for i in range(3)]
    g = dot_nt(cot, wo_ref[...]).astype(BF16)
    return q * jnp.asarray(SCALE, BF16), k, v, g


def row_part(
    x_any, cot_any, gain_any, wqkv_any, wout_any,
    out_ref, base_ref, normed_ref, inverse_ref, x_ref, cot_ref,
    gain_ref, w_ref, wo_ref, dk_ref, dv_ref, grads_ref, sems,
):
    first = started(
        pltpu.make_async_copy(x_any, x_ref, sems.at[4]),
        pltpu.make_async_copy(gain_any, gain_ref, sems.at[5]),
    )
    later = started(
        *weight_copies(wqkv_any, wout_any, w_ref, wo_ref, sems, 0),
        pltpu.make_async_copy(cot_any, cot_ref, sems.at[6]),
    )
    dk_ref[...] = jnp.zeros_like(dk_ref)
    dv_ref[...] = jnp.zeros_like(dv_ref)
    finished(*first)
    tokens = x_ref.shape[0]
    inverse_ref[...], normed_ref[...] = rms_parts(x_ref[...].astype(F32))
    hidden = (normed_ref[...] * gain_ref[...]).astype(BF16)
    hidden_t = transposed(hidden)
    finished(*later)
    cot = cot_ref[...]
    q, k, v, g = project(hidden, cot, w_ref, wo_ref)
    kt, vt, gt = transposed(k), transposed(v), transposed(g)
    step = math.gcd(tokens, QUERY_BLOCK)
    query = lax.broadcasted_iota(jnp.int32, (step, 2 * step), 1) % step
    mask = query >= lax.broadcasted_iota(jnp.int32, (step, 2 * step), 0)
    pairs = [slice(i * 2 * HD, (i + 1) * 2 * HD) for i in range(HH // 2)]
    att_blocks, dq_blocks = [], []
    for start in range(0, tokens, step):
        rows, keys = slice(start, start + step), slice(0, start + step)
        items = [
            (
                head_pair(q[rows, lanes]), head_pair(g[rows, lanes]), gt[lanes, rows],
                k[keys, lanes], v[keys, lanes], kt[lanes, keys], vt[lanes, keys],
            )
            for lanes in pairs
        ]
        results = pair_steps(items, step, mask)
        for lanes, (_, _, dk, dv) in zip(pairs, results):
            dk_ref[keys, lanes] += dk
            dv_ref[keys, lanes] += dv
        att_blocks.append(jnp.concatenate([result[0] for result in results], 0))
        dq_blocks.append(jnp.concatenate([result[1] for result in results], 0))
    grads_ref[:, :HW] = transposed(jnp.concatenate(dq_blocks, 1))
    grads_ref[:, HW : 2 * HW] = dk_ref[...].astype(BF16)
    grads_ref[:, 2 * HW :] = dv_ref[...].astype(BF16)
    term_qkv = dot_nn(hidden_t, grads_ref[...]).astype(BF16)
    out_ref[...] = dot_nn(jnp.concatenate(att_blocks, 1), cot).astype(BF16)
    grad_normed = dot_nt(grads_ref[...], w_ref[...]) * gain_ref[...]
    base_ref[...] = input_grad(
        cot_ref[...].astype(F32), normed_ref[...], inverse_ref[...], grad_normed
    )
    return term_qkv


def row_kernel(x_any, cot_any, gain_any, wqkv_any, wout_any, qkv_ref, *refs):
    qkv_ref[...] = row_part(x_any, cot_any, gain_any, wqkv_any, wout_any, *refs)


def row_chip_kernel(
    x_any, cot_any, gain_any, wqkv_any, wout_any,
    send_1, send_2, keep_1, keep_2, rows_ref, col_w_ref, col_wo_ref, *refs,
):
    chip, core, _ = here()
    sems, rows = refs[-1], rows_ref.shape[0]
    at = pl.multiple_of((chip * 2 + core) * rows, rows)
    handed = started(
        pltpu.make_async_copy(wqkv_any.at[pl.ds(at, rows), :], rows_ref, sems.at[7]),
        *weight_copies(wqkv_any, wout_any, col_w_ref, col_wo_ref, sems.at[pl.ds(8, 4)], 1),
    )
    term_qkv = row_part(x_any, cot_any, gain_any, wqkv_any, wout_any, *refs)
    chips, cut = send_1.shape[0], keep_1.shape[2]
    pieces = slice(0, chips), slice(0, cut)
    split_cores(term_qkv[:, :cut], send_1, keep_1, *pieces)
    split_cores(term_qkv[:, cut:], send_2, keep_2, *pieces)
    finished(*handed)


def column_part(x, cot, mask, gain, w_ref, wo_ref, weight_waits, grads_ref):
    tokens, block = x.shape[0], mask.shape[0]
    _, normed = rms_parts(x.astype(F32))
    hidden = (normed * gain).astype(BF16)
    hidden_t = transposed(hidden)
    finished(*weight_waits)
    q, k, v, g = project(hidden, cot, w_ref, wo_ref)
    kt, vt, gt = transposed(k), transposed(v), transposed(g)
    pairs = [slice(i * 2 * HD, (i + 1) * 2 * HD) for i in range(HH // 2)]
    blocks = [slice(at, at + block) for at in range(0, tokens, block)]
    items = [
        (
            head_pair(q[rows, lanes]), head_pair(g[rows, lanes]), gt[lanes, rows],
            k[rows, lanes], v[rows, lanes], kt[lanes, rows], vt[lanes, rows],
        )
        for lanes in pairs
        for rows in blocks
    ]
    results = pair_steps(items, block, mask)
    places = [(lanes, rows) for lanes in pairs for rows in blocks]
    for (lanes, rows), (_, _, dk, dv) in zip(places, results):
        grads_ref[rows, HW + lanes.start : HW + lanes.stop] = dk.astype(BF16)
        grads_ref[rows, 2 * HW + lanes.start : 2 * HW + lanes.stop] = dv.astype(BF16)
    by_pair = [results[i * len(blocks) : (i + 1) * len(blocks)] for i in range(len(pairs))]
    attended, grad_q = [
        jnp.concatenate([jnp.concatenate([r[i] for r in some], 1) for some in by_pair], 0)
        for i in range(2)
    ]
    grads_ref[:, :HW] = transposed(grad_q)
    term_qkv = dot_nn(hidden_t, grads_ref[...]).astype(BF16)
    term_out = dot_nn(attended, cot).astype(BF16)
    return term_qkv, term_out


def column_mask(all_rows, group, row_of):
    block = all_rows * group
    shape = (block, 2 * block)
    query = lax.broadcasted_iota(jnp.int32, shape, 1) % block
    key = lax.broadcasted_iota(jnp.int32, shape, 0)
    same_column = query % group == key % group
    return (row_of(query // group) >= row_of(key // group)) & same_column


def column_kernel(
    moved_any, gain_any, wqkv_any, wout_any, row_qkv_ref, row_out_ref,
    terms_ref, grads_ref, w_ref,
    moved_ref, gain_ref, wo_ref, sems,
):
    copies = started(
        pltpu.make_async_copy(moved_any, moved_ref, sems.at[4]),
        pltpu.make_async_copy(gain_any, gain_ref, sems.at[5]),
    )
    weights = started(*weight_copies(wqkv_any, wout_any, w_ref, wo_ref, sems, 1))
    finished(*copies)
    all_rows, _, share, width = moved_ref.shape
    group = math.gcd(share, 16)
    x, cot = [
        jnp.concatenate(
            [
                moved_ref[:, which, at : at + group, :].astype(F32).reshape(all_rows * group, width)
                for at in range(0, share, group)
            ],
            0,
        ).astype(BF16)
        for which in range(2)
    ]
    mask = column_mask(all_rows, group, lambda place: place)
    term_qkv, term_out = column_part(
        x, cot, mask, gain_ref[...], w_ref, wo_ref, weights, grads_ref
    )
    for i in range(3):
        at = i * width
        terms_ref[:, at : at + HW] = row_qkv_ref[:, i * HW : (i + 1) * HW]
        terms_ref[:, at + HW : at + 2 * HW] = term_qkv[:, i * HW : (i + 1) * HW]
    terms_ref[:HW, 3 * width :] = row_out_ref[...]
    terms_ref[HW:, 3 * width :] = term_out


def column_chip_kernel(
    x_ref, cot_ref, swapped_ref, corner_ref, near_2, near_3, far_ref, gain_ref, w_ref, wo_ref, row_out_ref,
    send_ref, keep_ref, grads_ref,
):
    chip, core, _ = here()
    share = far_ref.shape[2]
    half = pl.ds(pl.multiple_of(core * share, share), share)
    at = pl.ds(pl.multiple_of((chip * 2 + core) * share, share), share)
    group = math.gcd(share, 16)

    def tokens(which, mine):
        pieces = [
            mine[at, :], swapped_ref[0, which], corner_ref[0, which], corner_ref[1, which],
        ]
        for i, near in enumerate((near_2, near_3)):
            pieces += [near[which, half, :], far_ref[i, which]]
        starts = range(0, share, group)
        return jnp.concatenate(
            [piece[start : start + group] for start in starts for piece in pieces], 0
        )

    def row_of(place):
        step = (4 - (place >> 1)) & 3
        return ((step ^ chip) << 1) + ((place & 1) ^ core)

    mask = column_mask(2 * (len(CHIP_STEPS) + 1), group, row_of)
    term_qkv, term_out = column_part(
        tokens(0, x_ref), tokens(1, cot_ref), mask, gain_ref[...], w_ref, wo_ref, (), grads_ref
    )
    chips = send_ref.shape[0]
    refs = send_ref, keep_ref
    out_lanes = slice(3 * HW, send_ref.shape[2])
    split_cores(term_qkv, *refs, slice(0, chips), slice(0, 3 * HW))
    split_cores(row_out_ref[...], *refs, slice(0, chips // 2), out_lanes)
    split_cores(term_out, *refs, slice(chips // 2, chips), out_lanes)


def far_kernel(near_2, near_3, far_ref):
    share = far_ref.shape[2]
    at = pl.ds(pl.multiple_of((1 - here()[1]) * share, share), share)
    for i, near in enumerate((near_2, near_3)):
        far_ref[i] = near[:, at, :]


def back_kernel(grads_ref, w_ref, back_ref):
    grad_hidden = dot_nt(grads_ref[...], w_ref[...])
    all_rows, share, width = back_ref.shape
    group = math.gcd(share, 16)
    block = all_rows * group
    for i in range(share // group):
        piece = grad_hidden[i * block : (i + 1) * block].reshape(all_rows, group, width)
        back_ref[:, i * group : (i + 1) * group, :] = piece.astype(BF16)


def back_chip_kernel(grads_ref, w_ref, send_ref, keep_ref):
    grad_hidden = dot_nt(grads_ref[...], w_ref[...]).astype(BF16)
    chips, share, width = keep_ref.shape
    group = math.gcd(share, 16)
    block = 2 * chips * group
    for i in range(share // group):
        piece = grad_hidden[i * block : (i + 1) * block].reshape(chips, 2, group, width)
        at = slice(i * group, (i + 1) * group)
        keep_ref[:, at, :], send_ref[:, at, :] = piece[:, 0], piece[:, 1]


def back_pack_kernel(keep_ref, got_ref, *targets):
    share = keep_ref.shape[1]
    core = here()[1]
    kept_at = pl.ds(pl.multiple_of(core * share, share), share)
    got_at = pl.ds(pl.multiple_of((1 - core) * share, share), share)
    for i, target in enumerate(targets):
        target[kept_at, :] = keep_ref[i]
        target[got_at, :] = got_ref[i]


def input_kernel(base_ref, normed_ref, inverse_ref, gain_ref, back_ref, grad_ref):
    grad_ref[...] = input_grad(
        base_ref[...], normed_ref[...], inverse_ref[...], back_ref[...].astype(F32) * gain_ref[...]
    ).astype(BF16)


def input_grad(base, normed, inverse_rms, grad_normed):
    projected = jnp.mean(grad_normed * normed, -1, keepdims=True)
    return base + inverse_rms * (grad_normed - normed * projected)


def input_chip_kernel(
    base_ref, normed_ref, inverse_ref, gain_ref, own_ref, got_1, got_2, got_3,
    grad_any, grad_ref, sems,
):
    chip = here()[0]
    count = own_ref.shape[0]
    copies = []
    for i, (step, back_ref) in enumerate(zip((0, *CHIP_STEPS), (own_ref, got_1, got_2, got_3))):
        at = pl.ds(pl.multiple_of((chip ^ step) * count, count), count)
        grad_normed = back_ref[...].astype(F32) * gain_ref[...]
        grad = input_grad(base_ref[at, :], normed_ref[at, :], inverse_ref[at, :], grad_normed)
        grad_ref[i] = grad.astype(BF16)
        copies += started(pltpu.make_async_copy(grad_ref.at[i], grad_any.at[at, :], sems.at[i]))
    finished(*copies)


def pack_kernel(x_any, cot_any, swap_ref, corner_ref, off_2, off_3, sems):
    chip, core, _ = here()
    share = corner_ref.shape[1]

    def columns(step, of_core):
        return pl.multiple_of(((chip ^ step) * 2 + of_core) * share, share)

    corner = CHIP_STEPS[0]
    copies = []
    for which, source in enumerate((x_any, cot_any)):
        pieces = [
            (columns(0, 1 - core), share, swap_ref.at[0, which]),
            (columns(corner, 1 - core), share, swap_ref.at[1, which]),
            (columns(corner, core), share, corner_ref.at[which]),
            (columns(CHIP_STEPS[1], 0), 2 * share, off_2.at[which]),
            (columns(CHIP_STEPS[2], 0), 2 * share, off_3.at[which]),
        ]
        for i, (at, count, target) in enumerate(pieces):
            copies.append(
                pltpu.make_async_copy(
                    source.at[pl.ds(at, count), :], target, sems.at[5 * which + i]
                )
            )
    finished(*started(*copies))


def corner_kernel(corner_ref, swapped_ref, out_ref):
    out_ref[0], out_ref[1] = corner_ref[...], swapped_ref[1]


def split_rows(total, axis):
    upper = (here()[2] & 1) == 1
    low, high = jnp.split(total, 2, axis)
    return jnp.where(upper, low, high).astype(BF16), jnp.where(upper, high, low)


def row_cores_kernel(keep_1, keep_2, got_1, got_2, send_ref, kept_ref):
    total = [
        keep_ref[...].astype(F32) + got_ref[...].astype(F32)
        for keep_ref, got_ref in ((keep_1, got_1), (keep_2, got_2))
    ]
    send_ref[...], kept_ref[...] = split_rows(jnp.concatenate(total, 2), 1)


def cores_kernel(keep_ref, got_ref, send_ref, kept_ref, *targets):
    chip, cut = here()[0], kept_ref.shape[2]
    first = keep_ref[:, :, :cut].astype(F32) + got_ref[:, :, :cut].astype(F32)
    send_ref[...], kept_ref[...] = split_rows(first, 1)
    for step, target in zip((0, *CHIP_STEPS), targets):
        there = chip ^ step
        total = keep_ref[there, :, cut:].astype(F32) + got_ref[there, :, cut:].astype(F32)
        target[...] = total.astype(target.dtype)


def pair_kernel(kept_ref, got_ref, row_kept, row_got, *targets):
    chip, cut = here()[0], kept_ref.shape[2]
    for step, target in zip((0, *CHIP_STEPS), targets):
        there = chip ^ step
        total = kept_ref[there] + got_ref[there].astype(F32)
        target[:, :cut] = total.astype(target.dtype)
        total = row_kept[there] + row_got[there].astype(F32)
        target[:, cut:] = total.astype(target.dtype)


def layer_sum(own_ref, got_1, got_2, got_3):
    return own_ref[...] + (
        (got_1[...].astype(F32) + got_2[...].astype(F32)) + got_3[...].astype(F32)
    )


def layer_kernel(own_ref, got_1, got_2, got_3, send_ref, kept_ref):
    send_ref[...], kept_ref[...] = split_rows(layer_sum(own_ref, got_1, got_2, got_3), 0)


def join_kernel(own_ref, got_1, got_2, got_3, kept_ref, got_ref, out_ref):
    total = layer_sum(own_ref, got_1, got_2, got_3).astype(BF16)
    cut, width = FIRST_PART, kept_ref.shape[1]
    out_ref[:, :cut] = total[:, :cut]
    out_ref[:, cut : cut + width] = (kept_ref[...] + got_ref[...].astype(F32)).astype(BF16)
    out_ref[:, cut + width :] = total[:, cut:]


def add_kernel(kept_ref, got_ref, out_ref):
    out_ref[...] = (kept_ref[...].astype(F32) + got_ref[...].astype(F32)).astype(BF16)


def result_kernel(mine, *refs):
    half_ref, w_ref, gain_ref = refs[:3]
    qkv_any, out_any, grad_ref, qkv_ref, out_ref, sems = refs[-6:]
    chip, core, layer = here()
    half, width = out_ref.shape
    rows = 2 * half
    upper = layer & 1 if mine else 1 - (layer & 1)
    first = pl.multiple_of(upper * half, half)
    row_at = 3 * HW + width
    out_ref[...] = half_ref[:, 3 * HW : row_at].astype(F32)
    here_rows = pl.ds(first, half)
    copies = started(pltpu.make_async_copy(out_ref, out_any.at[here_rows, :], sems.at[0]))
    for i in range(3):
        at = i * width
        qkv_ref[:, at : at + HW] = half_ref[:, row_at + i * HW : row_at + (i + 1) * HW].astype(F32)
        qkv_ref[:, at + HW : at + 2 * HW] = half_ref[:, i * HW : (i + 1) * HW].astype(F32)
    copies += started(pltpu.make_async_copy(qkv_ref, qkv_any.at[here_rows, :], sems.at[1]))
    weight = w_ref[here_rows, :].astype(F32)
    total = jnp.sum(qkv_ref[...] * weight, -1, keepdims=True)
    shape = (half, width)
    row = lax.broadcasted_iota(jnp.int32, shape, 0) + (chip * 2 + core) * rows + first
    feature = lax.broadcasted_iota(jnp.int32, shape, 1)
    gain = jnp.sum(jnp.where(feature == row, gain_ref[...], 0.0), -1, keepdims=True)
    shape = (half, rows)
    same = lax.broadcasted_iota(jnp.int32, shape, 0) + first == lax.broadcasted_iota(jnp.int32, shape, 1)
    grad = jnp.sum(jnp.where(same, total / gain, 0.0), 0, keepdims=True)
    grad_ref[...] = grad if mine else refs[5][...] + grad
    finished(*copies)


def call(kernel, name, ins, outs, scratch=(), vmem=SMALL_VMEM, out_specs=None, aliases=None):
    out_specs = out_specs or [VMEM] * len(outs)
    places = [{id(HBM): pltpu.HBM, id(PINNED): pltpu.VMEM}.get(id(spec)) for spec in out_specs]
    outs = [place(*out) if place else shaped(*out) for place, out in zip(places, outs)]
    args = [
        pltpu.with_memory_space_constraint(array, pltpu.HBM) if spec is HBM else array
        for spec, array in ins
    ]
    return pl.pallas_call(
        kernel,
        out_shape=outs,
        in_specs=[spec for spec, _ in ins],
        out_specs=out_specs,
        scratch_shapes=scratch,
        input_output_aliases=aliases or {},
        name=name,
        cost_estimate=pl.CostEstimate(flops=0, bytes_accessed=0, transcendentals=0),
        compiler_params=pltpu.CompilerParams(vmem_limit_bytes=vmem),
    )(*args)


def swap(array, axis, bits):
    count = lax.axis_size(axis)
    return lax.ppermute(array, axis, [(i, i ^ bits) for i in range(count)])


def cross_chips(*offs):
    return [swap(off, "seq", 2 * step) for off, step in zip(offs, CHIP_STEPS)]


def add_two(kept, got, name):
    (total,) = call(add_kernel, name, [(VMEM, kept), (VMEM, got)], [(kept.shape, BF16)])
    return total


def body(inputs, norm_gain, qkv_weight, out_weight, out_cotan):
    columns, width = inputs.shape[2:]
    n = lax.axis_size("seq")
    m = lax.axis_size("dp")
    share = columns // n
    row_share = width // n
    row_width, col_width = 3 * HW, 3 * HW + width
    x = inputs.reshape(columns, width)
    cot = out_cotan.reshape(columns, width)
    gain = norm_gain.reshape(1, width)
    chips = 4
    layered = n == 2 * chips and m == 4 and row_share == share
    weight_scratch = [
        pltpu.VMEM((1, width), F32),
        pltpu.VMEM((width, 3 * HW), BF16),
        pltpu.VMEM((HW, width), BF16),
    ]
    weights = [(HBM, gain), (HBM, qkv_weight), (HBM, out_weight)]
    col_outs = [((columns, 3 * HW), BF16), ((width, 3 * HW), BF16)]

    if layered:
        packed = call(
            pack_kernel,
            "pack_columns",
            [(HBM, x), (HBM, cot)],
            [((2, 2, share, width), BF16), ((2, share, width), BF16)]
            + [((2, 2 * share, width), BF16)] * 2,
            [pltpu.SemaphoreType.DMA((10,))],
            out_specs=[ANY] * 4,
        )
        near = [swap(one, "seq", 2 * step) for one, step in zip(packed[2:], CHIP_STEPS[1:])]
        swapped = swap(packed[0], "seq", 1)
        (corner,) = call(
            corner_kernel,
            "pack_corner",
            [(VMEM, packed[1]), (VMEM, swapped)],
            [((2, 2, share, width), BF16)],
        )
        x_first, _ = lax.optimization_barrier((x, corner))
        corner = swap(corner, "seq", 2 * CHIP_STEPS[0])
    else:
        outgoing = jnp.stack([x.reshape(n, share, width), cot.reshape(n, share, width)], 1)
        moved = lax.all_to_all(outgoing, "seq", split_axis=0, concat_axis=0, tiled=True)
        x_first = x

    row_outs = [
        ((HW, width), BF16),
        ((columns, width), F32), ((columns, width), F32), ((columns, 1), F32),
        ((columns, width), BF16), ((columns, width), BF16),
    ]
    if layered:
        cut = row_width // 2
        split_outs = [((chips, row_share, cut), BF16)] * 4
        handed_outs = [
            ((row_share, 3 * width), BF16), ((width, 3 * HW), BF16), ((HW, width), BF16),
        ]
        row_outs = [*split_outs, *handed_outs, *row_outs]
        specs = [VMEM] * 4 + [PINNED] * (len(row_outs) - 4)
    else:
        row_outs = [((width, row_width), BF16), *row_outs]
        specs = [VMEM] * len(row_outs)
    *row_terms, row_out, base, normed, inverse_rms, x_near, cot_near = call(
        row_chip_kernel if layered else row_kernel,
        "row_heads",
        [(HBM, x_first), (HBM, cot), *weights],
        row_outs,
        [
            *weight_scratch,
            pltpu.VMEM((columns, HW), F32),
            pltpu.VMEM((columns, HW), F32),
            pltpu.VMEM((columns, 3 * HW), BF16),
            pltpu.SemaphoreType.DMA((12,)),
        ],
        BIG_VMEM,
        specs,
    )
    if layered:
        *row_terms, weight_rows, col_weight, col_out_weight = row_terms
        row_sent = [swap(one, "seq", 1) for one in row_terms[:2]]
        half_block = (chips, row_share // 2, row_width)
        row_next, row_kept = call(
            row_cores_kernel,
            "row_add_cores",
            [(VMEM, one) for one in (*row_terms[2:], *row_sent)],
            [(half_block, BF16), (half_block, F32)],
            out_specs=[VMEM, PINNED],
        )
        col_weight, row_kept = lax.optimization_barrier((col_weight, row_kept))
        *near, base = lax.optimization_barrier((*near, base))
        (far,) = call(
            far_kernel,
            "pack_other_core",
            [(VMEM, one) for one in near],
            [((2, 2, share, width), BF16)],
        )
        send, keep, col_grads = call(
            column_chip_kernel,
            "column_heads",
            [
                (VMEM, one)
                for one in (
                    x_near, cot_near, swapped, corner, *near, swap(far, "seq", 1),
                    gain, col_weight, col_out_weight, row_out,
                )
            ],
            [((chips, row_share, col_width), BF16)] * 2 + [col_outs[0]],
            vmem=BIG_VMEM,
            out_specs=[VMEM, VMEM, PINNED],
        )
        back_send, back_keep = call(
            back_chip_kernel,
            "column_grad_hidden",
            [(VMEM, col_grads), (VMEM, col_weight)],
            [((chips, share, width), BF16)] * 2,
        )
        row_next, _ = lax.optimization_barrier((row_next, send))
        keep, back_keep = lax.optimization_barrier((keep, back_keep))
        first_half = (chips, row_share // 2, FIRST_PART)
        second = (row_share, col_width - FIRST_PART)
        to_next, kept, owned, *off = call(
            cores_kernel,
            "column_add_cores",
            [(VMEM, keep), (VMEM, swap(send, "seq", 1))],
            [(first_half, BF16), (first_half, F32), (second, F32)] + [(second, BF16)] * 3,
            out_specs=[VMEM, PINNED, PINNED, VMEM, VMEM, VMEM],
        )
        got = cross_chips(*off)
        back = call(
            back_pack_kernel,
            "pack_grad_hidden",
            [(VMEM, back_keep), (VMEM, swap(back_send, "seq", 1))],
            [((2 * share, width), BF16)] * 4,
        )
        row_kept, *back = lax.optimization_barrier((row_kept, *back))
        joint = (row_share // 2, FIRST_PART + row_width)
        first_owned, *off = call(
            pair_kernel,
            "first_add_pair",
            [
                (VMEM, one)
                for one in (kept, swap(to_next, "dp", 1), row_kept, swap(row_next, "dp", 1))
            ],
            [(joint, F32)] + [(joint, BF16)] * 3,
            out_specs=[PINNED, VMEM, VMEM, VMEM],
        )
        first_got = cross_chips(*off)
        second_half = (row_share // 2, second[1])
        to_next, kept = call(
            layer_kernel,
            "second_add_chips",
            [(VMEM, one) for one in (owned, *got)],
            [(second_half, BF16), (second_half, F32)],
            out_specs=[VMEM, PINNED],
        )
        (pair_sum,) = call(
            join_kernel,
            "join_terms",
            [(VMEM, one) for one in (first_owned, *first_got, kept, swap(to_next, "dp", 1))],
            [((row_share // 2, col_width + row_width), BF16)],
        )
        *back, pair_sum = lax.optimization_barrier((*back, pair_sum))
        held = add_two(pair_sum, swap(pair_sum, "dp", 2), "add_pairs")
        other = swap(held, "dp", 1)
        (grad,) = call(
            input_chip_kernel,
            "input_grad",
            [
                (VMEM, one)
                for one in (base, normed, inverse_rms, gain, back[0], *cross_chips(*back[1:]))
            ],
            [((columns, width), BF16)],
            [pltpu.VMEM((chips, 2 * share, width), BF16), pltpu.SemaphoreType.DMA((chips,))],
            out_specs=[HBM],
        )
        half = row_share // 2
        results = []
        for mine, part in ((True, held), (False, other)):
            aliased = [(HBM, one) for one in results[:2]] + [(VMEM, one) for one in results[2:]]
            results = call(
                functools.partial(result_kernel, mine),
                "result_first" if mine else "result",
                [(VMEM, part), (VMEM, weight_rows), (VMEM, gain), *aliased],
                [((row_share, 3 * width), F32), ((row_share, width), F32), ((1, row_share), F32)],
                [
                    pltpu.VMEM((half, 3 * width), F32),
                    pltpu.VMEM((half, width), F32),
                    pltpu.SemaphoreType.DMA((2,)),
                ],
                out_specs=[HBM, HBM, VMEM],
                aliases={} if mine else {3: 0, 4: 1},
            )
        sum_qkv, sum_out, sum_gain = results
        sum_gain = sum_gain.reshape(row_share)
    else:
        terms, *col_grads = call(
            column_kernel,
            "column_heads",
            [(ANY, moved), *weights, (VMEM, row_terms[0]), (VMEM, row_out)],
            [((width, 4 * width), BF16), *col_outs],
            [
                pltpu.VMEM((n, 2, share, width), BF16),
                weight_scratch[0],
                weight_scratch[2],
                pltpu.SemaphoreType.DMA((6,)),
            ],
            BIG_VMEM,
        )
        (back,) = call(
            back_kernel,
            "column_grad_hidden",
            [(VMEM, one) for one in col_grads],
            [((n, share, width), BF16)],
        )
        returned = lax.all_to_all(back, "seq", split_axis=0, concat_axis=0, tiled=True)
        (grad,) = call(
            input_kernel,
            "input_grad",
            [
                (VMEM, base), (VMEM, normed), (VMEM, inverse_rms), (VMEM, gain),
                (VMEM, returned.reshape(columns, width)),
            ],
            [((columns, width), BF16)],
        )
        terms = lax.all_to_all(
            terms.reshape(n, row_share, 4 * width), "seq", split_axis=0, concat_axis=0, tiled=True
        )
        total = jnp.sum(terms.astype(F32), 0)
        for step in range(m.bit_length() - 1):
            sent = total.astype(BF16)
            total = sent.astype(F32) + swap(sent, "dp", 1 << step).astype(F32)
        sum_qkv, sum_out = total[:, : 3 * width], total[:, 3 * width :]
        here_at = lax.axis_index("seq") * row_share
        own_gain = lax.dynamic_slice_in_dim(norm_gain, here_at, row_share, 0)
        own_weight = lax.dynamic_slice_in_dim(qkv_weight, here_at, row_share, 0)
        sum_gain = jnp.sum(sum_qkv * own_weight.astype(F32), -1) / own_gain
    return (grad.reshape(inputs.shape), sum_qkv, sum_out, sum_gain)


def solution(mesh):
    return jax.shard_map(
        body,
        mesh=mesh,
        in_specs=(P("dp", "seq", None, None), P(), P(), P(), P("dp", "seq", None, None)),
        out_specs=(P("dp", "seq", None, None), P("seq", None), P("seq", None), P("seq")),
        check_vma=False,
    )
```

```python
import math

import jax
import jax.numpy as jnp
from jax import lax
from jax.experimental import pallas as pl
from jax.experimental.pallas import tpu as pltpu
from jax.sharding import PartitionSpec as P

H = 8
HD = 64
HH = H // 2
HW = HH * HD
SCALE = HD ** (-0.5)
F32 = jnp.float32
BF16 = jnp.bfloat16
QUERY_BLOCK = 128
BIG_VMEM = 20 * 1024 * 1024
SMALL_VMEM = 8 * 1024 * 1024
ANY = pl.BlockSpec(memory_space=pl.ANY)
VMEM = pl.BlockSpec(memory_space=pltpu.VMEM)
HBM = pl.BlockSpec(memory_space=pltpu.HBM)
CHIP_STEPS = (3, 2, 1)
FIRST_PART = 512
PINNED = pl.BlockSpec(memory_space=pltpu.VMEM)
shaped = jax.ShapeDtypeStruct


def here():
    device = lax.axis_index("seq")
    return device >> 1, device & 1, lax.axis_index("dp")


def dot_nn(a, b):
    return lax.dot_general(a, b, (((1,), (0,)), ((), ())), preferred_element_type=F32)


def dot_nt(a, b):
    return lax.dot_general(a, b, (((1,), (1,)), ((), ())), preferred_element_type=F32)


def rms_parts(x):
    inverse_rms = lax.rsqrt(jnp.mean(x * x, -1, keepdims=True) + 1e-05)
    return inverse_rms, x * inverse_rms


def transposed(x):
    block = math.gcd(x.shape[1], 256)
    eye = (
        lax.broadcasted_iota(jnp.int32, (block, block), 0)
        == lax.broadcasted_iota(jnp.int32, (block, block), 1)
    ).astype(F32).astype(BF16)
    parts = [
        dot_nt(eye, x[:, at : at + block]).astype(BF16) for at in range(0, x.shape[1], block)
    ]
    return parts[0] if len(parts) == 1 else jnp.concatenate(parts, 0)


def head_pair(x):
    lane = lax.broadcasted_iota(jnp.int32, x.shape, 1)
    zero = jnp.zeros_like(x)
    return jnp.concatenate([jnp.where(lane < HD, x, zero), jnp.where(lane < HD, zero, x)], 0)


def both_heads(both, count):
    return jnp.concatenate([both[:HD, :count], both[HD:, count:]], 0)


def pair_steps(items, mask_rows, mask):
    count = items[0][2].shape[1]
    scores = [dot_nt(k, q2) for q2, _, _, k, _, _, _ in items]
    prob_grads = [dot_nt(v, g2) for _, g2, _, _, v, _, _ in items]
    probs = []
    for score in scores:
        first = score.shape[0] - mask_rows
        tail = jnp.where(mask, score[first:], -1e30)
        score = tail if first == 0 else jnp.concatenate([score[:first], tail], 0)
        exponent = jnp.exp(score - jnp.max(score, 0, keepdims=True))
        probs.append(exponent * (1.0 / jnp.sum(exponent, 0, keepdims=True)))
    weights = [prob.astype(BF16) for prob in probs]
    attended = [
        both_heads(dot_nn(item[6], weight), count).astype(BF16)
        for item, weight in zip(items, weights)
    ]
    score_grads = []
    for item, att, prob, prob_grad in zip(items, attended, probs, prob_grads):
        product = item[2].astype(F32) * att.astype(F32)
        delta = [jnp.sum(part, 0, keepdims=True) for part in (product[:HD], product[HD:])]
        score_grads.append((prob * (prob_grad - jnp.concatenate(delta, 1))).astype(BF16))
    grad_q = [
        (both_heads(dot_nn(item[5], score_grad), count) * SCALE).astype(BF16)
        for item, score_grad in zip(items, score_grads)
    ]
    grad_k = [dot_nn(score_grad, item[0]) for item, score_grad in zip(items, score_grads)]
    grad_v = [dot_nn(weight, item[1]) for item, weight in zip(items, weights)]
    return list(zip(attended, grad_q, grad_k, grad_v))


def split_cores(piece, send_ref, keep_ref, chips, lanes):
    rows = send_ref.shape[1]
    parts = piece.reshape(chips.stop - chips.start, 2, rows, piece.shape[1])
    even, odd = parts[:, 0], parts[:, 1]
    first = here()[1] == 0
    send_ref[chips, :, lanes] = jnp.where(first, odd, even)
    keep_ref[chips, :, lanes] = jnp.where(first, even, odd)


def qkv_copies(wqkv_ref, w_ref, sems, second):
    width = wqkv_ref.shape[0]
    return [
        pltpu.make_async_copy(
            wqkv_ref.at[:, pl.ds(i * width + second * HW, HW)],
            w_ref.at[:, pl.ds(i * HW, HW)],
            sems.at[i],
        )
        for i in range(3)
    ]


def weight_copies(wqkv_ref, wout_ref, w_ref, wo_ref, sems, second):
    out_rows = wout_ref.at[pl.ds(second * HW, HW), :]
    return [
        *qkv_copies(wqkv_ref, w_ref, sems, second),
        pltpu.make_async_copy(out_rows, wo_ref, sems.at[3]),
    ]


def started(*copies):
    for copy in copies:
        copy.start()
    return copies


def finished(*copies):
    for copy in copies:
        copy.wait()


def project(hidden, cot, w_ref, wo_ref):
    projected = dot_nn(hidden, w_ref[...]).astype(BF16)
    q, k, v = [projected[:, i * HW : (i + 1) * HW] for i in range(3)]
    g = dot_nt(cot, wo_ref[...]).astype(BF16)
    return q * jnp.asarray(SCALE, BF16), k, v, g


def row_part(
    x_any, cot_any, gain_any, wqkv_any, wout_any,
    out_ref, base_ref, normed_ref, inverse_ref, x_ref, cot_ref,
    gain_ref, w_ref, wo_ref, dk_ref, dv_ref, grads_ref, sems,
):
    first = started(
        pltpu.make_async_copy(x_any, x_ref, sems.at[4]),
        pltpu.make_async_copy(gain_any, gain_ref, sems.at[5]),
    )
    later = started(
        *weight_copies(wqkv_any, wout_any, w_ref, wo_ref, sems, 0),
        pltpu.make_async_copy(cot_any, cot_ref, sems.at[6]),
    )
    dk_ref[...] = jnp.zeros_like(dk_ref)
    dv_ref[...] = jnp.zeros_like(dv_ref)
    finished(*first)
    tokens = x_ref.shape[0]
    inverse_ref[...], normed_ref[...] = rms_parts(x_ref[...].astype(F32))
    hidden = (normed_ref[...] * gain_ref[...]).astype(BF16)
    hidden_t = transposed(hidden)
    finished(*later)
    cot = cot_ref[...]
    q, k, v, g = project(hidden, cot, w_ref, wo_ref)
    kt, vt, gt = transposed(k), transposed(v), transposed(g)
    step = math.gcd(tokens, QUERY_BLOCK)
    query = lax.broadcasted_iota(jnp.int32, (step, 2 * step), 1) % step
    mask = query >= lax.broadcasted_iota(jnp.int32, (step, 2 * step), 0)
    pairs = [slice(i * 2 * HD, (i + 1) * 2 * HD) for i in range(HH // 2)]
    att_blocks, dq_blocks = [], []
    for start in range(0, tokens, step):
        rows, keys = slice(start, start + step), slice(0, start + step)
        items = [
            (
                head_pair(q[rows, lanes]), head_pair(g[rows, lanes]), gt[lanes, rows],
                k[keys, lanes], v[keys, lanes], kt[lanes, keys], vt[lanes, keys],
            )
            for lanes in pairs
        ]
        results = pair_steps(items, step, mask)
        for lanes, (_, _, dk, dv) in zip(pairs, results):
            dk_ref[keys, lanes] += dk
            dv_ref[keys, lanes] += dv
        att_blocks.append(jnp.concatenate([result[0] for result in results], 0))
        dq_blocks.append(jnp.concatenate([result[1] for result in results], 0))
    grads_ref[:, :HW] = transposed(jnp.concatenate(dq_blocks, 1))
    grads_ref[:, HW : 2 * HW] = dk_ref[...].astype(BF16)
    grads_ref[:, 2 * HW :] = dv_ref[...].astype(BF16)
    term_qkv = dot_nn(hidden_t, grads_ref[...]).astype(BF16)
    out_ref[...] = dot_nn(jnp.concatenate(att_blocks, 1), cot).astype(BF16)
    grad_normed = dot_nt(grads_ref[...], w_ref[...]) * gain_ref[...]
    base_ref[...] = input_grad(
        cot_ref[...].astype(F32), normed_ref[...], inverse_ref[...], grad_normed
    )
    return term_qkv


def row_kernel(x_any, cot_any, gain_any, wqkv_any, wout_any, qkv_ref, *refs):
    qkv_ref[...] = row_part(x_any, cot_any, gain_any, wqkv_any, wout_any, *refs)


def row_chip_kernel(
    x_any, cot_any, gain_any, wqkv_any, wout_any,
    send_1, send_2, keep_1, keep_2, rows_ref, col_w_ref, col_wo_ref, *refs,
):
    chip, core, _ = here()
    sems, rows = refs[-1], rows_ref.shape[0]
    at = pl.multiple_of((chip * 2 + core) * rows, rows)
    handed = started(
        pltpu.make_async_copy(wqkv_any.at[pl.ds(at, rows), :], rows_ref, sems.at[7]),
        *weight_copies(wqkv_any, wout_any, col_w_ref, col_wo_ref, sems.at[pl.ds(8, 4)], 1),
    )
    term_qkv = row_part(x_any, cot_any, gain_any, wqkv_any, wout_any, *refs)
    chips, cut = send_1.shape[0], keep_1.shape[2]
    pieces = slice(0, chips), slice(0, cut)
    split_cores(term_qkv[:, :cut], send_1, keep_1, *pieces)
    split_cores(term_qkv[:, cut:], send_2, keep_2, *pieces)
    finished(*handed)


def column_part(x, cot, mask, gain, w_ref, wo_ref, weight_waits, grads_ref):
    tokens, block = x.shape[0], mask.shape[0]
    _, normed = rms_parts(x.astype(F32))
    hidden = (normed * gain).astype(BF16)
    hidden_t = transposed(hidden)
    finished(*weight_waits)
    q, k, v, g = project(hidden, cot, w_ref, wo_ref)
    kt, vt, gt = transposed(k), transposed(v), transposed(g)
    pairs = [slice(i * 2 * HD, (i + 1) * 2 * HD) for i in range(HH // 2)]
    blocks = [slice(at, at + block) for at in range(0, tokens, block)]
    items = [
        (
            head_pair(q[rows, lanes]), head_pair(g[rows, lanes]), gt[lanes, rows],
            k[rows, lanes], v[rows, lanes], kt[lanes, rows], vt[lanes, rows],
        )
        for lanes in pairs
        for rows in blocks
    ]
    results = pair_steps(items, block, mask)
    places = [(lanes, rows) for lanes in pairs for rows in blocks]
    for (lanes, rows), (_, _, dk, dv) in zip(places, results):
        grads_ref[rows, HW + lanes.start : HW + lanes.stop] = dk.astype(BF16)
        grads_ref[rows, 2 * HW + lanes.start : 2 * HW + lanes.stop] = dv.astype(BF16)
    by_pair = [results[i * len(blocks) : (i + 1) * len(blocks)] for i in range(len(pairs))]
    attended, grad_q = [
        jnp.concatenate([jnp.concatenate([r[i] for r in some], 1) for some in by_pair], 0)
        for i in range(2)
    ]
    grads_ref[:, :HW] = transposed(grad_q)
    term_qkv = dot_nn(hidden_t, grads_ref[...]).astype(BF16)
    term_out = dot_nn(attended, cot).astype(BF16)
    return term_qkv, term_out


def column_mask(all_rows, group, row_of):
    block = all_rows * group
    shape = (block, 2 * block)
    query = lax.broadcasted_iota(jnp.int32, shape, 1) % block
    key = lax.broadcasted_iota(jnp.int32, shape, 0)
    same_column = query % group == key % group
    return (row_of(query // group) >= row_of(key // group)) & same_column


def column_kernel(
    moved_any, gain_any, wqkv_any, wout_any, row_qkv_ref, row_out_ref,
    terms_ref, grads_ref, w_ref,
    moved_ref, gain_ref, wo_ref, sems,
):
    copies = started(
        pltpu.make_async_copy(moved_any, moved_ref, sems.at[4]),
        pltpu.make_async_copy(gain_any, gain_ref, sems.at[5]),
    )
    weights = started(*weight_copies(wqkv_any, wout_any, w_ref, wo_ref, sems, 1))
    finished(*copies)
    all_rows, _, share, width = moved_ref.shape
    group = math.gcd(share, 16)
    x, cot = [
        jnp.concatenate(
            [
                moved_ref[:, which, at : at + group, :].astype(F32).reshape(all_rows * group, width)
                for at in range(0, share, group)
            ],
            0,
        ).astype(BF16)
        for which in range(2)
    ]
    mask = column_mask(all_rows, group, lambda place: place)
    term_qkv, term_out = column_part(
        x, cot, mask, gain_ref[...], w_ref, wo_ref, weights, grads_ref
    )
    for i in range(3):
        at = i * width
        terms_ref[:, at : at + HW] = row_qkv_ref[:, i * HW : (i + 1) * HW]
        terms_ref[:, at + HW : at + 2 * HW] = term_qkv[:, i * HW : (i + 1) * HW]
    terms_ref[:HW, 3 * width :] = row_out_ref[...]
    terms_ref[HW:, 3 * width :] = term_out


def column_chip_kernel(
    x_ref, cot_ref, swapped_ref, corner_ref, near_2, near_3, far_ref, gain_ref, w_ref, wo_ref, row_out_ref,
    send_ref, keep_ref, grads_ref,
):
    chip, core, _ = here()
    share = far_ref.shape[2]
    half = pl.ds(pl.multiple_of(core * share, share), share)
    at = pl.ds(pl.multiple_of((chip * 2 + core) * share, share), share)
    group = math.gcd(share, 16)

    def tokens(which, mine):
        pieces = [
            mine[at, :], swapped_ref[0, which], corner_ref[0, which], corner_ref[1, which],
        ]
        for i, near in enumerate((near_2, near_3)):
            pieces += [near[which, half, :], far_ref[i, which]]
        starts = range(0, share, group)
        return jnp.concatenate(
            [piece[start : start + group] for start in starts for piece in pieces], 0
        )

    def row_of(place):
        step = (4 - (place >> 1)) & 3
        return ((step ^ chip) << 1) + ((place & 1) ^ core)

    mask = column_mask(2 * (len(CHIP_STEPS) + 1), group, row_of)
    term_qkv, term_out = column_part(
        tokens(0, x_ref), tokens(1, cot_ref), mask, gain_ref[...], w_ref, wo_ref, (), grads_ref
    )
    chips = send_ref.shape[0]
    refs = send_ref, keep_ref
    out_lanes = slice(3 * HW, send_ref.shape[2])
    split_cores(term_qkv, *refs, slice(0, chips), slice(0, 3 * HW))
    split_cores(row_out_ref[...], *refs, slice(0, chips // 2), out_lanes)
    split_cores(term_out, *refs, slice(chips // 2, chips), out_lanes)


def far_kernel(near_2, near_3, far_ref):
    share = far_ref.shape[2]
    at = pl.ds(pl.multiple_of((1 - here()[1]) * share, share), share)
    for i, near in enumerate((near_2, near_3)):
        far_ref[i] = near[:, at, :]


def back_kernel(grads_ref, w_ref, back_ref):
    grad_hidden = dot_nt(grads_ref[...], w_ref[...])
    all_rows, share, width = back_ref.shape
    group = math.gcd(share, 16)
    block = all_rows * group
    for i in range(share // group):
        piece = grad_hidden[i * block : (i + 1) * block].reshape(all_rows, group, width)
        back_ref[:, i * group : (i + 1) * group, :] = piece.astype(BF16)


def back_chip_kernel(grads_ref, w_ref, send_ref, keep_ref):
    grad_hidden = dot_nt(grads_ref[...], w_ref[...]).astype(BF16)
    chips, share, width = keep_ref.shape
    group = math.gcd(share, 16)
    block = 2 * chips * group
    for i in range(share // group):
        piece = grad_hidden[i * block : (i + 1) * block].reshape(chips, 2, group, width)
        at = slice(i * group, (i + 1) * group)
        keep_ref[:, at, :], send_ref[:, at, :] = piece[:, 0], piece[:, 1]


def back_pack_kernel(keep_ref, got_ref, *targets):
    share = keep_ref.shape[1]
    core = here()[1]
    kept_at = pl.ds(pl.multiple_of(core * share, share), share)
    got_at = pl.ds(pl.multiple_of((1 - core) * share, share), share)
    for i, target in enumerate(targets):
        target[kept_at, :] = keep_ref[i]
        target[got_at, :] = got_ref[i]


def input_kernel(base_ref, normed_ref, inverse_ref, gain_ref, back_ref, grad_ref):
    grad_ref[...] = input_grad(
        base_ref[...], normed_ref[...], inverse_ref[...], back_ref[...].astype(F32) * gain_ref[...]
    ).astype(BF16)


def input_grad(base, normed, inverse_rms, grad_normed):
    projected = jnp.mean(grad_normed * normed, -1, keepdims=True)
    return base + inverse_rms * (grad_normed - normed * projected)


def input_chip_kernel(
    base_ref, normed_ref, inverse_ref, gain_ref, own_ref, got_1, got_2, got_3,
    grad_any, grad_ref, sems,
):
    chip = here()[0]
    count = own_ref.shape[0]
    copies = []
    for i, (step, back_ref) in enumerate(zip((0, *CHIP_STEPS), (own_ref, got_1, got_2, got_3))):
        at = pl.ds(pl.multiple_of((chip ^ step) * count, count), count)
        grad_normed = back_ref[...].astype(F32) * gain_ref[...]
        grad = input_grad(base_ref[at, :], normed_ref[at, :], inverse_ref[at, :], grad_normed)
        grad_ref[i] = grad.astype(BF16)
        copies += started(pltpu.make_async_copy(grad_ref.at[i], grad_any.at[at, :], sems.at[i]))
    finished(*copies)


def pack_kernel(x_any, cot_any, swap_ref, corner_ref, off_2, off_3, sems):
    chip, core, _ = here()
    share = corner_ref.shape[1]

    def columns(step, of_core):
        return pl.multiple_of(((chip ^ step) * 2 + of_core) * share, share)

    corner = CHIP_STEPS[0]
    copies = []
    for which, source in enumerate((x_any, cot_any)):
        pieces = [
            (columns(0, 1 - core), share, swap_ref.at[0, which]),
            (columns(corner, 1 - core), share, swap_ref.at[1, which]),
            (columns(corner, core), share, corner_ref.at[which]),
            (columns(CHIP_STEPS[1], 0), 2 * share, off_2.at[which]),
            (columns(CHIP_STEPS[2], 0), 2 * share, off_3.at[which]),
        ]
        for i, (at, count, target) in enumerate(pieces):
            copies.append(
                pltpu.make_async_copy(
                    source.at[pl.ds(at, count), :], target, sems.at[5 * which + i]
                )
            )
    finished(*started(*copies))


def corner_kernel(corner_ref, swapped_ref, out_ref):
    out_ref[0], out_ref[1] = corner_ref[...], swapped_ref[1]


def split_rows(total, axis):
    upper = (here()[2] & 1) == 1
    low, high = jnp.split(total, 2, axis)
    return jnp.where(upper, low, high).astype(BF16), jnp.where(upper, high, low)


def row_cores_kernel(keep_1, keep_2, got_1, got_2, send_ref, kept_ref):
    total = [
        keep_ref[...].astype(F32) + got_ref[...].astype(F32)
        for keep_ref, got_ref in ((keep_1, got_1), (keep_2, got_2))
    ]
    send_ref[...], kept_ref[...] = split_rows(jnp.concatenate(total, 2), 1)


def cores_kernel(keep_ref, got_ref, send_ref, kept_ref, *targets):
    chip, cut = here()[0], kept_ref.shape[2]
    first = keep_ref[:, :, :cut].astype(F32) + got_ref[:, :, :cut].astype(F32)
    send_ref[...], kept_ref[...] = split_rows(first, 1)
    for step, target in zip((0, *CHIP_STEPS), targets):
        there = chip ^ step
        total = keep_ref[there, :, cut:].astype(F32) + got_ref[there, :, cut:].astype(F32)
        target[...] = total.astype(target.dtype)


def pair_kernel(kept_ref, got_ref, row_kept, row_got, *targets):
    chip, cut = here()[0], kept_ref.shape[2]
    for step, target in zip((0, *CHIP_STEPS), targets):
        there = chip ^ step
        total = kept_ref[there] + got_ref[there].astype(F32)
        target[:, :cut] = total.astype(target.dtype)
        total = row_kept[there] + row_got[there].astype(F32)
        target[:, cut:] = total.astype(target.dtype)


def layer_sum(own_ref, got_1, got_2, got_3):
    return own_ref[...] + (
        (got_1[...].astype(F32) + got_2[...].astype(F32)) + got_3[...].astype(F32)
    )


def layer_kernel(own_ref, got_1, got_2, got_3, send_ref, kept_ref):
    send_ref[...], kept_ref[...] = split_rows(layer_sum(own_ref, got_1, got_2, got_3), 0)


def join_kernel(own_ref, got_1, got_2, got_3, kept_ref, got_ref, out_ref):
    total = layer_sum(own_ref, got_1, got_2, got_3).astype(BF16)
    cut, width = FIRST_PART, kept_ref.shape[1]
    out_ref[:, :cut] = total[:, :cut]
    out_ref[:, cut : cut + width] = (kept_ref[...] + got_ref[...].astype(F32)).astype(BF16)
    out_ref[:, cut + width :] = total[:, cut:]


def add_kernel(kept_ref, got_ref, out_ref):
    out_ref[...] = (kept_ref[...].astype(F32) + got_ref[...].astype(F32)).astype(BF16)


def result_kernel(held_ref, got_ref, w_ref, gain_ref, qkv_ref, out_ref, grad_ref):
    rows = qkv_ref.shape[0]
    chip, core, layer = here()
    at = (chip * 2 + core) * rows
    upper = (layer & 1) == 1
    half = rows // 2
    width = out_ref.shape[1]

    def ordered(lanes):
        held, got = held_ref[:, lanes].astype(F32), got_ref[:, lanes].astype(F32)
        return (jnp.where(upper, got, held), jnp.where(upper, held, got))

    row_at = 3 * HW + width
    for i in range(3):
        for at_from, at_to in ((row_at + i * HW, i * width), (i * HW, i * width + HW)):
            to = slice(at_to, at_to + HW)
            qkv_ref[:half, to], qkv_ref[half:, to] = ordered(slice(at_from, at_from + HW))
    out_ref[:half], out_ref[half:] = ordered(slice(3 * HW, row_at))
    total = jnp.sum(qkv_ref[...] * w_ref[...].astype(F32), -1, keepdims=True)
    shape = (rows, gain_ref.shape[1])
    row = lax.broadcasted_iota(jnp.int32, shape, 0)
    feature = lax.broadcasted_iota(jnp.int32, shape, 1)
    gain = jnp.sum(jnp.where(feature == row + at, gain_ref[...], 0.0), -1, keepdims=True)
    shape = (rows, grad_ref.shape[1])
    same = lax.broadcasted_iota(jnp.int32, shape, 0) == lax.broadcasted_iota(jnp.int32, shape, 1)
    grad_ref[...] = jnp.sum(jnp.where(same, total / gain, 0.0), 0, keepdims=True)


def call(kernel, name, ins, outs, scratch=(), vmem=SMALL_VMEM, out_specs=None):
    out_specs = out_specs or [VMEM] * len(outs)
    places = [{id(HBM): pltpu.HBM, id(PINNED): pltpu.VMEM}.get(id(spec)) for spec in out_specs]
    outs = [place(*out) if place else shaped(*out) for place, out in zip(places, outs)]
    args = [
        pltpu.with_memory_space_constraint(array, pltpu.HBM) if spec is HBM else array
        for spec, array in ins
    ]
    return pl.pallas_call(
        kernel,
        out_shape=outs,
        in_specs=[spec for spec, _ in ins],
        out_specs=out_specs,
        scratch_shapes=scratch,
        name=name,
        cost_estimate=pl.CostEstimate(flops=0, bytes_accessed=0, transcendentals=0),
        compiler_params=pltpu.CompilerParams(vmem_limit_bytes=vmem),
    )(*args)


def swap(array, axis, bits):
    count = lax.axis_size(axis)
    return lax.ppermute(array, axis, [(i, i ^ bits) for i in range(count)])


def cross_chips(*offs):
    return [swap(off, "seq", 2 * step) for off, step in zip(offs, CHIP_STEPS)]


def add_two(kept, got, name):
    (total,) = call(add_kernel, name, [(VMEM, kept), (VMEM, got)], [(kept.shape, BF16)])
    return total


def body(inputs, norm_gain, qkv_weight, out_weight, out_cotan):
    columns, width = inputs.shape[2:]
    n = lax.axis_size("seq")
    m = lax.axis_size("dp")
    share = columns // n
    row_share = width // n
    row_width, col_width = 3 * HW, 3 * HW + width
    x = inputs.reshape(columns, width)
    cot = out_cotan.reshape(columns, width)
    gain = norm_gain.reshape(1, width)
    chips = 4
    layered = n == 2 * chips and m == 4 and row_share == share
    weight_scratch = [
        pltpu.VMEM((1, width), F32),
        pltpu.VMEM((width, 3 * HW), BF16),
        pltpu.VMEM((HW, width), BF16),
    ]
    weights = [(HBM, gain), (HBM, qkv_weight), (HBM, out_weight)]
    col_outs = [((columns, 3 * HW), BF16), ((width, 3 * HW), BF16)]

    if layered:
        packed = call(
            pack_kernel,
            "pack_columns",
            [(HBM, x), (HBM, cot)],
            [((2, 2, share, width), BF16), ((2, share, width), BF16)]
            + [((2, 2 * share, width), BF16)] * 2,
            [pltpu.SemaphoreType.DMA((10,))],
            out_specs=[ANY] * 4,
        )
        near = [swap(one, "seq", 2 * step) for one, step in zip(packed[2:], CHIP_STEPS[1:])]
        swapped = swap(packed[0], "seq", 1)
        (corner,) = call(
            corner_kernel,
            "pack_corner",
            [(VMEM, packed[1]), (VMEM, swapped)],
            [((2, 2, share, width), BF16)],
        )
        x_first, _ = lax.optimization_barrier((x, corner))
        corner = swap(corner, "seq", 2 * CHIP_STEPS[0])
    else:
        outgoing = jnp.stack([x.reshape(n, share, width), cot.reshape(n, share, width)], 1)
        moved = lax.all_to_all(outgoing, "seq", split_axis=0, concat_axis=0, tiled=True)
        x_first = x

    row_outs = [
        ((HW, width), BF16),
        ((columns, width), F32), ((columns, width), F32), ((columns, 1), F32),
        ((columns, width), BF16), ((columns, width), BF16),
    ]
    if layered:
        cut = row_width // 2
        split_outs = [((chips, row_share, cut), BF16)] * 4
        handed_outs = [
            ((row_share, 3 * width), BF16), ((width, 3 * HW), BF16), ((HW, width), BF16),
        ]
        row_outs = [*split_outs, *handed_outs, *row_outs]
        specs = [VMEM] * 4 + [PINNED] * (len(row_outs) - 4)
    else:
        row_outs = [((width, row_width), BF16), *row_outs]
        specs = [VMEM] * len(row_outs)
    *row_terms, row_out, base, normed, inverse_rms, x_near, cot_near = call(
        row_chip_kernel if layered else row_kernel,
        "row_heads",
        [(HBM, x_first), (HBM, cot), *weights],
        row_outs,
        [
            *weight_scratch,
            pltpu.VMEM((columns, HW), F32),
            pltpu.VMEM((columns, HW), F32),
            pltpu.VMEM((columns, 3 * HW), BF16),
            pltpu.SemaphoreType.DMA((12,)),
        ],
        BIG_VMEM,
        specs,
    )
    if layered:
        *row_terms, weight_rows, col_weight, col_out_weight = row_terms
        row_sent = [swap(one, "seq", 1) for one in row_terms[:2]]
        half_block = (chips, row_share // 2, row_width)
        row_next, row_kept = call(
            row_cores_kernel,
            "row_add_cores",
            [(VMEM, one) for one in (*row_terms[2:], *row_sent)],
            [(half_block, BF16), (half_block, F32)],
            out_specs=[VMEM, PINNED],
        )
        col_weight, row_kept = lax.optimization_barrier((col_weight, row_kept))
        *near, base = lax.optimization_barrier((*near, base))
        (far,) = call(
            far_kernel,
            "pack_other_core",
            [(VMEM, one) for one in near],
            [((2, 2, share, width), BF16)],
        )
        send, keep, col_grads = call(
            column_chip_kernel,
            "column_heads",
            [
                (VMEM, one)
                for one in (
                    x_near, cot_near, swapped, corner, *near, swap(far, "seq", 1),
                    gain, col_weight, col_out_weight, row_out,
                )
            ],
            [((chips, row_share, col_width), BF16)] * 2 + [col_outs[0]],
            vmem=BIG_VMEM,
            out_specs=[VMEM, VMEM, PINNED],
        )
        back_send, back_keep = call(
            back_chip_kernel,
            "column_grad_hidden",
            [(VMEM, col_grads), (VMEM, col_weight)],
            [((chips, share, width), BF16)] * 2,
        )
        row_next, _ = lax.optimization_barrier((row_next, send))
        keep, back_keep = lax.optimization_barrier((keep, back_keep))
        first_half = (chips, row_share // 2, FIRST_PART)
        second = (row_share, col_width - FIRST_PART)
        to_next, kept, owned, *off = call(
            cores_kernel,
            "column_add_cores",
            [(VMEM, keep), (VMEM, swap(send, "seq", 1))],
            [(first_half, BF16), (first_half, F32), (second, F32)] + [(second, BF16)] * 3,
            out_specs=[VMEM, PINNED, PINNED, VMEM, VMEM, VMEM],
        )
        got = cross_chips(*off)
        back = call(
            back_pack_kernel,
            "pack_grad_hidden",
            [(VMEM, back_keep), (VMEM, swap(back_send, "seq", 1))],
            [((2 * share, width), BF16)] * 4,
        )
        row_kept, *back = lax.optimization_barrier((row_kept, *back))
        joint = (row_share // 2, FIRST_PART + row_width)
        first_owned, *off = call(
            pair_kernel,
            "first_add_pair",
            [
                (VMEM, one)
                for one in (kept, swap(to_next, "dp", 1), row_kept, swap(row_next, "dp", 1))
            ],
            [(joint, F32)] + [(joint, BF16)] * 3,
            out_specs=[PINNED, VMEM, VMEM, VMEM],
        )
        first_got = cross_chips(*off)
        second_half = (row_share // 2, second[1])
        to_next, kept = call(
            layer_kernel,
            "second_add_chips",
            [(VMEM, one) for one in (owned, *got)],
            [(second_half, BF16), (second_half, F32)],
            out_specs=[VMEM, PINNED],
        )
        (pair_sum,) = call(
            join_kernel,
            "join_terms",
            [(VMEM, one) for one in (first_owned, *first_got, kept, swap(to_next, "dp", 1))],
            [((row_share // 2, col_width + row_width), BF16)],
        )
        *back, pair_sum = lax.optimization_barrier((*back, pair_sum))
        held = add_two(pair_sum, swap(pair_sum, "dp", 2), "add_pairs")
        other = swap(held, "dp", 1)
        (grad,) = call(
            input_chip_kernel,
            "input_grad",
            [
                (VMEM, one)
                for one in (base, normed, inverse_rms, gain, back[0], *cross_chips(*back[1:]))
            ],
            [((columns, width), BF16)],
            [pltpu.VMEM((chips, 2 * share, width), BF16), pltpu.SemaphoreType.DMA((chips,))],
            out_specs=[HBM],
        )
        sum_qkv, sum_out, sum_gain = call(
            result_kernel,
            "result",
            [(VMEM, held), (VMEM, other), (VMEM, weight_rows), (VMEM, gain)],
            [((row_share, 3 * width), F32), ((row_share, width), F32), ((1, row_share), F32)],
        )
        sum_gain = sum_gain.reshape(row_share)
    else:
        terms, *col_grads = call(
            column_kernel,
            "column_heads",
            [(ANY, moved), *weights, (VMEM, row_terms[0]), (VMEM, row_out)],
            [((width, 4 * width), BF16), *col_outs],
            [
                pltpu.VMEM((n, 2, share, width), BF16),
                weight_scratch[0],
                weight_scratch[2],
                pltpu.SemaphoreType.DMA((6,)),
            ],
            BIG_VMEM,
        )
        (back,) = call(
            back_kernel,
            "column_grad_hidden",
            [(VMEM, one) for one in col_grads],
            [((n, share, width), BF16)],
        )
        returned = lax.all_to_all(back, "seq", split_axis=0, concat_axis=0, tiled=True)
        (grad,) = call(
            input_kernel,
            "input_grad",
            [
                (VMEM, base), (VMEM, normed), (VMEM, inverse_rms), (VMEM, gain),
                (VMEM, returned.reshape(columns, width)),
            ],
            [((columns, width), BF16)],
        )
        terms = lax.all_to_all(
            terms.reshape(n, row_share, 4 * width), "seq", split_axis=0, concat_axis=0, tiled=True
        )
        total = jnp.sum(terms.astype(F32), 0)
        for step in range(m.bit_length() - 1):
            sent = total.astype(BF16)
            total = sent.astype(F32) + swap(sent, "dp", 1 << step).astype(F32)
        sum_qkv, sum_out = total[:, : 3 * width], total[:, 3 * width :]
        here_at = lax.axis_index("seq") * row_share
        own_gain = lax.dynamic_slice_in_dim(norm_gain, here_at, row_share, 0)
        own_weight = lax.dynamic_slice_in_dim(qkv_weight, here_at, row_share, 0)
        sum_gain = jnp.sum(sum_qkv * own_weight.astype(F32), -1) / own_gain
    return (grad.reshape(inputs.shape), sum_qkv, sum_out, sum_gain)


def solution(mesh):
    return jax.shard_map(
        body,
        mesh=mesh,
        in_specs=(P("dp", "seq", None, None), P(), P(), P(), P("dp", "seq", None, None)),
        out_specs=(P("dp", "seq", None, None), P("seq", None), P("seq", None), P("seq")),
        check_vma=False,
    )
```

```python
import math

import jax
import jax.numpy as jnp
from jax import lax
from jax.experimental import pallas as pl
from jax.experimental.pallas import tpu as pltpu
from jax.sharding import PartitionSpec as P

H = 8
HD = 64
HH = H // 2
HW = HH * HD
SCALE = HD ** (-0.5)
F32 = jnp.float32
BF16 = jnp.bfloat16
QUERY_BLOCK = 128
BIG_VMEM = 20 * 1024 * 1024
SMALL_VMEM = 8 * 1024 * 1024
ANY = pl.BlockSpec(memory_space=pl.ANY)
VMEM = pl.BlockSpec(memory_space=pltpu.VMEM)
HBM = pl.BlockSpec(memory_space=pltpu.HBM)
CHIP_STEPS = (3, 2, 1)
FIRST_PART = 384
PINNED = pl.BlockSpec(memory_space=pltpu.VMEM)
shaped = jax.ShapeDtypeStruct


def here():
    device = lax.axis_index("seq")
    return device >> 1, device & 1, lax.axis_index("dp")


def dot_nn(a, b):
    return lax.dot_general(a, b, (((1,), (0,)), ((), ())), preferred_element_type=F32)


def dot_nt(a, b):
    return lax.dot_general(a, b, (((1,), (1,)), ((), ())), preferred_element_type=F32)


def rms_parts(x):
    inverse_rms = lax.rsqrt(jnp.mean(x * x, -1, keepdims=True) + 1e-05)
    return inverse_rms, x * inverse_rms


def transposed(x):
    block = math.gcd(x.shape[1], 256)
    eye = (
        lax.broadcasted_iota(jnp.int32, (block, block), 0)
        == lax.broadcasted_iota(jnp.int32, (block, block), 1)
    ).astype(F32).astype(BF16)
    parts = [
        dot_nt(eye, x[:, at : at + block]).astype(BF16) for at in range(0, x.shape[1], block)
    ]
    return parts[0] if len(parts) == 1 else jnp.concatenate(parts, 0)


def head_pair(x):
    lane = lax.broadcasted_iota(jnp.int32, x.shape, 1)
    zero = jnp.zeros_like(x)
    return jnp.concatenate([jnp.where(lane < HD, x, zero), jnp.where(lane < HD, zero, x)], 0)


def both_heads(both, count):
    return jnp.concatenate([both[:HD, :count], both[HD:, count:]], 0)


def pair_steps(items, mask_rows, mask):
    count = items[0][2].shape[1]
    scores = [dot_nt(k, q2) for q2, _, _, k, _, _, _ in items]
    prob_grads = [dot_nt(v, g2) for _, g2, _, _, v, _, _ in items]
    probs = []
    for score in scores:
        first = score.shape[0] - mask_rows
        tail = jnp.where(mask, score[first:], -1e30)
        score = tail if first == 0 else jnp.concatenate([score[:first], tail], 0)
        exponent = jnp.exp(score - jnp.max(score, 0, keepdims=True))
        probs.append(exponent * (1.0 / jnp.sum(exponent, 0, keepdims=True)))
    weights = [prob.astype(BF16) for prob in probs]
    attended = [
        both_heads(dot_nn(item[6], weight), count).astype(BF16)
        for item, weight in zip(items, weights)
    ]
    score_grads = []
    for item, att, prob, prob_grad in zip(items, attended, probs, prob_grads):
        product = item[2].astype(F32) * att.astype(F32)
        delta = [jnp.sum(part, 0, keepdims=True) for part in (product[:HD], product[HD:])]
        score_grads.append((prob * (prob_grad - jnp.concatenate(delta, 1))).astype(BF16))
    grad_q = [
        (both_heads(dot_nn(item[5], score_grad), count) * SCALE).astype(BF16)
        for item, score_grad in zip(items, score_grads)
    ]
    grad_k = [dot_nn(score_grad, item[0]) for item, score_grad in zip(items, score_grads)]
    grad_v = [dot_nn(weight, item[1]) for item, weight in zip(items, weights)]
    return list(zip(attended, grad_q, grad_k, grad_v))


def split_cores(piece, send_ref, keep_ref, chips, lanes):
    rows = send_ref.shape[1]
    parts = piece.reshape(chips.stop - chips.start, 2, rows, piece.shape[1])
    even, odd = parts[:, 0], parts[:, 1]
    first = here()[1] == 0
    send_ref[chips, :, lanes] = jnp.where(first, odd, even)
    keep_ref[chips, :, lanes] = jnp.where(first, even, odd)


def qkv_copies(wqkv_ref, w_ref, sems, second):
    width = wqkv_ref.shape[0]
    return [
        pltpu.make_async_copy(
            wqkv_ref.at[:, pl.ds(i * width + second * HW, HW)],
            w_ref.at[:, pl.ds(i * HW, HW)],
            sems.at[i],
        )
        for i in range(3)
    ]


def weight_copies(wqkv_ref, wout_ref, w_ref, wo_ref, sems, second):
    out_rows = wout_ref.at[pl.ds(second * HW, HW), :]
    return [
        *qkv_copies(wqkv_ref, w_ref, sems, second),
        pltpu.make_async_copy(out_rows, wo_ref, sems.at[3]),
    ]


def started(*copies):
    for copy in copies:
        copy.start()
    return copies


def finished(*copies):
    for copy in copies:
        copy.wait()


def project(hidden, cot, w_ref, wo_ref):
    projected = dot_nn(hidden, w_ref[...]).astype(BF16)
    q, k, v = [projected[:, i * HW : (i + 1) * HW] for i in range(3)]
    g = dot_nt(cot, wo_ref[...]).astype(BF16)
    return q * jnp.asarray(SCALE, BF16), k, v, g


def row_part(
    x_any, cot_any, gain_any, wqkv_any, wout_any,
    out_ref, base_ref, normed_ref, inverse_ref, x_ref, cot_ref,
    gain_ref, w_ref, wo_ref, dk_ref, dv_ref, grads_ref, sems,
):
    first = started(
        pltpu.make_async_copy(x_any, x_ref, sems.at[4]),
        pltpu.make_async_copy(gain_any, gain_ref, sems.at[5]),
    )
    later = started(
        *weight_copies(wqkv_any, wout_any, w_ref, wo_ref, sems, 0),
        pltpu.make_async_copy(cot_any, cot_ref, sems.at[6]),
    )
    dk_ref[...] = jnp.zeros_like(dk_ref)
    dv_ref[...] = jnp.zeros_like(dv_ref)
    finished(*first)
    tokens = x_ref.shape[0]
    inverse_ref[...], normed_ref[...] = rms_parts(x_ref[...].astype(F32))
    hidden = (normed_ref[...] * gain_ref[...]).astype(BF16)
    hidden_t = transposed(hidden)
    finished(*later)
    cot = cot_ref[...]
    q, k, v, g = project(hidden, cot, w_ref, wo_ref)
    kt, vt, gt = transposed(k), transposed(v), transposed(g)
    step = math.gcd(tokens, QUERY_BLOCK)
    query = lax.broadcasted_iota(jnp.int32, (step, 2 * step), 1) % step
    mask = query >= lax.broadcasted_iota(jnp.int32, (step, 2 * step), 0)
    pairs = [slice(i * 2 * HD, (i + 1) * 2 * HD) for i in range(HH // 2)]
    att_blocks, dq_blocks = [], []
    for start in range(0, tokens, step):
        rows, keys = slice(start, start + step), slice(0, start + step)
        items = [
            (
                head_pair(q[rows, lanes]), head_pair(g[rows, lanes]), gt[lanes, rows],
                k[keys, lanes], v[keys, lanes], kt[lanes, keys], vt[lanes, keys],
            )
            for lanes in pairs
        ]
        results = pair_steps(items, step, mask)
        for lanes, (_, _, dk, dv) in zip(pairs, results):
            dk_ref[keys, lanes] += dk
            dv_ref[keys, lanes] += dv
        att_blocks.append(jnp.concatenate([result[0] for result in results], 0))
        dq_blocks.append(jnp.concatenate([result[1] for result in results], 0))
    grads_ref[:, :HW] = transposed(jnp.concatenate(dq_blocks, 1))
    grads_ref[:, HW : 2 * HW] = dk_ref[...].astype(BF16)
    grads_ref[:, 2 * HW :] = dv_ref[...].astype(BF16)
    term_qkv = dot_nn(hidden_t, grads_ref[...]).astype(BF16)
    out_ref[...] = dot_nn(jnp.concatenate(att_blocks, 1), cot).astype(BF16)
    grad_normed = dot_nt(grads_ref[...], w_ref[...]) * gain_ref[...]
    base_ref[...] = input_grad(
        cot_ref[...].astype(F32), normed_ref[...], inverse_ref[...], grad_normed
    )
    return term_qkv


def row_kernel(x_any, cot_any, gain_any, wqkv_any, wout_any, qkv_ref, *refs):
    qkv_ref[...] = row_part(x_any, cot_any, gain_any, wqkv_any, wout_any, *refs)


def row_chip_kernel(
    x_any, cot_any, gain_any, wqkv_any, wout_any,
    send_1, send_2, keep_1, keep_2, rows_ref, col_w_ref, col_wo_ref, *refs,
):
    chip, core, _ = here()
    sems, rows = refs[-1], rows_ref.shape[0]
    at = pl.multiple_of((chip * 2 + core) * rows, rows)
    handed = started(
        pltpu.make_async_copy(wqkv_any.at[pl.ds(at, rows), :], rows_ref, sems.at[7]),
        *weight_copies(wqkv_any, wout_any, col_w_ref, col_wo_ref, sems.at[pl.ds(8, 4)], 1),
    )
    term_qkv = row_part(x_any, cot_any, gain_any, wqkv_any, wout_any, *refs)
    chips, cut = send_1.shape[0], keep_1.shape[2]
    pieces = slice(0, chips), slice(0, cut)
    split_cores(term_qkv[:, :cut], send_1, keep_1, *pieces)
    split_cores(term_qkv[:, cut:], send_2, keep_2, *pieces)
    finished(*handed)


def column_part(x, cot, mask, gain, w_ref, wo_ref, weight_waits, grads_ref):
    tokens, block = x.shape[0], mask.shape[0]
    _, normed = rms_parts(x.astype(F32))
    hidden = (normed * gain).astype(BF16)
    hidden_t = transposed(hidden)
    finished(*weight_waits)
    q, k, v, g = project(hidden, cot, w_ref, wo_ref)
    kt, vt, gt = transposed(k), transposed(v), transposed(g)
    pairs = [slice(i * 2 * HD, (i + 1) * 2 * HD) for i in range(HH // 2)]
    blocks = [slice(at, at + block) for at in range(0, tokens, block)]
    items = [
        (
            head_pair(q[rows, lanes]), head_pair(g[rows, lanes]), gt[lanes, rows],
            k[rows, lanes], v[rows, lanes], kt[lanes, rows], vt[lanes, rows],
        )
        for lanes in pairs
        for rows in blocks
    ]
    results = pair_steps(items, block, mask)
    places = [(lanes, rows) for lanes in pairs for rows in blocks]
    for (lanes, rows), (_, _, dk, dv) in zip(places, results):
        grads_ref[rows, HW + lanes.start : HW + lanes.stop] = dk.astype(BF16)
        grads_ref[rows, 2 * HW + lanes.start : 2 * HW + lanes.stop] = dv.astype(BF16)
    by_pair = [results[i * len(blocks) : (i + 1) * len(blocks)] for i in range(len(pairs))]
    attended, grad_q = [
        jnp.concatenate([jnp.concatenate([r[i] for r in some], 1) for some in by_pair], 0)
        for i in range(2)
    ]
    grads_ref[:, :HW] = transposed(grad_q)
    term_qkv = dot_nn(hidden_t, grads_ref[...]).astype(BF16)
    term_out = dot_nn(attended, cot).astype(BF16)
    return term_qkv, term_out


def column_mask(all_rows, group, row_of):
    block = all_rows * group
    shape = (block, 2 * block)
    query = lax.broadcasted_iota(jnp.int32, shape, 1) % block
    key = lax.broadcasted_iota(jnp.int32, shape, 0)
    same_column = query % group == key % group
    return (row_of(query // group) >= row_of(key // group)) & same_column


def column_kernel(
    moved_any, gain_any, wqkv_any, wout_any, row_qkv_ref, row_out_ref,
    terms_ref, grads_ref, w_ref,
    moved_ref, gain_ref, wo_ref, sems,
):
    copies = started(
        pltpu.make_async_copy(moved_any, moved_ref, sems.at[4]),
        pltpu.make_async_copy(gain_any, gain_ref, sems.at[5]),
    )
    weights = started(*weight_copies(wqkv_any, wout_any, w_ref, wo_ref, sems, 1))
    finished(*copies)
    all_rows, _, share, width = moved_ref.shape
    group = math.gcd(share, 16)
    x, cot = [
        jnp.concatenate(
            [
                moved_ref[:, which, at : at + group, :].astype(F32).reshape(all_rows * group, width)
                for at in range(0, share, group)
            ],
            0,
        ).astype(BF16)
        for which in range(2)
    ]
    mask = column_mask(all_rows, group, lambda place: place)
    term_qkv, term_out = column_part(
        x, cot, mask, gain_ref[...], w_ref, wo_ref, weights, grads_ref
    )
    for i in range(3):
        at = i * width
        terms_ref[:, at : at + HW] = row_qkv_ref[:, i * HW : (i + 1) * HW]
        terms_ref[:, at + HW : at + 2 * HW] = term_qkv[:, i * HW : (i + 1) * HW]
    terms_ref[:HW, 3 * width :] = row_out_ref[...]
    terms_ref[HW:, 3 * width :] = term_out


def column_chip_kernel(
    x_ref, cot_ref, swapped_ref, corner_ref, near_2, near_3, far_ref, gain_ref, w_ref, wo_ref, row_out_ref,
    send_ref, keep_ref, grads_ref,
):
    chip, core, _ = here()
    share = far_ref.shape[2]
    half = pl.ds(pl.multiple_of(core * share, share), share)
    at = pl.ds(pl.multiple_of((chip * 2 + core) * share, share), share)
    group = math.gcd(share, 16)

    def tokens(which, mine):
        pieces = [
            mine[at, :], swapped_ref[0, which], corner_ref[0, which], corner_ref[1, which],
        ]
        for i, near in enumerate((near_2, near_3)):
            pieces += [near[which, half, :], far_ref[i, which]]
        starts = range(0, share, group)
        return jnp.concatenate(
            [piece[start : start + group] for start in starts for piece in pieces], 0
        )

    def row_of(place):
        step = (4 - (place >> 1)) & 3
        return ((step ^ chip) << 1) + ((place & 1) ^ core)

    mask = column_mask(2 * (len(CHIP_STEPS) + 1), group, row_of)
    term_qkv, term_out = column_part(
        tokens(0, x_ref), tokens(1, cot_ref), mask, gain_ref[...], w_ref, wo_ref, (), grads_ref
    )
    chips = send_ref.shape[0]
    refs = send_ref, keep_ref
    out_lanes = slice(3 * HW, send_ref.shape[2])
    split_cores(term_qkv, *refs, slice(0, chips), slice(0, 3 * HW))
    split_cores(row_out_ref[...], *refs, slice(0, chips // 2), out_lanes)
    split_cores(term_out, *refs, slice(chips // 2, chips), out_lanes)


def far_kernel(near_2, near_3, far_ref):
    share = far_ref.shape[2]
    at = pl.ds(pl.multiple_of((1 - here()[1]) * share, share), share)
    for i, near in enumerate((near_2, near_3)):
        far_ref[i] = near[:, at, :]


def back_kernel(grads_ref, w_ref, back_ref):
    grad_hidden = dot_nt(grads_ref[...], w_ref[...])
    all_rows, share, width = back_ref.shape
    group = math.gcd(share, 16)
    block = all_rows * group
    for i in range(share // group):
        piece = grad_hidden[i * block : (i + 1) * block].reshape(all_rows, group, width)
        back_ref[:, i * group : (i + 1) * group, :] = piece.astype(BF16)


def back_chip_kernel(grads_ref, w_ref, send_ref, keep_ref):
    grad_hidden = dot_nt(grads_ref[...], w_ref[...]).astype(BF16)
    chips, share, width = keep_ref.shape
    group = math.gcd(share, 16)
    block = 2 * chips * group
    for i in range(share // group):
        piece = grad_hidden[i * block : (i + 1) * block].reshape(chips, 2, group, width)
        at = slice(i * group, (i + 1) * group)
        keep_ref[:, at, :], send_ref[:, at, :] = piece[:, 0], piece[:, 1]


def back_pack_kernel(keep_ref, got_ref, *targets):
    share = keep_ref.shape[1]
    core = here()[1]
    kept_at = pl.ds(pl.multiple_of(core * share, share), share)
    got_at = pl.ds(pl.multiple_of((1 - core) * share, share), share)
    for i, target in enumerate(targets):
        target[kept_at, :] = keep_ref[i]
        target[got_at, :] = got_ref[i]


def input_kernel(base_ref, normed_ref, inverse_ref, gain_ref, back_ref, grad_ref):
    grad_ref[...] = input_grad(
        base_ref[...], normed_ref[...], inverse_ref[...], back_ref[...].astype(F32) * gain_ref[...]
    ).astype(BF16)


def input_grad(base, normed, inverse_rms, grad_normed):
    projected = jnp.mean(grad_normed * normed, -1, keepdims=True)
    return base + inverse_rms * (grad_normed - normed * projected)


def input_chip_kernel(
    base_ref, normed_ref, inverse_ref, gain_ref, own_ref, got_1, got_2, got_3,
    grad_any, grad_ref, sems,
):
    chip = here()[0]
    count = own_ref.shape[0]
    copies = []
    for i, (step, back_ref) in enumerate(zip((0, *CHIP_STEPS), (own_ref, got_1, got_2, got_3))):
        at = pl.ds(pl.multiple_of((chip ^ step) * count, count), count)
        grad_normed = back_ref[...].astype(F32) * gain_ref[...]
        grad = input_grad(base_ref[at, :], normed_ref[at, :], inverse_ref[at, :], grad_normed)
        grad_ref[i] = grad.astype(BF16)
        copies += started(pltpu.make_async_copy(grad_ref.at[i], grad_any.at[at, :], sems.at[i]))
    finished(*copies)


def pack_kernel(x_any, cot_any, swap_ref, corner_ref, off_2, off_3, sems):
    chip, core, _ = here()
    share = corner_ref.shape[1]

    def columns(step, of_core):
        return pl.multiple_of(((chip ^ step) * 2 + of_core) * share, share)

    corner = CHIP_STEPS[0]
    copies = []
    for which, source in enumerate((x_any, cot_any)):
        pieces = [
            (columns(0, 1 - core), share, swap_ref.at[0, which]),
            (columns(corner, 1 - core), share, swap_ref.at[1, which]),
            (columns(corner, core), share, corner_ref.at[which]),
            (columns(CHIP_STEPS[1], 0), 2 * share, off_2.at[which]),
            (columns(CHIP_STEPS[2], 0), 2 * share, off_3.at[which]),
        ]
        for i, (at, count, target) in enumerate(pieces):
            copies.append(
                pltpu.make_async_copy(
                    source.at[pl.ds(at, count), :], target, sems.at[5 * which + i]
                )
            )
    finished(*started(*copies))


def corner_kernel(corner_ref, swapped_ref, out_ref):
    out_ref[0], out_ref[1] = corner_ref[...], swapped_ref[1]


def split_rows(total, axis):
    upper = (here()[2] & 1) == 1
    low, high = jnp.split(total, 2, axis)
    return jnp.where(upper, low, high).astype(BF16), jnp.where(upper, high, low)


def row_cores_kernel(keep_1, keep_2, got_1, got_2, send_ref, kept_ref):
    total = [
        keep_ref[...].astype(F32) + got_ref[...].astype(F32)
        for keep_ref, got_ref in ((keep_1, got_1), (keep_2, got_2))
    ]
    send_ref[...], kept_ref[...] = split_rows(jnp.concatenate(total, 2), 1)


def cores_kernel(keep_ref, got_ref, send_ref, kept_ref, *targets):
    chip, cut = here()[0], kept_ref.shape[2]
    first = keep_ref[:, :, :cut].astype(F32) + got_ref[:, :, :cut].astype(F32)
    send_ref[...], kept_ref[...] = split_rows(first, 1)
    for step, target in zip((0, *CHIP_STEPS), targets):
        there = chip ^ step
        total = keep_ref[there, :, cut:].astype(F32) + got_ref[there, :, cut:].astype(F32)
        target[...] = total.astype(target.dtype)


def pair_kernel(kept_ref, got_ref, row_kept, row_got, *targets):
    chip, cut = here()[0], kept_ref.shape[2]
    for step, target in zip((0, *CHIP_STEPS), targets):
        there = chip ^ step
        total = kept_ref[there] + got_ref[there].astype(F32)
        target[:, :cut] = total.astype(target.dtype)
        total = row_kept[there] + row_got[there].astype(F32)
        target[:, cut:] = total.astype(target.dtype)


def layer_sum(own_ref, got_1, got_2, got_3):
    return own_ref[...] + (
        (got_1[...].astype(F32) + got_2[...].astype(F32)) + got_3[...].astype(F32)
    )


def layer_kernel(own_ref, got_1, got_2, got_3, send_ref, kept_ref):
    send_ref[...], kept_ref[...] = split_rows(layer_sum(own_ref, got_1, got_2, got_3), 0)


def join_kernel(own_ref, got_1, got_2, got_3, kept_ref, got_ref, out_ref):
    total = layer_sum(own_ref, got_1, got_2, got_3).astype(BF16)
    cut, width = FIRST_PART, kept_ref.shape[1]
    out_ref[:, :cut] = total[:, :cut]
    out_ref[:, cut : cut + width] = (kept_ref[...] + got_ref[...].astype(F32)).astype(BF16)
    out_ref[:, cut + width :] = total[:, cut:]


def add_kernel(kept_ref, got_ref, out_ref):
    out_ref[...] = (kept_ref[...].astype(F32) + got_ref[...].astype(F32)).astype(BF16)


def result_kernel(held_ref, got_ref, w_ref, gain_ref, qkv_ref, out_ref, grad_ref):
    rows = qkv_ref.shape[0]
    chip, core, layer = here()
    at = (chip * 2 + core) * rows
    upper = (layer & 1) == 1
    half = rows // 2
    width = out_ref.shape[1]

    def ordered(lanes):
        held, got = held_ref[:, lanes].astype(F32), got_ref[:, lanes].astype(F32)
        return (jnp.where(upper, got, held), jnp.where(upper, held, got))

    row_at = 3 * HW + width
    for i in range(3):
        for at_from, at_to in ((row_at + i * HW, i * width), (i * HW, i * width + HW)):
            to = slice(at_to, at_to + HW)
            qkv_ref[:half, to], qkv_ref[half:, to] = ordered(slice(at_from, at_from + HW))
    out_ref[:half], out_ref[half:] = ordered(slice(3 * HW, row_at))
    total = jnp.sum(qkv_ref[...] * w_ref[...].astype(F32), -1, keepdims=True)
    shape = (rows, gain_ref.shape[1])
    row = lax.broadcasted_iota(jnp.int32, shape, 0)
    feature = lax.broadcasted_iota(jnp.int32, shape, 1)
    gain = jnp.sum(jnp.where(feature == row + at, gain_ref[...], 0.0), -1, keepdims=True)
    shape = (rows, grad_ref.shape[1])
    same = lax.broadcasted_iota(jnp.int32, shape, 0) == lax.broadcasted_iota(jnp.int32, shape, 1)
    grad_ref[...] = jnp.sum(jnp.where(same, total / gain, 0.0), 0, keepdims=True)


def call(kernel, name, ins, outs, scratch=(), vmem=SMALL_VMEM, out_specs=None):
    out_specs = out_specs or [VMEM] * len(outs)
    places = [{id(HBM): pltpu.HBM, id(PINNED): pltpu.VMEM}.get(id(spec)) for spec in out_specs]
    outs = [place(*out) if place else shaped(*out) for place, out in zip(places, outs)]
    args = [
        pltpu.with_memory_space_constraint(array, pltpu.HBM) if spec is HBM else array
        for spec, array in ins
    ]
    return pl.pallas_call(
        kernel,
        out_shape=outs,
        in_specs=[spec for spec, _ in ins],
        out_specs=out_specs,
        scratch_shapes=scratch,
        name=name,
        cost_estimate=pl.CostEstimate(flops=0, bytes_accessed=0, transcendentals=0),
        compiler_params=pltpu.CompilerParams(vmem_limit_bytes=vmem),
    )(*args)


def swap(array, axis, bits):
    count = lax.axis_size(axis)
    return lax.ppermute(array, axis, [(i, i ^ bits) for i in range(count)])


def cross_chips(*offs):
    return [swap(off, "seq", 2 * step) for off, step in zip(offs, CHIP_STEPS)]


def add_two(kept, got, name):
    (total,) = call(add_kernel, name, [(VMEM, kept), (VMEM, got)], [(kept.shape, BF16)])
    return total


def body(inputs, norm_gain, qkv_weight, out_weight, out_cotan):
    columns, width = inputs.shape[2:]
    n = lax.axis_size("seq")
    m = lax.axis_size("dp")
    share = columns // n
    row_share = width // n
    row_width, col_width = 3 * HW, 3 * HW + width
    x = inputs.reshape(columns, width)
    cot = out_cotan.reshape(columns, width)
    gain = norm_gain.reshape(1, width)
    chips = 4
    layered = n == 2 * chips and m == 4 and row_share == share
    weight_scratch = [
        pltpu.VMEM((1, width), F32),
        pltpu.VMEM((width, 3 * HW), BF16),
        pltpu.VMEM((HW, width), BF16),
    ]
    weights = [(HBM, gain), (HBM, qkv_weight), (HBM, out_weight)]
    col_outs = [((columns, 3 * HW), BF16), ((width, 3 * HW), BF16)]

    if layered:
        packed = call(
            pack_kernel,
            "pack_columns",
            [(HBM, x), (HBM, cot)],
            [((2, 2, share, width), BF16), ((2, share, width), BF16)]
            + [((2, 2 * share, width), BF16)] * 2,
            [pltpu.SemaphoreType.DMA((10,))],
            out_specs=[ANY] * 4,
        )
        near = [swap(one, "seq", 2 * step) for one, step in zip(packed[2:], CHIP_STEPS[1:])]
        swapped = swap(packed[0], "seq", 1)
        (corner,) = call(
            corner_kernel,
            "pack_corner",
            [(VMEM, packed[1]), (VMEM, swapped)],
            [((2, 2, share, width), BF16)],
        )
        x_first, _ = lax.optimization_barrier((x, corner))
        corner = swap(corner, "seq", 2 * CHIP_STEPS[0])
    else:
        outgoing = jnp.stack([x.reshape(n, share, width), cot.reshape(n, share, width)], 1)
        moved = lax.all_to_all(outgoing, "seq", split_axis=0, concat_axis=0, tiled=True)
        x_first = x

    row_outs = [
        ((HW, width), BF16),
        ((columns, width), F32), ((columns, width), F32), ((columns, 1), F32),
        ((columns, width), BF16), ((columns, width), BF16),
    ]
    if layered:
        cut = row_width // 2
        split_outs = [((chips, row_share, cut), BF16)] * 4
        handed_outs = [
            ((row_share, 3 * width), BF16), ((width, 3 * HW), BF16), ((HW, width), BF16),
        ]
        row_outs = [*split_outs, *handed_outs, *row_outs]
        specs = [VMEM] * 4 + [PINNED] * (len(row_outs) - 4)
    else:
        row_outs = [((width, row_width), BF16), *row_outs]
        specs = [VMEM] * len(row_outs)
    *row_terms, row_out, base, normed, inverse_rms, x_near, cot_near = call(
        row_chip_kernel if layered else row_kernel,
        "row_heads",
        [(HBM, x_first), (HBM, cot), *weights],
        row_outs,
        [
            *weight_scratch,
            pltpu.VMEM((columns, HW), F32),
            pltpu.VMEM((columns, HW), F32),
            pltpu.VMEM((columns, 3 * HW), BF16),
            pltpu.SemaphoreType.DMA((12,)),
        ],
        BIG_VMEM,
        specs,
    )
    if layered:
        *row_terms, weight_rows, col_weight, col_out_weight = row_terms
        row_sent = [swap(one, "seq", 1) for one in row_terms[:2]]
        half_block = (chips, row_share // 2, row_width)
        row_next, row_kept = call(
            row_cores_kernel,
            "row_add_cores",
            [(VMEM, one) for one in (*row_terms[2:], *row_sent)],
            [(half_block, BF16), (half_block, F32)],
            out_specs=[VMEM, PINNED],
        )
        col_weight, row_kept = lax.optimization_barrier((col_weight, row_kept))
        *near, base = lax.optimization_barrier((*near, base))
        (far,) = call(
            far_kernel,
            "pack_other_core",
            [(VMEM, one) for one in near],
            [((2, 2, share, width), BF16)],
        )
        send, keep, col_grads = call(
            column_chip_kernel,
            "column_heads",
            [
                (VMEM, one)
                for one in (
                    x_near, cot_near, swapped, corner, *near, swap(far, "seq", 1),
                    gain, col_weight, col_out_weight, row_out,
                )
            ],
            [((chips, row_share, col_width), BF16)] * 2 + [col_outs[0]],
            vmem=BIG_VMEM,
            out_specs=[VMEM, VMEM, PINNED],
        )
        back_send, back_keep = call(
            back_chip_kernel,
            "column_grad_hidden",
            [(VMEM, col_grads), (VMEM, col_weight)],
            [((chips, share, width), BF16)] * 2,
        )
        row_next, _ = lax.optimization_barrier((row_next, send))
        keep, back_keep = lax.optimization_barrier((keep, back_keep))
        first_half = (chips, row_share // 2, FIRST_PART)
        second = (row_share, col_width - FIRST_PART)
        to_next, kept, owned, *off = call(
            cores_kernel,
            "column_add_cores",
            [(VMEM, keep), (VMEM, swap(send, "seq", 1))],
            [(first_half, BF16), (first_half, F32), (second, F32)] + [(second, BF16)] * 3,
            out_specs=[VMEM, PINNED, PINNED, VMEM, VMEM, VMEM],
        )
        got = cross_chips(*off)
        back = call(
            back_pack_kernel,
            "pack_grad_hidden",
            [(VMEM, back_keep), (VMEM, swap(back_send, "seq", 1))],
            [((2 * share, width), BF16)] * 4,
        )
        joint = (row_share // 2, FIRST_PART + row_width)
        first_owned, *off = call(
            pair_kernel,
            "first_add_pair",
            [
                (VMEM, one)
                for one in (kept, swap(to_next, "dp", 1), row_kept, swap(row_next, "dp", 1))
            ],
            [(joint, F32)] + [(joint, BF16)] * 3,
            out_specs=[PINNED, VMEM, VMEM, VMEM],
        )
        first_got = cross_chips(*off)
        second_half = (row_share // 2, second[1])
        to_next, kept = call(
            layer_kernel,
            "second_add_chips",
            [(VMEM, one) for one in (owned, *got)],
            [(second_half, BF16), (second_half, F32)],
            out_specs=[VMEM, PINNED],
        )
        (pair_sum,) = call(
            join_kernel,
            "join_terms",
            [(VMEM, one) for one in (first_owned, *first_got, kept, swap(to_next, "dp", 1))],
            [((row_share // 2, col_width + row_width), BF16)],
        )
        *back, pair_sum = lax.optimization_barrier((*back, pair_sum))
        held = add_two(pair_sum, swap(pair_sum, "dp", 2), "add_pairs")
        other = swap(held, "dp", 1)
        (grad,) = call(
            input_chip_kernel,
            "input_grad",
            [
                (VMEM, one)
                for one in (base, normed, inverse_rms, gain, back[0], *cross_chips(*back[1:]))
            ],
            [((columns, width), BF16)],
            [pltpu.VMEM((chips, 2 * share, width), BF16), pltpu.SemaphoreType.DMA((chips,))],
            out_specs=[HBM],
        )
        sum_qkv, sum_out, sum_gain = call(
            result_kernel,
            "result",
            [(VMEM, held), (VMEM, other), (VMEM, weight_rows), (VMEM, gain)],
            [((row_share, 3 * width), F32), ((row_share, width), F32), ((1, row_share), F32)],
        )
        sum_gain = sum_gain.reshape(row_share)
    else:
        terms, *col_grads = call(
            column_kernel,
            "column_heads",
            [(ANY, moved), *weights, (VMEM, row_terms[0]), (VMEM, row_out)],
            [((width, 4 * width), BF16), *col_outs],
            [
                pltpu.VMEM((n, 2, share, width), BF16),
                weight_scratch[0],
                weight_scratch[2],
                pltpu.SemaphoreType.DMA((6,)),
            ],
            BIG_VMEM,
        )
        (back,) = call(
            back_kernel,
            "column_grad_hidden",
            [(VMEM, one) for one in col_grads],
            [((n, share, width), BF16)],
        )
        returned = lax.all_to_all(back, "seq", split_axis=0, concat_axis=0, tiled=True)
        (grad,) = call(
            input_kernel,
            "input_grad",
            [
                (VMEM, base), (VMEM, normed), (VMEM, inverse_rms), (VMEM, gain),
                (VMEM, returned.reshape(columns, width)),
            ],
            [((columns, width), BF16)],
        )
        terms = lax.all_to_all(
            terms.reshape(n, row_share, 4 * width), "seq", split_axis=0, concat_axis=0, tiled=True
        )
        total = jnp.sum(terms.astype(F32), 0)
        for step in range(m.bit_length() - 1):
            sent = total.astype(BF16)
            total = sent.astype(F32) + swap(sent, "dp", 1 << step).astype(F32)
        sum_qkv, sum_out = total[:, : 3 * width], total[:, 3 * width :]
        here_at = lax.axis_index("seq") * row_share
        own_gain = lax.dynamic_slice_in_dim(norm_gain, here_at, row_share, 0)
        own_weight = lax.dynamic_slice_in_dim(qkv_weight, here_at, row_share, 0)
        sum_gain = jnp.sum(sum_qkv * own_weight.astype(F32), -1) / own_gain
    return (grad.reshape(inputs.shape), sum_qkv, sum_out, sum_gain)


def solution(mesh):
    return jax.shard_map(
        body,
        mesh=mesh,
        in_specs=(P("dp", "seq", None, None), P(), P(), P(), P("dp", "seq", None, None)),
        out_specs=(P("dp", "seq", None, None), P("seq", None), P("seq", None), P("seq")),
        check_vma=False,
    )
```

```python
import math

import jax
import jax.numpy as jnp
from jax import lax
from jax.experimental import pallas as pl
from jax.experimental.pallas import tpu as pltpu
from jax.sharding import PartitionSpec as P

H = 8
HD = 64
HH = H // 2
HW = HH * HD
SCALE = HD ** (-0.5)
F32 = jnp.float32
BF16 = jnp.bfloat16
QUERY_BLOCK = 128
BIG_VMEM = 20 * 1024 * 1024
SMALL_VMEM = 8 * 1024 * 1024
ANY = pl.BlockSpec(memory_space=pl.ANY)
VMEM = pl.BlockSpec(memory_space=pltpu.VMEM)
HBM = pl.BlockSpec(memory_space=pltpu.HBM)
CHIP_STEPS = (3, 2, 1)
FIRST_PART = 512
PINNED = pl.BlockSpec(memory_space=pltpu.VMEM)
shaped = jax.ShapeDtypeStruct


def here():
    device = lax.axis_index("seq")
    return device >> 1, device & 1, lax.axis_index("dp")


def dot_nn(a, b):
    return lax.dot_general(a, b, (((1,), (0,)), ((), ())), preferred_element_type=F32)


def dot_nt(a, b):
    return lax.dot_general(a, b, (((1,), (1,)), ((), ())), preferred_element_type=F32)


def rms_parts(x):
    inverse_rms = lax.rsqrt(jnp.mean(x * x, -1, keepdims=True) + 1e-05)
    return inverse_rms, x * inverse_rms


def transposed(x):
    block = math.gcd(x.shape[1], 256)
    eye = (
        lax.broadcasted_iota(jnp.int32, (block, block), 0)
        == lax.broadcasted_iota(jnp.int32, (block, block), 1)
    ).astype(F32).astype(BF16)
    parts = [
        dot_nt(eye, x[:, at : at + block]).astype(BF16) for at in range(0, x.shape[1], block)
    ]
    return parts[0] if len(parts) == 1 else jnp.concatenate(parts, 0)


def head_pair(x):
    lane = lax.broadcasted_iota(jnp.int32, x.shape, 1)
    zero = jnp.zeros_like(x)
    return jnp.concatenate([jnp.where(lane < HD, x, zero), jnp.where(lane < HD, zero, x)], 0)


def both_heads(both, count):
    return jnp.concatenate([both[:HD, :count], both[HD:, count:]], 0)


def pair_steps(items, mask_rows, mask):
    count = items[0][2].shape[1]
    scores = [dot_nt(k, q2) for q2, _, _, k, _, _, _ in items]
    prob_grads = [dot_nt(v, g2) for _, g2, _, _, v, _, _ in items]
    probs = []
    for score in scores:
        first = score.shape[0] - mask_rows
        tail = jnp.where(mask, score[first:], -1e30)
        score = tail if first == 0 else jnp.concatenate([score[:first], tail], 0)
        exponent = jnp.exp(score - jnp.max(score, 0, keepdims=True))
        probs.append(exponent * (1.0 / jnp.sum(exponent, 0, keepdims=True)))
    weights = [prob.astype(BF16) for prob in probs]
    attended = [
        both_heads(dot_nn(item[6], weight), count).astype(BF16)
        for item, weight in zip(items, weights)
    ]
    score_grads = []
    for item, att, prob, prob_grad in zip(items, attended, probs, prob_grads):
        product = item[2].astype(F32) * att.astype(F32)
        delta = [jnp.sum(part, 0, keepdims=True) for part in (product[:HD], product[HD:])]
        score_grads.append((prob * (prob_grad - jnp.concatenate(delta, 1))).astype(BF16))
    grad_q = [
        (both_heads(dot_nn(item[5], score_grad), count) * SCALE).astype(BF16)
        for item, score_grad in zip(items, score_grads)
    ]
    grad_k = [dot_nn(score_grad, item[0]) for item, score_grad in zip(items, score_grads)]
    grad_v = [dot_nn(weight, item[1]) for item, weight in zip(items, weights)]
    return list(zip(attended, grad_q, grad_k, grad_v))


def split_cores(piece, send_ref, keep_ref, chips, lanes):
    rows = send_ref.shape[1]
    parts = piece.reshape(chips.stop - chips.start, 2, rows, piece.shape[1])
    even, odd = parts[:, 0], parts[:, 1]
    first = here()[1] == 0
    send_ref[chips, :, lanes] = jnp.where(first, odd, even)
    keep_ref[chips, :, lanes] = jnp.where(first, even, odd)


def qkv_copies(wqkv_ref, w_ref, sems, second):
    width = wqkv_ref.shape[0]
    return [
        pltpu.make_async_copy(
            wqkv_ref.at[:, pl.ds(i * width + second * HW, HW)],
            w_ref.at[:, pl.ds(i * HW, HW)],
            sems.at[i],
        )
        for i in range(3)
    ]


def weight_copies(wqkv_ref, wout_ref, w_ref, wo_ref, sems, second):
    out_rows = wout_ref.at[pl.ds(second * HW, HW), :]
    return [
        *qkv_copies(wqkv_ref, w_ref, sems, second),
        pltpu.make_async_copy(out_rows, wo_ref, sems.at[3]),
    ]


def started(*copies):
    for copy in copies:
        copy.start()
    return copies


def finished(*copies):
    for copy in copies:
        copy.wait()


def project(hidden, cot, w_ref, wo_ref):
    projected = dot_nn(hidden, w_ref[...]).astype(BF16)
    q, k, v = [projected[:, i * HW : (i + 1) * HW] for i in range(3)]
    g = dot_nt(cot, wo_ref[...]).astype(BF16)
    return q * jnp.asarray(SCALE, BF16), k, v, g


def row_part(
    x_any, cot_any, gain_any, wqkv_any, wout_any,
    out_ref, base_ref, normed_ref, inverse_ref, x_ref, cot_ref,
    gain_ref, w_ref, wo_ref, dk_ref, dv_ref, grads_ref, sems,
):
    first = started(
        pltpu.make_async_copy(x_any, x_ref, sems.at[4]),
        pltpu.make_async_copy(gain_any, gain_ref, sems.at[5]),
    )
    later = started(
        *weight_copies(wqkv_any, wout_any, w_ref, wo_ref, sems, 0),
        pltpu.make_async_copy(cot_any, cot_ref, sems.at[6]),
    )
    dk_ref[...] = jnp.zeros_like(dk_ref)
    dv_ref[...] = jnp.zeros_like(dv_ref)
    finished(*first)
    tokens = x_ref.shape[0]
    inverse_ref[...], normed_ref[...] = rms_parts(x_ref[...].astype(F32))
    hidden = (normed_ref[...] * gain_ref[...]).astype(BF16)
    hidden_t = transposed(hidden)
    finished(*later)
    cot = cot_ref[...]
    q, k, v, g = project(hidden, cot, w_ref, wo_ref)
    kt, vt, gt = transposed(k), transposed(v), transposed(g)
    step = math.gcd(tokens, QUERY_BLOCK)
    query = lax.broadcasted_iota(jnp.int32, (step, 2 * step), 1) % step
    mask = query >= lax.broadcasted_iota(jnp.int32, (step, 2 * step), 0)
    pairs = [slice(i * 2 * HD, (i + 1) * 2 * HD) for i in range(HH // 2)]
    att_blocks, dq_blocks = [], []
    for start in range(0, tokens, step):
        rows, keys = slice(start, start + step), slice(0, start + step)
        items = [
            (
                head_pair(q[rows, lanes]), head_pair(g[rows, lanes]), gt[lanes, rows],
                k[keys, lanes], v[keys, lanes], kt[lanes, keys], vt[lanes, keys],
            )
            for lanes in pairs
        ]
        results = pair_steps(items, step, mask)
        for lanes, (_, _, dk, dv) in zip(pairs, results):
            dk_ref[keys, lanes] += dk
            dv_ref[keys, lanes] += dv
        att_blocks.append(jnp.concatenate([result[0] for result in results], 0))
        dq_blocks.append(jnp.concatenate([result[1] for result in results], 0))
    grads_ref[:, :HW] = transposed(jnp.concatenate(dq_blocks, 1))
    grads_ref[:, HW : 2 * HW] = dk_ref[...].astype(BF16)
    grads_ref[:, 2 * HW :] = dv_ref[...].astype(BF16)
    term_qkv = dot_nn(hidden_t, grads_ref[...]).astype(BF16)
    out_ref[...] = dot_nn(jnp.concatenate(att_blocks, 1), cot).astype(BF16)
    grad_normed = dot_nt(grads_ref[...], w_ref[...]) * gain_ref[...]
    base_ref[...] = input_grad(
        cot_ref[...].astype(F32), normed_ref[...], inverse_ref[...], grad_normed
    )
    return term_qkv


def row_kernel(x_any, cot_any, gain_any, wqkv_any, wout_any, qkv_ref, *refs):
    qkv_ref[...] = row_part(x_any, cot_any, gain_any, wqkv_any, wout_any, *refs)


def row_chip_kernel(
    x_any, cot_any, gain_any, wqkv_any, wout_any,
    send_1, send_2, keep_1, keep_2, rows_ref, col_w_ref, col_wo_ref, *refs,
):
    chip, core, _ = here()
    sems, rows = refs[-1], rows_ref.shape[0]
    at = pl.multiple_of((chip * 2 + core) * rows, rows)
    handed = started(
        pltpu.make_async_copy(wqkv_any.at[pl.ds(at, rows), :], rows_ref, sems.at[7]),
        *weight_copies(wqkv_any, wout_any, col_w_ref, col_wo_ref, sems.at[pl.ds(8, 4)], 1),
    )
    term_qkv = row_part(x_any, cot_any, gain_any, wqkv_any, wout_any, *refs)
    chips, cut = send_1.shape[0], keep_1.shape[2]
    pieces = slice(0, chips), slice(0, cut)
    split_cores(term_qkv[:, :cut], send_1, keep_1, *pieces)
    split_cores(term_qkv[:, cut:], send_2, keep_2, *pieces)
    finished(*handed)


def column_part(x, cot, mask, gain, w_ref, wo_ref, weight_waits, grads_ref):
    tokens, block = x.shape[0], mask.shape[0]
    _, normed = rms_parts(x.astype(F32))
    hidden = (normed * gain).astype(BF16)
    hidden_t = transposed(hidden)
    finished(*weight_waits)
    q, k, v, g = project(hidden, cot, w_ref, wo_ref)
    kt, vt, gt = transposed(k), transposed(v), transposed(g)
    pairs = [slice(i * 2 * HD, (i + 1) * 2 * HD) for i in range(HH // 2)]
    blocks = [slice(at, at + block) for at in range(0, tokens, block)]
    items = [
        (
            head_pair(q[rows, lanes]), head_pair(g[rows, lanes]), gt[lanes, rows],
            k[rows, lanes], v[rows, lanes], kt[lanes, rows], vt[lanes, rows],
        )
        for lanes in pairs
        for rows in blocks
    ]
    results = pair_steps(items, block, mask)
    places = [(lanes, rows) for lanes in pairs for rows in blocks]
    for (lanes, rows), (_, _, dk, dv) in zip(places, results):
        grads_ref[rows, HW + lanes.start : HW + lanes.stop] = dk.astype(BF16)
        grads_ref[rows, 2 * HW + lanes.start : 2 * HW + lanes.stop] = dv.astype(BF16)
    by_pair = [results[i * len(blocks) : (i + 1) * len(blocks)] for i in range(len(pairs))]
    attended, grad_q = [
        jnp.concatenate([jnp.concatenate([r[i] for r in some], 1) for some in by_pair], 0)
        for i in range(2)
    ]
    grads_ref[:, :HW] = transposed(grad_q)
    term_qkv = dot_nn(hidden_t, grads_ref[...]).astype(BF16)
    term_out = dot_nn(attended, cot).astype(BF16)
    return term_qkv, term_out


def column_mask(all_rows, group, row_of):
    block = all_rows * group
    shape = (block, 2 * block)
    query = lax.broadcasted_iota(jnp.int32, shape, 1) % block
    key = lax.broadcasted_iota(jnp.int32, shape, 0)
    same_column = query % group == key % group
    return (row_of(query // group) >= row_of(key // group)) & same_column


def column_kernel(
    moved_any, gain_any, wqkv_any, wout_any, row_qkv_ref, row_out_ref,
    terms_ref, grads_ref, w_ref,
    moved_ref, gain_ref, wo_ref, sems,
):
    copies = started(
        pltpu.make_async_copy(moved_any, moved_ref, sems.at[4]),
        pltpu.make_async_copy(gain_any, gain_ref, sems.at[5]),
    )
    weights = started(*weight_copies(wqkv_any, wout_any, w_ref, wo_ref, sems, 1))
    finished(*copies)
    all_rows, _, share, width = moved_ref.shape
    group = math.gcd(share, 16)
    x, cot = [
        jnp.concatenate(
            [
                moved_ref[:, which, at : at + group, :].astype(F32).reshape(all_rows * group, width)
                for at in range(0, share, group)
            ],
            0,
        ).astype(BF16)
        for which in range(2)
    ]
    mask = column_mask(all_rows, group, lambda place: place)
    term_qkv, term_out = column_part(
        x, cot, mask, gain_ref[...], w_ref, wo_ref, weights, grads_ref
    )
    for i in range(3):
        at = i * width
        terms_ref[:, at : at + HW] = row_qkv_ref[:, i * HW : (i + 1) * HW]
        terms_ref[:, at + HW : at + 2 * HW] = term_qkv[:, i * HW : (i + 1) * HW]
    terms_ref[:HW, 3 * width :] = row_out_ref[...]
    terms_ref[HW:, 3 * width :] = term_out


def column_chip_kernel(
    x_ref, cot_ref, swapped_ref, corner_ref, near_2, near_3, far_ref, gain_ref, w_ref, wo_ref, row_out_ref,
    send_ref, keep_ref, grads_ref,
):
    chip, core, _ = here()
    share = far_ref.shape[2]
    half = pl.ds(pl.multiple_of(core * share, share), share)
    at = pl.ds(pl.multiple_of((chip * 2 + core) * share, share), share)
    group = math.gcd(share, 16)

    def tokens(which, mine):
        pieces = [
            mine[at, :], swapped_ref[0, which], corner_ref[0, which], corner_ref[1, which],
        ]
        for i, near in enumerate((near_2, near_3)):
            pieces += [near[which, half, :], far_ref[i, which]]
        starts = range(0, share, group)
        return jnp.concatenate(
            [piece[start : start + group] for start in starts for piece in pieces], 0
        )

    def row_of(place):
        step = (4 - (place >> 1)) & 3
        return ((step ^ chip) << 1) + ((place & 1) ^ core)

    mask = column_mask(2 * (len(CHIP_STEPS) + 1), group, row_of)
    term_qkv, term_out = column_part(
        tokens(0, x_ref), tokens(1, cot_ref), mask, gain_ref[...], w_ref, wo_ref, (), grads_ref
    )
    chips = send_ref.shape[0]
    refs = send_ref, keep_ref
    out_lanes = slice(3 * HW, send_ref.shape[2])
    split_cores(term_qkv, *refs, slice(0, chips), slice(0, 3 * HW))
    split_cores(row_out_ref[...], *refs, slice(0, chips // 2), out_lanes)
    split_cores(term_out, *refs, slice(chips // 2, chips), out_lanes)


def far_kernel(near_2, near_3, far_ref):
    share = far_ref.shape[2]
    at = pl.ds(pl.multiple_of((1 - here()[1]) * share, share), share)
    for i, near in enumerate((near_2, near_3)):
        far_ref[i] = near[:, at, :]


def back_kernel(grads_ref, w_ref, back_ref):
    grad_hidden = dot_nt(grads_ref[...], w_ref[...])
    all_rows, share, width = back_ref.shape
    group = math.gcd(share, 16)
    block = all_rows * group
    for i in range(share // group):
        piece = grad_hidden[i * block : (i + 1) * block].reshape(all_rows, group, width)
        back_ref[:, i * group : (i + 1) * group, :] = piece.astype(BF16)


def back_chip_kernel(grads_ref, w_ref, send_ref, keep_ref):
    grad_hidden = dot_nt(grads_ref[...], w_ref[...]).astype(BF16)
    chips, share, width = keep_ref.shape
    group = math.gcd(share, 16)
    block = 2 * chips * group
    for i in range(share // group):
        piece = grad_hidden[i * block : (i + 1) * block].reshape(chips, 2, group, width)
        at = slice(i * group, (i + 1) * group)
        keep_ref[:, at, :], send_ref[:, at, :] = piece[:, 0], piece[:, 1]


def back_pack_kernel(keep_ref, got_ref, *targets):
    share = keep_ref.shape[1]
    core = here()[1]
    kept_at = pl.ds(pl.multiple_of(core * share, share), share)
    got_at = pl.ds(pl.multiple_of((1 - core) * share, share), share)
    for i, target in enumerate(targets):
        target[kept_at, :] = keep_ref[i]
        target[got_at, :] = got_ref[i]


def input_kernel(base_ref, normed_ref, inverse_ref, gain_ref, back_ref, grad_ref):
    grad_ref[...] = input_grad(
        base_ref[...], normed_ref[...], inverse_ref[...], back_ref[...].astype(F32) * gain_ref[...]
    ).astype(BF16)


def input_grad(base, normed, inverse_rms, grad_normed):
    projected = jnp.mean(grad_normed * normed, -1, keepdims=True)
    return base + inverse_rms * (grad_normed - normed * projected)


def input_chip_kernel(
    base_ref, normed_ref, inverse_ref, gain_ref, own_ref, got_1, got_2, got_3,
    grad_any, grad_ref, sems,
):
    chip = here()[0]
    count = own_ref.shape[0]
    copies = []
    for i, (step, back_ref) in enumerate(zip((0, *CHIP_STEPS), (own_ref, got_1, got_2, got_3))):
        at = pl.ds(pl.multiple_of((chip ^ step) * count, count), count)
        grad_normed = back_ref[...].astype(F32) * gain_ref[...]
        grad = input_grad(base_ref[at, :], normed_ref[at, :], inverse_ref[at, :], grad_normed)
        grad_ref[i] = grad.astype(BF16)
        copies += started(pltpu.make_async_copy(grad_ref.at[i], grad_any.at[at, :], sems.at[i]))
    finished(*copies)


def pack_kernel(x_any, cot_any, swap_ref, corner_ref, off_2, off_3, sems):
    chip, core, _ = here()
    share = corner_ref.shape[1]

    def columns(step, of_core):
        return pl.multiple_of(((chip ^ step) * 2 + of_core) * share, share)

    corner = CHIP_STEPS[0]
    copies = []
    for which, source in enumerate((x_any, cot_any)):
        pieces = [
            (columns(0, 1 - core), share, swap_ref.at[0, which]),
            (columns(corner, 1 - core), share, swap_ref.at[1, which]),
            (columns(corner, core), share, corner_ref.at[which]),
            (columns(CHIP_STEPS[1], 0), 2 * share, off_2.at[which]),
            (columns(CHIP_STEPS[2], 0), 2 * share, off_3.at[which]),
        ]
        for i, (at, count, target) in enumerate(pieces):
            copies.append(
                pltpu.make_async_copy(
                    source.at[pl.ds(at, count), :], target, sems.at[5 * which + i]
                )
            )
    finished(*started(*copies))


def corner_kernel(corner_ref, swapped_ref, out_ref):
    out_ref[0], out_ref[1] = corner_ref[...], swapped_ref[1]


def split_rows(total, axis):
    upper = (here()[2] & 1) == 1
    low, high = jnp.split(total, 2, axis)
    return jnp.where(upper, low, high).astype(BF16), jnp.where(upper, high, low)


def row_cores_kernel(keep_1, keep_2, got_1, got_2, send_ref, kept_ref):
    total = [
        keep_ref[...].astype(F32) + got_ref[...].astype(F32)
        for keep_ref, got_ref in ((keep_1, got_1), (keep_2, got_2))
    ]
    send_ref[...], kept_ref[...] = split_rows(jnp.concatenate(total, 2), 1)


def cores_kernel(keep_ref, got_ref, send_ref, kept_ref, *targets):
    chip, cut = here()[0], kept_ref.shape[2]
    first = keep_ref[:, :, :cut].astype(F32) + got_ref[:, :, :cut].astype(F32)
    send_ref[...], kept_ref[...] = split_rows(first, 1)
    for step, target in zip((0, *CHIP_STEPS), targets):
        there = chip ^ step
        total = keep_ref[there, :, cut:].astype(F32) + got_ref[there, :, cut:].astype(F32)
        target[...] = total.astype(target.dtype)


def pair_kernel(kept_ref, got_ref, row_kept, row_got, *targets):
    chip, cut = here()[0], kept_ref.shape[2]
    for step, target in zip((0, *CHIP_STEPS), targets):
        there = chip ^ step
        total = kept_ref[there] + got_ref[there].astype(F32)
        target[:, :cut] = total.astype(target.dtype)
        total = row_kept[there] + row_got[there].astype(F32)
        target[:, cut:] = total.astype(target.dtype)


def layer_sum(own_ref, got_1, got_2, got_3):
    return own_ref[...] + (
        (got_1[...].astype(F32) + got_2[...].astype(F32)) + got_3[...].astype(F32)
    )


def layer_kernel(own_ref, got_1, got_2, got_3, send_ref, kept_ref):
    send_ref[...], kept_ref[...] = split_rows(layer_sum(own_ref, got_1, got_2, got_3), 0)


def join_kernel(own_ref, got_1, got_2, got_3, kept_ref, got_ref, out_ref):
    total = layer_sum(own_ref, got_1, got_2, got_3).astype(BF16)
    cut, width = FIRST_PART, kept_ref.shape[1]
    out_ref[:, :cut] = total[:, :cut]
    out_ref[:, cut : cut + width] = (kept_ref[...] + got_ref[...].astype(F32)).astype(BF16)
    out_ref[:, cut + width :] = total[:, cut:]


def add_kernel(kept_ref, got_ref, out_ref):
    out_ref[...] = (kept_ref[...].astype(F32) + got_ref[...].astype(F32)).astype(BF16)


def result_kernel(held_ref, got_ref, w_ref, gain_ref, qkv_ref, out_ref, grad_ref):
    rows = qkv_ref.shape[0]
    chip, core, layer = here()
    at = (chip * 2 + core) * rows
    upper = (layer & 1) == 1
    half = rows // 2
    width = out_ref.shape[1]

    def ordered(lanes):
        held, got = held_ref[:, lanes].astype(F32), got_ref[:, lanes].astype(F32)
        return (jnp.where(upper, got, held), jnp.where(upper, held, got))

    row_at = 3 * HW + width
    for i in range(3):
        for at_from, at_to in ((row_at + i * HW, i * width), (i * HW, i * width + HW)):
            to = slice(at_to, at_to + HW)
            qkv_ref[:half, to], qkv_ref[half:, to] = ordered(slice(at_from, at_from + HW))
    out_ref[:half], out_ref[half:] = ordered(slice(3 * HW, row_at))
    total = jnp.sum(qkv_ref[...] * w_ref[...].astype(F32), -1, keepdims=True)
    shape = (rows, gain_ref.shape[1])
    row = lax.broadcasted_iota(jnp.int32, shape, 0)
    feature = lax.broadcasted_iota(jnp.int32, shape, 1)
    gain = jnp.sum(jnp.where(feature == row + at, gain_ref[...], 0.0), -1, keepdims=True)
    shape = (rows, grad_ref.shape[1])
    same = lax.broadcasted_iota(jnp.int32, shape, 0) == lax.broadcasted_iota(jnp.int32, shape, 1)
    grad_ref[...] = jnp.sum(jnp.where(same, total / gain, 0.0), 0, keepdims=True)


def call(kernel, name, ins, outs, scratch=(), vmem=SMALL_VMEM, out_specs=None):
    out_specs = out_specs or [VMEM] * len(outs)
    places = [{id(HBM): pltpu.HBM, id(PINNED): pltpu.VMEM}.get(id(spec)) for spec in out_specs]
    outs = [place(*out) if place else shaped(*out) for place, out in zip(places, outs)]
    args = [
        pltpu.with_memory_space_constraint(array, pltpu.HBM) if spec is HBM else array
        for spec, array in ins
    ]
    return pl.pallas_call(
        kernel,
        out_shape=outs,
        in_specs=[spec for spec, _ in ins],
        out_specs=out_specs,
        scratch_shapes=scratch,
        name=name,
        cost_estimate=pl.CostEstimate(flops=0, bytes_accessed=0, transcendentals=0),
        compiler_params=pltpu.CompilerParams(vmem_limit_bytes=vmem),
    )(*args)


def swap(array, axis, bits):
    count = lax.axis_size(axis)
    return lax.ppermute(array, axis, [(i, i ^ bits) for i in range(count)])


def cross_chips(*offs):
    return [swap(off, "seq", 2 * step) for off, step in zip(offs, CHIP_STEPS)]


def add_two(kept, got, name):
    (total,) = call(add_kernel, name, [(VMEM, kept), (VMEM, got)], [(kept.shape, BF16)])
    return total


def body(inputs, norm_gain, qkv_weight, out_weight, out_cotan):
    columns, width = inputs.shape[2:]
    n = lax.axis_size("seq")
    m = lax.axis_size("dp")
    share = columns // n
    row_share = width // n
    row_width, col_width = 3 * HW, 3 * HW + width
    x = inputs.reshape(columns, width)
    cot = out_cotan.reshape(columns, width)
    gain = norm_gain.reshape(1, width)
    chips = 4
    layered = n == 2 * chips and m == 4 and row_share == share
    weight_scratch = [
        pltpu.VMEM((1, width), F32),
        pltpu.VMEM((width, 3 * HW), BF16),
        pltpu.VMEM((HW, width), BF16),
    ]
    weights = [(HBM, gain), (HBM, qkv_weight), (HBM, out_weight)]
    col_outs = [((columns, 3 * HW), BF16), ((width, 3 * HW), BF16)]

    if layered:
        packed = call(
            pack_kernel,
            "pack_columns",
            [(HBM, x), (HBM, cot)],
            [((2, 2, share, width), BF16), ((2, share, width), BF16)]
            + [((2, 2 * share, width), BF16)] * 2,
            [pltpu.SemaphoreType.DMA((10,))],
            out_specs=[ANY] * 4,
        )
        near = [swap(one, "seq", 2 * step) for one, step in zip(packed[2:], CHIP_STEPS[1:])]
        swapped = swap(packed[0], "seq", 1)
        (corner,) = call(
            corner_kernel,
            "pack_corner",
            [(VMEM, packed[1]), (VMEM, swapped)],
            [((2, 2, share, width), BF16)],
        )
        x_first, _ = lax.optimization_barrier((x, corner))
        corner = swap(corner, "seq", 2 * CHIP_STEPS[0])
    else:
        outgoing = jnp.stack([x.reshape(n, share, width), cot.reshape(n, share, width)], 1)
        moved = lax.all_to_all(outgoing, "seq", split_axis=0, concat_axis=0, tiled=True)
        x_first = x

    row_outs = [
        ((HW, width), BF16),
        ((columns, width), F32), ((columns, width), F32), ((columns, 1), F32),
        ((columns, width), BF16), ((columns, width), BF16),
    ]
    if layered:
        cut = row_width // 2
        split_outs = [((chips, row_share, cut), BF16)] * 4
        handed_outs = [
            ((row_share, 3 * width), BF16), ((width, 3 * HW), BF16), ((HW, width), BF16),
        ]
        row_outs = [*split_outs, *handed_outs, *row_outs]
        specs = [VMEM] * 4 + [PINNED] * (len(row_outs) - 4)
    else:
        row_outs = [((width, row_width), BF16), *row_outs]
        specs = [VMEM] * len(row_outs)
    *row_terms, row_out, base, normed, inverse_rms, x_near, cot_near = call(
        row_chip_kernel if layered else row_kernel,
        "row_heads",
        [(HBM, x_first), (HBM, cot), *weights],
        row_outs,
        [
            *weight_scratch,
            pltpu.VMEM((columns, HW), F32),
            pltpu.VMEM((columns, HW), F32),
            pltpu.VMEM((columns, 3 * HW), BF16),
            pltpu.SemaphoreType.DMA((12,)),
        ],
        BIG_VMEM,
        specs,
    )
    if layered:
        *row_terms, weight_rows, col_weight, col_out_weight = row_terms
        row_sent = [swap(one, "seq", 1) for one in row_terms[:2]]
        half_block = (chips, row_share // 2, row_width)
        row_next, row_kept = call(
            row_cores_kernel,
            "row_add_cores",
            [(VMEM, one) for one in (*row_terms[2:], *row_sent)],
            [(half_block, BF16), (half_block, F32)],
            out_specs=[VMEM, PINNED],
        )
        col_weight, row_kept = lax.optimization_barrier((col_weight, row_kept))
        *near, base = lax.optimization_barrier((*near, base))
        (far,) = call(
            far_kernel,
            "pack_other_core",
            [(VMEM, one) for one in near],
            [((2, 2, share, width), BF16)],
        )
        send, keep, col_grads = call(
            column_chip_kernel,
            "column_heads",
            [
                (VMEM, one)
                for one in (
                    x_near, cot_near, swapped, corner, *near, swap(far, "seq", 1),
                    gain, col_weight, col_out_weight, row_out,
                )
            ],
            [((chips, row_share, col_width), BF16)] * 2 + [col_outs[0]],
            vmem=BIG_VMEM,
            out_specs=[VMEM, VMEM, PINNED],
        )
        back_send, back_keep = call(
            back_chip_kernel,
            "column_grad_hidden",
            [(VMEM, col_grads), (VMEM, col_weight)],
            [((chips, share, width), BF16)] * 2,
        )
        row_next, _ = lax.optimization_barrier((row_next, send))
        keep, back_keep = lax.optimization_barrier((keep, back_keep))
        first_half = (chips, row_share // 2, FIRST_PART)
        second = (row_share, col_width - FIRST_PART)
        to_next, kept, owned, *off = call(
            cores_kernel,
            "column_add_cores",
            [(VMEM, keep), (VMEM, swap(send, "seq", 1))],
            [(first_half, BF16), (first_half, F32), (second, F32)] + [(second, BF16)] * 3,
            out_specs=[VMEM, PINNED, PINNED, VMEM, VMEM, VMEM],
        )
        got = cross_chips(*off)
        back = call(
            back_pack_kernel,
            "pack_grad_hidden",
            [(VMEM, back_keep), (VMEM, swap(back_send, "seq", 1))],
            [((2 * share, width), BF16)] * 4,
        )
        joint = (row_share // 2, FIRST_PART + row_width)
        first_owned, *off = call(
            pair_kernel,
            "first_add_pair",
            [
                (VMEM, one)
                for one in (kept, swap(to_next, "dp", 1), row_kept, swap(row_next, "dp", 1))
            ],
            [(joint, F32)] + [(joint, BF16)] * 3,
            out_specs=[PINNED, VMEM, VMEM, VMEM],
        )
        first_got = cross_chips(*off)
        second_half = (row_share // 2, second[1])
        to_next, kept = call(
            layer_kernel,
            "second_add_chips",
            [(VMEM, one) for one in (owned, *got)],
            [(second_half, BF16), (second_half, F32)],
            out_specs=[VMEM, PINNED],
        )
        (pair_sum,) = call(
            join_kernel,
            "join_terms",
            [(VMEM, one) for one in (first_owned, *first_got, kept, swap(to_next, "dp", 1))],
            [((row_share // 2, col_width + row_width), BF16)],
        )
        *back, pair_sum = lax.optimization_barrier((*back, pair_sum))
        held = add_two(pair_sum, swap(pair_sum, "dp", 2), "add_pairs")
        other = swap(held, "dp", 1)
        (grad,) = call(
            input_chip_kernel,
            "input_grad",
            [
                (VMEM, one)
                for one in (base, normed, inverse_rms, gain, back[0], *cross_chips(*back[1:]))
            ],
            [((columns, width), BF16)],
            [pltpu.VMEM((chips, 2 * share, width), BF16), pltpu.SemaphoreType.DMA((chips,))],
            out_specs=[HBM],
        )
        sum_qkv, sum_out, sum_gain = call(
            result_kernel,
            "result",
            [(VMEM, held), (VMEM, other), (VMEM, weight_rows), (VMEM, gain)],
            [((row_share, 3 * width), F32), ((row_share, width), F32), ((1, row_share), F32)],
        )
        sum_gain = sum_gain.reshape(row_share)
    else:
        terms, *col_grads = call(
            column_kernel,
            "column_heads",
            [(ANY, moved), *weights, (VMEM, row_terms[0]), (VMEM, row_out)],
            [((width, 4 * width), BF16), *col_outs],
            [
                pltpu.VMEM((n, 2, share, width), BF16),
                weight_scratch[0],
                weight_scratch[2],
                pltpu.SemaphoreType.DMA((6,)),
            ],
            BIG_VMEM,
        )
        (back,) = call(
            back_kernel,
            "column_grad_hidden",
            [(VMEM, one) for one in col_grads],
            [((n, share, width), BF16)],
        )
        returned = lax.all_to_all(back, "seq", split_axis=0, concat_axis=0, tiled=True)
        (grad,) = call(
            input_kernel,
            "input_grad",
            [
                (VMEM, base), (VMEM, normed), (VMEM, inverse_rms), (VMEM, gain),
                (VMEM, returned.reshape(columns, width)),
            ],
            [((columns, width), BF16)],
        )
        terms = lax.all_to_all(
            terms.reshape(n, row_share, 4 * width), "seq", split_axis=0, concat_axis=0, tiled=True
        )
        total = jnp.sum(terms.astype(F32), 0)
        for step in range(m.bit_length() - 1):
            sent = total.astype(BF16)
            total = sent.astype(F32) + swap(sent, "dp", 1 << step).astype(F32)
        sum_qkv, sum_out = total[:, : 3 * width], total[:, 3 * width :]
        here_at = lax.axis_index("seq") * row_share
        own_gain = lax.dynamic_slice_in_dim(norm_gain, here_at, row_share, 0)
        own_weight = lax.dynamic_slice_in_dim(qkv_weight, here_at, row_share, 0)
        sum_gain = jnp.sum(sum_qkv * own_weight.astype(F32), -1) / own_gain
    return (grad.reshape(inputs.shape), sum_qkv, sum_out, sum_gain)


def solution(mesh):
    return jax.shard_map(
        body,
        mesh=mesh,
        in_specs=(P("dp", "seq", None, None), P(), P(), P(), P("dp", "seq", None, None)),
        out_specs=(P("dp", "seq", None, None), P("seq", None), P("seq", None), P("seq")),
        check_vma=False,
    )
```

```python
import math

import jax
import jax.numpy as jnp
from jax import lax
from jax.experimental import pallas as pl
from jax.experimental.pallas import tpu as pltpu
from jax.sharding import PartitionSpec as P

H = 8
HD = 64
HH = H // 2
HW = HH * HD
SCALE = HD ** (-0.5)
F32 = jnp.float32
BF16 = jnp.bfloat16
QUERY_BLOCK = 128
BIG_VMEM = 20 * 1024 * 1024
SMALL_VMEM = 8 * 1024 * 1024
ANY = pl.BlockSpec(memory_space=pl.ANY)
VMEM = pl.BlockSpec(memory_space=pltpu.VMEM)
HBM = pl.BlockSpec(memory_space=pltpu.HBM)
CHIP_STEPS = (3, 2, 1)
FIRST_PART = 384
PINNED = pl.BlockSpec(memory_space=pltpu.VMEM)
shaped = jax.ShapeDtypeStruct


def here():
    device = lax.axis_index("seq")
    return device >> 1, device & 1, lax.axis_index("dp")


def dot_nn(a, b):
    return lax.dot_general(a, b, (((1,), (0,)), ((), ())), preferred_element_type=F32)


def dot_nt(a, b):
    return lax.dot_general(a, b, (((1,), (1,)), ((), ())), preferred_element_type=F32)


def rms_parts(x):
    inverse_rms = lax.rsqrt(jnp.mean(x * x, -1, keepdims=True) + 1e-05)
    return inverse_rms, x * inverse_rms


def transposed(x):
    block = math.gcd(x.shape[1], 256)
    eye = (
        lax.broadcasted_iota(jnp.int32, (block, block), 0)
        == lax.broadcasted_iota(jnp.int32, (block, block), 1)
    ).astype(F32).astype(BF16)
    parts = [
        dot_nt(eye, x[:, at : at + block]).astype(BF16) for at in range(0, x.shape[1], block)
    ]
    return parts[0] if len(parts) == 1 else jnp.concatenate(parts, 0)


def head_pair(x):
    lane = lax.broadcasted_iota(jnp.int32, x.shape, 1)
    zero = jnp.zeros_like(x)
    return jnp.concatenate([jnp.where(lane < HD, x, zero), jnp.where(lane < HD, zero, x)], 0)


def both_heads(both, count):
    return jnp.concatenate([both[:HD, :count], both[HD:, count:]], 0)


def pair_steps(items, mask_rows, mask):
    count = items[0][2].shape[1]
    scores = [dot_nt(k, q2) for q2, _, _, k, _, _, _ in items]
    prob_grads = [dot_nt(v, g2) for _, g2, _, _, v, _, _ in items]
    probs = []
    for score in scores:
        first = score.shape[0] - mask_rows
        tail = jnp.where(mask, score[first:], -1e30)
        score = tail if first == 0 else jnp.concatenate([score[:first], tail], 0)
        exponent = jnp.exp(score - jnp.max(score, 0, keepdims=True))
        probs.append(exponent * (1.0 / jnp.sum(exponent, 0, keepdims=True)))
    weights = [prob.astype(BF16) for prob in probs]
    attended = [
        both_heads(dot_nn(item[6], weight), count).astype(BF16)
        for item, weight in zip(items, weights)
    ]
    score_grads = []
    for item, att, prob, prob_grad in zip(items, attended, probs, prob_grads):
        product = item[2].astype(F32) * att.astype(F32)
        delta = [jnp.sum(part, 0, keepdims=True) for part in (product[:HD], product[HD:])]
        score_grads.append((prob * (prob_grad - jnp.concatenate(delta, 1))).astype(BF16))
    grad_q = [
        (both_heads(dot_nn(item[5], score_grad), count) * SCALE).astype(BF16)
        for item, score_grad in zip(items, score_grads)
    ]
    grad_k = [dot_nn(score_grad, item[0]) for item, score_grad in zip(items, score_grads)]
    grad_v = [dot_nn(weight, item[1]) for item, weight in zip(items, weights)]
    return list(zip(attended, grad_q, grad_k, grad_v))


def split_cores(piece, send_ref, keep_ref, chips, lanes):
    rows = send_ref.shape[1]
    parts = piece.reshape(chips.stop - chips.start, 2, rows, piece.shape[1])
    even, odd = parts[:, 0], parts[:, 1]
    first = here()[1] == 0
    send_ref[chips, :, lanes] = jnp.where(first, odd, even)
    keep_ref[chips, :, lanes] = jnp.where(first, even, odd)


def qkv_copies(wqkv_ref, w_ref, sems, second):
    width = wqkv_ref.shape[0]
    return [
        pltpu.make_async_copy(
            wqkv_ref.at[:, pl.ds(i * width + second * HW, HW)],
            w_ref.at[:, pl.ds(i * HW, HW)],
            sems.at[i],
        )
        for i in range(3)
    ]


def weight_copies(wqkv_ref, wout_ref, w_ref, wo_ref, sems, second):
    out_rows = wout_ref.at[pl.ds(second * HW, HW), :]
    return [
        *qkv_copies(wqkv_ref, w_ref, sems, second),
        pltpu.make_async_copy(out_rows, wo_ref, sems.at[3]),
    ]


def started(*copies):
    for copy in copies:
        copy.start()
    return copies


def finished(*copies):
    for copy in copies:
        copy.wait()


def project(hidden, cot, w_ref, wo_ref):
    projected = dot_nn(hidden, w_ref[...]).astype(BF16)
    q, k, v = [projected[:, i * HW : (i + 1) * HW] for i in range(3)]
    g = dot_nt(cot, wo_ref[...]).astype(BF16)
    return q * jnp.asarray(SCALE, BF16), k, v, g


def row_part(
    x_any, cot_any, gain_any, wqkv_any, wout_any,
    out_ref, base_ref, normed_ref, inverse_ref, x_ref, cot_ref,
    gain_ref, w_ref, wo_ref, dk_ref, dv_ref, grads_ref, sems,
):
    first = started(
        pltpu.make_async_copy(x_any, x_ref, sems.at[4]),
        pltpu.make_async_copy(gain_any, gain_ref, sems.at[5]),
    )
    later = started(
        *weight_copies(wqkv_any, wout_any, w_ref, wo_ref, sems, 0),
        pltpu.make_async_copy(cot_any, cot_ref, sems.at[6]),
    )
    dk_ref[...] = jnp.zeros_like(dk_ref)
    dv_ref[...] = jnp.zeros_like(dv_ref)
    finished(*first)
    tokens = x_ref.shape[0]
    inverse_ref[...], normed_ref[...] = rms_parts(x_ref[...].astype(F32))
    hidden = (normed_ref[...] * gain_ref[...]).astype(BF16)
    hidden_t = transposed(hidden)
    finished(*later)
    cot = cot_ref[...]
    q, k, v, g = project(hidden, cot, w_ref, wo_ref)
    kt, vt, gt = transposed(k), transposed(v), transposed(g)
    step = math.gcd(tokens, QUERY_BLOCK)
    query = lax.broadcasted_iota(jnp.int32, (step, 2 * step), 1) % step
    mask = query >= lax.broadcasted_iota(jnp.int32, (step, 2 * step), 0)
    pairs = [slice(i * 2 * HD, (i + 1) * 2 * HD) for i in range(HH // 2)]
    att_blocks, dq_blocks = [], []
    for start in range(0, tokens, step):
        rows, keys = slice(start, start + step), slice(0, start + step)
        items = [
            (
                head_pair(q[rows, lanes]), head_pair(g[rows, lanes]), gt[lanes, rows],
                k[keys, lanes], v[keys, lanes], kt[lanes, keys], vt[lanes, keys],
            )
            for lanes in pairs
        ]
        results = pair_steps(items, step, mask)
        for lanes, (_, _, dk, dv) in zip(pairs, results):
            dk_ref[keys, lanes] += dk
            dv_ref[keys, lanes] += dv
        att_blocks.append(jnp.concatenate([result[0] for result in results], 0))
        dq_blocks.append(jnp.concatenate([result[1] for result in results], 0))
    grads_ref[:, :HW] = transposed(jnp.concatenate(dq_blocks, 1))
    grads_ref[:, HW : 2 * HW] = dk_ref[...].astype(BF16)
    grads_ref[:, 2 * HW :] = dv_ref[...].astype(BF16)
    term_qkv = dot_nn(hidden_t, grads_ref[...]).astype(BF16)
    out_ref[...] = dot_nn(jnp.concatenate(att_blocks, 1), cot).astype(BF16)
    grad_normed = dot_nt(grads_ref[...], w_ref[...]) * gain_ref[...]
    base_ref[...] = input_grad(
        cot_ref[...].astype(F32), normed_ref[...], inverse_ref[...], grad_normed
    )
    return term_qkv


def row_kernel(x_any, cot_any, gain_any, wqkv_any, wout_any, qkv_ref, *refs):
    qkv_ref[...] = row_part(x_any, cot_any, gain_any, wqkv_any, wout_any, *refs)


def row_chip_kernel(
    x_any, cot_any, gain_any, wqkv_any, wout_any,
    send_1, send_2, keep_1, keep_2, rows_ref, col_w_ref, col_wo_ref, *refs,
):
    chip, core, _ = here()
    sems, rows = refs[-1], rows_ref.shape[0]
    at = pl.multiple_of((chip * 2 + core) * rows, rows)
    handed = started(
        pltpu.make_async_copy(wqkv_any.at[pl.ds(at, rows), :], rows_ref, sems.at[7]),
        *weight_copies(wqkv_any, wout_any, col_w_ref, col_wo_ref, sems.at[pl.ds(8, 4)], 1),
    )
    term_qkv = row_part(x_any, cot_any, gain_any, wqkv_any, wout_any, *refs)
    chips, cut = send_1.shape[0], keep_1.shape[2]
    pieces = slice(0, chips), slice(0, cut)
    split_cores(term_qkv[:, :cut], send_1, keep_1, *pieces)
    split_cores(term_qkv[:, cut:], send_2, keep_2, *pieces)
    finished(*handed)


def column_part(x, cot, mask, gain, w_ref, wo_ref, weight_waits, grads_ref):
    tokens, block = x.shape[0], mask.shape[0]
    _, normed = rms_parts(x.astype(F32))
    hidden = (normed * gain).astype(BF16)
    finished(*weight_waits)
    q, k, v, g = project(hidden, cot, w_ref, wo_ref)
    kt, vt, gt = transposed(k), transposed(v), transposed(g)
    pairs = [slice(i * 2 * HD, (i + 1) * 2 * HD) for i in range(HH // 2)]
    blocks = [slice(at, at + block) for at in range(0, tokens, block)]
    items = [
        (
            head_pair(q[rows, lanes]), head_pair(g[rows, lanes]), gt[lanes, rows],
            k[rows, lanes], v[rows, lanes], kt[lanes, rows], vt[lanes, rows],
        )
        for lanes in pairs
        for rows in blocks
    ]
    results = pair_steps(items, block, mask)
    places = [(lanes, rows) for lanes in pairs for rows in blocks]
    for (lanes, rows), (_, _, dk, dv) in zip(places, results):
        grads_ref[rows, HW + lanes.start : HW + lanes.stop] = dk.astype(BF16)
        grads_ref[rows, 2 * HW + lanes.start : 2 * HW + lanes.stop] = dv.astype(BF16)
    by_pair = [results[i * len(blocks) : (i + 1) * len(blocks)] for i in range(len(pairs))]
    attended, grad_q = [
        jnp.concatenate([jnp.concatenate([r[i] for r in some], 1) for some in by_pair], 0)
        for i in range(2)
    ]
    grads_ref[:, :HW] = transposed(grad_q)
    term_qkv = dot_nn(transposed(hidden), grads_ref[...]).astype(BF16)
    term_out = dot_nn(attended, cot).astype(BF16)
    return term_qkv, term_out


def column_mask(all_rows, group, row_of):
    block = all_rows * group
    shape = (block, 2 * block)
    query = lax.broadcasted_iota(jnp.int32, shape, 1) % block
    key = lax.broadcasted_iota(jnp.int32, shape, 0)
    same_column = query % group == key % group
    return (row_of(query // group) >= row_of(key // group)) & same_column


def column_kernel(
    moved_any, gain_any, wqkv_any, wout_any, row_qkv_ref, row_out_ref,
    terms_ref, grads_ref, w_ref,
    moved_ref, gain_ref, wo_ref, sems,
):
    copies = started(
        pltpu.make_async_copy(moved_any, moved_ref, sems.at[4]),
        pltpu.make_async_copy(gain_any, gain_ref, sems.at[5]),
    )
    weights = started(*weight_copies(wqkv_any, wout_any, w_ref, wo_ref, sems, 1))
    finished(*copies)
    all_rows, _, share, width = moved_ref.shape
    group = math.gcd(share, 16)
    x, cot = [
        jnp.concatenate(
            [
                moved_ref[:, which, at : at + group, :].astype(F32).reshape(all_rows * group, width)
                for at in range(0, share, group)
            ],
            0,
        ).astype(BF16)
        for which in range(2)
    ]
    mask = column_mask(all_rows, group, lambda place: place)
    term_qkv, term_out = column_part(
        x, cot, mask, gain_ref[...], w_ref, wo_ref, weights, grads_ref
    )
    for i in range(3):
        at = i * width
        terms_ref[:, at : at + HW] = row_qkv_ref[:, i * HW : (i + 1) * HW]
        terms_ref[:, at + HW : at + 2 * HW] = term_qkv[:, i * HW : (i + 1) * HW]
    terms_ref[:HW, 3 * width :] = row_out_ref[...]
    terms_ref[HW:, 3 * width :] = term_out


def column_chip_kernel(
    x_ref, cot_ref, swapped_ref, corner_ref, near_2, near_3, far_ref, gain_ref, w_ref, wo_ref, row_out_ref,
    send_ref, keep_ref, grads_ref,
):
    chip, core, _ = here()
    share = far_ref.shape[2]
    half = pl.ds(pl.multiple_of(core * share, share), share)
    at = pl.ds(pl.multiple_of((chip * 2 + core) * share, share), share)
    group = math.gcd(share, 16)

    def tokens(which, mine):
        pieces = [
            mine[at, :], swapped_ref[0, which], corner_ref[0, which], corner_ref[1, which],
        ]
        for i, near in enumerate((near_2, near_3)):
            pieces += [near[which, half, :], far_ref[i, which]]
        starts = range(0, share, group)
        return jnp.concatenate(
            [piece[start : start + group] for start in starts for piece in pieces], 0
        )

    def row_of(place):
        step = (4 - (place >> 1)) & 3
        return ((step ^ chip) << 1) + ((place & 1) ^ core)

    mask = column_mask(2 * (len(CHIP_STEPS) + 1), group, row_of)
    term_qkv, term_out = column_part(
        tokens(0, x_ref), tokens(1, cot_ref), mask, gain_ref[...], w_ref, wo_ref, (), grads_ref
    )
    chips = send_ref.shape[0]
    refs = send_ref, keep_ref
    out_lanes = slice(3 * HW, send_ref.shape[2])
    split_cores(term_qkv, *refs, slice(0, chips), slice(0, 3 * HW))
    split_cores(row_out_ref[...], *refs, slice(0, chips // 2), out_lanes)
    split_cores(term_out, *refs, slice(chips // 2, chips), out_lanes)


def far_kernel(near_2, near_3, far_ref):
    share = far_ref.shape[2]
    at = pl.ds(pl.multiple_of((1 - here()[1]) * share, share), share)
    for i, near in enumerate((near_2, near_3)):
        far_ref[i] = near[:, at, :]


def back_kernel(grads_ref, w_ref, back_ref):
    grad_hidden = dot_nt(grads_ref[...], w_ref[...])
    all_rows, share, width = back_ref.shape
    group = math.gcd(share, 16)
    block = all_rows * group
    for i in range(share // group):
        piece = grad_hidden[i * block : (i + 1) * block].reshape(all_rows, group, width)
        back_ref[:, i * group : (i + 1) * group, :] = piece.astype(BF16)


def back_chip_kernel(grads_ref, w_ref, send_ref, keep_ref):
    grad_hidden = dot_nt(grads_ref[...], w_ref[...]).astype(BF16)
    chips, share, width = keep_ref.shape
    group = math.gcd(share, 16)
    block = 2 * chips * group
    for i in range(share // group):
        piece = grad_hidden[i * block : (i + 1) * block].reshape(chips, 2, group, width)
        at = slice(i * group, (i + 1) * group)
        keep_ref[:, at, :], send_ref[:, at, :] = piece[:, 0], piece[:, 1]


def back_pack_kernel(keep_ref, got_ref, *targets):
    share = keep_ref.shape[1]
    core = here()[1]
    kept_at = pl.ds(pl.multiple_of(core * share, share), share)
    got_at = pl.ds(pl.multiple_of((1 - core) * share, share), share)
    for i, target in enumerate(targets):
        target[kept_at, :] = keep_ref[i]
        target[got_at, :] = got_ref[i]


def input_kernel(base_ref, normed_ref, inverse_ref, gain_ref, back_ref, grad_ref):
    grad_ref[...] = input_grad(
        base_ref[...], normed_ref[...], inverse_ref[...], back_ref[...].astype(F32) * gain_ref[...]
    ).astype(BF16)


def input_grad(base, normed, inverse_rms, grad_normed):
    projected = jnp.mean(grad_normed * normed, -1, keepdims=True)
    return base + inverse_rms * (grad_normed - normed * projected)


def input_chip_kernel(
    base_ref, normed_ref, inverse_ref, gain_ref, own_ref, got_1, got_2, got_3,
    grad_any, grad_ref, sems,
):
    chip = here()[0]
    count = own_ref.shape[0]
    copies = []
    for i, (step, back_ref) in enumerate(zip((0, *CHIP_STEPS), (own_ref, got_1, got_2, got_3))):
        at = pl.ds(pl.multiple_of((chip ^ step) * count, count), count)
        grad_normed = back_ref[...].astype(F32) * gain_ref[...]
        grad = input_grad(base_ref[at, :], normed_ref[at, :], inverse_ref[at, :], grad_normed)
        grad_ref[i] = grad.astype(BF16)
        copies += started(pltpu.make_async_copy(grad_ref.at[i], grad_any.at[at, :], sems.at[i]))
    finished(*copies)


def pack_kernel(x_any, cot_any, swap_ref, corner_ref, off_2, off_3, sems):
    chip, core, _ = here()
    share = corner_ref.shape[1]

    def columns(step, of_core):
        return pl.multiple_of(((chip ^ step) * 2 + of_core) * share, share)

    corner = CHIP_STEPS[0]
    copies = []
    for which, source in enumerate((x_any, cot_any)):
        pieces = [
            (columns(0, 1 - core), share, swap_ref.at[0, which]),
            (columns(corner, 1 - core), share, swap_ref.at[1, which]),
            (columns(corner, core), share, corner_ref.at[which]),
            (columns(CHIP_STEPS[1], 0), 2 * share, off_2.at[which]),
            (columns(CHIP_STEPS[2], 0), 2 * share, off_3.at[which]),
        ]
        for i, (at, count, target) in enumerate(pieces):
            copies.append(
                pltpu.make_async_copy(
                    source.at[pl.ds(at, count), :], target, sems.at[5 * which + i]
                )
            )
    finished(*started(*copies))


def corner_kernel(corner_ref, swapped_ref, out_ref):
    out_ref[0], out_ref[1] = corner_ref[...], swapped_ref[1]


def split_rows(total, axis):
    upper = (here()[2] & 1) == 1
    low, high = jnp.split(total, 2, axis)
    return jnp.where(upper, low, high).astype(BF16), jnp.where(upper, high, low)


def row_cores_kernel(keep_1, keep_2, got_1, got_2, send_ref, kept_ref):
    total = [
        keep_ref[...].astype(F32) + got_ref[...].astype(F32)
        for keep_ref, got_ref in ((keep_1, got_1), (keep_2, got_2))
    ]
    send_ref[...], kept_ref[...] = split_rows(jnp.concatenate(total, 2), 1)


def cores_kernel(keep_ref, got_ref, send_ref, kept_ref, *targets):
    chip, cut = here()[0], kept_ref.shape[2]
    first = keep_ref[:, :, :cut].astype(F32) + got_ref[:, :, :cut].astype(F32)
    send_ref[...], kept_ref[...] = split_rows(first, 1)
    for step, target in zip((0, *CHIP_STEPS), targets):
        there = chip ^ step
        total = keep_ref[there, :, cut:].astype(F32) + got_ref[there, :, cut:].astype(F32)
        target[...] = total.astype(target.dtype)


def pair_kernel(kept_ref, got_ref, row_kept, row_got, *targets):
    chip, cut = here()[0], kept_ref.shape[2]
    for step, target in zip((0, *CHIP_STEPS), targets):
        there = chip ^ step
        total = kept_ref[there] + got_ref[there].astype(F32)
        target[:, :cut] = total.astype(target.dtype)
        total = row_kept[there] + row_got[there].astype(F32)
        target[:, cut:] = total.astype(target.dtype)


def layer_sum(own_ref, got_1, got_2, got_3):
    return own_ref[...] + (
        (got_1[...].astype(F32) + got_2[...].astype(F32)) + got_3[...].astype(F32)
    )


def layer_kernel(own_ref, got_1, got_2, got_3, send_ref, kept_ref):
    send_ref[...], kept_ref[...] = split_rows(layer_sum(own_ref, got_1, got_2, got_3), 0)


def join_kernel(own_ref, got_1, got_2, got_3, kept_ref, got_ref, out_ref):
    total = layer_sum(own_ref, got_1, got_2, got_3).astype(BF16)
    cut, width = FIRST_PART, kept_ref.shape[1]
    out_ref[:, :cut] = total[:, :cut]
    out_ref[:, cut : cut + width] = (kept_ref[...] + got_ref[...].astype(F32)).astype(BF16)
    out_ref[:, cut + width :] = total[:, cut:]


def add_kernel(kept_ref, got_ref, out_ref):
    out_ref[...] = (kept_ref[...].astype(F32) + got_ref[...].astype(F32)).astype(BF16)


def result_kernel(held_ref, got_ref, w_ref, gain_ref, qkv_ref, out_ref, grad_ref):
    rows = qkv_ref.shape[0]
    chip, core, layer = here()
    at = (chip * 2 + core) * rows
    upper = (layer & 1) == 1
    half = rows // 2
    width = out_ref.shape[1]

    def ordered(lanes):
        held, got = held_ref[:, lanes].astype(F32), got_ref[:, lanes].astype(F32)
        return (jnp.where(upper, got, held), jnp.where(upper, held, got))

    row_at = 3 * HW + width
    for i in range(3):
        for at_from, at_to in ((row_at + i * HW, i * width), (i * HW, i * width + HW)):
            to = slice(at_to, at_to + HW)
            qkv_ref[:half, to], qkv_ref[half:, to] = ordered(slice(at_from, at_from + HW))
    out_ref[:half], out_ref[half:] = ordered(slice(3 * HW, row_at))
    total = jnp.sum(qkv_ref[...] * w_ref[...].astype(F32), -1, keepdims=True)
    shape = (rows, gain_ref.shape[1])
    row = lax.broadcasted_iota(jnp.int32, shape, 0)
    feature = lax.broadcasted_iota(jnp.int32, shape, 1)
    gain = jnp.sum(jnp.where(feature == row + at, gain_ref[...], 0.0), -1, keepdims=True)
    shape = (rows, grad_ref.shape[1])
    same = lax.broadcasted_iota(jnp.int32, shape, 0) == lax.broadcasted_iota(jnp.int32, shape, 1)
    grad_ref[...] = jnp.sum(jnp.where(same, total / gain, 0.0), 0, keepdims=True)


def call(kernel, name, ins, outs, scratch=(), vmem=SMALL_VMEM, out_specs=None):
    out_specs = out_specs or [VMEM] * len(outs)
    places = [{id(HBM): pltpu.HBM, id(PINNED): pltpu.VMEM}.get(id(spec)) for spec in out_specs]
    outs = [place(*out) if place else shaped(*out) for place, out in zip(places, outs)]
    args = [
        pltpu.with_memory_space_constraint(array, pltpu.HBM) if spec is HBM else array
        for spec, array in ins
    ]
    return pl.pallas_call(
        kernel,
        out_shape=outs,
        in_specs=[spec for spec, _ in ins],
        out_specs=out_specs,
        scratch_shapes=scratch,
        name=name,
        cost_estimate=pl.CostEstimate(flops=0, bytes_accessed=0, transcendentals=0),
        compiler_params=pltpu.CompilerParams(vmem_limit_bytes=vmem),
    )(*args)


def swap(array, axis, bits):
    count = lax.axis_size(axis)
    return lax.ppermute(array, axis, [(i, i ^ bits) for i in range(count)])


def cross_chips(*offs):
    return [swap(off, "seq", 2 * step) for off, step in zip(offs, CHIP_STEPS)]


def add_two(kept, got, name):
    (total,) = call(add_kernel, name, [(VMEM, kept), (VMEM, got)], [(kept.shape, BF16)])
    return total


def body(inputs, norm_gain, qkv_weight, out_weight, out_cotan):
    columns, width = inputs.shape[2:]
    n = lax.axis_size("seq")
    m = lax.axis_size("dp")
    share = columns // n
    row_share = width // n
    row_width, col_width = 3 * HW, 3 * HW + width
    x = inputs.reshape(columns, width)
    cot = out_cotan.reshape(columns, width)
    gain = norm_gain.reshape(1, width)
    chips = 4
    layered = n == 2 * chips and m == 4 and row_share == share
    weight_scratch = [
        pltpu.VMEM((1, width), F32),
        pltpu.VMEM((width, 3 * HW), BF16),
        pltpu.VMEM((HW, width), BF16),
    ]
    weights = [(HBM, gain), (HBM, qkv_weight), (HBM, out_weight)]
    col_outs = [((columns, 3 * HW), BF16), ((width, 3 * HW), BF16)]

    if layered:
        packed = call(
            pack_kernel,
            "pack_columns",
            [(HBM, x), (HBM, cot)],
            [((2, 2, share, width), BF16), ((2, share, width), BF16)]
            + [((2, 2 * share, width), BF16)] * 2,
            [pltpu.SemaphoreType.DMA((10,))],
            out_specs=[ANY] * 4,
        )
        near = [swap(one, "seq", 2 * step) for one, step in zip(packed[2:], CHIP_STEPS[1:])]
        swapped = swap(packed[0], "seq", 1)
        (corner,) = call(
            corner_kernel,
            "pack_corner",
            [(VMEM, packed[1]), (VMEM, swapped)],
            [((2, 2, share, width), BF16)],
        )
        x_first, _ = lax.optimization_barrier((x, corner))
        corner = swap(corner, "seq", 2 * CHIP_STEPS[0])
    else:
        outgoing = jnp.stack([x.reshape(n, share, width), cot.reshape(n, share, width)], 1)
        moved = lax.all_to_all(outgoing, "seq", split_axis=0, concat_axis=0, tiled=True)
        x_first = x

    row_outs = [
        ((HW, width), BF16),
        ((columns, width), F32), ((columns, width), F32), ((columns, 1), F32),
        ((columns, width), BF16), ((columns, width), BF16),
    ]
    if layered:
        cut = row_width // 2
        split_outs = [((chips, row_share, cut), BF16)] * 4
        handed_outs = [
            ((row_share, 3 * width), BF16), ((width, 3 * HW), BF16), ((HW, width), BF16),
        ]
        row_outs = [*split_outs, *handed_outs, *row_outs]
        specs = [VMEM] * 4 + [PINNED] * (len(row_outs) - 4)
    else:
        row_outs = [((width, row_width), BF16), *row_outs]
        specs = [VMEM] * len(row_outs)
    *row_terms, row_out, base, normed, inverse_rms, x_near, cot_near = call(
        row_chip_kernel if layered else row_kernel,
        "row_heads",
        [(HBM, x_first), (HBM, cot), *weights],
        row_outs,
        [
            *weight_scratch,
            pltpu.VMEM((columns, HW), F32),
            pltpu.VMEM((columns, HW), F32),
            pltpu.VMEM((columns, 3 * HW), BF16),
            pltpu.SemaphoreType.DMA((12,)),
        ],
        BIG_VMEM,
        specs,
    )
    if layered:
        *row_terms, weight_rows, col_weight, col_out_weight = row_terms
        row_sent = [swap(one, "seq", 1) for one in row_terms[:2]]
        half_block = (chips, row_share // 2, row_width)
        row_next, row_kept = call(
            row_cores_kernel,
            "row_add_cores",
            [(VMEM, one) for one in (*row_terms[2:], *row_sent)],
            [(half_block, BF16), (half_block, F32)],
            out_specs=[VMEM, PINNED],
        )
        col_weight, row_kept = lax.optimization_barrier((col_weight, row_kept))
        *near, base = lax.optimization_barrier((*near, base))
        (far,) = call(
            far_kernel,
            "pack_other_core",
            [(VMEM, one) for one in near],
            [((2, 2, share, width), BF16)],
        )
        send, keep, col_grads = call(
            column_chip_kernel,
            "column_heads",
            [
                (VMEM, one)
                for one in (
                    x_near, cot_near, swapped, corner, *near, swap(far, "seq", 1),
                    gain, col_weight, col_out_weight, row_out,
                )
            ],
            [((chips, row_share, col_width), BF16)] * 2 + [col_outs[0]],
            vmem=BIG_VMEM,
            out_specs=[VMEM, VMEM, PINNED],
        )
        back_send, back_keep = call(
            back_chip_kernel,
            "column_grad_hidden",
            [(VMEM, col_grads), (VMEM, col_weight)],
            [((chips, share, width), BF16)] * 2,
        )
        row_next, _ = lax.optimization_barrier((row_next, send))
        keep, back_keep = lax.optimization_barrier((keep, back_keep))
        first_half = (chips, row_share // 2, FIRST_PART)
        second = (row_share, col_width - FIRST_PART)
        to_next, kept, owned, *off = call(
            cores_kernel,
            "column_add_cores",
            [(VMEM, keep), (VMEM, swap(send, "seq", 1))],
            [(first_half, BF16), (first_half, F32), (second, F32)] + [(second, BF16)] * 3,
            out_specs=[VMEM, PINNED, PINNED, VMEM, VMEM, VMEM],
        )
        got = cross_chips(*off)
        back = call(
            back_pack_kernel,
            "pack_grad_hidden",
            [(VMEM, back_keep), (VMEM, swap(back_send, "seq", 1))],
            [((2 * share, width), BF16)] * 4,
        )
        row_kept, *back = lax.optimization_barrier((row_kept, *back))
        joint = (row_share // 2, FIRST_PART + row_width)
        first_owned, *off = call(
            pair_kernel,
            "first_add_pair",
            [
                (VMEM, one)
                for one in (kept, swap(to_next, "dp", 1), row_kept, swap(row_next, "dp", 1))
            ],
            [(joint, F32)] + [(joint, BF16)] * 3,
            out_specs=[PINNED, VMEM, VMEM, VMEM],
        )
        first_got = cross_chips(*off)
        second_half = (row_share // 2, second[1])
        to_next, kept = call(
            layer_kernel,
            "second_add_chips",
            [(VMEM, one) for one in (owned, *got)],
            [(second_half, BF16), (second_half, F32)],
            out_specs=[VMEM, PINNED],
        )
        (pair_sum,) = call(
            join_kernel,
            "join_terms",
            [(VMEM, one) for one in (first_owned, *first_got, kept, swap(to_next, "dp", 1))],
            [((row_share // 2, col_width + row_width), BF16)],
        )
        *back, pair_sum = lax.optimization_barrier((*back, pair_sum))
        held = add_two(pair_sum, swap(pair_sum, "dp", 2), "add_pairs")
        other = swap(held, "dp", 1)
        (grad,) = call(
            input_chip_kernel,
            "input_grad",
            [
                (VMEM, one)
                for one in (base, normed, inverse_rms, gain, back[0], *cross_chips(*back[1:]))
            ],
            [((columns, width), BF16)],
            [pltpu.VMEM((chips, 2 * share, width), BF16), pltpu.SemaphoreType.DMA((chips,))],
            out_specs=[HBM],
        )
        sum_qkv, sum_out, sum_gain = call(
            result_kernel,
            "result",
            [(VMEM, held), (VMEM, other), (VMEM, weight_rows), (VMEM, gain)],
            [((row_share, 3 * width), F32), ((row_share, width), F32), ((1, row_share), F32)],
        )
        sum_gain = sum_gain.reshape(row_share)
    else:
        terms, *col_grads = call(
            column_kernel,
            "column_heads",
            [(ANY, moved), *weights, (VMEM, row_terms[0]), (VMEM, row_out)],
            [((width, 4 * width), BF16), *col_outs],
            [
                pltpu.VMEM((n, 2, share, width), BF16),
                weight_scratch[0],
                weight_scratch[2],
                pltpu.SemaphoreType.DMA((6,)),
            ],
            BIG_VMEM,
        )
        (back,) = call(
            back_kernel,
            "column_grad_hidden",
            [(VMEM, one) for one in col_grads],
            [((n, share, width), BF16)],
        )
        returned = lax.all_to_all(back, "seq", split_axis=0, concat_axis=0, tiled=True)
        (grad,) = call(
            input_kernel,
            "input_grad",
            [
                (VMEM, base), (VMEM, normed), (VMEM, inverse_rms), (VMEM, gain),
                (VMEM, returned.reshape(columns, width)),
            ],
            [((columns, width), BF16)],
        )
        terms = lax.all_to_all(
            terms.reshape(n, row_share, 4 * width), "seq", split_axis=0, concat_axis=0, tiled=True
        )
        total = jnp.sum(terms.astype(F32), 0)
        for step in range(m.bit_length() - 1):
            sent = total.astype(BF16)
            total = sent.astype(F32) + swap(sent, "dp", 1 << step).astype(F32)
        sum_qkv, sum_out = total[:, : 3 * width], total[:, 3 * width :]
        here_at = lax.axis_index("seq") * row_share
        own_gain = lax.dynamic_slice_in_dim(norm_gain, here_at, row_share, 0)
        own_weight = lax.dynamic_slice_in_dim(qkv_weight, here_at, row_share, 0)
        sum_gain = jnp.sum(sum_qkv * own_weight.astype(F32), -1) / own_gain
    return (grad.reshape(inputs.shape), sum_qkv, sum_out, sum_gain)


def solution(mesh):
    return jax.shard_map(
        body,
        mesh=mesh,
        in_specs=(P("dp", "seq", None, None), P(), P(), P(), P("dp", "seq", None, None)),
        out_specs=(P("dp", "seq", None, None), P("seq", None), P("seq", None), P("seq")),
        check_vma=False,
    )
```
